32 devices in a mesh: shard: 4 (over z), ctx: 2 (over x), tp: 4 (over y, core).
Axes of the slice: x: 2, y: 2, z: 4, core: 2. Of those that a mesh axis runs over, the one named last changes fastest.
Arguments:
- hidden_in: bfloat16 [2048, 2048], P(('shard', 'ctx')), may hold values from -6 to 6
- att_choice: int32 [2048, 2], P(('shard', 'ctx')), may hold values from 0 to 3, all different within a row
- ffn_choice: int32 [2048, 2], P(('shard', 'ctx')), may hold values from 0 to 3, all different within a row
- span_ids: int32 [2048], P('shard'), may hold values from 0 to 8, as said below
- norm_att: bfloat16 [2048], P(('shard', 'ctx')), may hold values from 0.5 to 1.5
- router_att: bfloat16 [2048, 4], P(('shard', 'ctx')), may hold values from -0.09375 to 0.09375
- w_query: bfloat16 [4, 2048, 2048], P(None, ('shard', 'ctx'), 'tp'), may hold values from -0.125 to 0.125
- w_out: bfloat16 [4, 2048, 2048], P(None, 'tp', ('shard', 'ctx')), may hold values from -2 to 2
- w_key: bfloat16 [2048, 2048], P(('shard', 'ctx'), 'tp'), may hold values from -0.125 to 0.125
- w_value: bfloat16 [2048, 2048], P(('shard', 'ctx'), 'tp'), may hold values from -0.125 to 0.125
- norm_ffn: bfloat16 [2048], P(('shard', 'ctx')), may hold values from 0.5 to 1.5
- router_ffn: bfloat16 [2048, 4], P(('shard', 'ctx')), may hold values from -0.09375 to 0.09375
- w_gate: bfloat16 [4, 2048, 5632], P(None, ('shard', 'ctx'), 'tp'), may hold values from -0.125 to 0.125
- w_up: bfloat16 [4, 2048, 5632], P(None, ('shard', 'ctx'), 'tp'), may hold values from -0.125 to 0.125
- w_down: bfloat16 [4, 5632, 2048], P(None, 'tp', ('shard', 'ctx')), may hold values from -0.078125 to 0.078125
- cotangent: bfloat16 [2048, 2048], P(('shard', 'ctx')), may hold values from -6 to 6
Outputs:
- hidden_out: bfloat16 [2048, 2048], P(('shard', 'ctx'))
- grad_in: float32 [2048, 2048], P(('shard', 'ctx'))
- grad_norm_att: float32 [2048], P(('shard', 'ctx'))
- grad_router_att: float32 [2048, 4], P(('shard', 'ctx'))
- grad_query: float32 [4, 2048, 2048], P(None, ('shard', 'ctx'), 'tp')
- grad_out: float32 [4, 2048, 2048], P(None, 'tp', ('shard', 'ctx'))
- grad_key: float32 [2048, 2048], P(('shard', 'ctx'), 'tp')
- grad_value: float32 [2048, 2048], P(('shard', 'ctx'), 'tp')
- grad_norm_ffn: float32 [2048], P(('shard', 'ctx'))
- grad_router_ffn: float32 [2048, 4], P(('shard', 'ctx'))
- grad_gate: float32 [4, 2048, 5632], P(None, ('shard', 'ctx'), 'tp')
- grad_up: float32 [4, 2048, 5632], P(None, ('shard', 'ctx'), 'tp')
- grad_down: float32 [4, 5632, 2048], P(None, 'tp', ('shard', 'ctx'))
The draws below stay inside these ranges and needn't reach their ends.
Inputs may be any that keep to these rules, and one draw needn't show every extreme that they name: `span_ids`: each sequence holds two picture spans with ids of their own, one of them covering its middle token; a span has at most 256 consecutive tokens. `att_choice`: each token names two different attention experts. `ffn_choice`: each token names two different feed-forward experts.
All inputs are finite; a program needn't handle non-finite values.
Results may differ from the reference program's by a relative error of at most 0.02.
Values may be sent and summed in bfloat16 or wider, within the bound.
A program may use at most 512 MiB of HBM per device.

```python
import math
import jax
import jax.numpy as jnp
from jax import lax

D = 2048
H = 16
HD = 128
FF = 5632
EA = 4
EF = 4
IMG = 256
SEQ = 512
TOKENS = 2048
N_SHARD = 4


def draw_span_ids(key, part):
    key = jax.random.fold_in(key, 7)
    middle_key, early_key = jax.random.split(key)
    half_len = SEQ // 2
    middle_start = jax.random.randint(middle_key, (N_SHARD, 1), half_len - IMG + 1, half_len)
    early_start = jax.random.randint(early_key, (N_SHARD, 1), 0, half_len - IMG + 1)
    positions = jnp.arange(SEQ, dtype=jnp.int32)[None, :]
    sequence = jnp.arange(N_SHARD, dtype=jnp.int32)[:, None]
    in_middle = (positions >= middle_start) & (positions < middle_start + IMG)
    in_early = (positions >= early_start) & (positions < early_start + IMG)
    span_table = jnp.where(in_middle, 2 * sequence + 1, jnp.where(in_early, 2 * sequence + 2, 0))
    return span_table.reshape(-1).astype(jnp.int32)


def shard_levels(own_key, shape, shards, low, largest):
    loudness, own = 1.0, jax.random.fold_in(own_key, 6)
    for axis_at, parts in shards:
        steps = jnp.exp(jax.random.uniform(jax.random.fold_in(own, axis_at), (parts,), jnp.float32, low / len(shards), largest / len(shards)))
        loudness = loudness * jnp.repeat(steps, shape[axis_at] // parts).reshape([-1 if axis == axis_at else 1 for axis in range(len(shape))])
    return loudness


def choose_distinct(stream_key, rows, count, top, lift):
    ranking = jax.random.permutation(jax.random.fold_in(stream_key, 1), count)
    pull = ranking
    for power in range(3):
        pull = pull * pull // count
    pull = pull * lift // count
    tickets = jax.random.randint(jax.random.fold_in(stream_key, 2), (rows, count), 0, 4096) + pull
    sure = jax.random.permutation(jax.random.fold_in(stream_key, 3), rows)[jnp.arange(count) % rows]
    tickets = jnp.where(jnp.arange(rows)[:, None] == sure[None, :], 1 << 14, tickets)
    priority = tickets * count + jnp.arange(count)
    return lax.top_k(priority.astype(jnp.int32), top)[1].astype(jnp.int32)


def bell_draw(key, extent, scale, most, shards=(), kind=jnp.bfloat16):
    level = shard_levels(key, extent, shards, -0.22, 0.18) if shards else 1.0
    array = jax.random.normal(key, extent, jnp.float32) * scale * level
    return jnp.minimum(jnp.maximum(array, -most), most).astype(kind)


def setup_inputs(seed: int = 0) -> dict:
    keys = jax.random.split(jax.random.key(seed), 17)
    hidden_in = bell_draw(keys[0], (TOKENS, D), 1.0, 6.0, ((0, 8),))
    att_choice = choose_distinct(keys[1], TOKENS, EA, 2, 4096)
    ffn_choice = choose_distinct(keys[2], TOKENS, EF, 2, 4096)
    span_ids = draw_span_ids(jax.random.fold_in(keys[16], 71), 0)
    norm_att = jnp.clip(1.0 + 0.1 * jax.random.normal(keys[4], (D,), jnp.float32), 0.5, 1.5).astype(jnp.bfloat16)
    router_att = bell_draw(keys[5], (D, EA), (2 * D) ** -0.5, 0.09375, ((0, 8),))
    w_query = bell_draw(keys[6], (EA, D, H * HD), D ** -0.5, 0.125, ((1, 8), (2, 4)))
    w_out = bell_draw(keys[7], (EA, H * HD, D), 8 ** -0.5, 2.0, ((1, 4), (2, 8)))
    w_key = bell_draw(keys[8], (D, H * HD), D ** -0.5, 0.125, ((0, 8), (1, 4)))
    w_value = bell_draw(keys[9], (D, H * HD), D ** -0.5, 0.125, ((0, 8), (1, 4)))
    norm_ffn = jnp.clip(1.0 + 0.1 * jax.random.normal(keys[10], (D,), jnp.float32), 0.5, 1.5).astype(jnp.bfloat16)
    router_ffn = bell_draw(keys[11], (D, EF), (2 * D) ** -0.5, 0.09375, ((0, 8),))
    w_gate = bell_draw(keys[12], (EF, D, FF), D ** -0.5, 0.125, ((1, 8), (2, 4)))
    w_up = bell_draw(keys[13], (EF, D, FF), D ** -0.5, 0.125, ((1, 8), (2, 4)))
    w_down = bell_draw(keys[14], (EF, FF, D), FF ** -0.5, 0.078125, ((1, 4), (2, 8)))
    cotangent = bell_draw(keys[15], (TOKENS, D), 1.0, 6.0, ((0, 8),))
    return {"hidden_in": hidden_in, "att_choice": att_choice, "ffn_choice": ffn_choice, "span_ids": span_ids, "norm_att": norm_att, "router_att": router_att, "w_query": w_query, "w_out": w_out, "w_key": w_key, "w_value": w_value, "norm_ffn": norm_ffn, "router_ffn": router_ffn, "w_gate": w_gate, "w_up": w_up, "w_down": w_down, "cotangent": cotangent}


@jax.custom_vjp
def low(v):
    return lax.optimization_barrier(v.astype(jnp.bfloat16)).astype(jnp.float32)

@jax.custom_vjp
def low_back(v):
    return v

def low_keep(v):
    return (low(v), None)

def low_pass(kept, grad):
    return (grad,)

def back_keep(v):
    return (v, None)

def back_low(kept, grad):
    return (low(grad),)
low.defvjp(low_keep, low_pass)
low_back.defvjp(back_keep, back_low)

def dense_dot(left, right):
    return jnp.dot(left, right, precision=lax.Precision.HIGHEST, preferred_element_type=jnp.float32)

def rms_norm(rows_in, gain):
    return rows_in * lax.rsqrt(lax.optimization_barrier(jnp.mean(rows_in * rows_in, axis=-1, keepdims=True)) + 1e-06) * gain

def rope_tables(positions, head_dim):
    half_dim = head_dim // 2
    freq_index = (jnp.arange(head_dim) % half_dim).astype(jnp.float32)
    frequency = 10000.0 ** (-2.0 * freq_index / head_dim)
    angles = positions.astype(jnp.float32)[:, None] * frequency[None, :]
    return (jnp.cos(angles)[:, None, :], jnp.sin(angles)[:, None, :])

def rotate(head_rows, cosine_table, sine_table):
    half_dim = head_rows.shape[-1] // 2
    turned = jnp.concatenate([-head_rows[..., half_dim:], head_rows[..., :half_dim]], axis=-1)
    return head_rows * cosine_table + turned * sine_table

def choice_hits(choices, experts):
    return (choices[:, :, None] == jnp.arange(experts, dtype=jnp.int32)[None, None, :]).astype(jnp.int32)

def route_pairs(choices, experts, capacity, offset):
    hits_table = choice_hits(choices, experts)
    per_token = lax.optimization_barrier(jnp.sum(hits_table, axis=1))
    before = jnp.cumsum(per_token, axis=0) - per_token + offset[None, :]
    slot_place = lax.optimization_barrier(jnp.sum(hits_table * before[:, None, :], axis=2))
    kept_mask = slot_place < capacity
    slot_index = jnp.where(kept_mask, choices * capacity + slot_place, experts * capacity).astype(jnp.int32)
    return (slot_index, kept_mask)

def invert(slot_index, slot_count):
    source = jnp.broadcast_to(jnp.arange(slot_index.shape[0], dtype=jnp.int32)[:, None], slot_index.shape).reshape(-1)
    target = slot_index.reshape(-1)
    token_of_slot = jnp.zeros((slot_count + 1,), jnp.int32).at[target].set(source)[:slot_count]
    filled = jnp.zeros((slot_count + 1,), jnp.int32).at[target].set(1)[:slot_count]
    return (token_of_slot, filled)

def pick_gates(logits, choices):
    hits_table = choice_hits(choices, logits.shape[1]).astype(logits.dtype)
    picked = lax.optimization_barrier(jnp.sum(hits_table * logits[:, None, :], axis=2))
    return jax.nn.softmax(picked, axis=1)

def combine(branch_rows, slot_index, kept_mask, gate_values):
    index_rows = jnp.minimum(slot_index, branch_rows.shape[0] - 1)
    weights = gate_values * kept_mask.astype(gate_values.dtype)
    return lax.optimization_barrier(jnp.sum(branch_rows[index_rows] * weights[:, :, None], axis=1))

def allowed_keys(query_pos, span_table):
    key_pos = jnp.arange(span_table.shape[0], dtype=jnp.int32)
    query_span = span_table[query_pos]
    return (key_pos[None, :] <= query_pos[:, None]) | (query_span[:, None] == span_table[None, :]) & (query_span[:, None] > 0)

def attention(normed, router, w_query, w_out, w_key, w_value, choices, span_table):
    seq_len = normed.shape[0]
    experts = w_query.shape[0]
    capacity = 2 * seq_len // experts
    positions = jnp.arange(seq_len, dtype=jnp.int32)
    cosine_table, sine_table = rope_tables(positions, HD)
    key_rows = low(rotate(low_back(dense_dot(normed, w_key)).reshape(seq_len, -1, HD), cosine_table, sine_table))
    value_rows = low(low_back(dense_dot(normed, w_value))).reshape(seq_len, -1, HD)
    slot_index, kept_mask = route_pairs(choices, experts, capacity, jnp.zeros((experts,), jnp.int32))
    token_of_slot, filled = invert(slot_index, experts * capacity)
    gate_values = pick_gates(dense_dot(normed, router), choices)
    scale = 1.0 / math.sqrt(HD)

    def expert_apply(expert_item):
        expert_query, expert_out, row_ids, live_mask = expert_item
        taken_rows = normed[row_ids] * live_mask.astype(normed.dtype)[:, None]
        query_pre = low_back(dense_dot(taken_rows, expert_query)).reshape(capacity, -1, HD)
        query_rows = low(rotate(query_pre, cosine_table[row_ids], sine_table[row_ids]))
        scores = low_back(jnp.einsum('qhd,khd->hqk', query_rows, key_rows, precision=lax.Precision.HIGHEST) * scale)
        scores = jnp.where(allowed_keys(row_ids, span_table)[None], scores, -1e+30)
        soft_low = low(jax.nn.softmax(scores, axis=-1))
        mixed_heads = low_back(low(jnp.einsum('hqk,khd->qhd', soft_low, value_rows, precision=lax.Precision.HIGHEST)))
        return low_back(dense_dot(mixed_heads.reshape(capacity, -1), expert_out))
    branch = lax.map(jax.checkpoint(expert_apply), (w_query, w_out, token_of_slot.reshape(experts, capacity), filled.reshape(experts, capacity)))
    return combine(branch.reshape(experts * capacity, -1), slot_index, kept_mask, gate_values)

def feed_forward(normed, router, w_gate, w_up, w_down, choices):
    seq_len = normed.shape[0]
    experts = w_gate.shape[0]
    capacity = 2 * seq_len // experts
    slot_index, kept_mask = route_pairs(choices, experts, capacity, jnp.zeros((experts,), jnp.int32))
    token_of_slot, filled = invert(slot_index, experts * capacity)
    gate_values = pick_gates(dense_dot(normed, router), choices)

    def expert_apply(expert_item):
        expert_gate, expert_up, expert_down, row_ids, live_mask = expert_item
        taken_rows = normed[row_ids] * live_mask.astype(normed.dtype)[:, None]
        gate_pre = low_back(dense_dot(taken_rows, expert_gate))
        up_pre = low_back(dense_dot(taken_rows, expert_up))
        hidden = low(jax.nn.silu(gate_pre) * up_pre)
        return low_back(dense_dot(hidden, expert_down))
    branch = lax.map(expert_apply, (w_gate, w_up, w_down, token_of_slot.reshape(experts, capacity), filled.reshape(experts, capacity)))
    return combine(branch.reshape(experts * capacity, -1), slot_index, kept_mask, gate_values)

def whole_layer(rows_in, weights, att_pick, ffn_pick, span_table):
    norm_att, router_att, w_query, w_out, w_key, w_value, norm_ffn, router_ffn, w_gate, w_up, w_down = weights
    first_normed = low(rms_norm(rows_in, norm_att))
    mid_rows = rows_in + attention(first_normed, router_att, w_query, w_out, w_key, w_value, att_pick, span_table)
    second_normed = low(rms_norm(mid_rows, norm_ffn))
    return mid_rows + feed_forward(second_normed, router_ffn, w_gate, w_up, w_down, ffn_pick)

def reference(hidden_in, att_choice, ffn_choice, span_ids, norm_att, router_att, w_query, w_out, w_key, w_value, norm_ffn, router_ffn, w_gate, w_up, w_down, cotangent):
    params = tuple((weight.astype(jnp.float32) for weight in (norm_att, router_att, w_query, w_out, w_key, w_value, norm_ffn, router_ffn, w_gate, w_up, w_down)))
    width = hidden_in.shape[1]
    seq_count = span_ids.shape[0] // SEQ
    items = (hidden_in.astype(jnp.float32).reshape(seq_count, SEQ, width), att_choice.reshape(seq_count, SEQ, 2), ffn_choice.reshape(seq_count, SEQ, 2), span_ids.reshape(seq_count, SEQ), cotangent.astype(jnp.float32).reshape(seq_count, SEQ, width))

    def per_sequence(totals, seq_item):
        rows_in, att_pick, ffn_pick, span_table, grad_rows = seq_item

        def apply_layer(layer_in, *weights):
            return whole_layer(layer_in, weights, att_pick, ffn_pick, span_table)
        layer_out, pull_back = jax.vjp(apply_layer, rows_in, *params)
        grads = pull_back(grad_rows)
        return (tuple((total + grad for total, grad in zip(totals, grads[1:]))), (layer_out, grads[0]))
    totals, (outputs, grad_rows) = lax.scan(per_sequence, tuple((jnp.zeros_like(weight) for weight in params)), items)
    return (outputs.reshape(-1, width).astype(jnp.bfloat16), grad_rows.reshape(-1, width), totals[0], totals[1], totals[2], totals[3], totals[4], totals[5], totals[6], totals[7], totals[8], totals[9], totals[10])
```

```python
from functools import partial
import math

import numpy as np

import jax
import jax.numpy as jnp
from jax import lax
from jax.sharding import PartitionSpec as P

HD = 128
EPS = 1e-06
BF = jnp.bfloat16
F32 = jnp.float32
GROUP = ("shard", "ctx")
ALL = ("shard", "ctx", "tp")


def dot(spec, left, right):
    return jnp.einsum(spec, left, right, preferred_element_type=F32)


def dot_exact(spec, left, right):
    return jnp.einsum(
        spec, left, right, preferred_element_type=F32, precision=lax.Precision.HIGHEST
    )


def after(value, *others):
    return lax.optimization_barrier((value, *others))[0]


def rope_tables(count):
    half_dim = HD // 2
    freq_index = (jnp.arange(HD) % half_dim).astype(F32)
    frequency = 10000.0 ** (-2.0 * freq_index / HD)
    angles = jnp.arange(count, dtype=F32)[:, None] * frequency[None, :]
    return jnp.cos(angles), jnp.sin(angles)


def rotate(rows, cosine, sine):
    half_dim = HD // 2
    turned = jnp.concatenate([-rows[..., half_dim:], rows[..., :half_dim]], axis=-1)
    return rows * cosine + turned * sine


def rotate_back(rows, cosine, sine):
    half_dim = HD // 2
    turned = rows * sine
    return rows * cosine + jnp.concatenate(
        [turned[..., half_dim:], -turned[..., :half_dim]], axis=-1
    )


class Axes:
    def __init__(self, experts, shard, ctx, tp):
        self.experts = experts
        self.sub = shard * ctx // experts
        self.tp = tp
        if self.sub == ctx:
            self.layer, self.exp = (("ctx", "tp"), None), ("shard", None)
            self.part = ("ctx", None)
        else:
            devices = np.arange(shard * ctx * tp).reshape(experts, self.sub, tp)
            self.layer = (ALL, devices.reshape(experts, -1).tolist())
            self.exp = (ALL, devices.reshape(experts, -1).T.tolist())
            self.part = (ALL, devices.transpose(0, 2, 1).reshape(-1, self.sub).tolist())

    def swap(self, value, over):
        axes, groups = over
        return lax.all_to_all(value, axes, 0, 0, axis_index_groups=groups)


class Routing:
    def __init__(self, choice, seqs, seq_len, experts, cap, mine, own_first, own_seqs):
        columns = jnp.arange(experts, dtype=jnp.int32)
        hits = jnp.sum((choice[:, :, None] == columns[None, None, :]).astype(F32), axis=1)
        self.hits = hits.reshape(seqs, seq_len, experts)
        rows = jnp.arange(seq_len, dtype=jnp.int32)
        earlier = (rows[None, :] < rows[:, None]).astype(BF)
        before = dot("tu,sue->ste", earlier, self.hits.astype(BF))
        self.valid = self.hits * (before < cap).astype(F32)
        self.place = jnp.where(self.valid > 0, before, -1.0)
        self.cap = cap
        is_mine = (columns == mine).astype(F32)
        place_mine = jnp.sum(self.place * is_mine, axis=2)
        slots = jnp.arange(cap, dtype=jnp.int32).astype(F32)
        self.is_mine = is_mine
        self.pick = (place_mine[:, None, :] == slots[None, :, None]).astype(BF)
        place_own = lax.dynamic_slice_in_dim(self.place, own_first, own_seqs, 0)
        self.put = (
            place_own.transpose(0, 2, 1)[:, :, :, None] == slots[None, None, None, :]
        ).astype(BF)

    def gates(self, logits):
        logits = logits.reshape(self.hits.shape)
        top = jnp.max(jnp.where(self.hits > 0, logits, -jnp.inf), axis=2, keepdims=True)
        raised = jnp.where(self.hits > 0, jnp.exp(logits - top), 0.0)
        return raised / jnp.sum(raised, axis=2, keepdims=True)

    def slot_gates(self, gates):
        gate_mine = jnp.sum(gates * self.is_mine, axis=2)
        return jnp.sum(self.pick.astype(F32) * gate_mine[:, None, :], axis=2)

    def take(self, rows):
        seqs, cap, seq_len = self.pick.shape
        picked = dot("spt,stf->spf", self.pick, rows.reshape(seqs, seq_len, -1))
        return picked.astype(BF).reshape(seqs * cap, -1)

    def home(self, slots):
        own_seqs, experts, seq_len, cap = self.put.shape
        slots = slots.reshape(experts, own_seqs, cap, -1)
        return dot("setp,espf->stf", self.put, slots).reshape(own_seqs * seq_len, -1)

    def token_grads(self, slot_grads):
        slots = jnp.arange(self.cap, dtype=jnp.int32).astype(F32)
        here = self.place[:, :, :, None] == slots[None, None, None, :]
        grads = slot_grads.transpose(1, 0, 2)[:, None, :, :]
        return jnp.sum(jnp.where(here, grads, 0.0), axis=3)


def logit_grads(gates, gate_grads):
    mean = jnp.sum(gates * gate_grads, axis=2, keepdims=True)
    grads = gates * (gate_grads - mean)
    return grads.reshape(-1, grads.shape[-1])


def shards(
    sizes,
    hidden_in,
    att_choice,
    ffn_choice,
    span_ids,
    norm_att,
    router_att,
    w_query,
    w_out,
    w_key,
    w_value,
    norm_ffn,
    router_ffn,
    w_gate,
    w_up,
    w_down,
    cotangent,
):
    shard, ctx, tp = sizes
    experts = w_query.shape[0]
    axes = Axes(experts, shard, ctx, tp)
    sub = axes.sub
    group = experts * sub
    layer = sub * tp
    tokens, width = hidden_in.shape
    total = tokens * group
    seq_len = tokens * ctx
    seqs = total // seq_len
    own_seqs = seqs // experts
    own_tokens = own_seqs * seq_len
    cap = 2 * seq_len // experts
    slots = seqs * cap
    rows_own = width // group
    feats = width // layer
    group_at, tp_at = lax.axis_index(GROUP), lax.axis_index("tp")
    exp_at, sub_at = group_at // sub, group_at % sub
    layer_at = sub_at * tp + tp_at

    token_pack = jnp.concatenate(
        [att_choice, ffn_choice, span_ids[:, None]], axis=1
    ).astype(BF)
    feature_pack = jnp.concatenate(
        [norm_att[:, None], router_att, norm_ffn[:, None], router_ffn], axis=1
    )
    wide = 16
    pack = jnp.concatenate(
        [
            jnp.pad(token_pack, ((0, 0), (0, wide - token_pack.shape[1]))),
            jnp.pad(feature_pack, ((0, 0), (0, wide - feature_pack.shape[1]))),
        ],
        axis=0,
    )
    packs = lax.all_gather(pack, GROUP)
    token_facts = packs[:, :tokens].reshape(total, wide).astype(jnp.int32)
    feature_facts = packs[:, tokens:].reshape(width, wide)
    gain_att = feature_facts[:, 0].astype(F32)
    route_att = feature_facts[:, 1 : 1 + experts]
    gain_ffn = feature_facts[:, 1 + experts].astype(F32)
    route_ffn = feature_facts[:, 2 + experts : 2 + 2 * experts]

    def everywhere(block):
        quarter = width // tp
        part = lax.dynamic_slice_in_dim(block, tp_at * quarter, quarter, 1)
        parts = lax.all_gather(part, ALL)
        return parts.reshape(group, tp, tokens, quarter).transpose(0, 2, 1, 3).reshape(total, width)

    def everywhere_layer(block):
        parts = lax.all_gather(block, ALL)
        return (
            parts.reshape(experts, layer, own_tokens, feats)
            .transpose(0, 2, 1, 3)
            .reshape(total, width)
        )

    def layer_sum(rows):
        m = rows.shape[0]
        parts = rows.astype(BF).reshape(m, layer, feats).transpose(1, 0, 2)
        parts = axes.swap(parts, axes.layer)
        return jnp.sum(parts.astype(F32), axis=0)

    def go_home(rows):
        return axes.swap(rows.astype(BF).reshape(experts, own_seqs * cap, feats), axes.exp)

    head_parts = math.gcd(sub, w_query.shape[2] // HD)
    copies = sub // head_parts
    heads_wide = w_query.shape[2] // head_parts
    hidden_local = w_gate.shape[2]
    hidden_wide = -(-hidden_local // (sub * 128)) * 128
    hidden_pad = hidden_wide * sub - hidden_local

    def columns_out(weight, wide, dup=1):
        parts = weight.reshape(experts, rows_own, sub // dup, wide).transpose(0, 2, 1, 3)
        return jnp.repeat(parts, dup, axis=1).reshape(group, rows_own, wide)

    def rows_out(weight, wide, dup=1):
        parts = weight.reshape(experts, sub // dup, wide, rows_own)
        return jnp.repeat(parts, dup, axis=1).reshape(group, wide, rows_own)

    key_value = jnp.concatenate(
        [
            columns_out(jnp.broadcast_to(weight, (experts, *weight.shape)), heads_wide, copies)
            for weight in (w_key, w_value)
        ],
        axis=2,
    )
    qkv = jnp.concatenate([columns_out(w_query, heads_wide, copies), key_value], axis=2)
    qkv = lax.all_to_all(qkv, GROUP, 0, 0).reshape(width, 3 * heads_wide)
    my_query = qkv[:, :heads_wide]
    my_key_value = qkv[:, heads_wide:]
    out_parts = rows_out(w_out, heads_wide, copies)
    out_parts = after(out_parts, qkv)
    my_out = lax.all_to_all(out_parts, GROUP, 0, 0)
    my_out = my_out.transpose(1, 0, 2).reshape(heads_wide, width)
    gate_parts = columns_out(jnp.pad(w_gate, ((0, 0), (0, 0), (0, hidden_pad))), hidden_wide)
    up_parts = columns_out(jnp.pad(w_up, ((0, 0), (0, 0), (0, hidden_pad))), hidden_wide)
    down_parts = rows_out(jnp.pad(w_down, ((0, 0), (0, hidden_pad), (0, 0))), hidden_wide)
    my_gate = lax.all_to_all(after(gate_parts, my_out), GROUP, 0, 0).reshape(width, hidden_wide)
    my_up = lax.all_to_all(after(up_parts, my_gate), GROUP, 0, 0).reshape(width, hidden_wide)
    my_down = lax.all_to_all(after(down_parts, my_up), GROUP, 0, 0)
    my_down = my_down.transpose(1, 0, 2).reshape(hidden_wide, width)

    own_first = exp_at * own_seqs
    where = partial(
        Routing,
        seqs=seqs,
        seq_len=seq_len,
        experts=experts,
        cap=cap,
        mine=exp_at,
        own_first=own_first,
        own_seqs=own_seqs,
    )
    att = where(token_facts[:, 0:2])
    if copies > 1:
        turn = jnp.arange(seqs, dtype=jnp.int32) % copies == sub_at % copies
        att.pick = att.pick * turn.astype(BF)[:, None, None]
    ffn = where(token_facts[:, 2:4])
    spans = token_facts[:, 4].reshape(seqs, seq_len).astype(F32)
    cosine, sine = rope_tables(seq_len)
    positions = jnp.arange(seq_len, dtype=jnp.int32).astype(F32)
    pick_f32 = att.pick.astype(F32)
    slot_position = jnp.sum(pick_f32 * positions[None, None, :], axis=2)
    slot_span = jnp.sum(pick_f32 * spans[:, None, :], axis=2)
    slot_cosine = dot_exact("spt,tf->spf", pick_f32, cosine)
    slot_sine = dot_exact("spt,tf->spf", pick_f32, sine)
    allowed = (positions[None, None, :] <= slot_position[:, :, None]) | (
        (slot_span[:, :, None] == spans[:, None, :]) & (slot_span[:, :, None] > 0)
    )

    all_in = everywhere(hidden_in)
    x_all = all_in.astype(F32)
    scale_in = lax.rsqrt(jnp.mean(x_all * x_all, axis=1, keepdims=True) + EPS)
    h1 = (x_all * scale_in * gain_att[None, :]).astype(BF)
    heads = heads_wide // HD
    scale = 1.0 / math.sqrt(HD)
    kv = dot("td,dm->tm", h1, my_key_value)
    keys = rotate(
        kv[:, :heads_wide].reshape(seqs, seq_len, heads, HD),
        cosine[None, :, None, :],
        sine[None, :, None, :],
    ).astype(BF)
    values = kv[:, heads_wide:].astype(BF).reshape(seqs, seq_len, heads, HD)
    att_gates = att.gates(dot("td,de->te", h1, route_att))
    att_slot_gate = att.slot_gates(att_gates).reshape(slots, 1)
    h1_slots = att.take(h1)
    queries = rotate(
        dot("td,dm->tm", h1_slots, my_query).reshape(seqs, cap, heads, HD),
        slot_cosine[:, :, None, :],
        slot_sine[:, :, None, :],
    ).astype(BF)
    scores = dot("sqhd,skhd->shqk", queries, keys) * scale
    scores = jnp.where(allowed[:, None], scores, -1e30)
    expo = jnp.exp(scores - jnp.max(scores, axis=-1, keepdims=True))
    probs = expo / jnp.sum(expo, axis=-1, keepdims=True)
    probs_low = probs.astype(BF)
    mixed = dot("shqk,skhd->sqhd", probs_low, values).astype(BF).reshape(slots, heads_wide)
    branch_att = dot("cm,md->cd", mixed, my_out) * att_slot_gate
    att_home = go_home(layer_sum(branch_att))
    own_in = lax.dynamic_slice(
        x_all, (exp_at * own_tokens, layer_at * feats), (own_tokens, feats)
    )
    mid = own_in + att.home(att_home)
    mid_all = everywhere_layer(mid.astype(BF)).astype(F32)

    scale_mid = lax.rsqrt(jnp.mean(mid_all * mid_all, axis=1, keepdims=True) + EPS)
    unit_mid = mid_all * scale_mid
    h2 = (unit_mid * gain_ffn[None, :]).astype(BF)
    ffn_gates = ffn.gates(dot("td,de->te", h2, route_ffn))
    ffn_slot_gate = ffn.slot_gates(ffn_gates).reshape(slots, 1)
    h2_slots = ffn.take(h2)
    pre_gate = dot("cd,df->cf", h2_slots, my_gate)
    pre_up = dot("cd,df->cf", h2_slots, my_up)
    sigma = jax.nn.sigmoid(pre_gate)
    swish = pre_gate * sigma
    hidden = (swish * pre_up).astype(BF)
    branch_ffn = dot("cf,fd->cd", hidden, my_down) * ffn_slot_gate

    top_all = everywhere(cotangent)
    top_slots = ffn.take(top_all)
    grad_hidden = dot("cd,fd->cf", top_slots, my_down)
    ffn_gate_part = jnp.sum(hidden.astype(F32) * grad_hidden, axis=1)
    grad_hidden = grad_hidden * ffn_slot_gate
    grad_branch = (top_slots.astype(F32) * ffn_slot_gate).astype(BF)
    grad_pre_gate = (
        grad_hidden * pre_up * sigma * (1.0 + pre_gate * (1.0 - sigma))
    ).astype(BF)
    grad_pre_up = (grad_hidden * swish).astype(BF)
    ffn_taken = dot("cf,df->cd", grad_pre_gate, my_gate) + dot("cf,df->cd", grad_pre_up, my_up)
    ffn_grad_home = go_home(layer_sum(ffn_taken))
    ffn_gate_grads = ffn.token_grads(
        jnp.sum(
            lax.all_gather(ffn_gate_part, ALL).reshape(experts, layer, seqs, cap), axis=1
        )
    )
    ffn_logit_grads = logit_grads(ffn_gates, ffn_gate_grads)
    own_ffn_logits = lax.dynamic_slice_in_dim(
        ffn_logit_grads, exp_at * own_tokens, own_tokens, 0
    )
    own_route_ffn = lax.dynamic_slice_in_dim(
        route_ffn.astype(F32), layer_at * feats, feats, 0
    )
    grad_second = ffn.home(ffn_grad_home) + dot_exact(
        "te,fe->tf", own_ffn_logits, own_route_ffn
    )
    own_at = (exp_at * own_tokens, layer_at * feats)
    own_unit_mid = lax.dynamic_slice(unit_mid, own_at, (own_tokens, feats))
    own_scale_mid = lax.dynamic_slice_in_dim(scale_mid, exp_at * own_tokens, own_tokens, 0)
    own_gain_ffn = lax.dynamic_slice_in_dim(gain_ffn, layer_at * feats, feats, 0)
    norm_ffn_part = jnp.sum(grad_second * own_unit_mid, axis=0)
    scaled_second = (grad_second * own_gain_ffn[None, :] * own_scale_mid).astype(BF)
    second_all = everywhere_layer(scaled_second).astype(F32)
    grad_mid = (
        top_all.astype(F32)
        + second_all
        - unit_mid * jnp.mean(second_all * unit_mid, axis=1, keepdims=True)
    )

    mid_slots = att.take(grad_mid.astype(BF))
    grad_mixed = dot("cd,md->cm", mid_slots, my_out)
    att_gate_part = jnp.sum(mixed.astype(F32) * grad_mixed, axis=1)
    grad_mixed = (grad_mixed * att_slot_gate).astype(BF).reshape(seqs, cap, heads, HD)
    grad_att_branch = (mid_slots.astype(F32) * att_slot_gate).astype(BF)
    grad_soft = dot("sqhd,skhd->shqk", grad_mixed, values)
    grad_values = dot("shqk,sqhd->skhd", probs_low, grad_mixed)
    grad_scores = (
        probs * (grad_soft - jnp.sum(probs * grad_soft, axis=-1, keepdims=True))
    ).astype(BF)
    grad_queries = dot("shqk,skhd->sqhd", grad_scores, keys) * scale
    grad_keys = dot("shqk,sqhd->skhd", grad_scores, queries) * scale
    grad_qpre = (
        rotate_back(grad_queries, slot_cosine[:, :, None, :], slot_sine[:, :, None, :])
        .astype(BF)
        .reshape(slots, heads_wide)
    )
    att_taken = dot("cm,dm->cd", grad_qpre, my_query)
    kv_grads = jnp.concatenate(
        [grad_keys.reshape(total, heads_wide), grad_values.reshape(total, heads_wide)], axis=1
    )
    kv_grads = axes.swap(
        kv_grads.astype(BF).reshape(experts, own_tokens, 2 * heads_wide), axes.exp
    )
    kv_grads = jnp.sum(kv_grads.astype(F32), axis=0)
    own_keys = rotate_back(
        kv_grads[:, :heads_wide].reshape(own_seqs, seq_len, heads, HD),
        cosine[None, :, None, :],
        sine[None, :, None, :],
    )
    kv_low = jnp.concatenate(
        [own_keys.reshape(own_tokens, heads_wide), kv_grads[:, heads_wide:]], axis=1
    ).astype(BF)
    own_h1 = lax.dynamic_slice_in_dim(h1, exp_at * own_tokens, own_tokens, 0)
    kv_taken = dot("tm,dm->td", kv_low, my_key_value)
    both = layer_sum(jnp.concatenate([att_taken, kv_taken], axis=0))
    att_grad_home = go_home(both[:slots])
    att_gate_grads = att.token_grads(
        jnp.sum(
            lax.all_gather(att_gate_part, ALL).reshape(experts, layer, seqs, cap), axis=1
        )
    )
    att_logit_grads = logit_grads(att_gates, att_gate_grads)
    own_att_logits = lax.dynamic_slice_in_dim(
        att_logit_grads, exp_at * own_tokens, own_tokens, 0
    )
    own_route_att = lax.dynamic_slice_in_dim(
        route_att.astype(F32), layer_at * feats, feats, 0
    )
    grad_first = (
        both[slots:]
        + att.home(att_grad_home)
        + dot_exact("te,fe->tf", own_att_logits, own_route_att)
    )
    own_scale_in = lax.dynamic_slice_in_dim(scale_in, exp_at * own_tokens, own_tokens, 0)
    own_gain_att = lax.dynamic_slice_in_dim(gain_att, layer_at * feats, feats, 0)
    norm_att_part = jnp.sum(grad_first * own_in * own_scale_in, axis=0)
    scaled_first = (grad_first * own_gain_att[None, :] * own_scale_in).astype(BF)

    def to_tokens(block):
        parts = axes.swap(block.reshape(sub, tokens, feats), axes.part)
        parts = lax.all_gather(parts, "tp")
        return parts.transpose(2, 1, 0, 3).reshape(tokens, width)

    first_tokens = to_tokens(scaled_first).astype(F32)
    token_at = group_at * tokens
    unit_in = lax.dynamic_slice_in_dim(x_all * scale_in, token_at, tokens, 0)
    grad_in = (
        lax.dynamic_slice_in_dim(grad_mid, token_at, tokens, 0)
        + first_tokens
        - unit_in * jnp.mean(first_tokens * unit_in, axis=1, keepdims=True)
    )

    ffn_home = go_home(layer_sum(branch_ffn))
    hidden_out = to_tokens((mid + ffn.home(ffn_home)).astype(BF))

    norm_parts = lax.all_gather(jnp.concatenate([norm_att_part, norm_ffn_part]), ALL)
    norm_parts = jnp.sum(norm_parts.reshape(experts, layer, 2, feats), axis=0)
    norm_parts = norm_parts.transpose(1, 0, 2).reshape(2, width)
    norm_grads = lax.dynamic_slice_in_dim(norm_parts, group_at * rows_own, rows_own, 1)

    def router_grad(rows, grads):
        own = lax.dynamic_slice_in_dim(rows, group_at * rows_own, rows_own, 1)
        return dot_exact("tf,te->fe", own.astype(F32), grads)

    grad_router_att = router_grad(h1, att_logit_grads)
    grad_router_ffn = router_grad(h2, ffn_logit_grads)

    def copies_summed(back, dup):
        back = back.reshape(experts, sub // dup, dup, *back.shape[1:])
        if dup == 1:
            return back[:, :, 0]
        return jnp.sum(back.astype(F32), axis=2)

    def columns_home(parts, columns, dup=1):
        back = copies_summed(lax.all_to_all(parts, GROUP, 0, 0), dup)
        back = back.transpose(0, 2, 1, 3)
        return back.reshape(experts, rows_own, -1)[:, :, :columns].astype(F32)

    def rows_home(grads, rows, dup=1):
        wide = grads.shape[0]
        parts = grads.reshape(wide, group, rows_own).transpose(1, 0, 2)
        back = copies_summed(lax.all_to_all(parts, GROUP, 0, 0), dup)
        return back.reshape(experts, -1, rows_own)[:, :rows].astype(F32)

    grad_down_w = dot("cf,cd->fd", hidden, grad_branch).astype(BF)
    grad_gate_w = dot("cd,cf->df", h2_slots, grad_pre_gate).astype(BF)
    grad_up_w = dot("cd,cf->df", h2_slots, grad_pre_up).astype(BF)
    grad_down = rows_home(grad_down_w, hidden_local)
    grad_gate = columns_home(grad_gate_w.reshape(group, rows_own, hidden_wide), hidden_local)
    grad_up = columns_home(grad_up_w.reshape(group, rows_own, hidden_wide), hidden_local)
    grad_query_w = dot("cd,cm->dm", h1_slots, grad_qpre).astype(BF)
    grad_out_w = dot("cm,cd->md", mixed, grad_att_branch).astype(BF)
    grad_kv_w = dot("td,tm->dm", own_h1, kv_low).astype(BF)
    grad_out = rows_home(grad_out_w, head_parts * heads_wide, copies)
    grad_query = columns_home(
        grad_query_w.reshape(group, rows_own, heads_wide), head_parts * heads_wide, copies
    )
    kv_back = lax.all_to_all(grad_kv_w.reshape(group, rows_own, 2 * heads_wide), GROUP, 0, 0)
    kv_back = jnp.sum(copies_summed(kv_back, copies).astype(F32), axis=0)
    kv_back = kv_back.reshape(head_parts, rows_own, 2, heads_wide).transpose(2, 1, 0, 3)
    kv_back = kv_back.reshape(2, rows_own, head_parts * heads_wide)
    return (
        hidden_out,
        grad_in,
        norm_grads[0],
        grad_router_att,
        grad_query,
        grad_out,
        kv_back[0],
        kv_back[1],
        norm_grads[1],
        grad_router_ffn,
        grad_gate,
        grad_up,
        grad_down,
    )


def solution(mesh):
    ctx, tp = mesh.shape["ctx"], mesh.shape["tp"]
    shard = mesh.shape["shard"]
    by_token, by_feature = P(GROUP, None), P(GROUP)
    columns, rows = P(None, GROUP, "tp"), P(None, "tp", GROUP)

    return jax.shard_map(
        partial(shards, (shard, ctx, tp)),
        mesh=mesh,
        in_specs=(
            by_token,
            by_token,
            by_token,
            P(GROUP),
            by_feature,
            by_token,
            columns,
            rows,
            P(GROUP, "tp"),
            P(GROUP, "tp"),
            by_feature,
            by_token,
            columns,
            columns,
            rows,
            by_token,
        ),
        out_specs=(
            by_token,
            by_token,
            by_feature,
            by_token,
            columns,
            rows,
            P(GROUP, "tp"),
            P(GROUP, "tp"),
            by_feature,
            by_token,
            columns,
            columns,
            rows,
        ),
        check_vma=False,
    )
```

```python
from functools import partial
import math

import numpy as np

import jax
import jax.numpy as jnp
from jax import lax
from jax.experimental import pallas as pl
from jax.experimental.pallas import tpu as pltpu
from jax.sharding import PartitionSpec as P

HD = 128
EPS = 1e-06
BF = jnp.bfloat16
F32 = jnp.float32
MESH = pl.DeviceIdType.MESH
VMEM_BYTES = 40 * 2**20
GROUP = ("shard", "ctx")
ALL = ("shard", "ctx", "tp")


def dot(spec, left, right):
    return jnp.einsum(spec, left, right, preferred_element_type=F32)


def dot_exact(spec, left, right):
    return jnp.einsum(
        spec, left, right, preferred_element_type=F32, precision=lax.Precision.HIGHEST
    )


def after(value, *others):
    return lax.optimization_barrier((value, *others))[0]


def rope_tables(count):
    half_dim = HD // 2
    freq_index = (jnp.arange(HD) % half_dim).astype(F32)
    frequency = 10000.0 ** (-2.0 * freq_index / HD)
    angles = jnp.arange(count, dtype=F32)[:, None] * frequency[None, :]
    return jnp.cos(angles), jnp.sin(angles)


def rotate(rows, cosine, sine):
    half_dim = HD // 2
    turned = jnp.concatenate([-rows[..., half_dim:], rows[..., :half_dim]], axis=-1)
    return rows * cosine + turned * sine


def rotate_back(rows, cosine, sine):
    half_dim = HD // 2
    turned = rows * sine
    return rows * cosine + jnp.concatenate(
        [turned[..., half_dim:], -turned[..., :half_dim]], axis=-1
    )


class Place:
    def __init__(self, sizes):
        self.experts, self.sub, self.ctx, self.tp = sizes
        self.chips = self.sub * self.tp // 2
        self.members = self.experts * self.sub
        self.group = lax.axis_index(GROUP)
        self.tp_at = lax.axis_index("tp")
        self.exp = self.group // self.sub
        here = (self.group % self.sub) * self.tp + self.tp_at
        self.chip, self.core = here // 2, here % 2

    def device(self, exp, chip, core):
        here = chip * 2 + core
        group = exp * self.sub + here // self.tp
        return (group // self.ctx, group % self.ctx, here % self.tp)

    def member(self, group):
        return (group // self.ctx, group % self.ctx, self.tp_at)

    def sibling(self):
        return self.device(self.exp, self.chip, 1 - self.core)

    def other_exp(self, k):
        return (self.exp + k) % self.experts

    def other_chip(self, k):
        return (self.chip + k) % self.chips

    def meet(self, whole_group):
        barrier = pltpu.get_barrier_semaphore()
        peers = [self.sibling()]
        peers += [
            self.device(self.exp, self.other_chip(k), self.core) for k in range(1, self.chips)
        ]
        if whole_group:
            peers += [
                self.member((self.group + k) % self.members) for k in range(1, self.members)
            ]
        else:
            peers += [
                self.device(self.other_exp(k), self.chip, self.core)
                for k in range(1, self.experts)
            ]
        for peer in peers:
            pl.semaphore_signal(barrier, inc=1, device_id=peer, device_id_type=MESH)
        pl.semaphore_wait(barrier, len(peers))


def block(start, size, unit):
    return pl.ds(pl.multiple_of(start, unit), size)


def send(src, dst, sems, at, device):
    copy = pltpu.make_async_remote_copy(
        src_ref=src,
        dst_ref=dst,
        send_sem=sems.at[(0, *at)],
        recv_sem=sems.at[(1, *at)],
        device_id=device,
        device_id_type=MESH,
    )
    copy.start()
    return copy


class Mover:
    def __init__(self, number, kind, cuts, src, dst, sems, own_sems):
        self.number, self.kind, self.cuts = number, kind, cuts
        self.src, self.dst, self.sems, self.own_sems = src, dst, sems, own_sems
        self.copies = []

    def ends(self, place, group, low, size):
        exp, sub = group // place.sub, group % place.sub
        me, src, dst = place.group, self.src, self.dst
        if self.kind == "columns_out":
            rows, step = src.shape[1], (src.shape[2] - dst.shape[1]) // max(place.sub - 1, 1)
            return (
                src.at[exp, :, block(sub * step + low, size, 128)],
                dst.at[block(me * rows, rows, 16), pl.ds(low, size)],
            )
        if self.kind == "pair_out":
            rows, half = src.shape[1], size
            return (
                src.at[low // half, :, block(sub * half, half, 128)],
                dst.at[block(me * rows, rows, 16), pl.ds(low, half)],
            )
        if self.kind == "rows_out":
            cols, step = src.shape[2], (src.shape[1] - dst.shape[0]) // max(place.sub - 1, 1)
            return (
                src.at[exp, block(sub * step + low, size, 16)],
                dst.at[pl.ds(low, size), block(me * cols, cols, 128)],
            )
        if self.kind == "columns_home":
            rows = dst.shape[1]
            return (
                src.at[block(group * rows, rows, 16), pl.ds(low, size)],
                dst.at[me, :, pl.ds(low, size)],
            )
        cols = dst.shape[2]
        return (
            src.at[pl.ds(low, size), block(group * cols, cols, 128)],
            dst.at[me, pl.ds(low, size)],
        )

    def start(self, place, late):
        for cut, (low, size, is_late) in enumerate(self.cuts):
            if is_late != late or not size:
                continue
            for k in range(1, place.members):
                group = (place.group + k) % place.members
                src, dst = self.ends(place, group, low, size)
                at = (self.number, cut, k - 1)
                self.copies.append(send(src, dst, self.sems, at, place.member(group)))
            src, dst = self.ends(place, place.group, low, size)
            own = pltpu.make_async_copy(src, dst, self.own_sems.at[self.number, cut])
            own.start()
            self.copies.append(own)

    def wait(self):
        for copy in self.copies:
            copy.wait()


def moved_shape(sizes, kind, array, wide):
    experts, sub, _, _ = sizes
    group = experts * sub
    if kind in ("columns_out", "pair_out"):
        return (array.shape[1] * group, wide)
    if kind == "rows_out":
        return (wide, array.shape[2] * group)
    if kind == "columns_home":
        return (group, array.shape[0] // group, array.shape[1])
    return (group, array.shape[0], array.shape[1] // group)


class Spread:
    def __init__(self, place, mine, out, by_token, exp_sems, chip_sems, core_sems):
        self.place, self.mine, self.out, self.by_token = place, mine, out, by_token
        self.rows, self.cols = mine.shape
        self.exp_sems, self.chip_sems, self.core_sems = exp_sems, chip_sems, core_sems

    def spot(self, exp, chip):
        place = self.place
        here = chip * 2 + place.core
        if self.by_token:
            row = (exp * place.sub + here // place.tp) * self.rows
            col = (here % place.tp) * self.cols
        else:
            row, col = exp * self.rows, here * self.cols
        unit = math.gcd(self.rows, 16)
        return self.out.at[block(row, self.rows, unit), block(col, self.cols, 128)]

    def to_chips(self, exp, src, turn):
        place = self.place
        for k in range(1, place.chips):
            device = place.device(place.exp, place.other_chip(k), place.core)
            self.chip_copies[turn].append(
                send(src, self.spot(exp, place.chip), self.chip_sems, (turn, k - 1), device)
            )

    def to_core(self, exp, chip, src, turn, k):
        self.core_copies.append(
            send(src, self.spot(exp, chip), self.core_sems, (turn, k), self.place.sibling())
        )

    def start(self, own_sem):
        place = self.place
        home = self.spot(place.exp, place.chip)
        self.own = pltpu.make_async_copy(self.mine, home, own_sem)
        self.own.start()
        self.chip_copies = [[] for _ in range(place.experts)]
        self.core_copies = []
        self.exp_copies = [
            send(
                self.mine,
                home,
                self.exp_sems,
                (k - 1,),
                place.device(place.other_exp(k), place.chip, place.core),
            )
            for k in range(1, place.experts)
        ]
        self.to_chips(place.exp, self.mine, 0)
        self.to_core(place.exp, place.chip, self.mine, 0, 0)

    def run(self):
        place = self.place
        experts, chips = place.experts, place.chips
        for turn in range(1, experts):
            self.exp_copies[turn - 1].wait_recv()
            source = (place.exp + experts - turn) % experts
            here = self.spot(source, place.chip)
            self.to_chips(source, here, turn)
            self.to_core(source, place.chip, here, turn, 0)
        for turn in range(experts):
            source = (place.exp + experts - turn) % experts
            for k in range(1, chips):
                self.chip_copies[turn][k - 1].wait_recv()
                chip = (place.chip + chips - k) % chips
                self.to_core(source, chip, self.spot(source, chip), turn, k)
        for copy in self.core_copies:
            copy.wait()
        for copy in self.exp_copies:
            copy.wait_send()
        for copies in self.chip_copies:
            for copy in copies:
                copy.wait_send()
        self.own.wait()


class ToTokens:
    def __init__(self, place, mine, out, chip_sems, core_sems):
        self.place, self.mine, self.out = place, mine, out
        self.chip_sems, self.core_sems = chip_sems, core_sems
        self.rows, self.cols = out.shape[0], mine.shape[1]

    def spot(self, chip):
        here = chip * 2 + self.place.core
        return self.out.at[:, block(here * self.cols, self.cols, 128)]

    def part(self, chip):
        sub = (chip * 2) // self.place.tp
        return self.mine.at[block(sub * self.rows, self.rows, 16)]

    def run(self, own_sem):
        place = self.place
        mine = self.part(place.chip)
        own = pltpu.make_async_copy(mine, self.spot(place.chip), own_sem)
        own.start()
        copies = []
        for k in range(1, place.chips):
            chip = place.other_chip(k)
            copies.append(
                send(
                    self.part(chip),
                    self.spot(place.chip),
                    self.chip_sems,
                    (k - 1,),
                    place.device(place.exp, chip, place.core),
                )
            )
        core = [send(mine, self.spot(place.chip), self.core_sems, (0,), place.sibling())]
        for k in range(1, place.chips):
            copies[k - 1].wait_recv()
            spot = self.spot((place.chip + place.chips - k) % place.chips)
            core.append(send(spot, spot, self.core_sems, (k,), place.sibling()))
        for copy in core:
            copy.wait()
        for copy in copies:
            copy.wait_send()
        own.wait()


class Fold:
    def __init__(self, place, part, home, scratch):
        self.place, self.part, self.home = place, part, home
        (
            self.core_got,
            self.chip_out,
            self.chip_got,
            self.exp_out,
            self.core_sems,
            self.chip_sems,
            self.exp_sems,
        ) = scratch
        self.feats = home.shape[2]

    def columns(self, chip, core):
        return block((chip * 2 + core) * self.feats, self.feats, 128)

    def run(self):
        place, part = self.place, self.part
        experts, chips = place.experts, place.chips
        each = self.home.shape[1]
        core_copies = {}
        for k in [*range(1, chips), 0]:
            away = part.at[:, self.columns(place.other_chip(k), 1 - place.core)]
            core_copies[k] = send(away, self.core_got.at[k], self.core_sems, (k,), place.sibling())
        chip_copies = []
        for k in range(1, chips):
            chip = place.other_chip(k)
            core_copies[k].wait_recv()
            mine = part[:, self.columns(chip, place.core)].astype(F32)
            self.chip_out[k - 1] = (mine + self.core_got[k].astype(F32)).astype(BF)
            chip_copies.append(
                send(
                    self.chip_out.at[k - 1],
                    self.chip_got.at[k - 1],
                    self.chip_sems,
                    (k - 1,),
                    place.device(place.exp, chip, place.core),
                )
            )
        core_copies[0].wait_recv()
        total = part[:, self.columns(place.chip, place.core)].astype(F32)
        total = total + self.core_got[0].astype(F32)
        for k in range(1, chips):
            chip_copies[k - 1].wait_recv()
            total = total + self.chip_got[k - 1].astype(F32)
        self.exp_out[...] = total.astype(BF)
        exp_copies = []
        for k in range(1, experts):
            exp = place.other_exp(k)
            exp_copies.append(
                send(
                    self.exp_out.at[block(exp * each, each, 16)],
                    self.home.at[place.exp],
                    self.exp_sems,
                    (k - 1,),
                    place.device(exp, place.chip, place.core),
                )
            )
        self.home[place.exp] = self.exp_out[block(place.exp * each, each, 16)]
        for copy in exp_copies:
            copy.wait_recv()
        for copy in [*core_copies.values(), *chip_copies, *exp_copies]:
            copy.wait_send()


def start_kernel(sizes, count, moves, *refs):
    place = Place(sizes)
    blocks, sources, refs = refs[:count], refs[count : count + len(moves)], refs[count + len(moves) :]
    outs, landings, refs = refs[:count], refs[count : count + len(moves)], refs[count + len(moves) :]
    own_sems, exp_sems, chip_sems, core_sems, *refs = refs
    movers = [
        Mover(i, kind, cuts, source, landing, *refs)
        for i, ((kind, cuts), source, landing) in enumerate(zip(moves, sources, landings))
    ]
    spreads = []
    for i, (rows, out) in enumerate(zip(blocks, outs)):
        quarter = rows.shape[1] // place.tp
        mine = rows.at[:, block(place.tp_at * quarter, quarter, 128)]
        sems = (s.at[i] for s in (exp_sems, chip_sems, core_sems))
        spreads.append(Spread(place, mine, out, True, *sems))
    place.meet(bool(moves))
    for i, spread in enumerate(spreads[:-1]):
        spread.start(own_sems.at[i])
    for mover in movers:
        mover.start(place, False)
    spreads[-1].start(own_sems.at[count - 1])
    for mover in movers:
        mover.start(place, True)
    for spread in spreads:
        spread.run()
    for mover in movers:
        mover.wait()


def exchange_kernel(sizes, tail, moves, *refs):
    place = Place(sizes)
    count = len(moves)
    part, put, add, scale, facts, *refs = refs
    sources, refs = refs[:count], refs[count:]
    raw, out, all_facts, *refs = refs
    landings, refs = refs[:count], refs[count:]
    home, mine, own_sem, fact_sem, *refs = refs
    fact_sems, refs = refs[:3], refs[3:]
    fold_scratch, refs = refs[:7], refs[7:]
    tail_sems, refs = refs[: 3 if tail == "spread" else 2], refs[3 if tail == "spread" else 2 :]
    movers = []
    if count:
        movers = [
            Mover(i, kind, cuts, source, landing, *refs)
            for i, ((kind, cuts), source, landing) in enumerate(zip(moves, sources, landings))
        ]
    place.meet(bool(count))
    told = Spread(place, facts, all_facts, False, *fact_sems)
    told.start(fact_sem)
    for mover in movers:
        mover.start(place, False)
    Fold(place, part, home, fold_scratch).run()
    if put.shape[1] == 128:
        summed = jnp.sum(home[...].astype(F32), axis=0)
    else:
        summed = jnp.dot(
            put[...],
            home[...].reshape(-1, home.shape[2]),
            preferred_element_type=F32,
        )
    value = add[...] + summed
    raw[...] = value
    mine[...] = (value * scale[...]).astype(BF)
    if tail == "spread":
        spread = Spread(place, mine, out, False, *tail_sems)
        spread.start(own_sem)
        for mover in movers:
            mover.start(place, True)
        spread.run()
    else:
        for mover in movers:
            mover.start(place, True)
        ToTokens(place, mine, out, *tail_sems).run(own_sem)
    told.run()
    for mover in movers:
        mover.wait()


def dma_sems(*shape):
    return pltpu.SemaphoreType.DMA(shape)


def move_scratch(sizes, moves):
    most = max(len(cuts) for _, cuts, _, _ in moves)
    members = sizes[0] * sizes[1]
    return [dma_sems(2, len(moves), most, members - 1), dma_sems(len(moves), most)]


def start(sizes, arrays, moves, number):
    experts, sub, _, tp = sizes
    chips = sub * tp // 2
    count = len(arrays)
    results = pl.pallas_call(
        partial(start_kernel, sizes, count, [(kind, cuts) for kind, cuts, _, _ in moves]),
        out_shape=[
            *[
                jax.ShapeDtypeStruct((rows.shape[0] * experts * sub, rows.shape[1]), rows.dtype)
                for rows in arrays
            ],
            *[
                jax.ShapeDtypeStruct(moved_shape(sizes, kind, array, wide), BF)
                for kind, _, array, wide in moves
            ],
        ],
        in_specs=[pl.BlockSpec(memory_space=pl.ANY)] * (count + len(moves)),
        out_specs=[pl.BlockSpec(memory_space=pl.ANY)] * (count + len(moves)),
        scratch_shapes=[
            dma_sems(count),
            dma_sems(count, 2, experts - 1),
            dma_sems(count, 2, experts, chips - 1),
            dma_sems(count, 2, experts, chips),
            *move_scratch(sizes, moves),
        ],
        compiler_params=pltpu.CompilerParams(
            collective_id=number, has_side_effects=True, vmem_limit_bytes=VMEM_BYTES
        ),
        name=f"start_{number}",
    )(*arrays, *[array for _, _, array, _ in moves])
    return results[:count], results[count:]


def exchange(sizes, part, put, add, scale, facts, tail, moves, number):
    experts, sub, ctx, tp = sizes
    chips = sub * tp // 2
    rows, width = part.shape
    tokens, feats = add.shape
    each = rows // experts
    vmem, anywhere = (pl.BlockSpec(memory_space=m) for m in (pltpu.VMEM, pl.ANY))
    if put is None:
        put = jnp.zeros((8, 128), BF)
    out_rows = tokens * experts if tail == "spread" else tokens // sub
    landings = [
        jax.ShapeDtypeStruct(moved_shape(sizes, kind, array, wide), BF)
        for kind, _, array, wide in moves
    ]
    spread_sems = [
        dma_sems(2, experts - 1),
        dma_sems(2, experts, chips - 1),
        dma_sems(2, experts, chips),
    ]
    tail_sems = spread_sems
    if tail == "tokens":
        tail_sems = [dma_sems(2, chips - 1), dma_sems(2, chips)]
    fact_shape = (facts.shape[0] * experts, facts.shape[1] * sub * tp)
    raw, out, all_facts, *moved = pl.pallas_call(
        partial(exchange_kernel, sizes, tail, [(kind, cuts) for kind, cuts, _, _ in moves]),
        out_shape=[
            jax.ShapeDtypeStruct((tokens, feats), F32),
            jax.ShapeDtypeStruct((out_rows, width), BF),
            jax.ShapeDtypeStruct(fact_shape, F32),
            *landings,
        ],
        in_specs=[vmem] * 4 + [anywhere] * (1 + len(moves)),
        out_specs=[vmem] + [anywhere] * (2 + len(moves)),
        scratch_shapes=[
            pltpu.VMEM((experts, each, feats), BF),
            pltpu.VMEM((tokens, feats), BF),
            pltpu.SemaphoreType.DMA,
            pltpu.SemaphoreType.DMA,
            *spread_sems,
            pltpu.VMEM((chips, rows, feats), BF),
            pltpu.VMEM((chips - 1, rows, feats), BF),
            pltpu.VMEM((chips - 1, rows, feats), BF),
            pltpu.VMEM((rows, feats), BF),
            dma_sems(2, chips),
            dma_sems(2, chips - 1),
            dma_sems(2, experts - 1),
            *tail_sems,
            *move_scratch(sizes, moves),
        ],
        compiler_params=pltpu.CompilerParams(
            collective_id=number, has_side_effects=True, vmem_limit_bytes=VMEM_BYTES
        ),
        name=f"exchange_{number}",
    )(part, put, add, scale, facts, *[array for _, _, array, _ in moves])
    return raw, out, all_facts, moved


class Axes:
    def __init__(self, experts, shard, ctx, tp):
        self.experts = experts
        self.sub = shard * ctx // experts
        self.tp = tp
        if self.sub == ctx:
            self.layer, self.exp = (("ctx", "tp"), None), ("shard", None)
            self.part = ("ctx", None)
        else:
            devices = np.arange(shard * ctx * tp).reshape(experts, self.sub, tp)
            self.layer = (ALL, devices.reshape(experts, -1).tolist())
            self.exp = (ALL, devices.reshape(experts, -1).T.tolist())
            self.part = (ALL, devices.transpose(0, 2, 1).reshape(-1, self.sub).tolist())

    def swap(self, value, over):
        axes, groups = over
        return lax.all_to_all(value, axes, 0, 0, axis_index_groups=groups)


class Routing:
    def __init__(self, choice, seqs, seq_len, experts, cap, mine, own_first, own_seqs):
        columns = jnp.arange(experts, dtype=jnp.int32)
        hits = jnp.sum((choice[:, :, None] == columns[None, None, :]).astype(F32), axis=1)
        self.hits = hits.reshape(seqs, seq_len, experts)
        rows = jnp.arange(seq_len, dtype=jnp.int32)
        earlier = (rows[None, :] < rows[:, None]).astype(BF)
        before = dot("tu,sue->ste", earlier, self.hits.astype(BF))
        self.valid = self.hits * (before < cap).astype(F32)
        self.place = jnp.where(self.valid > 0, before, -1.0)
        self.cap = cap
        is_mine = (columns == mine).astype(F32)
        place_mine = jnp.sum(self.place * is_mine, axis=2)
        slots = jnp.arange(cap, dtype=jnp.int32).astype(F32)
        self.is_mine = is_mine
        self.pick = (place_mine[:, None, :] == slots[None, :, None]).astype(BF)
        place_own = lax.dynamic_slice_in_dim(self.place, own_first, own_seqs, 0)
        place_own = place_own.transpose(1, 0, 2)[:, :, :, None]
        seq_of = jnp.arange(own_seqs, dtype=jnp.int32)
        here = place_own == slots
        same = (seq_of[:, None] == seq_of[None, :])[:, None, None, :, None]
        put = here.transpose(1, 0, 2, 3)[:, :, :, None, :] & same
        self.put = put.astype(BF).reshape(own_seqs * seq_len, experts * own_seqs * cap)

    def gates(self, logits):
        logits = logits.reshape(self.hits.shape)
        top = jnp.max(jnp.where(self.hits > 0, logits, -jnp.inf), axis=2, keepdims=True)
        raised = jnp.where(self.hits > 0, jnp.exp(logits - top), 0.0)
        return raised / jnp.sum(raised, axis=2, keepdims=True)

    def slot_gates(self, gates):
        gate_mine = jnp.sum(gates * self.is_mine, axis=2)
        return jnp.sum(self.pick.astype(F32) * gate_mine[:, None, :], axis=2)

    def take(self, rows):
        seqs, cap, seq_len = self.pick.shape
        picked = dot("spt,stf->spf", self.pick, rows.reshape(seqs, seq_len, -1))
        return picked.astype(BF).reshape(seqs * cap, -1)

    def give(self, slots):
        seqs, cap, seq_len = self.pick.shape
        rows = dot("spt,spf->stf", self.pick, slots.reshape(seqs, cap, -1))
        return rows.reshape(seqs * seq_len, -1)

    def token_grads(self, slot_grads):
        slots = jnp.arange(self.cap, dtype=jnp.int32).astype(F32)
        here = self.place[:, :, :, None] == slots[None, None, None, :]
        grads = slot_grads.transpose(1, 0, 2)[:, None, :, :]
        return jnp.sum(jnp.where(here, grads, 0.0), axis=3)


def put_home(put, home):
    return dot("tp,pf->tf", put, home.reshape(-1, home.shape[-1]))


def router_rows(grads, router):
    high = grads.astype(BF)
    low = (grads - high.astype(F32)).astype(BF)
    return dot(
        "te,fe->tf",
        jnp.concatenate([high, low], axis=1),
        jnp.concatenate([router, router], axis=1),
    )


def logit_grads(gates, gate_grads):
    mean = jnp.sum(gates * gate_grads, axis=2, keepdims=True)
    grads = gates * (gate_grads - mean)
    return grads.reshape(-1, grads.shape[-1])


def shards(
    sizes,
    hidden_in,
    att_choice,
    ffn_choice,
    span_ids,
    norm_att,
    router_att,
    w_query,
    w_out,
    w_key,
    w_value,
    norm_ffn,
    router_ffn,
    w_gate,
    w_up,
    w_down,
    cotangent,
):
    shard, ctx, tp = sizes
    experts = w_query.shape[0]
    axes = Axes(experts, shard, ctx, tp)
    sub = axes.sub
    group = experts * sub
    layer = sub * tp
    tokens, width = hidden_in.shape
    total = tokens * group
    seq_len = tokens * ctx
    seqs = total // seq_len
    own_seqs = seqs // experts
    own_tokens = own_seqs * seq_len
    cap = 2 * seq_len // experts
    slots = seqs * cap
    rows_own = width // group
    feats = width // layer
    sizes = (experts, sub, ctx, tp)
    kernels = feats % 128 == 0 and rows_own % 128 == 0 and tokens % 16 == 0
    group_at, tp_at = lax.axis_index(GROUP), lax.axis_index("tp")
    exp_at, sub_at = group_at // sub, group_at % sub
    layer_at = sub_at * tp + tp_at

    token_pack = jnp.concatenate(
        [att_choice, ffn_choice, span_ids[:, None]], axis=1
    ).astype(BF)
    feature_pack = jnp.concatenate(
        [norm_att[:, None], router_att, norm_ffn[:, None], router_ffn], axis=1
    )
    def everywhere(rows):
        quarter = width // tp
        part = lax.dynamic_slice_in_dim(rows, tp_at * quarter, quarter, 1)
        parts = lax.all_gather(part, ALL)
        return parts.reshape(group, tp, tokens, quarter).transpose(0, 2, 1, 3).reshape(total, width)

    def everywhere_layer(rows):
        parts = lax.all_gather(rows, ALL)
        return (
            parts.reshape(experts, layer, own_tokens, feats)
            .transpose(0, 2, 1, 3)
            .reshape(total, width)
        )

    def layer_sum(rows):
        m = rows.shape[0]
        parts = rows.astype(BF).reshape(m, layer, feats).transpose(1, 0, 2)
        parts = axes.swap(parts, axes.layer)
        return jnp.sum(parts.astype(F32), axis=0)

    def go_home(rows):
        return axes.swap(rows.astype(BF).reshape(experts, -1, feats), axes.exp)

    def to_tokens(rows):
        parts = axes.swap(rows.reshape(sub, tokens, feats), axes.part)
        parts = lax.all_gather(parts, "tp")
        return parts.transpose(2, 1, 0, 3).reshape(tokens, width)

    head_parts = math.gcd(sub, w_query.shape[2] // HD)
    copies = sub // head_parts
    heads_wide = w_query.shape[2] // head_parts
    hidden_local = w_gate.shape[2]
    hidden_wide = -(-hidden_local // (sub * 128)) * 128
    windows = sub == 2 and (hidden_local - hidden_wide) % 128 == 0
    hidden_pad = 0 if windows else hidden_wide * sub - hidden_local
    overlap = hidden_wide * sub - hidden_local if windows else 0
    hidden_mine = jnp.arange(hidden_wide) >= overlap * sub_at
    kernels = kernels and windows and copies == 1

    def to_windows(weight, axis):
        if windows:
            size = weight.shape[axis]
            parts = [
                lax.slice_in_dim(weight, 0, hidden_wide, axis=axis),
                lax.slice_in_dim(weight, size - hidden_wide, size, axis=axis),
            ]
        else:
            pad = [(0, 0)] * 3
            pad[axis] = (0, hidden_pad)
            parts = jnp.split(jnp.pad(weight, pad), sub, axis=axis)
        parts = jnp.stack(parts, axis=1)
        return parts.reshape(group, *parts.shape[2:])

    def to_heads(weight, axis):
        parts = jnp.stack(jnp.split(weight, head_parts, axis=axis), axis=1)
        return jnp.repeat(parts, copies, axis=1).reshape(group, *parts.shape[2:])

    def to_all(weight):
        return to_heads(jnp.broadcast_to(weight, (experts, *weight.shape)), 2)

    def swap_group(value):
        return lax.all_to_all(value, GROUP, 0, 0)

    def as_columns(parts):
        return parts.reshape(width, parts.shape[2])

    def as_rows(parts):
        return parts.transpose(1, 0, 2).reshape(parts.shape[1], width)

    pack = jnp.concatenate(
        [jnp.pad(facts.T, ((0, 16 - facts.shape[1]), (0, 0))) for facts in (token_pack, feature_pack)],
        axis=1,
    )
    if kernels:
        (packs, all_in, top_all), (my_query, my_key_value, my_out) = start(
            sizes,
            [pack, hidden_in, cotangent],
            [
                ("columns_out", ((0, heads_wide, False),), w_query, heads_wide),
                (
                    "pair_out",
                    ((0, heads_wide, False), (heads_wide, heads_wide, False)),
                    jnp.stack([w_key, w_value]),
                    2 * heads_wide,
                ),
                ("rows_out", ((0, heads_wide, True),), w_out, heads_wide),
            ],
            0,
        )
        packs = packs.reshape(group, 16, -1)
    else:
        packs = lax.all_gather(pack, GROUP)
        all_in, top_all = everywhere(hidden_in), everywhere(cotangent)
        first = [to_heads(w_query, 2), to_all(w_key), to_all(w_value), to_heads(w_out, 1)]
        first = swap_group(jnp.concatenate(first, axis=2))
        my_query = as_columns(first[:, :, :heads_wide])
        my_key_value = as_columns(first[:, :, heads_wide : 3 * heads_wide])
        my_out = as_rows(first[:, :, 3 * heads_wide :])
    packs = packs.transpose(0, 2, 1)
    token_facts = packs[:, :tokens].reshape(total, 16).astype(jnp.int32)
    feature_facts = packs[:, tokens:].reshape(width, 16)
    gain_att = feature_facts[:, 0].astype(F32)
    route_att = feature_facts[:, 1 : 1 + experts]
    gain_ffn = feature_facts[:, 1 + experts].astype(F32)
    route_ffn = feature_facts[:, 2 + experts : 2 + 2 * experts]

    def move(kind, weight):
        if kind == "columns_out":
            return as_columns(swap_group(to_windows(weight, 2)))
        if kind == "rows_out":
            return as_rows(swap_group(to_windows(weight, 1)))
        if kind == "columns_home":
            return swap_group(weight.reshape(group, rows_own, -1))
        return swap_group(weight.reshape(-1, group, rows_own).transpose(1, 0, 2))

    def exchanged(part, put, add, scale, facts, tail, moves, number):
        if kernels:
            moves = [
                (kind, ((0, early, False), (early, wide - early, True)), weight, wide)
                for kind, weight, wide, early in moves
            ]
            raw, out, told, moved = exchange(
                sizes, part, put, add, scale, facts, tail, moves, number
            )
            told = told.reshape(experts, facts.shape[0], layer, facts.shape[1])
            return raw, out, told.transpose(0, 2, 1, 3), moved
        home = go_home(layer_sum(part))
        summed = jnp.sum(home.astype(F32), axis=0) if put is None else put_home(put, home)
        raw = add + summed
        out = (raw * scale).astype(BF)
        out = everywhere_layer(out) if tail == "spread" else to_tokens(out)
        told = lax.all_gather(facts, ALL).reshape(experts, layer, *facts.shape)
        return raw, out, told, [move(kind, weight) for kind, weight, _, _ in moves]

    own_first = exp_at * own_seqs
    where = partial(
        Routing,
        seqs=seqs,
        seq_len=seq_len,
        experts=experts,
        cap=cap,
        mine=exp_at,
        own_first=own_first,
        own_seqs=own_seqs,
    )
    att = where(token_facts[:, 0:2])
    if copies > 1:
        turn = jnp.arange(seqs, dtype=jnp.int32) % copies == sub_at % copies
        att.pick = att.pick * turn.astype(BF)[:, None, None]
    ffn = where(token_facts[:, 2:4])
    spans = token_facts[:, 4].reshape(seqs, seq_len).astype(F32)
    cosine, sine = rope_tables(seq_len)
    positions = jnp.arange(seq_len, dtype=jnp.int32).astype(F32)
    pick_f32 = att.pick.astype(F32)
    slot_position = jnp.sum(pick_f32 * positions[None, None, :], axis=2)
    slot_span = jnp.sum(pick_f32 * spans[:, None, :], axis=2)
    slot_cosine = dot_exact("spt,tf->spf", pick_f32, cosine)
    slot_sine = dot_exact("spt,tf->spf", pick_f32, sine)
    allowed = (positions[None, None, :] <= slot_position[:, :, None]) | (
        (slot_span[:, :, None] == spans[:, None, :]) & (slot_span[:, :, None] > 0)
    )

    my_gate = move("columns_out", after(w_gate, all_in))
    x_all = all_in.astype(F32)
    scale_in = lax.rsqrt(jnp.mean(x_all * x_all, axis=1, keepdims=True) + EPS)
    h1 = (x_all * scale_in * gain_att[None, :]).astype(BF)
    heads = heads_wide // HD
    scale = 1.0 / math.sqrt(HD)
    kv = dot("td,dm->tm", h1, my_key_value)
    keys = rotate(
        kv[:, :heads_wide].reshape(seqs, seq_len, heads, HD),
        cosine[None, :, None, :],
        sine[None, :, None, :],
    ).astype(BF)
    values = kv[:, heads_wide:].astype(BF).reshape(seqs, seq_len, heads, HD)
    att_gates = att.gates(dot("td,de->te", h1, route_att))
    att_slot_gate = att.slot_gates(att_gates).reshape(slots, 1)
    h1_slots = att.take(h1)
    queries = rotate(
        dot("td,dm->tm", h1_slots, my_query).reshape(seqs, cap, heads, HD),
        slot_cosine[:, :, None, :],
        slot_sine[:, :, None, :],
    ).astype(BF)
    scores = dot("sqhd,skhd->shqk", queries, keys) * scale
    scores = jnp.where(allowed[:, None], scores, -1e30)
    expo = jnp.exp(scores - jnp.max(scores, axis=-1, keepdims=True))
    probs = expo / jnp.sum(expo, axis=-1, keepdims=True)
    probs_low = probs.astype(BF)
    mixed = dot("shqk,skhd->sqhd", probs_low, values).astype(BF).reshape(slots, heads_wide)
    branch_att = dot("cm,md->cd", mixed, my_out) * att_slot_gate
    own_in = lax.dynamic_slice(
        x_all, (exp_at * own_tokens, layer_at * feats), (own_tokens, feats)
    )
    nothing = jnp.zeros((8, 128), F32)
    mid, mid_all, _, (my_up,) = exchanged(
        branch_att.astype(BF),
        att.put,
        own_in,
        jnp.ones((1, feats), F32),
        nothing,
        "spread",
        [("columns_out", w_up, hidden_wide, hidden_wide // 3)],
        1,
    )
    my_down = move("rows_out", after(w_down, mid_all))
    mid_all = mid_all.astype(F32)

    scale_mid = lax.rsqrt(jnp.mean(mid_all * mid_all, axis=1, keepdims=True) + EPS)
    unit_mid = mid_all * scale_mid
    h2 = (unit_mid * gain_ffn[None, :]).astype(BF)
    ffn_gates = ffn.gates(dot("td,de->te", h2, route_ffn))
    ffn_slot_gate = ffn.slot_gates(ffn_gates).reshape(slots, 1)
    h2_slots = ffn.take(h2)
    pre_gate = dot("cd,df->cf", h2_slots, my_gate)
    pre_up = dot("cd,df->cf", h2_slots, my_up)
    sigma = jax.nn.sigmoid(pre_gate)
    swish = pre_gate * sigma
    hidden = jnp.where(hidden_mine, swish * pre_up, 0.0).astype(BF)
    branch_ffn = dot("cf,fd->cd", hidden, my_down) * ffn_slot_gate

    top_slots = ffn.take(top_all)
    grad_hidden = dot("cd,fd->cf", top_slots, my_down)
    ffn_gate_part = jnp.sum(hidden.astype(F32) * grad_hidden, axis=1)
    grad_hidden = jnp.where(hidden_mine, grad_hidden * ffn_slot_gate, 0.0)
    grad_branch = (top_slots.astype(F32) * ffn_slot_gate).astype(BF)
    grad_pre_gate = (
        grad_hidden * pre_up * sigma * (1.0 + pre_gate * (1.0 - sigma))
    ).astype(BF)
    grad_pre_up = (grad_hidden * swish).astype(BF)
    ffn_taken = dot("cf,df->cd", grad_pre_gate, my_gate) + dot("cf,df->cd", grad_pre_up, my_up)
    own_at = (exp_at * own_tokens, layer_at * feats)
    own_unit_mid = lax.dynamic_slice(unit_mid, own_at, (own_tokens, feats))
    own_scale_mid = lax.dynamic_slice_in_dim(scale_mid, exp_at * own_tokens, own_tokens, 0)
    own_gain_ffn = lax.dynamic_slice_in_dim(gain_ffn, layer_at * feats, feats, 0)
    grad_down_w = dot("cf,cd->fd", hidden, grad_branch).astype(BF)
    def gate_facts(told):
        return jnp.sum(told, axis=1).reshape(experts, seqs, cap)

    grad_second, second_all, ffn_told, (grad_down,) = exchanged(
        ffn_taken.astype(BF),
        ffn.put,
        jnp.zeros((own_tokens, feats), F32),
        own_gain_ffn[None, :] * own_scale_mid,
        ffn_gate_part.reshape(-1, 128),
        "spread",
        [("rows_home", grad_down_w, hidden_wide, hidden_wide // 3)],
        2,
    )
    ffn_logit_grads = logit_grads(ffn_gates, ffn.token_grads(gate_facts(ffn_told)))
    own_ffn_logits = lax.dynamic_slice_in_dim(
        ffn_logit_grads, exp_at * own_tokens, own_tokens, 0
    )
    own_route_ffn = lax.dynamic_slice_in_dim(
        route_ffn.astype(F32), layer_at * feats, feats, 0
    )
    grad_second = grad_second + dot_exact("te,fe->tf", own_ffn_logits, own_route_ffn)
    norm_ffn_part = jnp.sum(grad_second * own_unit_mid, axis=0)
    grad_gate_w = dot("cd,cf->df", h2_slots, grad_pre_gate).astype(BF)
    grad_gate = move("columns_home", after(grad_gate_w, second_all))
    second_all = second_all.astype(F32) + router_rows(ffn_logit_grads, route_ffn) * (
        gain_ffn[None, :] * scale_mid
    )
    grad_mid = (
        top_all.astype(F32)
        + second_all
        - unit_mid * jnp.mean(second_all * unit_mid, axis=1, keepdims=True)
    )

    mid_slots = att.take(grad_mid.astype(BF))
    grad_mixed = dot("cd,md->cm", mid_slots, my_out)
    att_gate_part = jnp.sum(mixed.astype(F32) * grad_mixed, axis=1)
    grad_mixed = (grad_mixed * att_slot_gate).astype(BF).reshape(seqs, cap, heads, HD)
    grad_att_branch = (mid_slots.astype(F32) * att_slot_gate).astype(BF)
    grad_soft = dot("sqhd,skhd->shqk", grad_mixed, values)
    grad_values = dot("shqk,sqhd->skhd", probs_low, grad_mixed)
    grad_scores = (
        probs * (grad_soft - jnp.sum(probs * grad_soft, axis=-1, keepdims=True))
    ).astype(BF)
    grad_queries = dot("shqk,skhd->sqhd", grad_scores, keys) * scale
    grad_keys = dot("shqk,sqhd->skhd", grad_scores, queries) * scale
    grad_qpre = (
        rotate_back(grad_queries, slot_cosine[:, :, None, :], slot_sine[:, :, None, :])
        .astype(BF)
        .reshape(slots, heads_wide)
    )
    att_taken = dot("cm,dm->cd", grad_qpre, my_query)
    grad_kpre = rotate_back(
        grad_keys, cosine[None, :, None, :], sine[None, :, None, :]
    ).reshape(total, heads_wide)
    kv_low = jnp.concatenate([grad_kpre, grad_values.reshape(total, heads_wide)], axis=1)
    kv_low = kv_low.astype(BF)
    first_part = dot("tm,dm->td", kv_low, my_key_value) + att.give(att_taken.astype(BF))
    own_scale_in = lax.dynamic_slice_in_dim(scale_in, exp_at * own_tokens, own_tokens, 0)
    own_gain_att = lax.dynamic_slice_in_dim(gain_att, layer_at * feats, feats, 0)
    grad_up_w = dot("cd,cf->df", h2_slots, grad_pre_up).astype(BF)
    grad_first, first_tokens, att_told, (grad_up,) = exchanged(
        first_part.astype(BF),
        None,
        jnp.zeros((own_tokens, feats), F32),
        own_gain_att[None, :] * own_scale_in,
        att_gate_part.reshape(-1, 128),
        "tokens",
        [("columns_home", grad_up_w, hidden_wide, hidden_wide // 3)],
        3,
    )
    att_logit_grads = logit_grads(att_gates, att.token_grads(gate_facts(att_told)))
    own_att_logits = lax.dynamic_slice_in_dim(
        att_logit_grads, exp_at * own_tokens, own_tokens, 0
    )
    own_route_att = lax.dynamic_slice_in_dim(
        route_att.astype(F32), layer_at * feats, feats, 0
    )
    grad_first = grad_first + dot_exact("te,fe->tf", own_att_logits, own_route_att)
    norm_att_part = jnp.sum(grad_first * own_in * own_scale_in, axis=0)
    token_at = group_at * tokens
    first_tokens = first_tokens.astype(F32) + router_rows(
        lax.dynamic_slice_in_dim(att_logit_grads, token_at, tokens, 0), route_att
    ) * (gain_att[None, :] * lax.dynamic_slice_in_dim(scale_in, token_at, tokens, 0))
    unit_in = lax.dynamic_slice_in_dim(x_all * scale_in, token_at, tokens, 0)
    grad_in = (
        lax.dynamic_slice_in_dim(grad_mid, token_at, tokens, 0)
        + first_tokens
        - unit_in * jnp.mean(first_tokens * unit_in, axis=1, keepdims=True)
    )


    def router_grad(rows, grads):
        own = lax.dynamic_slice_in_dim(rows, group_at * rows_own, rows_own, 1)
        return dot_exact("tf,te->fe", own.astype(F32), grads)

    grad_router_att = router_grad(h1, att_logit_grads)
    grad_router_ffn = router_grad(h2, ffn_logit_grads)

    def windows_home(back, axis):
        back = back.reshape(experts, sub, *back.shape[1:])
        parts = [lax.index_in_dim(back, i, 1, keepdims=False) for i in range(sub)]
        parts[1:] = [
            lax.slice_in_dim(part, overlap, part.shape[axis], axis=axis) for part in parts[1:]
        ]
        whole = jnp.concatenate(parts, axis=axis)
        return lax.slice_in_dim(whole, 0, hidden_local, axis=axis).astype(F32)

    def heads_home(back, axis):
        back = back.reshape(experts, head_parts, copies, *back.shape[1:])
        if copies > 1:
            back = jnp.sum(back.astype(F32), axis=2, keepdims=True)
        parts = [back[:, i, 0] for i in range(head_parts)]
        return jnp.concatenate(parts, axis=axis).astype(F32)

    grad_query_w = dot("cd,cm->dm", h1_slots, grad_qpre).astype(BF)
    grad_out_w = dot("cm,cd->md", mixed, grad_att_branch).astype(BF)
    grad_kv_w = dot("td,tm->dm", h1, kv_low).astype(BF)
    _, hidden_out, norm_told, (grad_out, grad_query, grad_kv) = exchanged(
        after(branch_ffn.astype(BF), first_tokens),
        ffn.put,
        mid,
        jnp.ones((1, feats), F32),
        jnp.pad(jnp.stack([norm_att_part, norm_ffn_part]), ((0, 6), (0, 0))),
        "tokens",
        [
            ("rows_home", grad_out_w, heads_wide, heads_wide),
            ("columns_home", grad_query_w, heads_wide, heads_wide),
            ("columns_home", grad_kv_w, 2 * heads_wide, 2 * heads_wide),
        ],
        4,
    )
    norm_parts = jnp.sum(norm_told[:, :, :2], axis=0).transpose(1, 0, 2).reshape(2, width)
    norm_grads = lax.dynamic_slice_in_dim(norm_parts, group_at * rows_own, rows_own, 1)
    grad_out = heads_home(grad_out, 1)
    grad_query = heads_home(grad_query, 2)
    grad_key, grad_value = (
        jnp.sum(heads_home(grad_kv[:, :, i * heads_wide : (i + 1) * heads_wide], 2), axis=0)
        for i in (0, 1)
    )
    return (
        hidden_out,
        grad_in,
        norm_grads[0],
        grad_router_att,
        grad_query,
        grad_out,
        grad_key,
        grad_value,
        norm_grads[1],
        grad_router_ffn,
        windows_home(grad_gate, 2),
        windows_home(grad_up, 2),
        windows_home(grad_down, 1),
    )


def solution(mesh):
    ctx, tp = mesh.shape["ctx"], mesh.shape["tp"]
    shard = mesh.shape["shard"]
    by_token, by_feature = P(GROUP, None), P(GROUP)
    columns, rows = P(None, GROUP, "tp"), P(None, "tp", GROUP)

    return jax.shard_map(
        partial(shards, (shard, ctx, tp)),
        mesh=mesh,
        in_specs=(
            by_token,
            by_token,
            by_token,
            P(GROUP),
            by_feature,
            by_token,
            columns,
            rows,
            P(GROUP, "tp"),
            P(GROUP, "tp"),
            by_feature,
            by_token,
            columns,
            columns,
            rows,
            by_token,
        ),
        out_specs=(
            by_token,
            by_token,
            by_feature,
            by_token,
            columns,
            rows,
            P(GROUP, "tp"),
            P(GROUP, "tp"),
            by_feature,
            by_token,
            columns,
            columns,
            rows,
        ),
        check_vma=False,
    )
```

```python
from functools import partial
import math

import numpy as np

import jax
import jax.numpy as jnp
from jax import lax
from jax.experimental import pallas as pl
from jax.experimental.pallas import tpu as pltpu
from jax.sharding import PartitionSpec as P

HD = 128
EPS = 1e-06
BF = jnp.bfloat16
F32 = jnp.float32
MESH = pl.DeviceIdType.MESH
VMEM_BYTES = 40 * 2**20
GROUP = ("shard", "ctx")
ALL = ("shard", "ctx", "tp")


def dot(spec, left, right):
    return jnp.einsum(spec, left, right, preferred_element_type=F32)


def dot_exact(spec, left, right):
    return jnp.einsum(
        spec, left, right, preferred_element_type=F32, precision=lax.Precision.HIGHEST
    )


def after(value, *others):
    return lax.optimization_barrier((value, *others))[0]


def rope_tables(count):
    half_dim = HD // 2
    freq_index = (jnp.arange(HD) % half_dim).astype(F32)
    frequency = 10000.0 ** (-2.0 * freq_index / HD)
    angles = jnp.arange(count, dtype=F32)[:, None] * frequency[None, :]
    return jnp.cos(angles), jnp.sin(angles)


def rotate(rows, cosine, sine):
    half_dim = HD // 2
    turned = jnp.concatenate([-rows[..., half_dim:], rows[..., :half_dim]], axis=-1)
    return rows * cosine + turned * sine


def rotate_back(rows, cosine, sine):
    half_dim = HD // 2
    turned = rows * sine
    return rows * cosine + jnp.concatenate(
        [turned[..., half_dim:], -turned[..., :half_dim]], axis=-1
    )


class Place:
    def __init__(self, sizes):
        self.experts, self.sub, self.ctx, self.tp = sizes
        self.chips = self.sub * self.tp // 2
        self.members = self.experts * self.sub
        self.group = lax.axis_index(GROUP)
        self.tp_at = lax.axis_index("tp")
        self.exp = self.group // self.sub
        here = (self.group % self.sub) * self.tp + self.tp_at
        self.chip, self.core = here // 2, here % 2

    def device(self, exp, chip, core):
        here = chip * 2 + core
        group = exp * self.sub + here // self.tp
        return (group // self.ctx, group % self.ctx, here % self.tp)

    def member(self, group):
        return (group // self.ctx, group % self.ctx, self.tp_at)

    def sibling(self):
        return self.device(self.exp, self.chip, 1 - self.core)

    def other_exp(self, k):
        return (self.exp + k) % self.experts

    def other_chip(self, k):
        return (self.chip + k) % self.chips

    def meet(self, whole_group):
        barrier = pltpu.get_barrier_semaphore()
        layer = 2 * self.chips
        here = self.chip * 2 + self.core
        others = [(here + k) % layer for k in range(1, layer)]
        peers = [self.device(self.exp, there // 2, there % 2) for there in others]
        if whole_group:
            peers += [
                self.member((self.group + k) % self.members) for k in range(1, self.members)
            ]
        else:
            peers += [
                self.device(self.other_exp(k), self.chip, self.core)
                for k in range(1, self.experts)
            ]
        for peer in peers:
            pl.semaphore_signal(barrier, inc=1, device_id=peer, device_id_type=MESH)
        pl.semaphore_wait(barrier, len(peers))


def block(start, size, unit):
    return pl.ds(pl.multiple_of(start, unit), size)


def send(src, dst, sems, at, device):
    copy = pltpu.make_async_remote_copy(
        src_ref=src,
        dst_ref=dst,
        send_sem=sems.at[(0, *at)],
        recv_sem=sems.at[(1, *at)],
        device_id=device,
        device_id_type=MESH,
    )
    copy.start()
    return copy


class Mover:
    def __init__(self, number, kind, cuts, src, dst, sems, own_sems):
        self.number, self.kind, self.cuts = number, kind, cuts
        self.src, self.dst, self.sems, self.own_sems = src, dst, sems, own_sems
        self.copies = []

    def ends(self, place, group, low, size):
        exp, sub = group // place.sub, group % place.sub
        me, src, dst = place.group, self.src, self.dst
        if self.kind == "columns_out":
            rows, step = src.shape[1], (src.shape[2] - dst.shape[1]) // max(place.sub - 1, 1)
            return (
                src.at[exp, :, block(sub * step + low, size, 128)],
                dst.at[block(me * rows, rows, 16), pl.ds(low, size)],
            )
        if self.kind == "rows_out":
            cols, step = src.shape[2], (src.shape[1] - dst.shape[0]) // max(place.sub - 1, 1)
            return (
                src.at[exp, block(sub * step + low, size, 16)],
                dst.at[pl.ds(low, size), block(me * cols, cols, 128)],
            )
        if self.kind == "columns_home":
            rows = dst.shape[1]
            return (
                src.at[block(group * rows, rows, 16), pl.ds(low, size)],
                dst.at[me, :, pl.ds(low, size)],
            )
        cols = dst.shape[2]
        return (
            src.at[pl.ds(low, size), block(group * cols, cols, 128)],
            dst.at[me, pl.ds(low, size)],
        )

    def start(self, place, late):
        for cut, (low, size, is_late) in enumerate(self.cuts):
            if is_late != late or not size:
                continue
            for k in range(1, place.members):
                group = (place.group + k) % place.members
                src, dst = self.ends(place, group, low, size)
                at = (self.number, cut, k - 1)
                self.copies.append(send(src, dst, self.sems, at, place.member(group)))
            src, dst = self.ends(place, place.group, low, size)
            own = pltpu.make_async_copy(src, dst, self.own_sems.at[self.number, cut])
            own.start()
            self.copies.append(own)

    def wait(self):
        for copy in self.copies:
            copy.wait()


def moved_shape(sizes, kind, array, wide):
    experts, sub, _, _ = sizes
    group = experts * sub
    if kind == "columns_out":
        return (array.shape[1] * group, wide)
    if kind == "rows_out":
        return (wide, array.shape[2] * group)
    if kind == "columns_home":
        return (group, array.shape[0] // group, array.shape[1])
    return (group, array.shape[0], array.shape[1] // group)


class Line:
    def __init__(self, place, spot, sems):
        self.place, self.spot, self.sems = place, spot, sems

    def give(self, src, origin, up, step):
        place = self.place
        to = place.exp + 1 if up else place.exp - 1
        return pltpu.make_async_remote_copy(
            src_ref=src,
            dst_ref=self.spot(origin),
            send_sem=self.sems.at[0, 0 if up else 1, step],
            recv_sem=self.sems.at[1, 0 if up else 1, step],
            device_id=place.device(to, place.chip, place.core),
            device_id_type=MESH,
        )

    def start(self, src):
        place = self.place
        self.src = src

        @pl.when(place.exp < place.experts - 1)
        def _():
            self.give(src, place.exp, True, 0).start()

        @pl.when(place.exp > 0)
        def _():
            self.give(src, place.exp, False, 0).start()

    def origin(self, turn):
        place = self.place
        if place.experts != 4:
            return (place.exp + place.experts - turn) % place.experts
        high = place.exp // 2
        at = place.exp * (1 - high) + (3 - place.exp) * high
        origin = 1 - at if turn == 1 else turn
        return origin * (1 - high) + (3 - origin) * high

    def arrived(self, turn):
        place = self.place
        origin = self.origin(turn)

        @pl.when(origin < place.exp)
        def _():
            step = place.exp - origin - 1
            self.give(self.spot(origin), origin, True, step).wait_recv()

            @pl.when(place.exp < place.experts - 1)
            def _():
                self.give(self.spot(origin), origin, True, step + 1).start()

        @pl.when(origin > place.exp)
        def _():
            step = origin - place.exp - 1
            self.give(self.spot(origin), origin, False, step).wait_recv()

            @pl.when(place.exp > 0)
            def _():
                self.give(self.spot(origin), origin, False, step + 1).start()

        return origin

    def finish(self):
        place = self.place
        for step in range(place.experts - 1):

            @pl.when((place.exp < place.experts - 1) & (place.exp >= step))
            def _():
                self.give(self.src, place.exp, True, step).wait_send()

            @pl.when((place.exp > 0) & (place.exp + step < place.experts))
            def _():
                self.give(self.src, place.exp, False, step).wait_send()


class Spread:
    def __init__(self, place, mine, out, by_token, exp_sems, chip_sems, core_sems, pieces=1):
        self.place, self.mine, self.out, self.by_token = place, mine, out, by_token
        self.rows, self.cols = mine.shape[0] // pieces, mine.shape[1]
        self.pieces = pieces
        self.exp_sems, self.chip_sems, self.core_sems = exp_sems, chip_sems, core_sems
        self.square = place.chips == 4 and place.tp == 4 and self.rows % 64 == 0
        self.line = None
        if pieces == 1 and self.rows % 64 == 0:
            self.line = Line(place, lambda origin: self.spot(origin, place.chip), exp_sems)

    def spot(self, exp, chip, low=0, size=None):
        place = self.place
        here = chip * 2 + place.core
        if self.by_token:
            row = (exp * place.sub + here // place.tp) * self.rows
            col = (here % place.tp) * self.cols
        else:
            row, col = exp * self.rows, here * self.cols
        unit = math.gcd(self.rows, 16)
        size = size or self.rows
        return self.out.at[block(row + low, size, unit), block(col, self.cols, 128)]

    def piece(self, exp):
        if self.pieces == 1:
            return self.mine
        return self.mine.at[block(exp * self.rows, self.rows, 16)]

    def near(self):
        place = self.place
        side = place.chip // 2
        along = place.chip % 2
        return [(1 - side) * 2 + along, side * 2 + 1 - along]

    def to_chip(self, src, dst, turn, k, chip):
        device = self.place.device(self.place.exp, chip, self.place.core)
        self.chip_copies[turn].append(send(src, dst, self.chip_sems, (turn, k), device))

    def to_chips(self, exp, src, turn):
        place = self.place
        if self.square:
            chips = self.near()
        else:
            chips = [place.other_chip(k) for k in range(1, place.chips)]
        for k, chip in enumerate(chips):
            self.to_chip(src, self.spot(exp, place.chip), turn, k, chip)

    def to_core(self, exp, chip, src, turn, k):
        self.core_copies.append(
            send(src, self.spot(exp, chip), self.core_sems, (turn, k), self.place.sibling())
        )

    def start(self, own_sem):
        place = self.place
        home = self.spot(place.exp, place.chip)
        mine = self.piece(place.exp)
        self.own = pltpu.make_async_copy(mine, home, own_sem)
        self.own.start()
        self.chip_copies = [[] for _ in range(place.experts)]
        self.core_copies = []
        if self.line:
            self.line.start(mine)
        else:
            self.exp_copies = [
                send(
                    self.piece(place.other_exp(k)),
                    home,
                    self.exp_sems,
                    (0, k - 1),
                    place.device(place.other_exp(k), place.chip, place.core),
                )
                for k in range(1, place.experts)
            ]
        self.to_chips(place.exp, mine, 0)
        self.to_core(place.exp, place.chip, mine, 0, 0)

    def from_layer(self, turn):
        place = self.place
        if self.line:
            source = self.line.arrived(turn)
        else:
            self.exp_copies[turn - 1].wait_recv()
            source = (place.exp + place.experts - turn) % place.experts
        self.sources[turn] = source
        here = self.spot(source, place.chip)
        self.to_chips(source, here, turn)
        self.to_core(source, place.chip, here, turn, 0)

    def from_near(self, turn):
        source, copies = self.sources[turn], self.chip_copies[turn]
        if not self.square:
            return
        half = self.rows // 2
        side, along = self.near()
        copies[0].wait_recv()
        part = self.spot(source, side, 0, half)
        self.to_chip(part, part, turn, 2, along)
        self.to_core(source, side, self.spot(source, side), turn, 1)
        copies[1].wait_recv()
        part = self.spot(source, along, half, half)
        self.to_chip(part, part, turn, 3, side)
        self.to_core(source, along, self.spot(source, along), turn, 2)

    def from_far(self, turn):
        place = self.place
        source, copies = self.sources[turn], self.chip_copies[turn]
        if self.square:
            copies[2].wait_recv()
            copies[3].wait_recv()
            far = 3 - place.chip
            self.to_core(source, far, self.spot(source, far), turn, 3)
            return
        for k in range(1, place.chips):
            copies[k - 1].wait_recv()
            chip = (place.chip + place.chips - k) % place.chips
            self.to_core(source, chip, self.spot(source, chip), turn, k)

    def run(self):
        place = self.place
        self.sources = {0: place.exp}
        for stage in range(place.experts + 2):
            if 1 <= stage + 1 < place.experts:
                self.from_layer(stage + 1)
            if 0 <= stage < place.experts:
                self.from_near(stage)
            if 0 <= stage - 1 < place.experts:
                self.from_far(stage - 1)
        for copy in self.core_copies:
            copy.wait()
        if self.line:
            self.line.finish()
        else:
            for copy in self.exp_copies:
                copy.wait_send()
        for copies in self.chip_copies:
            for copy in copies:
                copy.wait_send()
        self.own.wait()


class Pair:
    def __init__(self, place, src, out, line_sems, sems, own_sems):
        self.place, self.src, self.out, self.sems, self.own_sems = place, src, out, sems, own_sems
        self.rows = src.shape[1]
        self.half = src.shape[2] // place.sub
        size = self.rows * place.sub

        def spot(exp):
            return out.at[block(exp * size, size, 16)]

        self.line = Line(place, spot, line_sems)

    def start(self):
        place = self.place
        land = block(place.group * self.rows, self.rows, 16)
        sub = place.group % place.sub
        self.copies = []
        for i in range(2):
            dst = self.out.at[land, pl.ds(i * self.half, self.half)]
            for k in range(1, place.sub):
                other = (sub + k) % place.sub
                src = self.src.at[i, :, block(other * self.half, self.half, 128)]
                group = place.exp * place.sub + other
                self.copies.append(send(src, dst, self.sems, (i, k - 1), place.member(group)))
            src = self.src.at[i, :, block(sub * self.half, self.half, 128)]
            own = pltpu.make_async_copy(src, dst, self.own_sems.at[i])
            own.start()
            self.copies.append(own)

    def share(self):
        for copy in self.copies:
            copy.wait()
        self.line.start(self.line.spot(self.place.exp))

    def run(self):
        for turn in range(1, self.place.experts):
            self.line.arrived(turn)
        self.line.finish()


class ToTokens:
    def __init__(self, place, mine, out, chip_sems, core_sems):
        self.place, self.mine, self.out = place, mine, out
        self.chip_sems, self.core_sems = chip_sems, core_sems
        self.rows, self.cols = out.shape[0], mine.shape[1]

    def spot(self, chip):
        here = chip * 2 + self.place.core
        return self.out.at[:, block(here * self.cols, self.cols, 128)]

    def part(self, chip):
        sub = (chip * 2) // self.place.tp
        return self.mine.at[block(sub * self.rows, self.rows, 16)]

    def start(self, own_sem):
        place = self.place
        mine = self.part(place.chip)
        self.own = pltpu.make_async_copy(mine, self.spot(place.chip), own_sem)
        self.own.start()
        self.copies = []
        for k in range(1, place.chips):
            chip = place.other_chip(k)
            self.copies.append(
                send(
                    self.part(chip),
                    self.spot(place.chip),
                    self.chip_sems,
                    (k - 1,),
                    place.device(place.exp, chip, place.core),
                )
            )
        self.core = [send(mine, self.spot(place.chip), self.core_sems, (0,), place.sibling())]

    def run(self):
        place, core, copies = self.place, self.core, self.copies
        for k in range(1, place.chips):
            copies[k - 1].wait_recv()
            spot = self.spot((place.chip + place.chips - k) % place.chips)
            core.append(send(spot, spot, self.core_sems, (k,), place.sibling()))
        for copy in core:
            copy.wait()
        for copy in copies:
            copy.wait_send()
        self.own.wait()


class Fold:
    def __init__(self, place, part, home, scratch):
        self.place, self.part, self.home = place, part, home
        (
            self.core_got,
            self.chip_out,
            self.chip_got,
            self.exp_out,
            self.core_sems,
            self.chip_sems,
            self.exp_sems,
        ) = scratch
        self.feats = home.shape[2]

    def columns(self, chip, core):
        return block((chip * 2 + core) * self.feats, self.feats, 128)

    def run(self):
        place, part = self.place, self.part
        experts, chips = place.experts, place.chips
        each = self.home.shape[1]
        core_copies = {}
        for k in [*range(1, chips), 0]:
            away = part.at[:, self.columns(place.other_chip(k), 1 - place.core)]
            core_copies[k] = send(away, self.core_got.at[k], self.core_sems, (k,), place.sibling())
        chip_copies = []
        for k in range(1, chips):
            chip = place.other_chip(k)
            core_copies[k].wait_recv()
            mine = part[:, self.columns(chip, place.core)].astype(F32)
            self.chip_out[k - 1] = (mine + self.core_got[k].astype(F32)).astype(BF)
            chip_copies.append(
                send(
                    self.chip_out.at[k - 1],
                    self.chip_got.at[k - 1],
                    self.chip_sems,
                    (k - 1,),
                    place.device(place.exp, chip, place.core),
                )
            )
        core_copies[0].wait_recv()
        total = part[:, self.columns(place.chip, place.core)].astype(F32)
        total = total + self.core_got[0].astype(F32)
        for k in range(1, chips):
            chip_copies[k - 1].wait_recv()
            total = total + self.chip_got[k - 1].astype(F32)
        self.exp_out[...] = total.astype(BF)
        exp_copies = []
        for k in range(1, experts):
            exp = place.other_exp(k)
            exp_copies.append(
                send(
                    self.exp_out.at[block(exp * each, each, 16)],
                    self.home.at[place.exp],
                    self.exp_sems,
                    (k - 1,),
                    place.device(exp, place.chip, place.core),
                )
            )
        self.home[place.exp] = self.exp_out[block(place.exp * each, each, 16)]
        for copy in exp_copies:
            copy.wait_recv()
        for copy in [*core_copies.values(), *chip_copies, *exp_copies]:
            copy.wait_send()


def start_kernel(sizes, count, moves, *refs):
    place = Place(sizes)
    blocks, refs = take(refs, count)
    (pair_src,), refs = take(refs, 1)
    sources, refs = take(refs, len(moves))
    outs, refs = take(refs, count)
    (pair_out,), refs = take(refs, 1)
    landings, refs = take(refs, len(moves))
    (own_sems, exp_sems, chip_sems, core_sems), refs = take(refs, 4)
    pair_sems, refs = take(refs, 3)
    movers = make_movers(moves, sources, landings, refs)
    pair = Pair(place, pair_src, pair_out, *pair_sems)
    spreads = []
    for i, (rows, out) in enumerate(zip(blocks, outs)):
        quarter = rows.shape[1] // place.tp
        mine = rows.at[:, block(place.tp_at * quarter, quarter, 128)]
        sems = (s.at[i] for s in (exp_sems, chip_sems, core_sems))
        spreads.append(Spread(place, mine, out, True, *sems))
    place.meet(True)
    pair.start()
    for i, spread in enumerate(spreads[:-1]):
        spread.start(own_sems.at[i])
    pair.share()
    for mover in movers:
        mover.start(place, False)
    spreads[-1].start(own_sems.at[count - 1])
    for spread in spreads:
        spread.run()
    pair.run()
    for mover in movers:
        mover.wait()


def take(refs, count):
    return refs[:count], refs[count:]


def turned(left, right):
    return lax.dot_general(left, right, (((0,), (0,)), ((), ())), preferred_element_type=F32)


def row_sums(weights, rows):
    return lax.dot_general(
        weights,
        rows,
        (((1,), (1,)), ((), ())),
        preferred_element_type=F32,
        precision=lax.Precision.HIGHEST,
    )


def make_movers(moves, sources, landings, sems):
    return [
        Mover(i, kind, cuts, source, landing, *sems)
        for i, ((kind, cuts), source, landing) in enumerate(zip(moves, sources, landings))
    ]


def exchange_kernel(sizes, tail, extras, moves, *refs):
    place = Place(sizes)
    (part, put, add, scale), refs = take(refs, 4)
    if tail == "slots":
        (next_put, linear, square), refs = take(refs, 3)
    else:
        (facts, *more), refs = take(refs, extras)
    sources, refs = take(refs, len(moves))
    (raw, all_facts), refs = take(refs, 2)
    outs, refs = take(refs, {"slots": 1, "tokens": extras, None: 0}[tail])
    landings, refs = take(refs, len(moves))
    (home, own_sems), refs = take(refs, 2)
    fact_sems, refs = take(refs, 3)
    fold_scratch, refs = take(refs, 7)
    if tail == "slots":
        (picked, facts), refs = take(refs, 2)
        tail_sems, refs = take(refs, 3)
    elif tail == "tokens":
        (mine,), refs = take(refs, 1)
        tail_sems, refs = take(refs, 2 * extras)
    movers = make_movers(moves, sources, landings, refs)
    place.meet(bool(moves))
    told = Spread(place, facts, all_facts, False, *fact_sems)
    if tail != "slots":
        told.start(own_sems.at[0])
    if tail == "tokens" and more:
        second = ToTokens(place, more[0], outs[1], *tail_sems[2:])
        second.start(own_sems.at[2])
    for mover in movers:
        mover.start(place, False)
    Fold(place, part, home, fold_scratch).run()
    if put.shape[1] == 128:
        summed = jnp.sum(home[...].astype(F32), axis=0)
    else:
        rows = home[...].reshape(-1, home.shape[2])
        summed = jnp.dot(put[...], rows, preferred_element_type=F32)
    value = add[...] + summed
    raw[...] = value
    if tail == "slots":
        picked[...] = turned(next_put[...], value.astype(BF)).astype(BF)
        slots = Spread(place, picked, outs[0], False, *tail_sems, pieces=place.experts)
        slots.start(own_sems.at[1])
        facts[...] = row_sums(linear[...], value) + row_sums(square[...], value * value)
        told.start(own_sems.at[0])
    elif tail == "tokens":
        mine[...] = (value * scale[...]).astype(BF)
        first = ToTokens(place, mine, outs[0], *tail_sems[:2])
        first.start(own_sems.at[1])
    for mover in movers:
        mover.start(place, True)
    if tail == "slots":
        slots.run()
    elif tail == "tokens":
        if more:
            second.run()
        first.run()
    told.run()
    for mover in movers:
        mover.wait()


def finish_kernel(sizes, moves, *refs):
    place = Place(sizes)
    (plus, product, unit, next_put), refs = take(refs, 4)
    sources, refs = take(refs, len(moves))
    (raw, out), refs = take(refs, 2)
    landings, refs = take(refs, len(moves))
    (sums, got, picked, own_sem, sum_sems), refs = take(refs, 5)
    tail_sems, refs = take(refs, 3)
    movers = make_movers(moves, sources, landings, refs)
    sums[...] = row_sums(jnp.ones((8, product.shape[1]), F32), product[...])
    place.meet(bool(moves))
    layer = place.chips * 2
    here = place.chip * 2 + place.core
    copies = []
    for k in range(1, layer):
        there = (here + k) % layer
        device = place.device(place.exp, there // 2, there % 2)
        copies.append(send(sums, got.at[k - 1], sum_sems, (k - 1,), device))
    for mover in movers:
        mover.start(place, False)
    total = sums[...]
    for k in range(1, layer):
        copies[k - 1].wait_recv()
        total = total + got[k - 1]
    mean = total.T[:, :1] * (1.0 / (layer * product.shape[1]))
    value = plus[...] - unit[...] * mean
    raw[...] = value
    picked[...] = turned(next_put[...], value.astype(BF)).astype(BF)
    slots = Spread(place, picked, out, False, *tail_sems, pieces=place.experts)
    slots.start(own_sem)
    for mover in movers:
        mover.start(place, True)
    slots.run()
    for copy in copies:
        copy.wait_send()
    for mover in movers:
        mover.wait()


def dma_sems(*shape):
    return pltpu.SemaphoreType.DMA(shape)


def move_scratch(sizes, moves):
    most = max(len(cuts) for _, cuts, _, _ in moves)
    members = sizes[0] * sizes[1]
    return [dma_sems(2, len(moves), most, members - 1), dma_sems(len(moves), most)]


def start(sizes, arrays, pair, moves, number):
    experts, sub, _, tp = sizes
    count = len(arrays)
    exp_sems, chip_sems, core_sems = (
        dma_sems(count, *shape) for shape in spread_shapes(sizes)
    )
    anywhere = pl.BlockSpec(memory_space=pl.ANY)
    total = count + 1 + len(moves)
    results = pl.pallas_call(
        partial(start_kernel, sizes, count, [(kind, cuts) for kind, cuts, _, _ in moves]),
        out_shape=[
            *[
                jax.ShapeDtypeStruct((rows.shape[0] * experts * sub, rows.shape[1]), rows.dtype)
                for rows in arrays
            ],
            jax.ShapeDtypeStruct((pair.shape[1] * experts * sub, 2 * pair.shape[2] // sub), BF),
            *landing_shapes(sizes, moves),
        ],
        in_specs=[anywhere] * total,
        out_specs=[anywhere] * total,
        scratch_shapes=[
            dma_sems(count),
            exp_sems,
            chip_sems,
            core_sems,
            dma_sems(2, 2, experts - 1),
            dma_sems(2, 2, sub - 1),
            dma_sems(2),
            *move_scratch(sizes, moves),
        ],
        compiler_params=pltpu.CompilerParams(
            collective_id=number, has_side_effects=True, vmem_limit_bytes=VMEM_BYTES
        ),
        name=f"start_{number}",
    )(*arrays, pair, *[array for _, _, array, _ in moves])
    return results[:count], results[count], results[count + 1 :]


def landing_shapes(sizes, moves):
    return [
        jax.ShapeDtypeStruct(moved_shape(sizes, kind, array, wide), BF)
        for kind, _, array, wide in moves
    ]


def spread_shapes(sizes):
    experts, sub, _, tp = sizes
    chips = sub * tp // 2
    return (2, 2, experts - 1), (2, experts, chips), (2, experts, chips)


def spread_sems(sizes):
    return [dma_sems(*shape) for shape in spread_shapes(sizes)]


def exchange(sizes, part, put, add, scale, extra, tail, moves, number):
    experts, sub, ctx, tp = sizes
    layer = sub * tp
    chips = layer // 2
    rows, width = part.shape
    tokens, feats = add.shape
    each = rows // experts
    vmem, anywhere = (pl.BlockSpec(memory_space=m) for m in (pltpu.VMEM, pl.ANY))
    if put is None:
        put = jnp.zeros((8, 128), BF)
    fact_shape = (8, tokens) if tail == "slots" else extra[0].shape
    outs, scratch, extra_specs = [], [], [vmem] * len(extra)
    if tail == "slots":
        picks = extra[0].shape[1]
        outs = [jax.ShapeDtypeStruct((picks, width), BF)]
        scratch = [pltpu.VMEM((picks, feats), BF), pltpu.VMEM(fact_shape, F32)]
        scratch += spread_sems(sizes)
    elif tail == "tokens":
        outs = [jax.ShapeDtypeStruct((tokens // sub, width), BF)] * len(extra)
        scratch = [pltpu.VMEM((tokens, feats), BF)]
        scratch += [dma_sems(2, chips - 1), dma_sems(2, chips)] * len(extra)
    if tail != "slots":
        extra_specs[0] = anywhere
    all_facts = jax.ShapeDtypeStruct((fact_shape[0] * experts, fact_shape[1] * layer), F32)
    raw, all_facts, *results = pl.pallas_call(
        partial(
            exchange_kernel, sizes, tail, len(extra), [(kind, cuts) for kind, cuts, _, _ in moves]
        ),
        out_shape=[
            jax.ShapeDtypeStruct((tokens, feats), F32),
            all_facts,
            *outs,
            *landing_shapes(sizes, moves),
        ],
        in_specs=[vmem] * 4 + extra_specs + [anywhere] * len(moves),
        out_specs=[vmem] + [anywhere] * (1 + len(outs) + len(moves)),
        scratch_shapes=[
            pltpu.VMEM((experts, each, feats), BF),
            dma_sems(3),
            *spread_sems(sizes),
            pltpu.VMEM((chips, rows, feats), BF),
            pltpu.VMEM((chips - 1, rows, feats), BF),
            pltpu.VMEM((chips - 1, rows, feats), BF),
            pltpu.VMEM((rows, feats), BF),
            dma_sems(2, chips),
            dma_sems(2, chips - 1),
            dma_sems(2, experts - 1),
            *scratch,
            *move_scratch(sizes, moves),
        ],
        compiler_params=pltpu.CompilerParams(
            collective_id=number, has_side_effects=True, vmem_limit_bytes=VMEM_BYTES
        ),
        name=f"exchange_{number}",
    )(part, put, add, scale, *extra, *[array for _, _, array, _ in moves])
    outs, moved = results[: len(outs)], results[len(outs) :]
    all_facts = all_facts.reshape(experts, fact_shape[0], layer, fact_shape[1])
    return raw, outs, all_facts.transpose(0, 2, 1, 3), moved


def finish(sizes, plus, product, unit, next_put, moves, number):
    experts, sub, ctx, tp = sizes
    layer = sub * tp
    tokens, feats = plus.shape
    picks = next_put.shape[1]
    vmem, anywhere = (pl.BlockSpec(memory_space=m) for m in (pltpu.VMEM, pl.ANY))
    raw, out, *moved = pl.pallas_call(
        partial(finish_kernel, sizes, [(kind, cuts) for kind, cuts, _, _ in moves]),
        out_shape=[
            jax.ShapeDtypeStruct((tokens, feats), F32),
            jax.ShapeDtypeStruct((picks, feats * layer), BF),
            *landing_shapes(sizes, moves),
        ],
        in_specs=[vmem] * 4 + [anywhere] * len(moves),
        out_specs=[vmem] + [anywhere] * (1 + len(moves)),
        scratch_shapes=[
            pltpu.VMEM((8, tokens), F32),
            pltpu.VMEM((layer - 1, 8, tokens), F32),
            pltpu.VMEM((picks, feats), BF),
            pltpu.SemaphoreType.DMA,
            dma_sems(2, layer - 1),
            *spread_sems(sizes),
            *move_scratch(sizes, moves),
        ],
        compiler_params=pltpu.CompilerParams(
            collective_id=number, has_side_effects=True, vmem_limit_bytes=VMEM_BYTES
        ),
        name=f"finish_{number}",
    )(plus, product, unit, next_put, *[array for _, _, array, _ in moves])
    return raw, out, moved


class Axes:
    def __init__(self, experts, shard, ctx, tp):
        self.experts = experts
        self.sub = shard * ctx // experts
        self.tp = tp
        if self.sub == ctx:
            self.layer, self.exp = (("ctx", "tp"), None), ("shard", None)
            self.part = ("ctx", None)
        else:
            devices = np.arange(shard * ctx * tp).reshape(experts, self.sub, tp)
            self.layer = (ALL, devices.reshape(experts, -1).tolist())
            self.exp = (ALL, devices.reshape(experts, -1).T.tolist())
            self.part = (ALL, devices.transpose(0, 2, 1).reshape(-1, self.sub).tolist())

    def swap(self, value, over):
        axes, groups = over
        return lax.all_to_all(value, axes, 0, 0, axis_index_groups=groups)


class Routing:
    def __init__(self, choice, seqs, seq_len, experts, cap, mine, own_first, own_seqs):
        columns = jnp.arange(experts, dtype=jnp.int32)
        hits = jnp.sum((choice[:, :, None] == columns[None, None, :]).astype(F32), axis=1)
        self.hits = hits.reshape(seqs, seq_len, experts)
        rows = jnp.arange(seq_len, dtype=jnp.int32)
        earlier = (rows[None, :] < rows[:, None]).astype(BF)
        before = dot("tu,sue->ste", earlier, self.hits.astype(BF))
        self.valid = self.hits * (before < cap).astype(F32)
        self.place = jnp.where(self.valid > 0, before, -1.0)
        self.cap = cap
        is_mine = (columns == mine).astype(F32)
        place_mine = jnp.sum(self.place * is_mine, axis=2)
        slots = jnp.arange(cap, dtype=jnp.int32).astype(F32)
        self.is_mine = is_mine
        self.pick = (place_mine[:, None, :] == slots[None, :, None]).astype(BF)
        place_own = lax.dynamic_slice_in_dim(self.place, own_first, own_seqs, 0)
        place_own = place_own.transpose(1, 0, 2)[:, :, :, None]
        seq_of = jnp.arange(own_seqs, dtype=jnp.int32)
        here = place_own == slots
        same = (seq_of[:, None] == seq_of[None, :])[:, None, None, :, None]
        put = here.transpose(1, 0, 2, 3)[:, :, :, None, :] & same
        self.put = put.astype(BF).reshape(own_seqs * seq_len, experts * own_seqs * cap)

    def gates(self, logits):
        logits = logits.reshape(self.hits.shape)
        top = jnp.max(jnp.where(self.hits > 0, logits, -jnp.inf), axis=2, keepdims=True)
        raised = jnp.where(self.hits > 0, jnp.exp(logits - top), 0.0)
        return raised / jnp.sum(raised, axis=2, keepdims=True)

    def slot_gates(self, gates):
        gate_mine = jnp.sum(gates * self.is_mine, axis=2)
        return jnp.sum(self.pick.astype(F32) * gate_mine[:, None, :], axis=2)

    def take(self, rows):
        seqs, cap, seq_len = self.pick.shape
        picked = dot("spt,stf->spf", self.pick, rows.reshape(seqs, seq_len, -1))
        return picked.astype(BF).reshape(seqs * cap, -1)

    def give(self, slots):
        seqs, cap, seq_len = self.pick.shape
        rows = dot("spt,spf->stf", self.pick, slots.reshape(seqs, cap, -1))
        return rows.reshape(seqs * seq_len, -1)

    def token_grads(self, slot_grads):
        slots = jnp.arange(self.cap, dtype=jnp.int32).astype(F32)
        here = self.place[:, :, :, None] == slots[None, None, None, :]
        grads = slot_grads.transpose(1, 0, 2)[:, None, :, :]
        return jnp.sum(jnp.where(here, grads, 0.0), axis=3)


def put_home(put, home):
    return dot("tp,pf->tf", put, home.reshape(-1, home.shape[-1]))


def router_rows(grads, router):
    high = grads.astype(BF)
    low = (grads - high.astype(F32)).astype(BF)
    return dot(
        "te,fe->tf",
        jnp.concatenate([high, low], axis=1),
        jnp.concatenate([router, router], axis=1),
    )


def logit_grads(gates, gate_grads):
    mean = jnp.sum(gates * gate_grads, axis=2, keepdims=True)
    grads = gates * (gate_grads - mean)
    return grads.reshape(-1, grads.shape[-1])


def shards(
    sizes,
    hidden_in,
    att_choice,
    ffn_choice,
    span_ids,
    norm_att,
    router_att,
    w_query,
    w_out,
    w_key,
    w_value,
    norm_ffn,
    router_ffn,
    w_gate,
    w_up,
    w_down,
    cotangent,
):
    shard, ctx, tp = sizes
    experts = w_query.shape[0]
    axes = Axes(experts, shard, ctx, tp)
    sub = axes.sub
    group = experts * sub
    layer = sub * tp
    tokens, width = hidden_in.shape
    total = tokens * group
    seq_len = tokens * ctx
    seqs = total // seq_len
    own_seqs = seqs // experts
    own_tokens = own_seqs * seq_len
    cap = 2 * seq_len // experts
    slots = seqs * cap
    rows_own = width // group
    feats = width // layer
    sizes = (experts, sub, ctx, tp)
    kernels = feats % 128 == 0 and rows_own % 128 == 0 and tokens % 16 == 0
    group_at, tp_at = lax.axis_index(GROUP), lax.axis_index("tp")
    exp_at, sub_at = group_at // sub, group_at % sub
    layer_at = sub_at * tp + tp_at

    token_pack = jnp.concatenate(
        [att_choice, ffn_choice, span_ids[:, None]], axis=1
    ).astype(BF)
    feature_pack = jnp.concatenate(
        [norm_att[:, None], router_att, norm_ffn[:, None], router_ffn], axis=1
    )
    def everywhere(rows):
        quarter = width // tp
        part = lax.dynamic_slice_in_dim(rows, tp_at * quarter, quarter, 1)
        parts = lax.all_gather(part, ALL)
        return parts.reshape(group, tp, tokens, quarter).transpose(0, 2, 1, 3).reshape(total, width)

    def everywhere_layer(rows):
        parts = lax.all_gather(rows, ALL)
        return (
            parts.reshape(experts, layer, own_tokens, feats)
            .transpose(0, 2, 1, 3)
            .reshape(total, width)
        )

    def layer_sum(rows):
        m = rows.shape[0]
        parts = rows.astype(BF).reshape(m, layer, feats).transpose(1, 0, 2)
        parts = axes.swap(parts, axes.layer)
        return jnp.sum(parts.astype(F32), axis=0)

    def go_home(rows):
        return axes.swap(rows.astype(BF).reshape(experts, -1, feats), axes.exp)

    def to_tokens(rows):
        parts = axes.swap(rows.reshape(sub, tokens, feats), axes.part)
        parts = lax.all_gather(parts, "tp")
        return parts.transpose(2, 1, 0, 3).reshape(tokens, width)

    head_parts = math.gcd(sub, w_query.shape[2] // HD)
    copies = sub // head_parts
    heads_wide = w_query.shape[2] // head_parts
    hidden_local = w_gate.shape[2]
    hidden_wide = -(-hidden_local // (sub * 128)) * 128
    windows = sub == 2 and (hidden_local - hidden_wide) % 128 == 0
    hidden_pad = 0 if windows else hidden_wide * sub - hidden_local
    overlap = hidden_wide * sub - hidden_local if windows else 0
    hidden_mine = jnp.arange(hidden_wide) >= overlap * sub_at
    gate_early = hidden_wide // 384 * 128
    kernels = kernels and windows and copies == 1

    def to_windows(weight, axis):
        if windows:
            size = weight.shape[axis]
            parts = [
                lax.slice_in_dim(weight, 0, hidden_wide, axis=axis),
                lax.slice_in_dim(weight, size - hidden_wide, size, axis=axis),
            ]
        else:
            pad = [(0, 0)] * 3
            pad[axis] = (0, hidden_pad)
            parts = jnp.split(jnp.pad(weight, pad), sub, axis=axis)
        parts = jnp.stack(parts, axis=1)
        return parts.reshape(group, *parts.shape[2:])

    def to_heads(weight, axis):
        parts = jnp.stack(jnp.split(weight, head_parts, axis=axis), axis=1)
        return jnp.repeat(parts, copies, axis=1).reshape(group, *parts.shape[2:])

    def to_all(weight):
        return to_heads(jnp.broadcast_to(weight, (experts, *weight.shape)), 2)

    def swap_group(value):
        return lax.all_to_all(value, GROUP, 0, 0)

    def as_columns(parts):
        return parts.reshape(width, parts.shape[2])

    def as_rows(parts):
        return parts.transpose(1, 0, 2).reshape(parts.shape[1], width)

    pack = jnp.concatenate(
        [jnp.pad(facts.T, ((0, 16 - facts.shape[1]), (0, 0))) for facts in (token_pack, feature_pack)],
        axis=1,
    )
    if kernels:
        (packs, all_in, top_all), my_key_value, (my_query,) = start(
            sizes,
            [pack, hidden_in, cotangent],
            jnp.stack([w_key, w_value]),
            [("columns_out", ((0, heads_wide, False),), w_query, heads_wide)],
            0,
        )
        my_out = as_rows(swap_group(to_heads(after(w_out, all_in), 1)))
        packs = packs.reshape(group, 16, -1)
    else:
        packs = lax.all_gather(pack, GROUP)
        all_in, top_all = everywhere(hidden_in), everywhere(cotangent)
        first = [to_heads(w_query, 2), to_all(w_key), to_all(w_value), to_heads(w_out, 1)]
        first = swap_group(jnp.concatenate(first, axis=2))
        my_query = as_columns(first[:, :, :heads_wide])
        my_key_value = as_columns(first[:, :, heads_wide : 3 * heads_wide])
        my_out = as_rows(first[:, :, 3 * heads_wide :])
    packs = packs.transpose(0, 2, 1)
    token_facts = packs[:, :tokens].reshape(total, 16).astype(jnp.int32)
    feature_facts = packs[:, tokens:].reshape(width, 16)
    gain_att = feature_facts[:, 0].astype(F32)
    route_att = feature_facts[:, 1 : 1 + experts]
    gain_ffn = feature_facts[:, 1 + experts].astype(F32)
    route_ffn = feature_facts[:, 2 + experts : 2 + 2 * experts]

    def move(kind, weight):
        if kind == "columns_out":
            return as_columns(swap_group(to_windows(weight, 2)))
        if kind == "rows_out":
            return as_rows(swap_group(to_windows(weight, 1)))
        if kind == "columns_home":
            return swap_group(weight.reshape(group, rows_own, -1))
        return swap_group(weight.reshape(-1, group, rows_own).transpose(1, 0, 2))

    def to_cuts(moves):
        return [
            (kind, ((0, early, False), (early, wide - early, True)), weight, wide)
            for kind, weight, wide, early in moves
        ]

    def to_slots(rows, next_put):
        picked = dot("tp,tf->pf", next_put, rows).astype(BF)
        picked = axes.swap(picked.reshape(experts, -1, feats), axes.exp)
        picked = lax.all_gather(
            picked.reshape(-1, feats), axes.layer[0], axis_index_groups=axes.layer[1]
        )
        return picked.transpose(1, 0, 2).reshape(-1, width)

    def exchanged(part, put, add, scale, extra, tail, moves, number):
        if kernels:
            return exchange(sizes, part, put, add, scale, extra, tail, to_cuts(moves), number)
        home = go_home(layer_sum(part))
        summed = jnp.sum(home.astype(F32), axis=0) if put is None else put_home(put, home)
        raw, outs = add + summed, []
        if tail == "slots":
            next_put, linear, square = extra
            outs = [to_slots(raw.astype(BF), next_put)]
            facts = dot_exact("ef,tf->et", linear, raw) + dot_exact("ef,tf->et", square, raw * raw)
        else:
            facts = extra[0]
        if tail == "tokens":
            outs = [to_tokens(rows) for rows in ((raw * scale).astype(BF), *extra[1:])]
        told = lax.all_gather(facts, ALL).reshape(experts, layer, *facts.shape)
        return raw, outs, told, [move(kind, weight) for kind, weight, _, _ in moves]

    def finished(plus, product, unit, next_put, moves, number):
        if kernels:
            return finish(sizes, plus, product, unit, next_put, to_cuts(moves), number)
        sums = lax.all_gather(jnp.sum(product, axis=1), ALL).reshape(experts, layer, own_tokens)
        mean = lax.dynamic_index_in_dim(jnp.sum(sums, axis=1), exp_at, 0, keepdims=False) / width
        raw = plus - unit * mean[:, None]
        moved = [move(kind, weight) for kind, weight, _, _ in moves]
        return raw, to_slots(raw.astype(BF), next_put), moved

    own_first = exp_at * own_seqs
    where = partial(
        Routing,
        seqs=seqs,
        seq_len=seq_len,
        experts=experts,
        cap=cap,
        mine=exp_at,
        own_first=own_first,
        own_seqs=own_seqs,
    )
    att = where(token_facts[:, 0:2])
    if copies > 1:
        turn = jnp.arange(seqs, dtype=jnp.int32) % copies == sub_at % copies
        att.pick = att.pick * turn.astype(BF)[:, None, None]
    ffn = where(token_facts[:, 2:4])
    spans = token_facts[:, 4].reshape(seqs, seq_len).astype(F32)
    cosine, sine = rope_tables(seq_len)
    positions = jnp.arange(seq_len, dtype=jnp.int32).astype(F32)
    pick_f32 = att.pick.astype(F32)
    slot_position = jnp.sum(pick_f32 * positions[None, None, :], axis=2)
    slot_span = jnp.sum(pick_f32 * spans[:, None, :], axis=2)
    slot_cosine = dot_exact("spt,tf->spf", pick_f32, cosine)
    slot_sine = dot_exact("spt,tf->spf", pick_f32, sine)
    allowed = (positions[None, None, :] <= slot_position[:, :, None]) | (
        (slot_span[:, :, None] == spans[:, None, :]) & (slot_span[:, :, None] > 0)
    )

    my_gate = move("columns_out", after(w_gate, all_in))
    x_all = all_in.astype(F32)
    scale_in = lax.rsqrt(jnp.mean(x_all * x_all, axis=1, keepdims=True) + EPS)
    h1 = (x_all * scale_in * gain_att[None, :]).astype(BF)
    heads = heads_wide // HD
    scale = 1.0 / math.sqrt(HD)
    kv = dot("td,dm->tm", h1, my_key_value)
    keys = rotate(
        kv[:, :heads_wide].reshape(seqs, seq_len, heads, HD),
        cosine[None, :, None, :],
        sine[None, :, None, :],
    ).astype(BF)
    values = kv[:, heads_wide:].astype(BF).reshape(seqs, seq_len, heads, HD)
    att_gates = att.gates(dot("td,de->te", h1, route_att))
    att_slot_gate = att.slot_gates(att_gates).reshape(slots, 1)
    h1_slots = att.take(h1)
    queries = rotate(
        dot("td,dm->tm", h1_slots, my_query).reshape(seqs, cap, heads, HD),
        slot_cosine[:, :, None, :],
        slot_sine[:, :, None, :],
    ).astype(BF)
    scores = dot("sqhd,skhd->shqk", queries, keys) * scale
    scores = jnp.where(allowed[:, None], scores, -1e30)
    expo = jnp.exp(scores - jnp.max(scores, axis=-1, keepdims=True))
    probs = expo / jnp.sum(expo, axis=-1, keepdims=True)
    probs_low = probs.astype(BF)
    mixed = dot("shqk,skhd->sqhd", probs_low, values).astype(BF).reshape(slots, heads_wide)
    branch_att = dot("cm,md->cd", mixed, my_out) * att_slot_gate
    own_in = lax.dynamic_slice(
        x_all, (exp_at * own_tokens, layer_at * feats), (own_tokens, feats)
    )
    own_gain_ffn = lax.dynamic_slice_in_dim(gain_ffn, layer_at * feats, feats, 0)
    own_route_ffn = lax.dynamic_slice_in_dim(
        route_ffn.astype(F32), layer_at * feats, feats, 0
    )
    linear = jnp.pad((own_route_ffn * own_gain_ffn[:, None]).T, ((0, 8 - experts), (0, 0)))
    square = (jnp.arange(8) == experts).astype(F32)[:, None] * jnp.ones((1, feats), F32)
    mid, (mid_slots,), ffn_facts, (my_up,) = exchanged(
        after(branch_att.astype(BF), my_gate),
        att.put,
        own_in,
        jnp.ones((1, feats), F32),
        (ffn.put, linear, square),
        "slots",
        [("columns_out", w_up, hidden_wide, hidden_wide // 3)],
        1,
    )
    my_down = move("rows_out", after(w_down, mid_slots))

    ffn_facts = jnp.sum(ffn_facts, axis=1)
    scale_mid = lax.rsqrt(ffn_facts[:, experts].reshape(total, 1) / width + EPS)
    ffn_logits = ffn_facts[:, :experts].transpose(0, 2, 1).reshape(total, experts) * scale_mid
    ffn_gates = ffn.gates(ffn_logits)
    ffn_slot_gate = ffn.slot_gates(ffn_gates).reshape(slots, 1)
    mid_slots = mid_slots.astype(F32)
    scale_slots = lax.rsqrt(jnp.mean(mid_slots * mid_slots, axis=1, keepdims=True) + EPS)
    h2_slots = (mid_slots * scale_slots * gain_ffn[None, :]).astype(BF)
    pre_gate = dot("cd,df->cf", h2_slots, my_gate)
    pre_up = dot("cd,df->cf", h2_slots, my_up)
    sigma = jax.nn.sigmoid(pre_gate)
    swish = pre_gate * sigma
    hidden = jnp.where(hidden_mine, swish * pre_up, 0.0).astype(BF)
    branch_ffn = dot("cf,fd->cd", hidden, my_down) * ffn_slot_gate

    top_slots = ffn.take(top_all)
    grad_hidden = dot("cd,fd->cf", top_slots, my_down)
    ffn_gate_part = jnp.sum(hidden.astype(F32) * grad_hidden, axis=1)
    grad_hidden = jnp.where(hidden_mine, grad_hidden * ffn_slot_gate, 0.0)
    grad_branch = (top_slots.astype(F32) * ffn_slot_gate).astype(BF)
    grad_pre_gate = (
        grad_hidden * pre_up * sigma * (1.0 + pre_gate * (1.0 - sigma))
    ).astype(BF)
    grad_pre_up = (grad_hidden * swish).astype(BF)
    ffn_taken = dot("cf,df->cd", grad_pre_gate, my_gate) + dot("cf,df->cd", grad_pre_up, my_up)
    grad_down_w = dot("cf,cd->fd", hidden, grad_branch).astype(BF)

    def gate_facts(told):
        return jnp.sum(told, axis=1).reshape(experts, seqs, cap)

    grad_second, _, ffn_told, (grad_down,) = exchanged(
        ffn_taken.astype(BF),
        ffn.put,
        jnp.zeros((own_tokens, feats), F32),
        jnp.ones((1, feats), F32),
        (ffn_gate_part.reshape(-1, 128),),
        None,
        [("rows_home", grad_down_w, hidden_wide, hidden_wide)],
        2,
    )
    ffn_logit_grads = logit_grads(ffn_gates, ffn.token_grads(gate_facts(ffn_told)))
    own_ffn_logits = lax.dynamic_slice_in_dim(
        ffn_logit_grads, exp_at * own_tokens, own_tokens, 0
    )
    own_at = (exp_at * own_tokens, layer_at * feats)
    own_scale_mid = lax.dynamic_slice_in_dim(scale_mid, exp_at * own_tokens, own_tokens, 0)
    own_unit_mid = mid * own_scale_mid
    grad_second = grad_second + router_rows(own_ffn_logits, own_route_ffn)
    norm_ffn_part = jnp.sum(grad_second * own_unit_mid, axis=0)
    own_second = grad_second * own_gain_ffn[None, :] * own_scale_mid
    grad_gate_w = dot("cd,cf->df", h2_slots, grad_pre_gate).astype(BF)
    grad_mid, mid_slots, (grad_gate_early,) = finished(
        lax.dynamic_slice(top_all, own_at, (own_tokens, feats)).astype(F32) + own_second,
        own_second * own_unit_mid,
        own_unit_mid,
        att.put,
        [("columns_home", grad_gate_w[:, :gate_early], gate_early, 128)],
        5,
    )
    grad_gate = move("columns_home", after(grad_gate_w[:, gate_early:], mid_slots))
    grad_gate = jnp.concatenate([grad_gate_early, grad_gate], axis=2)

    if copies > 1:
        mid_slots = mid_slots * jnp.repeat(turn, cap).astype(BF)[:, None]
    grad_mixed = dot("cd,md->cm", mid_slots, my_out)
    att_gate_part = jnp.sum(mixed.astype(F32) * grad_mixed, axis=1)
    grad_mixed = (grad_mixed * att_slot_gate).astype(BF).reshape(seqs, cap, heads, HD)
    grad_att_branch = (mid_slots.astype(F32) * att_slot_gate).astype(BF)
    grad_soft = dot("sqhd,skhd->shqk", grad_mixed, values)
    grad_values = dot("shqk,sqhd->skhd", probs_low, grad_mixed)
    grad_scores = (
        probs * (grad_soft - jnp.sum(probs * grad_soft, axis=-1, keepdims=True))
    ).astype(BF)
    grad_queries = dot("shqk,skhd->sqhd", grad_scores, keys) * scale
    grad_keys = dot("shqk,sqhd->skhd", grad_scores, queries) * scale
    grad_qpre = (
        rotate_back(grad_queries, slot_cosine[:, :, None, :], slot_sine[:, :, None, :])
        .astype(BF)
        .reshape(slots, heads_wide)
    )
    att_taken = dot("cm,dm->cd", grad_qpre, my_query)
    grad_kpre = rotate_back(
        grad_keys, cosine[None, :, None, :], sine[None, :, None, :]
    ).reshape(total, heads_wide)
    kv_low = jnp.concatenate([grad_kpre, grad_values.reshape(total, heads_wide)], axis=1)
    kv_low = kv_low.astype(BF)
    first_part = dot("tm,dm->td", kv_low, my_key_value) + att.give(att_taken.astype(BF))
    own_scale_in = lax.dynamic_slice_in_dim(scale_in, exp_at * own_tokens, own_tokens, 0)
    own_gain_att = lax.dynamic_slice_in_dim(gain_att, layer_at * feats, feats, 0)
    grad_up_w = dot("cd,cf->df", h2_slots, grad_pre_up).astype(BF)
    grad_first, (first_tokens, mid_tokens), att_told, (grad_up,) = exchanged(
        after(first_part.astype(BF), grad_gate),
        None,
        jnp.zeros((own_tokens, feats), F32),
        own_gain_att[None, :] * own_scale_in,
        (att_gate_part.reshape(-1, 128), grad_mid.astype(BF)),
        "tokens",
        [("columns_home", grad_up_w, hidden_wide, hidden_wide // 3)],
        3,
    )
    att_logit_grads = logit_grads(att_gates, att.token_grads(gate_facts(att_told)))
    own_att_logits = lax.dynamic_slice_in_dim(
        att_logit_grads, exp_at * own_tokens, own_tokens, 0
    )
    own_route_att = lax.dynamic_slice_in_dim(
        route_att.astype(F32), layer_at * feats, feats, 0
    )
    grad_first = grad_first + dot_exact("te,fe->tf", own_att_logits, own_route_att)
    norm_att_part = jnp.sum(grad_first * own_in * own_scale_in, axis=0)
    token_at = group_at * tokens
    first_tokens = first_tokens.astype(F32) + router_rows(
        lax.dynamic_slice_in_dim(att_logit_grads, token_at, tokens, 0), route_att
    ) * (gain_att[None, :] * lax.dynamic_slice_in_dim(scale_in, token_at, tokens, 0))
    unit_in = lax.dynamic_slice_in_dim(x_all * scale_in, token_at, tokens, 0)
    grad_in = (
        mid_tokens.astype(F32)
        + first_tokens
        - unit_in * jnp.mean(first_tokens * unit_in, axis=1, keepdims=True)
    )


    def windows_home(back, axis):
        back = back.reshape(experts, sub, *back.shape[1:])
        parts = [lax.index_in_dim(back, i, 1, keepdims=False) for i in range(sub)]
        parts[1:] = [
            lax.slice_in_dim(part, overlap, part.shape[axis], axis=axis) for part in parts[1:]
        ]
        whole = jnp.concatenate(parts, axis=axis)
        return lax.slice_in_dim(whole, 0, hidden_local, axis=axis).astype(F32)

    def heads_home(back, axis):
        back = back.reshape(experts, head_parts, copies, *back.shape[1:])
        if copies > 1:
            back = jnp.sum(back.astype(F32), axis=2, keepdims=True)
        parts = [back[:, i, 0] for i in range(head_parts)]
        return jnp.concatenate(parts, axis=axis).astype(F32)

    grad_query_w = dot("cd,cm->dm", h1_slots, grad_qpre).astype(BF)
    grad_out_w = dot("cm,cd->md", mixed, grad_att_branch).astype(BF)
    grad_kv_w = dot("td,tm->dm", h1, kv_low).astype(BF)
    own_h1 = lax.dynamic_slice(h1, own_at, (own_tokens, feats)).astype(F32)
    own_h2 = (own_unit_mid * own_gain_ffn[None, :]).astype(BF).astype(F32)
    own_parts = jnp.concatenate(
        [
            norm_att_part[None],
            norm_ffn_part[None],
            dot_exact("te,tf->ef", own_att_logits, own_h1),
            dot_exact("te,tf->ef", own_ffn_logits, own_h2),
        ],
        axis=0,
    )
    own_parts = jnp.pad(own_parts, ((0, 16 - own_parts.shape[0]), (0, 0)))
    _, (hidden_out,), own_told, (grad_out, grad_query, grad_kv) = exchanged(
        after(branch_ffn.astype(BF), first_tokens),
        ffn.put,
        mid,
        jnp.ones((1, feats), F32),
        (own_parts,),
        "tokens",
        [
            ("rows_home", grad_out_w, heads_wide, heads_wide),
            ("columns_home", grad_query_w, heads_wide, heads_wide),
            ("columns_home", grad_kv_w, 2 * heads_wide, 2 * heads_wide),
        ],
        4,
    )
    own_told = jnp.sum(own_told, axis=0).transpose(1, 0, 2).reshape(16, width)
    own_told = lax.dynamic_slice_in_dim(own_told, group_at * rows_own, rows_own, 1)
    grad_router_att = own_told[2 : 2 + experts].T
    grad_router_ffn = own_told[2 + experts : 2 + 2 * experts].T
    grad_out = heads_home(grad_out, 1)
    grad_query = heads_home(grad_query, 2)
    grad_key, grad_value = (
        jnp.sum(heads_home(grad_kv[:, :, i * heads_wide : (i + 1) * heads_wide], 2), axis=0)
        for i in (0, 1)
    )
    return (
        hidden_out,
        grad_in,
        own_told[0],
        grad_router_att,
        grad_query,
        grad_out,
        grad_key,
        grad_value,
        own_told[1],
        grad_router_ffn,
        windows_home(grad_gate, 2),
        windows_home(grad_up, 2),
        windows_home(grad_down, 1),
    )


def solution(mesh):
    ctx, tp = mesh.shape["ctx"], mesh.shape["tp"]
    shard = mesh.shape["shard"]
    by_token, by_feature = P(GROUP, None), P(GROUP)
    columns, rows = P(None, GROUP, "tp"), P(None, "tp", GROUP)

    return jax.shard_map(
        partial(shards, (shard, ctx, tp)),
        mesh=mesh,
        in_specs=(
            by_token,
            by_token,
            by_token,
            P(GROUP),
            by_feature,
            by_token,
            columns,
            rows,
            P(GROUP, "tp"),
            P(GROUP, "tp"),
            by_feature,
            by_token,
            columns,
            columns,
            rows,
            by_token,
        ),
        out_specs=(
            by_token,
            by_token,
            by_feature,
            by_token,
            columns,
            rows,
            P(GROUP, "tp"),
            P(GROUP, "tp"),
            by_feature,
            by_token,
            columns,
            columns,
            rows,
        ),
        check_vma=False,
    )
```

```python
from functools import partial
import math

import numpy as np

import jax
import jax.numpy as jnp
from jax import lax
from jax.experimental import pallas as pl
from jax.experimental.pallas import tpu as pltpu
from jax.sharding import PartitionSpec as P

HD = 128
EPS = 1e-06
BF = jnp.bfloat16
F32 = jnp.float32
MESH = pl.DeviceIdType.MESH
VMEM_BYTES = 40 * 2**20
LOCAL_VMEM_BYTES = 56 * 2**20
GROUP = ("shard", "ctx")
ALL = ("shard", "ctx", "tp")


def dot(spec, left, right):
    return jnp.einsum(spec, left, right, preferred_element_type=F32)


def dot_exact(spec, left, right):
    return jnp.einsum(
        spec, left, right, preferred_element_type=F32, precision=lax.Precision.HIGHEST
    )


def after(value, *others):
    return lax.optimization_barrier((value, *others))[0]


def rope_tables(count):
    half_dim = HD // 2
    freq_index = (jnp.arange(HD) % half_dim).astype(F32)
    frequency = 10000.0 ** (-2.0 * freq_index / HD)
    angles = jnp.arange(count, dtype=F32)[:, None] * frequency[None, :]
    return jnp.cos(angles), jnp.sin(angles)


def rotate(rows, cosine, sine):
    half_dim = HD // 2
    turned = jnp.concatenate([-rows[..., half_dim:], rows[..., :half_dim]], axis=-1)
    return rows * cosine + turned * sine


def rotate_back(rows, cosine, sine):
    half_dim = HD // 2
    turned = rows * sine
    return rows * cosine + jnp.concatenate(
        [turned[..., half_dim:], -turned[..., :half_dim]], axis=-1
    )


class Place:
    def __init__(self, sizes):
        self.experts, self.sub, self.ctx, self.tp = sizes
        self.chips = self.sub * self.tp // 2
        self.members = self.experts * self.sub
        self.group = lax.axis_index(GROUP)
        self.tp_at = lax.axis_index("tp")
        self.exp = self.group // self.sub
        here = (self.group % self.sub) * self.tp + self.tp_at
        self.chip, self.core = here // 2, here % 2

    def device(self, exp, chip, core):
        here = chip * 2 + core
        group = exp * self.sub + here // self.tp
        return (group // self.ctx, group % self.ctx, here % self.tp)

    def member(self, group):
        return (group // self.ctx, group % self.ctx, self.tp_at)

    def sibling(self):
        return self.device(self.exp, self.chip, 1 - self.core)

    def other_exp(self, k):
        return (self.exp + k) % self.experts

    def other_chip(self, k):
        return (self.chip + k) % self.chips

    def meet(self, whole_group):
        barrier = pltpu.get_barrier_semaphore()
        layer = 2 * self.chips
        here = self.chip * 2 + self.core
        others = [(here + k) % layer for k in range(1, layer)]
        peers = [self.device(self.exp, there // 2, there % 2) for there in others]
        if whole_group:
            peers += [
                self.member((self.group + k) % self.members) for k in range(1, self.members)
            ]
        else:
            peers += [
                self.device(self.other_exp(k), self.chip, self.core)
                for k in range(1, self.experts)
            ]
        for peer in peers:
            pl.semaphore_signal(barrier, inc=1, device_id=peer, device_id_type=MESH)
        pl.semaphore_wait(barrier, len(peers))


def block(start, size, unit):
    return pl.ds(pl.multiple_of(start, unit), size)


def send(src, dst, sems, at, device):
    copy = pltpu.make_async_remote_copy(
        src_ref=src,
        dst_ref=dst,
        send_sem=sems.at[(0, *at)],
        recv_sem=sems.at[(1, *at)],
        device_id=device,
        device_id_type=MESH,
    )
    copy.start()
    return copy


class Mover:
    def __init__(self, number, kind, cuts, src, dst, sems, own_sems):
        self.number, self.kind, self.cuts = number, kind, cuts
        self.src, self.dst, self.sems, self.own_sems = src, dst, sems, own_sems
        self.copies = []

    def ends(self, place, group, low, size):
        exp, sub = group // place.sub, group % place.sub
        me, src, dst = place.group, self.src, self.dst
        if self.kind == "columns_out":
            rows, step = src.shape[1], (src.shape[2] - dst.shape[1]) // max(place.sub - 1, 1)
            return (
                src.at[exp, :, block(sub * step + low, size, 128)],
                dst.at[block(me * rows, rows, 16), pl.ds(low, size)],
            )
        if self.kind == "rows_out":
            cols, step = src.shape[2], (src.shape[1] - dst.shape[0]) // max(place.sub - 1, 1)
            return (
                src.at[exp, block(sub * step + low, size, 16)],
                dst.at[pl.ds(low, size), block(me * cols, cols, 128)],
            )
        if self.kind == "columns_home":
            rows = dst.shape[1]
            return (
                src.at[block(group * rows, rows, 16), pl.ds(low, size)],
                dst.at[me, :, pl.ds(low, size)],
            )
        cols = dst.shape[2]
        return (
            src.at[pl.ds(low, size), block(group * cols, cols, 128)],
            dst.at[me, pl.ds(low, size)],
        )

    def start(self, place, late):
        for cut, (low, size, is_late) in enumerate(self.cuts):
            if is_late != late or not size:
                continue
            for k in range(1, place.members):
                group = (place.group + k) % place.members
                src, dst = self.ends(place, group, low, size)
                at = (self.number, cut, k - 1)
                self.copies.append(send(src, dst, self.sems, at, place.member(group)))
            src, dst = self.ends(place, place.group, low, size)
            own = pltpu.make_async_copy(src, dst, self.own_sems.at[self.number, cut])
            own.start()
            self.copies.append(own)

    def wait(self):
        for copy in self.copies:
            copy.wait()


def moved_shape(sizes, kind, array, wide):
    experts, sub, _, _ = sizes
    group = experts * sub
    if kind == "columns_out":
        return (array.shape[1] * group, wide)
    if kind == "rows_out":
        return (wide, array.shape[2] * group)
    if kind == "columns_home":
        return (group, array.shape[0] // group, array.shape[1])
    return (group, array.shape[0], array.shape[1] // group)


class Line:
    def __init__(self, place, spot, sems):
        self.place, self.spot, self.sems = place, spot, sems

    def give(self, src, origin, up, step):
        place = self.place
        to = place.exp + 1 if up else place.exp - 1
        return pltpu.make_async_remote_copy(
            src_ref=src,
            dst_ref=self.spot(origin),
            send_sem=self.sems.at[0, 0 if up else 1, step],
            recv_sem=self.sems.at[1, 0 if up else 1, step],
            device_id=place.device(to, place.chip, place.core),
            device_id_type=MESH,
        )

    def start(self, src):
        place = self.place
        self.src = src

        @pl.when(place.exp < place.experts - 1)
        def _():
            self.give(src, place.exp, True, 0).start()

        @pl.when(place.exp > 0)
        def _():
            self.give(src, place.exp, False, 0).start()

    def origin(self, turn):
        place = self.place
        if place.experts != 4:
            return (place.exp + place.experts - turn) % place.experts
        high = place.exp // 2
        at = place.exp * (1 - high) + (3 - place.exp) * high
        origin = 1 - at if turn == 1 else turn
        return origin * (1 - high) + (3 - origin) * high

    def arrived(self, turn):
        place = self.place
        origin = self.origin(turn)

        @pl.when(origin < place.exp)
        def _():
            step = place.exp - origin - 1
            self.give(self.spot(origin), origin, True, step).wait_recv()

            @pl.when(place.exp < place.experts - 1)
            def _():
                self.give(self.spot(origin), origin, True, step + 1).start()

        @pl.when(origin > place.exp)
        def _():
            step = origin - place.exp - 1
            self.give(self.spot(origin), origin, False, step).wait_recv()

            @pl.when(place.exp > 0)
            def _():
                self.give(self.spot(origin), origin, False, step + 1).start()

        return origin

    def finish(self):
        place = self.place
        for step in range(place.experts - 1):

            @pl.when((place.exp < place.experts - 1) & (place.exp >= step))
            def _():
                self.give(self.src, place.exp, True, step).wait_send()

            @pl.when((place.exp > 0) & (place.exp + step < place.experts))
            def _():
                self.give(self.src, place.exp, False, step).wait_send()


class Spread:
    def __init__(self, place, mine, out, by_token, exp_sems, chip_sems, core_sems, pieces=1):
        self.place, self.mine, self.out, self.by_token = place, mine, out, by_token
        self.rows, self.cols = mine.shape[0] // pieces, mine.shape[1]
        self.pieces = pieces
        self.exp_sems, self.chip_sems, self.core_sems = exp_sems, chip_sems, core_sems
        self.square = place.chips == 4 and place.tp == 4 and self.rows % 64 == 0
        self.line = None
        if pieces == 1 and self.rows % 64 == 0:
            self.line = Line(place, lambda origin: self.spot(origin, place.chip), exp_sems)

    def spot(self, exp, chip, low=0, size=None):
        place = self.place
        here = chip * 2 + place.core
        if self.by_token:
            row = (exp * place.sub + here // place.tp) * self.rows
            col = (here % place.tp) * self.cols
        else:
            row, col = exp * self.rows, here * self.cols
        unit = math.gcd(self.rows, 16)
        size = size or self.rows
        return self.out.at[block(row + low, size, unit), block(col, self.cols, 128)]

    def piece(self, exp):
        if self.pieces == 1:
            return self.mine
        return self.mine.at[block(exp * self.rows, self.rows, 16)]

    def near(self):
        place = self.place
        side = place.chip // 2
        along = place.chip % 2
        return [(1 - side) * 2 + along, side * 2 + 1 - along]

    def to_chip(self, src, dst, turn, k, chip):
        device = self.place.device(self.place.exp, chip, self.place.core)
        self.chip_copies[turn].append(send(src, dst, self.chip_sems, (turn, k), device))

    def to_chips(self, exp, src, turn):
        place = self.place
        if self.square:
            chips = self.near()
        else:
            chips = [place.other_chip(k) for k in range(1, place.chips)]
        for k, chip in enumerate(chips):
            self.to_chip(src, self.spot(exp, place.chip), turn, k, chip)

    def to_core(self, exp, chip, src, turn, k):
        self.core_copies.append(
            send(src, self.spot(exp, chip), self.core_sems, (turn, k), self.place.sibling())
        )

    def start(self, own_sem):
        place = self.place
        home = self.spot(place.exp, place.chip)
        mine = self.piece(place.exp)
        self.own = pltpu.make_async_copy(mine, home, own_sem)
        self.own.start()
        self.chip_copies = [[] for _ in range(place.experts)]
        self.core_copies = []
        if self.line:
            self.line.start(mine)
        else:
            self.exp_copies = [
                send(
                    self.piece(place.other_exp(k)),
                    home,
                    self.exp_sems,
                    (0, k - 1),
                    place.device(place.other_exp(k), place.chip, place.core),
                )
                for k in range(1, place.experts)
            ]
        self.to_chips(place.exp, mine, 0)
        self.to_core(place.exp, place.chip, mine, 0, 0)

    def from_layer(self, turn):
        place = self.place
        if self.line:
            source = self.line.arrived(turn)
        else:
            self.exp_copies[turn - 1].wait_recv()
            source = (place.exp + place.experts - turn) % place.experts
        self.sources[turn] = source
        here = self.spot(source, place.chip)
        self.to_chips(source, here, turn)
        self.to_core(source, place.chip, here, turn, 0)

    def from_near(self, turn):
        source, copies = self.sources[turn], self.chip_copies[turn]
        if not self.square:
            return
        half = self.rows // 2
        side, along = self.near()
        copies[0].wait_recv()
        part = self.spot(source, side, 0, half)
        self.to_chip(part, part, turn, 2, along)
        self.to_core(source, side, self.spot(source, side), turn, 1)
        copies[1].wait_recv()
        part = self.spot(source, along, half, half)
        self.to_chip(part, part, turn, 3, side)
        self.to_core(source, along, self.spot(source, along), turn, 2)

    def from_far(self, turn):
        place = self.place
        source, copies = self.sources[turn], self.chip_copies[turn]
        if self.square:
            copies[2].wait_recv()
            copies[3].wait_recv()
            far = 3 - place.chip
            self.to_core(source, far, self.spot(source, far), turn, 3)
            return
        for k in range(1, place.chips):
            copies[k - 1].wait_recv()
            chip = (place.chip + place.chips - k) % place.chips
            self.to_core(source, chip, self.spot(source, chip), turn, k)

    def run(self):
        for stage in range(self.place.experts + 1):
            self.step(stage)
        self.finish()

    def step(self, stage):
        experts = self.place.experts
        if stage == 0:
            self.sources = {0: self.place.exp}
        if 1 <= stage + 1 < experts:
            self.from_layer(stage + 1)
        if 0 <= stage < experts:
            self.from_near(stage)
        if 0 <= stage - 1 < experts:
            self.from_far(stage - 1)

    def finish(self):
        for copy in self.core_copies:
            copy.wait()
        if self.line:
            self.line.finish()
        else:
            for copy in self.exp_copies:
                copy.wait_send()
        for copies in self.chip_copies:
            for copy in copies:
                copy.wait_send()
        self.own.wait()


class Pair:
    def __init__(self, place, src, out, line_sems, sems, own_sems):
        self.place, self.src, self.out, self.sems, self.own_sems = place, src, out, sems, own_sems
        self.rows = src.shape[1]
        self.half = src.shape[2] // place.sub
        size = self.rows * place.sub

        def spot(exp):
            return out.at[block(exp * size, size, 16)]

        self.line = Line(place, spot, line_sems)

    def start(self):
        place = self.place
        land = block(place.group * self.rows, self.rows, 16)
        sub = place.group % place.sub
        self.copies = []
        for i in range(2):
            dst = self.out.at[land, pl.ds(i * self.half, self.half)]
            for k in range(1, place.sub):
                other = (sub + k) % place.sub
                src = self.src.at[i, :, block(other * self.half, self.half, 128)]
                group = place.exp * place.sub + other
                self.copies.append(send(src, dst, self.sems, (i, k - 1), place.member(group)))
            src = self.src.at[i, :, block(sub * self.half, self.half, 128)]
            own = pltpu.make_async_copy(src, dst, self.own_sems.at[i])
            own.start()
            self.copies.append(own)

    def share(self):
        for copy in self.copies:
            copy.wait()
        self.line.start(self.line.spot(self.place.exp))

    def step(self, stage):
        if stage + 1 < self.place.experts:
            self.line.arrived(stage + 1)

    def finish(self):
        self.line.finish()


class ToTokens:
    def __init__(self, place, mine, out, chip_sems, core_sems):
        self.place, self.mine, self.out = place, mine, out
        self.chip_sems, self.core_sems = chip_sems, core_sems
        self.rows, self.cols = out.shape[0], mine.shape[1]

    def spot(self, chip):
        here = chip * 2 + self.place.core
        return self.out.at[:, block(here * self.cols, self.cols, 128)]

    def part(self, chip):
        sub = (chip * 2) // self.place.tp
        return self.mine.at[block(sub * self.rows, self.rows, 16)]

    def start(self, own_sem):
        place = self.place
        mine = self.part(place.chip)
        self.own = pltpu.make_async_copy(mine, self.spot(place.chip), own_sem)
        self.own.start()
        self.copies = []
        for k in range(1, place.chips):
            chip = place.other_chip(k)
            self.copies.append(
                send(
                    self.part(chip),
                    self.spot(place.chip),
                    self.chip_sems,
                    (k - 1,),
                    place.device(place.exp, chip, place.core),
                )
            )
        self.core = [send(mine, self.spot(place.chip), self.core_sems, (0,), place.sibling())]

    def run(self):
        place, core, copies = self.place, self.core, self.copies
        for k in range(1, place.chips):
            copies[k - 1].wait_recv()
            spot = self.spot((place.chip + place.chips - k) % place.chips)
            core.append(send(spot, spot, self.core_sems, (k,), place.sibling()))
        for copy in core:
            copy.wait()
        for copy in copies:
            copy.wait_send()
        self.own.wait()


class Fold:
    def __init__(self, place, part, home, scratch):
        self.place, self.part, self.home = place, part, home
        (
            self.core_got,
            self.chip_out,
            self.chip_got,
            self.exp_out,
            self.core_sems,
            self.chip_sems,
            self.exp_sems,
        ) = scratch
        self.feats = home.shape[2]

    def columns(self, chip, core):
        return block((chip * 2 + core) * self.feats, self.feats, 128)

    def run(self):
        place, part = self.place, self.part
        experts, chips = place.experts, place.chips
        each = self.home.shape[1]
        core_copies = {}
        for k in [*range(1, chips), 0]:
            away = part.at[:, self.columns(place.other_chip(k), 1 - place.core)]
            core_copies[k] = send(away, self.core_got.at[k], self.core_sems, (k,), place.sibling())
        chip_copies = []
        for k in range(1, chips):
            chip = place.other_chip(k)
            core_copies[k].wait_recv()
            mine = part[:, self.columns(chip, place.core)].astype(F32)
            self.chip_out[k - 1] = (mine + self.core_got[k].astype(F32)).astype(BF)
            chip_copies.append(
                send(
                    self.chip_out.at[k - 1],
                    self.chip_got.at[k - 1],
                    self.chip_sems,
                    (k - 1,),
                    place.device(place.exp, chip, place.core),
                )
            )
        core_copies[0].wait_recv()
        total = part[:, self.columns(place.chip, place.core)].astype(F32)
        total = total + self.core_got[0].astype(F32)
        for k in range(1, chips):
            chip_copies[k - 1].wait_recv()
            total = total + self.chip_got[k - 1].astype(F32)
        self.exp_out[...] = total.astype(BF)
        exp_copies = []
        for k in range(1, experts):
            exp = place.other_exp(k)
            exp_copies.append(
                send(
                    self.exp_out.at[block(exp * each, each, 16)],
                    self.home.at[place.exp],
                    self.exp_sems,
                    (k - 1,),
                    place.device(exp, place.chip, place.core),
                )
            )
        self.home[place.exp] = self.exp_out[block(place.exp * each, each, 16)]
        for copy in exp_copies:
            copy.wait_recv()
        for copy in [*core_copies.values(), *chip_copies, *exp_copies]:
            copy.wait_send()


def start_kernel(sizes, count, moves, *refs):
    place = Place(sizes)
    blocks, refs = take(refs, count)
    (pair_src,), refs = take(refs, 1)
    sources, refs = take(refs, len(moves))
    outs, refs = take(refs, count)
    (pair_out,), refs = take(refs, 1)
    landings, refs = take(refs, len(moves))
    (own_sems, exp_sems, chip_sems, core_sems), refs = take(refs, 4)
    pair_sems, refs = take(refs, 3)
    movers = make_movers(moves, sources, landings, refs)
    pair = Pair(place, pair_src, pair_out, *pair_sems)
    spreads = []
    for i, (rows, out) in enumerate(zip(blocks, outs)):
        quarter = rows.shape[1] // place.tp
        mine = rows.at[:, block(place.tp_at * quarter, quarter, 128)]
        sems = (s.at[i] for s in (exp_sems, chip_sems, core_sems))
        spreads.append(Spread(place, mine, out, True, *sems))
    place.meet(True)
    pair.start()
    for i, spread in enumerate(spreads[:-1]):
        spread.start(own_sems.at[i])
    pair.share()
    for mover in movers:
        mover.start(place, False)
    spreads[-1].start(own_sems.at[count - 1])
    for mover in movers:
        mover.start(place, True)
    for stage in range(place.experts + 2):
        for runner in (*spreads[:-1], pair):
            if stage <= place.experts:
                runner.step(stage)
        if stage:
            spreads[-1].step(stage - 1)
    for runner in (*spreads, pair):
        runner.finish()
    for mover in movers:
        mover.wait()


def take(refs, count):
    return refs[:count], refs[count:]


def turned(left, right):
    return lax.dot_general(left, right, (((0,), (0,)), ((), ())), preferred_element_type=F32)


def row_sums(weights, rows):
    return lax.dot_general(
        weights,
        rows,
        (((1,), (1,)), ((), ())),
        preferred_element_type=F32,
        precision=lax.Precision.HIGHEST,
    )


def make_movers(moves, sources, landings, sems):
    return [
        Mover(i, kind, cuts, source, landing, *sems)
        for i, ((kind, cuts), source, landing) in enumerate(zip(moves, sources, landings))
    ]


def exchange_kernel(sizes, tail, extras, moves, *refs):
    place = Place(sizes)
    (part, put, add, scale), refs = take(refs, 4)
    if tail == "slots":
        (next_put, linear, square), refs = take(refs, 3)
    else:
        (facts, *more), refs = take(refs, extras)
    sources, refs = take(refs, len(moves))
    (raw, all_facts), refs = take(refs, 2)
    outs, refs = take(refs, {"slots": 1, "tokens": extras, None: 0}[tail])
    landings, refs = take(refs, len(moves))
    (home, own_sems), refs = take(refs, 2)
    fact_sems, refs = take(refs, 3)
    fold_scratch, refs = take(refs, 7)
    if tail == "slots":
        (picked, facts), refs = take(refs, 2)
        tail_sems, refs = take(refs, 3)
    elif tail == "tokens":
        (mine,), refs = take(refs, 1)
        tail_sems, refs = take(refs, 2 * extras)
    movers = make_movers(moves, sources, landings, refs)
    place.meet(bool(moves))
    told = Spread(place, facts, all_facts, False, *fact_sems)
    if tail != "slots":
        told.start(own_sems.at[0])
    if tail == "tokens" and more:
        second = ToTokens(place, more[0], outs[1], *tail_sems[2:])
        second.start(own_sems.at[2])
    for mover in movers:
        mover.start(place, False)
    Fold(place, part, home, fold_scratch).run()
    if put.shape[1] == 128:
        summed = jnp.sum(home[...].astype(F32), axis=0)
    else:
        rows = home[...].reshape(-1, home.shape[2])
        summed = jnp.dot(put[...], rows, preferred_element_type=F32)
    value = add[...] + summed
    raw[...] = value
    if tail == "slots":
        picked[...] = turned(next_put[...], value.astype(BF)).astype(BF)
        slots = Spread(place, picked, outs[0], False, *tail_sems, pieces=place.experts)
        slots.start(own_sems.at[1])
        facts[...] = row_sums(linear[...], value) + row_sums(square[...], value * value)
        told.start(own_sems.at[0])
    elif tail == "tokens":
        mine[...] = (value * scale[...]).astype(BF)
        first = ToTokens(place, mine, outs[0], *tail_sems[:2])
        first.start(own_sems.at[1])
    for mover in movers:
        mover.start(place, True)
    if tail == "slots":
        slots.run()
    elif tail == "tokens":
        if more:
            second.run()
        first.run()
    told.run()
    for mover in movers:
        mover.wait()


def finish_kernel(sizes, moves, *refs):
    place = Place(sizes)
    (plus, product, unit, next_put), refs = take(refs, 4)
    sources, refs = take(refs, len(moves))
    (raw, out), refs = take(refs, 2)
    landings, refs = take(refs, len(moves))
    (sums, got, picked, own_sem, sum_sems), refs = take(refs, 5)
    tail_sems, refs = take(refs, 3)
    movers = make_movers(moves, sources, landings, refs)
    sums[...] = row_sums(jnp.ones((8, product.shape[1]), F32), product[...])
    place.meet(bool(moves))
    layer = place.chips * 2
    here = place.chip * 2 + place.core
    copies = []
    for k in range(1, layer):
        there = (here + k) % layer
        device = place.device(place.exp, there // 2, there % 2)
        copies.append(send(sums, got.at[k - 1], sum_sems, (k - 1,), device))
    for mover in movers:
        mover.start(place, False)
    total = sums[...]
    for k in range(1, layer):
        copies[k - 1].wait_recv()
        total = total + got[k - 1]
    mean = total.T[:, :1] * (1.0 / (layer * product.shape[1]))
    value = plus[...] - unit[...] * mean
    raw[...] = value
    picked[...] = turned(next_put[...], value.astype(BF)).astype(BF)
    slots = Spread(place, picked, out, False, *tail_sems, pieces=place.experts)
    slots.start(own_sem)
    for mover in movers:
        mover.start(place, True)
    slots.run()
    for copy in copies:
        copy.wait_send()
    for mover in movers:
        mover.wait()


def dma_sems(*shape):
    return pltpu.SemaphoreType.DMA(shape)


def move_scratch(sizes, moves):
    most = max(len(cuts) for _, cuts, _, _ in moves)
    members = sizes[0] * sizes[1]
    return [dma_sems(2, len(moves), most, members - 1), dma_sems(len(moves), most)]


def start(sizes, arrays, pair, moves, number):
    experts, sub, _, tp = sizes
    count = len(arrays)
    exp_sems, chip_sems, core_sems = (
        dma_sems(count, *shape) for shape in spread_shapes(sizes)
    )
    anywhere = pl.BlockSpec(memory_space=pl.ANY)
    total = count + 1 + len(moves)
    results = pl.pallas_call(
        partial(start_kernel, sizes, count, [(kind, cuts) for kind, cuts, _, _ in moves]),
        out_shape=[
            *[
                jax.ShapeDtypeStruct((rows.shape[0] * experts * sub, rows.shape[1]), rows.dtype)
                for rows in arrays
            ],
            jax.ShapeDtypeStruct((pair.shape[1] * experts * sub, 2 * pair.shape[2] // sub), BF),
            *landing_shapes(sizes, moves),
        ],
        in_specs=[anywhere] * total,
        out_specs=[anywhere] * total,
        scratch_shapes=[
            dma_sems(count),
            exp_sems,
            chip_sems,
            core_sems,
            dma_sems(2, 2, experts - 1),
            dma_sems(2, 2, sub - 1),
            dma_sems(2),
            *move_scratch(sizes, moves),
        ],
        compiler_params=pltpu.CompilerParams(
            collective_id=number, has_side_effects=True, vmem_limit_bytes=VMEM_BYTES
        ),
        name=f"start_{number}",
    )(*arrays, pair, *[array for _, _, array, _ in moves])
    return results[:count], results[count], results[count + 1 :]


def landing_shapes(sizes, moves):
    return [
        jax.ShapeDtypeStruct(moved_shape(sizes, kind, array, wide), BF)
        for kind, _, array, wide in moves
    ]


def spread_shapes(sizes):
    experts, sub, _, tp = sizes
    chips = sub * tp // 2
    return (2, 2, experts - 1), (2, experts, chips), (2, experts, chips)


def spread_sems(sizes):
    return [dma_sems(*shape) for shape in spread_shapes(sizes)]


def exchange(sizes, part, put, add, scale, extra, tail, moves, number):
    experts, sub, ctx, tp = sizes
    layer = sub * tp
    chips = layer // 2
    rows, width = part.shape
    tokens, feats = add.shape
    each = rows // experts
    vmem, anywhere = (pl.BlockSpec(memory_space=m) for m in (pltpu.VMEM, pl.ANY))
    if put is None:
        put = jnp.zeros((8, 128), BF)
    fact_shape = (8, tokens) if tail == "slots" else extra[0].shape
    outs, scratch, extra_specs = [], [], [vmem] * len(extra)
    if tail == "slots":
        picks = extra[0].shape[1]
        outs = [jax.ShapeDtypeStruct((picks, width), BF)]
        scratch = [pltpu.VMEM((picks, feats), BF), pltpu.VMEM(fact_shape, F32)]
        scratch += spread_sems(sizes)
    elif tail == "tokens":
        outs = [jax.ShapeDtypeStruct((tokens // sub, width), BF)] * len(extra)
        scratch = [pltpu.VMEM((tokens, feats), BF)]
        scratch += [dma_sems(2, chips - 1), dma_sems(2, chips)] * len(extra)
    if tail != "slots":
        extra_specs[0] = anywhere
    all_facts = jax.ShapeDtypeStruct((fact_shape[0] * experts, fact_shape[1] * layer), F32)
    raw, all_facts, *results = pl.pallas_call(
        partial(
            exchange_kernel, sizes, tail, len(extra), [(kind, cuts) for kind, cuts, _, _ in moves]
        ),
        out_shape=[
            jax.ShapeDtypeStruct((tokens, feats), F32),
            all_facts,
            *outs,
            *landing_shapes(sizes, moves),
        ],
        in_specs=[vmem] * 4 + extra_specs + [anywhere] * len(moves),
        out_specs=[vmem] + [anywhere] * (1 + len(outs) + len(moves)),
        scratch_shapes=[
            pltpu.VMEM((experts, each, feats), BF),
            dma_sems(3),
            *spread_sems(sizes),
            pltpu.VMEM((chips, rows, feats), BF),
            pltpu.VMEM((chips - 1, rows, feats), BF),
            pltpu.VMEM((chips - 1, rows, feats), BF),
            pltpu.VMEM((rows, feats), BF),
            dma_sems(2, chips),
            dma_sems(2, chips - 1),
            dma_sems(2, experts - 1),
            *scratch,
            *move_scratch(sizes, moves),
        ],
        compiler_params=pltpu.CompilerParams(
            collective_id=number, has_side_effects=True, vmem_limit_bytes=VMEM_BYTES
        ),
        name=f"exchange_{number}",
    )(part, put, add, scale, *extra, *[array for _, _, array, _ in moves])
    outs, moved = results[: len(outs)], results[len(outs) :]
    all_facts = all_facts.reshape(experts, fact_shape[0], layer, fact_shape[1])
    return raw, outs, all_facts.transpose(0, 2, 1, 3), moved


def finish(sizes, plus, product, unit, next_put, moves, number):
    experts, sub, ctx, tp = sizes
    layer = sub * tp
    tokens, feats = plus.shape
    picks = next_put.shape[1]
    vmem, anywhere = (pl.BlockSpec(memory_space=m) for m in (pltpu.VMEM, pl.ANY))
    raw, out, *moved = pl.pallas_call(
        partial(finish_kernel, sizes, [(kind, cuts) for kind, cuts, _, _ in moves]),
        out_shape=[
            jax.ShapeDtypeStruct((tokens, feats), F32),
            jax.ShapeDtypeStruct((picks, feats * layer), BF),
            *landing_shapes(sizes, moves),
        ],
        in_specs=[vmem] * 4 + [anywhere] * len(moves),
        out_specs=[vmem] + [anywhere] * (1 + len(moves)),
        scratch_shapes=[
            pltpu.VMEM((8, tokens), F32),
            pltpu.VMEM((layer - 1, 8, tokens), F32),
            pltpu.VMEM((picks, feats), BF),
            pltpu.SemaphoreType.DMA,
            dma_sems(2, layer - 1),
            *spread_sems(sizes),
            *move_scratch(sizes, moves),
        ],
        compiler_params=pltpu.CompilerParams(
            collective_id=number, has_side_effects=True, vmem_limit_bytes=VMEM_BYTES
        ),
        name=f"finish_{number}",
    )(plus, product, unit, next_put, *[array for _, _, array, _ in moves])
    return raw, out, moved


def parted(pick, table):
    total = None
    for _ in range(3):
        part = table.astype(BF)
        product = jnp.dot(pick, part, preferred_element_type=F32)
        total = product if total is None else total + product
        table = table - part.astype(F32)
    return total


def times(left, right):
    return jnp.dot(left, right, preferred_element_type=F32)


def times_turned(left, right):
    return lax.dot_general(left, right, (((1,), (1,)), ((), ())), preferred_element_type=F32)


def one_hot(places, shape, axis):
    return (lax.broadcasted_iota(jnp.int32, shape, axis).astype(F32) == places).astype(BF)


def allowed_keys(position, span, spans):
    shape = (position.shape[0], spans.shape[1])
    keys = lax.broadcasted_iota(jnp.int32, shape, 1).astype(F32)
    return (keys <= position) | ((span == spans) & (span > 0))


def softmax_rows(scores, allowed):
    scores = jnp.where(allowed, scores, -1e30)
    expo = jnp.exp(scores - jnp.max(scores, axis=-1, keepdims=True))
    return expo / jnp.sum(expo, axis=-1, keepdims=True)


def head_columns(head):
    return pl.ds(head * HD, HD)


def turn_heads(rows, cosine, sine):
    parts = []
    for head in range(rows.shape[1] // HD):
        u = rows[:, head * HD : (head + 1) * HD]
        parts.append(u * cosine + pltpu.roll(u, HD // 2, 1) * sine)
    return jnp.concatenate(parts, axis=1)


def turn_heads_back(rows, cosine, sine):
    parts = []
    for head in range(rows.shape[1] // HD):
        u = rows[:, head * HD : (head + 1) * HD]
        parts.append(u * cosine + pltpu.roll(u * sine, HD // 2, 1))
    return jnp.concatenate(parts, axis=1)


def attend_kernel(
    experts,
    x_ref,
    gain_ref,
    query_ref,
    key_value_ref,
    route_ref,
    rows_ref,
    hits_ref,
    cosine_ref,
    sine_ref,
    mine_ref,
    h1_ref,
    slots_ref,
    queries_ref,
    keys_ref,
    values_ref,
    mixed_ref,
    gates_ref,
    tables_ref,
):
    seq_len = x_ref.shape[0]
    cap = slots_ref.shape[0]
    wide = query_ref.shape[1]
    x = x_ref[...].astype(F32)
    scale_in = lax.rsqrt(jnp.mean(x * x, axis=1, keepdims=True) + EPS)
    h1 = (x * scale_in * gain_ref[...]).astype(BF)
    h1_ref[...] = h1
    cosine, sine = cosine_ref[...], sine_ref[...]
    kv = times(h1, key_value_ref[...])
    keys_ref[...] = turn_heads(kv[:, :wide], cosine, sine).astype(BF)
    values_ref[...] = kv[:, wide:].astype(BF)
    logits = times(h1, route_ref[...])
    hits = hits_ref[...]
    lane = lax.broadcasted_iota(jnp.int32, hits.shape, 1)
    chosen = (hits > 0) & (lane < experts)
    top = jnp.max(jnp.where(chosen, logits, -1e30), axis=1, keepdims=True)
    raised = jnp.where(chosen, jnp.exp(jnp.minimum(logits - top, 0.0)), 0.0)
    gates = raised / jnp.sum(raised, axis=1, keepdims=True)
    gates_ref[...] = gates
    pick = one_hot(rows_ref[0, 0:1], (cap, seq_len), 0)
    slots = times(pick, h1).astype(BF)
    slots_ref[...] = slots
    row = lax.broadcasted_iota(jnp.int32, hits.shape, 0).astype(F32)
    gate_mine = jnp.sum(gates * mine_ref[...], axis=1, keepdims=True)
    facts = jnp.where(lane == 0, gate_mine, jnp.where(lane == 1, row, hits))
    tables = parted(pick, jnp.concatenate([cosine, sine, facts], axis=1))
    tables_ref[...] = tables
    queries = turn_heads(times(slots, query_ref[...]), tables[:, :HD], tables[:, HD : 2 * HD])
    queries_ref[...] = queries.astype(BF)
    at = 2 * HD
    allowed = allowed_keys(
        tables[:, at + 1 : at + 2], tables[:, at + experts : at + experts + 1], rows_ref[0, 1:2]
    )
    for head in range(wide // HD):
        part = head_columns(head)
        scores = times_turned(queries_ref[:, part], keys_ref[:, part]) * HD**-0.5
        probs = softmax_rows(scores, allowed).astype(BF)
        mixed_ref[:, part] = times(probs, values_ref[:, part]).astype(BF)


def attend(experts, seqs, x, gain, query, key_value, route, rows, hits, cosine, sine, mine):
    total, width = x.shape
    seq_len = total // seqs
    cap = 2 * seq_len // experts
    wide = query.shape[1]

    def each(*shape):
        zeros = (0,) * (len(shape) - 1)
        return pl.BlockSpec(shape, lambda s: (s, *zeros))

    def whole(array):
        zeros = (0,) * array.ndim
        return pl.BlockSpec(array.shape, lambda s: zeros)

    def out(rows, columns, dtype):
        return jax.ShapeDtypeStruct((seqs * rows, columns), dtype)

    return pl.pallas_call(
        partial(attend_kernel, experts),
        grid=(seqs,),
        in_specs=[
            each(seq_len, width),
            whole(gain),
            whole(query),
            whole(key_value),
            whole(route),
            each(1, 8, seq_len),
            each(seq_len, HD),
            whole(cosine),
            whole(sine),
            whole(mine),
        ],
        out_specs=[
            each(seq_len, width),
            each(cap, width),
            each(cap, wide),
            each(seq_len, wide),
            each(seq_len, wide),
            each(cap, wide),
            each(seq_len, HD),
            each(cap, 3 * HD),
        ],
        out_shape=[
            out(seq_len, width, BF),
            out(cap, width, BF),
            out(cap, wide, BF),
            out(seq_len, wide, BF),
            out(seq_len, wide, BF),
            out(cap, wide, BF),
            out(seq_len, HD, F32),
            out(cap, 3 * HD, F32),
        ],
        compiler_params=pltpu.CompilerParams(vmem_limit_bytes=LOCAL_VMEM_BYTES),
        cost_estimate=pl.CostEstimate(
            flops=2 * total * width * (3 * wide + seq_len // 2),
            bytes_accessed=6 * total * width,
            transcendentals=total * seq_len,
        ),
        name="attend",
    )(x, gain, query, key_value, route, rows, hits, cosine, sine, mine)


def attend_back_kernel(
    experts,
    grad_ref,
    out_ref,
    query_ref,
    key_value_ref,
    rows_ref,
    hits_ref,
    cosine_ref,
    sine_ref,
    queries_ref,
    keys_ref,
    values_ref,
    mixed_ref,
    tables_ref,
    grad_query_ref,
    grad_kv_ref,
    grad_branch_ref,
    gate_ref,
    first_ref,
):
    seq_len, wide = keys_ref.shape
    cap = queries_ref.shape[0]
    tables = tables_ref[...]
    at = 2 * HD
    gate = tables[:, at : at + 1]
    allowed = allowed_keys(
        tables[:, at + 1 : at + 2], tables[:, at + experts : at + experts + 1], rows_ref[0, 1:2]
    )
    grad = grad_ref[...]
    grad_branch_ref[...] = (grad.astype(F32) * gate).astype(BF)
    grad_mixed = times_turned(grad, out_ref[...])
    gates = jnp.sum(mixed_ref[...].astype(F32) * grad_mixed, axis=1, keepdims=True)
    gate_ref[...] = jnp.broadcast_to(gates, gate_ref.shape)
    grad_mixed = (grad_mixed * gate).astype(BF)
    grad_queries, grad_keys, grad_values = [], [], []
    for head in range(wide // HD):
        part = head_columns(head)
        queries, keys = queries_ref[:, part], keys_ref[:, part]
        own = grad_mixed[:, head * HD : (head + 1) * HD]
        probs = softmax_rows(times_turned(queries, keys) * HD**-0.5, allowed)
        grad_probs = times_turned(own, values_ref[:, part])
        grad_values.append(turned(probs.astype(BF), own))
        inner = jnp.sum(probs * grad_probs, axis=1, keepdims=True)
        grad_scores = (probs * (grad_probs - inner)).astype(BF)
        grad_queries.append(times(grad_scores, keys) * HD**-0.5)
        grad_keys.append(turned(grad_scores, queries) * HD**-0.5)
    grad_queries = jnp.concatenate(grad_queries, axis=1)
    grad_qpre = turn_heads_back(grad_queries, tables[:, :HD], tables[:, HD : 2 * HD]).astype(BF)
    grad_query_ref[...] = grad_qpre
    grad_keys = turn_heads_back(
        jnp.concatenate(grad_keys, axis=1), cosine_ref[...], sine_ref[...]
    )
    kv_low = jnp.concatenate([grad_keys, *grad_values], axis=1).astype(BF)
    grad_kv_ref[...] = kv_low
    taken = times_turned(grad_qpre, query_ref[...]).astype(BF)
    give = one_hot(hits_ref[:, experts + 1 : experts + 2], (seq_len, cap), 1)
    first = times_turned(kv_low, key_value_ref[...]) + times(give, taken)
    first_ref[...] = first.astype(BF)


def attend_back(
    experts, seqs, grad, out, query, key_value, rows, hits, cosine, sine, saved
):
    queries, keys, values, mixed, tables = saved
    width = grad.shape[1]
    cap = grad.shape[0] // seqs
    total, wide = keys.shape
    seq_len = total // seqs

    def each(*shape):
        zeros = (0,) * (len(shape) - 1)
        return pl.BlockSpec(shape, lambda s: (s, *zeros))

    def whole(array):
        zeros = (0,) * array.ndim
        return pl.BlockSpec(array.shape, lambda s: zeros)

    def result(rows, columns, dtype):
        return jax.ShapeDtypeStruct((seqs * rows, columns), dtype)

    return pl.pallas_call(
        partial(attend_back_kernel, experts),
        grid=(seqs,),
        in_specs=[
            each(cap, width),
            whole(out),
            whole(query),
            whole(key_value),
            each(1, 8, seq_len),
            each(seq_len, HD),
            whole(cosine),
            whole(sine),
            each(cap, wide),
            each(seq_len, wide),
            each(seq_len, wide),
            each(cap, wide),
            each(cap, 3 * HD),
        ],
        out_specs=[
            each(cap, wide),
            each(seq_len, 2 * wide),
            each(cap, width),
            each(cap, HD),
            each(seq_len, width),
        ],
        out_shape=[
            result(cap, wide, BF),
            result(seq_len, 2 * wide, BF),
            result(cap, width, BF),
            result(cap, HD, F32),
            result(seq_len, width, BF),
        ],
        compiler_params=pltpu.CompilerParams(vmem_limit_bytes=LOCAL_VMEM_BYTES),
        cost_estimate=pl.CostEstimate(
            flops=2 * total * width * (3 * wide + seq_len // 2),
            bytes_accessed=6 * total * width,
            transcendentals=total * seq_len,
        ),
        name="attend_back",
    )(
        grad, out, query, key_value, rows, hits, cosine, sine, queries, keys, values, mixed, tables
    )


class Axes:
    def __init__(self, experts, shard, ctx, tp):
        self.experts = experts
        self.sub = shard * ctx // experts
        self.tp = tp
        if self.sub == ctx:
            self.layer, self.exp = (("ctx", "tp"), None), ("shard", None)
            self.part = ("ctx", None)
        else:
            devices = np.arange(shard * ctx * tp).reshape(experts, self.sub, tp)
            self.layer = (ALL, devices.reshape(experts, -1).tolist())
            self.exp = (ALL, devices.reshape(experts, -1).T.tolist())
            self.part = (ALL, devices.transpose(0, 2, 1).reshape(-1, self.sub).tolist())

    def swap(self, value, over):
        axes, groups = over
        return lax.all_to_all(value, axes, 0, 0, axis_index_groups=groups)


class Routing:
    def __init__(self, choice, seqs, seq_len, experts, cap, mine, own_first, own_seqs):
        columns = jnp.arange(experts, dtype=jnp.int32)
        hits = jnp.sum((choice[:, :, None] == columns[None, None, :]).astype(F32), axis=1)
        self.hits = hits.reshape(seqs, seq_len, experts)
        rows = jnp.arange(seq_len, dtype=jnp.int32)
        earlier = (rows[None, :] < rows[:, None]).astype(BF)
        before = dot("tu,sue->ste", earlier, self.hits.astype(BF))
        self.valid = self.hits * (before < cap).astype(F32)
        self.place = jnp.where(self.valid > 0, before, -1.0)
        self.cap = cap
        is_mine = (columns == mine).astype(F32)
        place_mine = jnp.sum(self.place * is_mine, axis=2)
        self.place_mine = place_mine
        slots = jnp.arange(cap, dtype=jnp.int32).astype(F32)
        self.is_mine = is_mine
        self.pick = (place_mine[:, None, :] == slots[None, :, None]).astype(BF)
        place_own = lax.dynamic_slice_in_dim(self.place, own_first, own_seqs, 0)
        place_own = place_own.transpose(1, 0, 2)[:, :, :, None]
        seq_of = jnp.arange(own_seqs, dtype=jnp.int32)
        here = place_own == slots
        same = (seq_of[:, None] == seq_of[None, :])[:, None, None, :, None]
        put = here.transpose(1, 0, 2, 3)[:, :, :, None, :] & same
        self.put = put.astype(BF).reshape(own_seqs * seq_len, experts * own_seqs * cap)

    def gates(self, logits):
        logits = logits.reshape(self.hits.shape)
        top = jnp.max(jnp.where(self.hits > 0, logits, -jnp.inf), axis=2, keepdims=True)
        raised = jnp.where(self.hits > 0, jnp.exp(logits - top), 0.0)
        return raised / jnp.sum(raised, axis=2, keepdims=True)

    def slot_gates(self, gates):
        gate_mine = jnp.sum(gates * self.is_mine, axis=2)
        return jnp.sum(self.pick.astype(F32) * gate_mine[:, None, :], axis=2)

    def take(self, rows):
        seqs, cap, seq_len = self.pick.shape
        picked = dot("spt,stf->spf", self.pick, rows.reshape(seqs, seq_len, -1))
        return picked.astype(BF).reshape(seqs * cap, -1)

    def give(self, slots):
        seqs, cap, seq_len = self.pick.shape
        rows = dot("spt,spf->stf", self.pick, slots.reshape(seqs, cap, -1))
        return rows.reshape(seqs * seq_len, -1)

    def token_grads(self, slot_grads):
        slots = jnp.arange(self.cap, dtype=jnp.int32).astype(F32)
        here = self.place[:, :, :, None] == slots[None, None, None, :]
        grads = slot_grads.transpose(1, 0, 2)[:, None, :, :]
        return jnp.sum(jnp.where(here, grads, 0.0), axis=3)


def put_home(put, home):
    return dot("tp,pf->tf", put, home.reshape(-1, home.shape[-1]))


def router_rows(grads, router):
    high = grads.astype(BF)
    low = (grads - high.astype(F32)).astype(BF)
    return dot(
        "te,fe->tf",
        jnp.concatenate([high, low], axis=1),
        jnp.concatenate([router, router], axis=1),
    )


def logit_grads(gates, gate_grads):
    mean = jnp.sum(gates * gate_grads, axis=2, keepdims=True)
    grads = gates * (gate_grads - mean)
    return grads.reshape(-1, grads.shape[-1])


def shards(
    sizes,
    hidden_in,
    att_choice,
    ffn_choice,
    span_ids,
    norm_att,
    router_att,
    w_query,
    w_out,
    w_key,
    w_value,
    norm_ffn,
    router_ffn,
    w_gate,
    w_up,
    w_down,
    cotangent,
):
    shard, ctx, tp = sizes
    experts = w_query.shape[0]
    axes = Axes(experts, shard, ctx, tp)
    sub = axes.sub
    group = experts * sub
    layer = sub * tp
    tokens, width = hidden_in.shape
    total = tokens * group
    seq_len = tokens * ctx
    seqs = total // seq_len
    own_seqs = seqs // experts
    own_tokens = own_seqs * seq_len
    cap = 2 * seq_len // experts
    slots = seqs * cap
    rows_own = width // group
    feats = width // layer
    sizes = (experts, sub, ctx, tp)
    kernels = feats % 128 == 0 and rows_own % 128 == 0 and tokens % 16 == 0
    group_at, tp_at = lax.axis_index(GROUP), lax.axis_index("tp")
    exp_at, sub_at = group_at // sub, group_at % sub
    layer_at = sub_at * tp + tp_at

    token_pack = jnp.concatenate(
        [att_choice, ffn_choice, span_ids[:, None]], axis=1
    ).astype(BF)
    feature_pack = jnp.concatenate(
        [norm_att[:, None], router_att, norm_ffn[:, None], router_ffn], axis=1
    )
    def everywhere(rows):
        quarter = width // tp
        part = lax.dynamic_slice_in_dim(rows, tp_at * quarter, quarter, 1)
        parts = lax.all_gather(part, ALL)
        return parts.reshape(group, tp, tokens, quarter).transpose(0, 2, 1, 3).reshape(total, width)

    def everywhere_layer(rows):
        parts = lax.all_gather(rows, ALL)
        return (
            parts.reshape(experts, layer, own_tokens, feats)
            .transpose(0, 2, 1, 3)
            .reshape(total, width)
        )

    def layer_sum(rows):
        m = rows.shape[0]
        parts = rows.astype(BF).reshape(m, layer, feats).transpose(1, 0, 2)
        parts = axes.swap(parts, axes.layer)
        return jnp.sum(parts.astype(F32), axis=0)

    def go_home(rows):
        return axes.swap(rows.astype(BF).reshape(experts, -1, feats), axes.exp)

    def to_tokens(rows):
        parts = axes.swap(rows.reshape(sub, tokens, feats), axes.part)
        parts = lax.all_gather(parts, "tp")
        return parts.transpose(2, 1, 0, 3).reshape(tokens, width)

    head_parts = math.gcd(sub, w_query.shape[2] // HD)
    copies = sub // head_parts
    heads_wide = w_query.shape[2] // head_parts
    hidden_local = w_gate.shape[2]
    hidden_wide = -(-hidden_local // (sub * 128)) * 128
    windows = sub == 2 and (hidden_local - hidden_wide) % 128 == 0
    hidden_pad = 0 if windows else hidden_wide * sub - hidden_local
    overlap = hidden_wide * sub - hidden_local if windows else 0
    hidden_mine = jnp.arange(hidden_wide) >= overlap * sub_at
    kernels = kernels and windows and copies == 1

    def to_windows(weight, axis):
        if windows:
            size = weight.shape[axis]
            parts = [
                lax.slice_in_dim(weight, 0, hidden_wide, axis=axis),
                lax.slice_in_dim(weight, size - hidden_wide, size, axis=axis),
            ]
        else:
            pad = [(0, 0)] * 3
            pad[axis] = (0, hidden_pad)
            parts = jnp.split(jnp.pad(weight, pad), sub, axis=axis)
        parts = jnp.stack(parts, axis=1)
        return parts.reshape(group, *parts.shape[2:])

    def to_heads(weight, axis):
        parts = jnp.stack(jnp.split(weight, head_parts, axis=axis), axis=1)
        return jnp.repeat(parts, copies, axis=1).reshape(group, *parts.shape[2:])

    def to_all(weight):
        return to_heads(jnp.broadcast_to(weight, (experts, *weight.shape)), 2)

    def swap_group(value):
        return lax.all_to_all(value, GROUP, 0, 0)

    def as_columns(parts):
        return parts.reshape(width, parts.shape[2])

    def as_rows(parts):
        return parts.transpose(1, 0, 2).reshape(parts.shape[1], width)

    pack = jnp.concatenate(
        [jnp.pad(facts.T, ((0, 16 - facts.shape[1]), (0, 0))) for facts in (token_pack, feature_pack)],
        axis=1,
    )
    if kernels:
        (packs, all_in, top_all), my_key_value, (my_query, my_out) = start(
            sizes,
            [pack, hidden_in, cotangent],
            jnp.stack([w_key, w_value]),
            [
                ("columns_out", ((0, heads_wide, False),), w_query, heads_wide),
                ("rows_out", ((0, heads_wide, True),), w_out, heads_wide),
            ],
            0,
        )
        packs = packs.reshape(group, 16, -1)
    else:
        packs = lax.all_gather(pack, GROUP)
        all_in, top_all = everywhere(hidden_in), everywhere(cotangent)
        first = [to_heads(w_query, 2), to_all(w_key), to_all(w_value), to_heads(w_out, 1)]
        first = swap_group(jnp.concatenate(first, axis=2))
        my_query = as_columns(first[:, :, :heads_wide])
        my_key_value = as_columns(first[:, :, heads_wide : 3 * heads_wide])
        my_out = as_rows(first[:, :, 3 * heads_wide :])
    packs = packs.transpose(0, 2, 1)
    token_facts = packs[:, :tokens].reshape(total, 16).astype(jnp.int32)
    feature_facts = packs[:, tokens:].reshape(width, 16)
    gain_att = feature_facts[:, 0].astype(F32)
    route_att = feature_facts[:, 1 : 1 + experts]
    gain_ffn = feature_facts[:, 1 + experts].astype(F32)
    route_ffn = feature_facts[:, 2 + experts : 2 + 2 * experts]

    def move(kind, weight):
        if kind == "columns_out":
            return as_columns(swap_group(to_windows(weight, 2)))
        if kind == "rows_out":
            return as_rows(swap_group(to_windows(weight, 1)))
        if kind == "columns_home":
            return swap_group(weight.reshape(group, rows_own, -1))
        return swap_group(weight.reshape(-1, group, rows_own).transpose(1, 0, 2))

    def to_cuts(moves):
        return [
            (kind, ((0, early, False), (early, wide - early, True)), weight, wide)
            for kind, weight, wide, early in moves
        ]

    def to_slots(rows, next_put):
        picked = dot("tp,tf->pf", next_put, rows).astype(BF)
        picked = axes.swap(picked.reshape(experts, -1, feats), axes.exp)
        picked = lax.all_gather(
            picked.reshape(-1, feats), axes.layer[0], axis_index_groups=axes.layer[1]
        )
        return picked.transpose(1, 0, 2).reshape(-1, width)

    def exchanged(part, put, add, scale, extra, tail, moves, number):
        if kernels:
            return exchange(sizes, part, put, add, scale, extra, tail, to_cuts(moves), number)
        home = go_home(layer_sum(part))
        summed = jnp.sum(home.astype(F32), axis=0) if put is None else put_home(put, home)
        raw, outs = add + summed, []
        if tail == "slots":
            next_put, linear, square = extra
            outs = [to_slots(raw.astype(BF), next_put)]
            facts = dot_exact("ef,tf->et", linear, raw) + dot_exact("ef,tf->et", square, raw * raw)
        else:
            facts = extra[0]
        if tail == "tokens":
            outs = [to_tokens(rows) for rows in ((raw * scale).astype(BF), *extra[1:])]
        told = lax.all_gather(facts, ALL).reshape(experts, layer, *facts.shape)
        return raw, outs, told, [move(kind, weight) for kind, weight, _, _ in moves]

    def finished(plus, product, unit, next_put, moves, number):
        if kernels:
            return finish(sizes, plus, product, unit, next_put, to_cuts(moves), number)
        sums = lax.all_gather(jnp.sum(product, axis=1), ALL).reshape(experts, layer, own_tokens)
        mean = lax.dynamic_index_in_dim(jnp.sum(sums, axis=1), exp_at, 0, keepdims=False) / width
        raw = plus - unit * mean[:, None]
        moved = [move(kind, weight) for kind, weight, _, _ in moves]
        return raw, to_slots(raw.astype(BF), next_put), moved

    own_first = exp_at * own_seqs
    where = partial(
        Routing,
        seqs=seqs,
        seq_len=seq_len,
        experts=experts,
        cap=cap,
        mine=exp_at,
        own_first=own_first,
        own_seqs=own_seqs,
    )
    att = where(token_facts[:, 0:2])
    if copies > 1:
        turn = jnp.arange(seqs, dtype=jnp.int32) % copies == sub_at % copies
        att.pick = att.pick * turn.astype(BF)[:, None, None]
    ffn = where(token_facts[:, 2:4])
    spans = token_facts[:, 4].reshape(seqs, seq_len).astype(F32)
    cosine, sine = rope_tables(seq_len)

    my_gate = move("columns_out", after(w_gate, all_in))
    heads = heads_wide // HD
    scale = 1.0 / math.sqrt(HD)
    if kernels:
        att_rows = jnp.pad(jnp.stack([att.place_mine, spans], axis=1), ((0, 0), (0, 6), (0, 0)))
        att_hits = jnp.concatenate(
            [att.hits, spans[:, :, None], att.place_mine[:, :, None]], axis=2
        ).reshape(total, -1)
        att_hits = jnp.pad(att_hits, ((0, 0), (0, HD - att_hits.shape[1])))
        sine = sine * jnp.where(jnp.arange(HD) < HD // 2, -1.0, 1.0)
        h1, h1_slots, *saved, att_gates, att_tables = attend(
            experts,
            seqs,
            all_in,
            gain_att[None, :],
            my_query,
            my_key_value,
            jnp.pad(route_att, ((0, 0), (0, HD - experts))),
            att_rows,
            att_hits,
            cosine,
            sine,
            (jnp.arange(HD) == exp_at).astype(F32)[None, :],
        )
        mixed = saved[3]
        saved.append(att_tables)
        att_gates = att_gates[:, :experts].reshape(seqs, seq_len, experts)
        att_slot_gate = att_tables[:, 2 * HD : 2 * HD + 1]
    else:
        positions = jnp.arange(seq_len, dtype=jnp.int32).astype(F32)
        pick_f32 = att.pick.astype(F32)
        slot_position = jnp.sum(pick_f32 * positions[None, None, :], axis=2)
        slot_span = jnp.sum(pick_f32 * spans[:, None, :], axis=2)
        slot_cosine = dot_exact("spt,tf->spf", pick_f32, cosine)
        slot_sine = dot_exact("spt,tf->spf", pick_f32, sine)
        allowed = (positions[None, None, :] <= slot_position[:, :, None]) | (
            (slot_span[:, :, None] == spans[:, None, :]) & (slot_span[:, :, None] > 0)
        )
        x_all = all_in.astype(F32)
        scale_in = lax.rsqrt(jnp.mean(x_all * x_all, axis=1, keepdims=True) + EPS)
        h1 = (x_all * scale_in * gain_att[None, :]).astype(BF)
        kv = dot("td,dm->tm", h1, my_key_value)
        keys = rotate(
            kv[:, :heads_wide].reshape(seqs, seq_len, heads, HD),
            cosine[None, :, None, :],
            sine[None, :, None, :],
        ).astype(BF)
        values = kv[:, heads_wide:].astype(BF).reshape(seqs, seq_len, heads, HD)
        att_gates = att.gates(dot("td,de->te", h1, route_att))
        att_slot_gate = att.slot_gates(att_gates).reshape(slots, 1)
        h1_slots = att.take(h1)
        queries = rotate(
            dot("td,dm->tm", h1_slots, my_query).reshape(seqs, cap, heads, HD),
            slot_cosine[:, :, None, :],
            slot_sine[:, :, None, :],
        ).astype(BF)
        scores = dot("sqhd,skhd->shqk", queries, keys) * scale
        scores = jnp.where(allowed[:, None], scores, -1e30)
        expo = jnp.exp(scores - jnp.max(scores, axis=-1, keepdims=True))
        probs = expo / jnp.sum(expo, axis=-1, keepdims=True)
        probs_low = probs.astype(BF)
        mixed = dot("shqk,skhd->sqhd", probs_low, values).astype(BF).reshape(slots, heads_wide)
    branch_att = dot("cm,md->cd", mixed, my_out) * att_slot_gate
    own_at = (exp_at * own_tokens, layer_at * feats)
    own_in = lax.dynamic_slice(all_in, own_at, (own_tokens, feats)).astype(F32)
    own_gain_ffn = lax.dynamic_slice_in_dim(gain_ffn, layer_at * feats, feats, 0)
    own_route_ffn = lax.dynamic_slice_in_dim(
        route_ffn.astype(F32), layer_at * feats, feats, 0
    )
    linear = jnp.pad((own_route_ffn * own_gain_ffn[:, None]).T, ((0, 8 - experts), (0, 0)))
    square = (jnp.arange(8) == experts).astype(F32)[:, None] * jnp.ones((1, feats), F32)
    mid, (mid_slots,), ffn_facts, (my_up,) = exchanged(
        after(branch_att.astype(BF), my_gate),
        att.put,
        own_in,
        jnp.ones((1, feats), F32),
        (ffn.put, linear, square),
        "slots",
        [("columns_out", w_up, hidden_wide, hidden_wide // 3)],
        1,
    )
    my_down = move("rows_out", after(w_down, mid_slots))

    ffn_facts = jnp.sum(ffn_facts, axis=1)
    scale_mid = lax.rsqrt(ffn_facts[:, experts].reshape(total, 1) / width + EPS)
    ffn_logits = ffn_facts[:, :experts].transpose(0, 2, 1).reshape(total, experts) * scale_mid
    ffn_gates = ffn.gates(ffn_logits)
    ffn_slot_gate = ffn.slot_gates(ffn_gates).reshape(slots, 1)
    mid_slots = mid_slots.astype(F32)
    scale_slots = lax.rsqrt(jnp.mean(mid_slots * mid_slots, axis=1, keepdims=True) + EPS)
    h2_slots = (mid_slots * scale_slots * gain_ffn[None, :]).astype(BF)
    pre_gate = dot("cd,df->cf", h2_slots, my_gate)
    pre_up = dot("cd,df->cf", h2_slots, my_up)
    sigma = jax.nn.sigmoid(pre_gate)
    swish = pre_gate * sigma
    hidden = jnp.where(hidden_mine, swish * pre_up, 0.0).astype(BF)

    top_slots = ffn.take(top_all)
    grad_branch = (top_slots.astype(F32) * ffn_slot_gate).astype(BF)
    grad_down_w = dot("cf,cd->fd", hidden, grad_branch).astype(BF)
    grad_down = move("rows_home", grad_down_w)
    my_down = after(my_down, grad_down_w)
    branch_ffn = dot("cf,fd->cd", hidden, my_down) * ffn_slot_gate
    grad_hidden = dot("cd,fd->cf", top_slots, my_down)
    ffn_gate_part = jnp.sum(hidden.astype(F32) * grad_hidden, axis=1)
    grad_hidden = jnp.where(hidden_mine, grad_hidden * ffn_slot_gate, 0.0)
    grad_pre_gate = (
        grad_hidden * pre_up * sigma * (1.0 + pre_gate * (1.0 - sigma))
    ).astype(BF)
    grad_pre_up = (grad_hidden * swish).astype(BF)
    ffn_taken = dot("cf,df->cd", grad_pre_gate, my_gate) + dot("cf,df->cd", grad_pre_up, my_up)
    grad_gate_w = dot("cd,cf->df", h2_slots, grad_pre_gate).astype(BF)
    gate_half = hidden_wide // 256 * 128

    def gate_facts(told):
        return jnp.sum(told, axis=1).reshape(experts, seqs, cap)

    grad_second, _, ffn_told, (gate_first,) = exchanged(
        ffn_taken.astype(BF),
        ffn.put,
        jnp.zeros((own_tokens, feats), F32),
        jnp.ones((1, feats), F32),
        (ffn_gate_part.reshape(-1, 128),),
        None,
        [("columns_home", grad_gate_w[:, :gate_half], gate_half, 128)],
        2,
    )
    ffn_logit_grads = logit_grads(ffn_gates, ffn.token_grads(gate_facts(ffn_told)))
    own_ffn_logits = lax.dynamic_slice_in_dim(
        ffn_logit_grads, exp_at * own_tokens, own_tokens, 0
    )
    own_scale_mid = lax.dynamic_slice_in_dim(scale_mid, exp_at * own_tokens, own_tokens, 0)
    own_unit_mid = mid * own_scale_mid
    grad_second = grad_second + router_rows(own_ffn_logits, own_route_ffn)
    norm_ffn_part = jnp.sum(grad_second * own_unit_mid, axis=0)
    own_second = grad_second * own_gain_ffn[None, :] * own_scale_mid
    gate_rest = hidden_wide - gate_half
    grad_mid, mid_slots, (gate_second,) = finished(
        lax.dynamic_slice(top_all, own_at, (own_tokens, feats)).astype(F32) + own_second,
        own_second * own_unit_mid,
        own_unit_mid,
        att.put,
        [("columns_home", grad_gate_w[:, gate_half:], gate_rest, 128)],
        5,
    )
    grad_gate = jnp.concatenate([gate_first, gate_second], axis=2)
    grad_up_w = dot("cd,cf->df", h2_slots, grad_pre_up).astype(BF)
    grad_up = move("columns_home", after(grad_up_w, mid_slots))

    if copies > 1:
        mid_slots = mid_slots * jnp.repeat(turn, cap).astype(BF)[:, None]
    if kernels:
        grad_qpre, kv_low, grad_att_branch, att_gate_part, first_part = attend_back(
            experts,
            seqs,
            mid_slots,
            my_out,
            my_query,
            my_key_value,
            att_rows,
            att_hits,
            cosine,
            sine,
            saved,
        )
        att_gate_part = att_gate_part[:, 0]
    else:
        grad_mixed = dot("cd,md->cm", mid_slots, my_out)
        att_gate_part = jnp.sum(mixed.astype(F32) * grad_mixed, axis=1)
        grad_mixed = (grad_mixed * att_slot_gate).astype(BF).reshape(seqs, cap, heads, HD)
        grad_att_branch = (mid_slots.astype(F32) * att_slot_gate).astype(BF)
        grad_soft = dot("sqhd,skhd->shqk", grad_mixed, values)
        grad_values = dot("shqk,sqhd->skhd", probs_low, grad_mixed)
        grad_scores = (
            probs * (grad_soft - jnp.sum(probs * grad_soft, axis=-1, keepdims=True))
        ).astype(BF)
        grad_queries = dot("shqk,skhd->sqhd", grad_scores, keys) * scale
        grad_keys = dot("shqk,sqhd->skhd", grad_scores, queries) * scale
        grad_qpre = (
            rotate_back(grad_queries, slot_cosine[:, :, None, :], slot_sine[:, :, None, :])
            .astype(BF)
            .reshape(slots, heads_wide)
        )
        att_taken = dot("cm,dm->cd", grad_qpre, my_query)
        grad_kpre = rotate_back(
            grad_keys, cosine[None, :, None, :], sine[None, :, None, :]
        ).reshape(total, heads_wide)
        kv_low = jnp.concatenate([grad_kpre, grad_values.reshape(total, heads_wide)], axis=1)
        kv_low = kv_low.astype(BF)
        first_part = dot("tm,dm->td", kv_low, my_key_value) + att.give(att_taken.astype(BF))
    own_rows = lax.dynamic_slice_in_dim(all_in, exp_at * own_tokens, own_tokens, 0).astype(F32)
    own_scale_in = lax.rsqrt(jnp.mean(own_rows * own_rows, axis=1, keepdims=True) + EPS)
    own_gain_att = lax.dynamic_slice_in_dim(gain_att, layer_at * feats, feats, 0)
    grad_query_w = dot("cd,cm->dm", h1_slots, grad_qpre).astype(BF)
    grad_out_w = dot("cm,cd->md", mixed, grad_att_branch).astype(BF)
    grad_kv_w = dot("td,tm->dm", h1, kv_low).astype(BF)
    grad_first, (first_tokens, mid_tokens), att_told, (grad_out, grad_query, kv_first) = exchanged(
        after(first_part.astype(BF), grad_up),
        None,
        jnp.zeros((own_tokens, feats), F32),
        own_gain_att[None, :] * own_scale_in,
        (att_gate_part.reshape(-1, 128), grad_mid.astype(BF)),
        "tokens",
        [
            ("rows_home", grad_out_w, heads_wide, heads_wide),
            ("columns_home", grad_query_w, heads_wide, 0),
            ("columns_home", grad_kv_w[:, :heads_wide], heads_wide, 0),
        ],
        3,
    )
    att_logit_grads = logit_grads(att_gates, att.token_grads(gate_facts(att_told)))
    own_att_logits = lax.dynamic_slice_in_dim(
        att_logit_grads, exp_at * own_tokens, own_tokens, 0
    )
    own_route_att = lax.dynamic_slice_in_dim(
        route_att.astype(F32), layer_at * feats, feats, 0
    )
    grad_first = grad_first + dot_exact("te,fe->tf", own_att_logits, own_route_att)
    norm_att_part = jnp.sum(grad_first * own_in * own_scale_in, axis=0)
    token_at = group_at * tokens
    rows_in = hidden_in.astype(F32)
    unit_in = lax.rsqrt(jnp.mean(rows_in * rows_in, axis=1, keepdims=True) + EPS)
    first_tokens = first_tokens.astype(F32) + router_rows(
        lax.dynamic_slice_in_dim(att_logit_grads, token_at, tokens, 0), route_att
    ) * (gain_att[None, :] * unit_in)
    unit_in = rows_in * unit_in
    grad_in = (
        mid_tokens.astype(F32)
        + first_tokens
        - unit_in * jnp.mean(first_tokens * unit_in, axis=1, keepdims=True)
    )


    def windows_home(back, axis):
        back = back.reshape(experts, sub, *back.shape[1:])
        parts = [lax.index_in_dim(back, i, 1, keepdims=False) for i in range(sub)]
        parts[1:] = [
            lax.slice_in_dim(part, overlap, part.shape[axis], axis=axis) for part in parts[1:]
        ]
        whole = jnp.concatenate(parts, axis=axis)
        return lax.slice_in_dim(whole, 0, hidden_local, axis=axis).astype(F32)

    def heads_home(back, axis):
        back = back.reshape(experts, head_parts, copies, *back.shape[1:])
        if copies > 1:
            back = jnp.sum(back.astype(F32), axis=2, keepdims=True)
        parts = [back[:, i, 0] for i in range(head_parts)]
        return jnp.concatenate(parts, axis=axis).astype(F32)

    own_h1 = lax.dynamic_slice(h1, own_at, (own_tokens, feats)).astype(F32)
    own_h2 = (own_unit_mid * own_gain_ffn[None, :]).astype(BF).astype(F32)
    own_parts = jnp.concatenate(
        [
            norm_att_part[None],
            norm_ffn_part[None],
            dot_exact("te,tf->ef", own_att_logits, own_h1),
            dot_exact("te,tf->ef", own_ffn_logits, own_h2),
        ],
        axis=0,
    )
    own_parts = jnp.pad(own_parts, ((0, 16 - own_parts.shape[0]), (0, 0)))
    _, (hidden_out,), own_told, (kv_second,) = exchanged(
        after(branch_ffn.astype(BF), first_tokens),
        ffn.put,
        mid,
        jnp.ones((1, feats), F32),
        (own_parts,),
        "tokens",
        [
            ("columns_home", grad_kv_w[:, heads_wide:], heads_wide, heads_wide),
        ],
        4,
    )
    own_told = jnp.sum(own_told, axis=0).transpose(1, 0, 2).reshape(16, width)
    own_told = lax.dynamic_slice_in_dim(own_told, group_at * rows_own, rows_own, 1)
    grad_router_att = own_told[2 : 2 + experts].T
    grad_router_ffn = own_told[2 + experts : 2 + 2 * experts].T
    grad_out = heads_home(grad_out, 1)
    grad_query = heads_home(grad_query, 2)
    grad_key, grad_value = (
        jnp.sum(heads_home(part, 2), axis=0) for part in (kv_first, kv_second)
    )
    return (
        hidden_out,
        grad_in,
        own_told[0],
        grad_router_att,
        grad_query,
        grad_out,
        grad_key,
        grad_value,
        own_told[1],
        grad_router_ffn,
        windows_home(grad_gate, 2),
        windows_home(grad_up, 2),
        windows_home(grad_down, 1),
    )


def solution(mesh):
    ctx, tp = mesh.shape["ctx"], mesh.shape["tp"]
    shard = mesh.shape["shard"]
    by_token, by_feature = P(GROUP, None), P(GROUP)
    columns, rows = P(None, GROUP, "tp"), P(None, "tp", GROUP)

    return jax.shard_map(
        partial(shards, (shard, ctx, tp)),
        mesh=mesh,
        in_specs=(
            by_token,
            by_token,
            by_token,
            P(GROUP),
            by_feature,
            by_token,
            columns,
            rows,
            P(GROUP, "tp"),
            P(GROUP, "tp"),
            by_feature,
            by_token,
            columns,
            columns,
            rows,
            by_token,
        ),
        out_specs=(
            by_token,
            by_token,
            by_feature,
            by_token,
            columns,
            rows,
            P(GROUP, "tp"),
            P(GROUP, "tp"),
            by_feature,
            by_token,
            columns,
            columns,
            rows,
        ),
        check_vma=False,
    )
```

```python
from functools import partial
import math

import numpy as np

import jax
import jax.numpy as jnp
from jax import lax
from jax.experimental import pallas as pl
from jax.experimental.pallas import tpu as pltpu
from jax.sharding import PartitionSpec as P

HD = 128
EPS = 1e-06
BF = jnp.bfloat16
F32 = jnp.float32
MESH = pl.DeviceIdType.MESH
VMEM_BYTES = 40 * 2**20
LOCAL_VMEM_BYTES = 56 * 2**20
GROUP = ("shard", "ctx")
ALL = ("shard", "ctx", "tp")


def dot(spec, left, right):
    return jnp.einsum(spec, left, right, preferred_element_type=F32)


def dot_exact(spec, left, right):
    return jnp.einsum(
        spec, left, right, preferred_element_type=F32, precision=lax.Precision.HIGHEST
    )


def after(value, *others):
    return lax.optimization_barrier((value, *others))[0]


def rope_tables(count):
    half_dim = HD // 2
    freq_index = (jnp.arange(HD) % half_dim).astype(F32)
    frequency = 10000.0 ** (-2.0 * freq_index / HD)
    angles = jnp.arange(count, dtype=F32)[:, None] * frequency[None, :]
    return jnp.cos(angles), jnp.sin(angles)


def rotate(rows, cosine, sine):
    half_dim = HD // 2
    turned = jnp.concatenate([-rows[..., half_dim:], rows[..., :half_dim]], axis=-1)
    return rows * cosine + turned * sine


def rotate_back(rows, cosine, sine):
    half_dim = HD // 2
    turned = rows * sine
    return rows * cosine + jnp.concatenate(
        [turned[..., half_dim:], -turned[..., :half_dim]], axis=-1
    )


class Place:
    def __init__(self, sizes):
        self.experts, self.sub, self.ctx, self.tp = sizes
        self.chips = self.sub * self.tp // 2
        self.members = self.experts * self.sub
        self.group = lax.axis_index(GROUP)
        self.tp_at = lax.axis_index("tp")
        self.exp = self.group // self.sub
        here = (self.group % self.sub) * self.tp + self.tp_at
        self.chip, self.core = here // 2, here % 2

    def device(self, exp, chip, core):
        here = chip * 2 + core
        group = exp * self.sub + here // self.tp
        return (group // self.ctx, group % self.ctx, here % self.tp)

    def member(self, group):
        return (group // self.ctx, group % self.ctx, self.tp_at)

    def sibling(self):
        return self.device(self.exp, self.chip, 1 - self.core)

    def other_exp(self, k):
        return (self.exp + k) % self.experts

    def other_chip(self, k):
        return (self.chip + k) % self.chips

    def meet(self, whole_group):
        barrier = pltpu.get_barrier_semaphore()
        layer = 2 * self.chips
        here = self.chip * 2 + self.core
        others = [(here + k) % layer for k in range(1, layer)]
        peers = [self.device(self.exp, there // 2, there % 2) for there in others]
        if whole_group:
            peers += [
                self.member((self.group + k) % self.members) for k in range(1, self.members)
            ]
        else:
            peers += [
                self.device(self.other_exp(k), self.chip, self.core)
                for k in range(1, self.experts)
            ]
        for peer in peers:
            pl.semaphore_signal(barrier, inc=1, device_id=peer, device_id_type=MESH)
        pl.semaphore_wait(barrier, len(peers))


def block(start, size, unit):
    return pl.ds(pl.multiple_of(start, unit), size)


def send(src, dst, sems, at, device):
    copy = pltpu.make_async_remote_copy(
        src_ref=src,
        dst_ref=dst,
        send_sem=sems.at[(0, *at)],
        recv_sem=sems.at[(1, *at)],
        device_id=device,
        device_id_type=MESH,
    )
    copy.start()
    return copy


class Mover:
    def __init__(self, number, kind, cuts, src, dst, sems, own_sems):
        self.number, self.kind, self.cuts = number, kind, cuts
        self.src, self.dst, self.sems, self.own_sems = src, dst, sems, own_sems
        self.copies = []

    def ends(self, place, group, low, size):
        exp, sub = group // place.sub, group % place.sub
        me, src, dst = place.group, self.src, self.dst
        if self.kind == "columns_out":
            rows, step = src.shape[1], (src.shape[2] - dst.shape[1]) // max(place.sub - 1, 1)
            return (
                src.at[exp, :, block(sub * step + low, size, 128)],
                dst.at[block(me * rows, rows, 16), pl.ds(low, size)],
            )
        if self.kind == "rows_out":
            cols, step = src.shape[2], (src.shape[1] - dst.shape[0]) // max(place.sub - 1, 1)
            return (
                src.at[exp, block(sub * step + low, size, 16)],
                dst.at[pl.ds(low, size), block(me * cols, cols, 128)],
            )
        if self.kind == "columns_home":
            rows = dst.shape[1]
            return (
                src.at[block(group * rows, rows, 16), pl.ds(low, size)],
                dst.at[me, :, pl.ds(low, size)],
            )
        cols = dst.shape[2]
        return (
            src.at[pl.ds(low, size), block(group * cols, cols, 128)],
            dst.at[me, pl.ds(low, size)],
        )

    def start(self, place, late):
        for cut, (low, size, is_late) in enumerate(self.cuts):
            if is_late != late or not size:
                continue
            for k in range(1, place.members):
                group = (place.group + k) % place.members
                src, dst = self.ends(place, group, low, size)
                at = (self.number, cut, k - 1)
                self.copies.append(send(src, dst, self.sems, at, place.member(group)))
            src, dst = self.ends(place, place.group, low, size)
            own = pltpu.make_async_copy(src, dst, self.own_sems.at[self.number, cut])
            own.start()
            self.copies.append(own)

    def wait(self):
        for copy in self.copies:
            copy.wait()


def moved_shape(sizes, kind, array, wide):
    experts, sub, _, _ = sizes
    group = experts * sub
    if kind == "columns_out":
        return (array.shape[1] * group, wide)
    if kind == "rows_out":
        return (wide, array.shape[2] * group)
    if kind == "columns_home":
        return (group, array.shape[0] // group, array.shape[1])
    return (group, array.shape[0], array.shape[1] // group)


class Line:
    def __init__(self, place, spot, sems):
        self.place, self.spot, self.sems = place, spot, sems

    def give(self, src, origin, up, step):
        place = self.place
        to = place.exp + 1 if up else place.exp - 1
        return pltpu.make_async_remote_copy(
            src_ref=src,
            dst_ref=self.spot(origin),
            send_sem=self.sems.at[0, 0 if up else 1, step],
            recv_sem=self.sems.at[1, 0 if up else 1, step],
            device_id=place.device(to, place.chip, place.core),
            device_id_type=MESH,
        )

    def start(self, src):
        place = self.place
        self.src = src

        @pl.when(place.exp < place.experts - 1)
        def _():
            self.give(src, place.exp, True, 0).start()

        @pl.when(place.exp > 0)
        def _():
            self.give(src, place.exp, False, 0).start()

    def origin(self, turn):
        place = self.place
        if place.experts != 4:
            return (place.exp + place.experts - turn) % place.experts
        high = place.exp // 2
        at = place.exp * (1 - high) + (3 - place.exp) * high
        origin = 1 - at if turn == 1 else turn
        return origin * (1 - high) + (3 - origin) * high

    def arrived(self, turn):
        place = self.place
        origin = self.origin(turn)

        @pl.when(origin < place.exp)
        def _():
            step = place.exp - origin - 1
            self.give(self.spot(origin), origin, True, step).wait_recv()

            @pl.when(place.exp < place.experts - 1)
            def _():
                self.give(self.spot(origin), origin, True, step + 1).start()

        @pl.when(origin > place.exp)
        def _():
            step = origin - place.exp - 1
            self.give(self.spot(origin), origin, False, step).wait_recv()

            @pl.when(place.exp > 0)
            def _():
                self.give(self.spot(origin), origin, False, step + 1).start()

        return origin

    def finish(self):
        place = self.place
        for step in range(place.experts - 1):

            @pl.when((place.exp < place.experts - 1) & (place.exp >= step))
            def _():
                self.give(self.src, place.exp, True, step).wait_send()

            @pl.when((place.exp > 0) & (place.exp + step < place.experts))
            def _():
                self.give(self.src, place.exp, False, step).wait_send()


class Spread:
    def __init__(self, place, mine, out, by_token, exp_sems, chip_sems, core_sems, pieces=1):
        self.place, self.mine, self.out, self.by_token = place, mine, out, by_token
        self.rows, self.cols = mine.shape[0] // pieces, mine.shape[1]
        self.pieces = pieces
        self.exp_sems, self.chip_sems, self.core_sems = exp_sems, chip_sems, core_sems
        self.square = place.chips == 4 and place.tp == 4 and self.rows % 64 == 0
        self.line = None
        if pieces == 1 and self.rows % 64 == 0:
            self.line = Line(place, lambda origin: self.spot(origin, place.chip), exp_sems)

    def spot(self, exp, chip, low=0, size=None):
        place = self.place
        here = chip * 2 + place.core
        if self.by_token:
            row = (exp * place.sub + here // place.tp) * self.rows
            col = (here % place.tp) * self.cols
        else:
            row, col = exp * self.rows, here * self.cols
        unit = math.gcd(self.rows, 16)
        size = size or self.rows
        return self.out.at[block(row + low, size, unit), block(col, self.cols, 128)]

    def piece(self, exp):
        if self.pieces == 1:
            return self.mine
        return self.mine.at[block(exp * self.rows, self.rows, 16)]

    def near(self):
        place = self.place
        side = place.chip // 2
        along = place.chip % 2
        return [(1 - side) * 2 + along, side * 2 + 1 - along]

    def to_chip(self, src, dst, turn, k, chip):
        device = self.place.device(self.place.exp, chip, self.place.core)
        self.chip_copies[turn].append(send(src, dst, self.chip_sems, (turn, k), device))

    def to_chips(self, exp, src, turn):
        place = self.place
        if self.square:
            chips = self.near()
        else:
            chips = [place.other_chip(k) for k in range(1, place.chips)]
        for k, chip in enumerate(chips):
            self.to_chip(src, self.spot(exp, place.chip), turn, k, chip)

    def to_core(self, exp, chip, src, turn, k):
        self.core_copies.append(
            send(src, self.spot(exp, chip), self.core_sems, (turn, k), self.place.sibling())
        )

    def start(self, own_sem):
        place = self.place
        home = self.spot(place.exp, place.chip)
        mine = self.piece(place.exp)
        self.own = pltpu.make_async_copy(mine, home, own_sem)
        self.own.start()
        self.chip_copies = [[] for _ in range(place.experts)]
        self.core_copies = []
        if self.line:
            self.line.start(mine)
        else:
            self.exp_copies = [
                send(
                    self.piece(place.other_exp(k)),
                    home,
                    self.exp_sems,
                    (0, k - 1),
                    place.device(place.other_exp(k), place.chip, place.core),
                )
                for k in range(1, place.experts)
            ]
        self.to_chips(place.exp, mine, 0)
        self.to_core(place.exp, place.chip, mine, 0, 0)

    def from_layer(self, turn):
        place = self.place
        if self.line:
            source = self.line.arrived(turn)
        else:
            self.exp_copies[turn - 1].wait_recv()
            source = (place.exp + place.experts - turn) % place.experts
        self.sources[turn] = source
        here = self.spot(source, place.chip)
        self.to_chips(source, here, turn)
        self.to_core(source, place.chip, here, turn, 0)

    def from_near(self, turn):
        source, copies = self.sources[turn], self.chip_copies[turn]
        if not self.square:
            return
        half = self.rows // 2
        side, along = self.near()
        copies[0].wait_recv()
        part = self.spot(source, side, 0, half)
        self.to_chip(part, part, turn, 2, along)
        self.to_core(source, side, self.spot(source, side), turn, 1)
        copies[1].wait_recv()
        part = self.spot(source, along, half, half)
        self.to_chip(part, part, turn, 3, side)
        self.to_core(source, along, self.spot(source, along), turn, 2)

    def from_far(self, turn):
        place = self.place
        source, copies = self.sources[turn], self.chip_copies[turn]
        if self.square:
            copies[2].wait_recv()
            copies[3].wait_recv()
            far = 3 - place.chip
            self.to_core(source, far, self.spot(source, far), turn, 3)
            return
        for k in range(1, place.chips):
            copies[k - 1].wait_recv()
            chip = (place.chip + place.chips - k) % place.chips
            self.to_core(source, chip, self.spot(source, chip), turn, k)

    def run(self):
        for stage in range(self.place.experts + 1):
            self.step(stage)
        self.finish()

    def step(self, stage):
        experts = self.place.experts
        if stage == 0:
            self.sources = {0: self.place.exp}
        if 1 <= stage + 1 < experts:
            self.from_layer(stage + 1)
        if 0 <= stage < experts:
            self.from_near(stage)
        if 0 <= stage - 1 < experts:
            self.from_far(stage - 1)

    def finish(self):
        for copy in self.core_copies:
            copy.wait()
        if self.line:
            self.line.finish()
        else:
            for copy in self.exp_copies:
                copy.wait_send()
        for copies in self.chip_copies:
            for copy in copies:
                copy.wait_send()
        self.own.wait()


class Pair:
    def __init__(self, place, src, out, line_sems, sems, own_sems):
        self.place, self.src, self.out, self.sems, self.own_sems = place, src, out, sems, own_sems
        self.rows = src.shape[1]
        self.half = src.shape[2] // place.sub
        size = self.rows * place.sub

        def spot(exp):
            return out.at[block(exp * size, size, 16)]

        self.line = Line(place, spot, line_sems)

    def start(self):
        place = self.place
        land = block(place.group * self.rows, self.rows, 16)
        sub = place.group % place.sub
        self.copies = []
        for i in range(2):
            dst = self.out.at[land, pl.ds(i * self.half, self.half)]
            for k in range(1, place.sub):
                other = (sub + k) % place.sub
                src = self.src.at[i, :, block(other * self.half, self.half, 128)]
                group = place.exp * place.sub + other
                self.copies.append(send(src, dst, self.sems, (i, k - 1), place.member(group)))
            src = self.src.at[i, :, block(sub * self.half, self.half, 128)]
            own = pltpu.make_async_copy(src, dst, self.own_sems.at[i])
            own.start()
            self.copies.append(own)

    def share(self):
        for copy in self.copies:
            copy.wait()
        self.line.start(self.line.spot(self.place.exp))

    def step(self, stage):
        if stage + 1 < self.place.experts:
            self.line.arrived(stage + 1)

    def finish(self):
        self.line.finish()


class ToTokens:
    def __init__(self, place, mine, out, chip_sems, core_sems):
        self.place, self.mine, self.out = place, mine, out
        self.chip_sems, self.core_sems = chip_sems, core_sems
        self.rows, self.cols = out.shape[0], mine.shape[1]

    def spot(self, chip):
        here = chip * 2 + self.place.core
        return self.out.at[:, block(here * self.cols, self.cols, 128)]

    def part(self, chip):
        sub = (chip * 2) // self.place.tp
        return self.mine.at[block(sub * self.rows, self.rows, 16)]

    def start(self, own_sem):
        place = self.place
        mine = self.part(place.chip)
        self.own = pltpu.make_async_copy(mine, self.spot(place.chip), own_sem)
        self.own.start()
        self.copies = []
        for k in range(1, place.chips):
            chip = place.other_chip(k)
            self.copies.append(
                send(
                    self.part(chip),
                    self.spot(place.chip),
                    self.chip_sems,
                    (k - 1,),
                    place.device(place.exp, chip, place.core),
                )
            )
        self.core = [send(mine, self.spot(place.chip), self.core_sems, (0,), place.sibling())]

    def run(self):
        place, core, copies = self.place, self.core, self.copies
        for k in range(1, place.chips):
            copies[k - 1].wait_recv()
            spot = self.spot((place.chip + place.chips - k) % place.chips)
            core.append(send(spot, spot, self.core_sems, (k,), place.sibling()))
        for copy in core:
            copy.wait()
        for copy in copies:
            copy.wait_send()
        self.own.wait()


class Fold:
    def __init__(self, place, parts, homes, scratch):
        self.place, self.parts, self.homes = place, parts, homes
        (
            self.core_got,
            self.chip_out,
            self.chip_got,
            self.turn_out,
            self.turn_got,
            self.exp_out,
            self.core_sems,
            self.chip_sems,
            self.turn_sems,
            self.exp_sems,
        ) = scratch
        self.each, self.feats = homes[0].shape[1:]
        side, along = place.chip // 2, place.chip % 2
        self.chips = [
            place.chip,
            (1 - side) * 2 + along,
            side * 2 + 1 - along,
            (1 - side) * 2 + 1 - along,
        ]

    def rows(self, chunk):
        return (self.place.exp + 1 + chunk % self.place.experts) % self.place.experts * self.each

    def mine(self, chunk, to, low, size):
        place = self.place
        col = (self.chips[to] * 2 + place.core) * self.feats
        rows = block(self.rows(chunk) + low, size, 16)
        part = self.parts[chunk // place.experts][rows, block(col, self.feats, 128)]
        return part.astype(F32) + self.core_got[chunk, to, low : low + size].astype(F32)

    def between_cores(self, chunk):
        place = self.place
        part = self.parts[chunk // place.experts]
        rows = block(self.rows(chunk), self.each, 16)
        copies = []
        for to in (1, 2, 3, 0):
            col = (self.chips[to] * 2 + 1 - place.core) * self.feats
            src = part.at[rows, block(col, self.feats, 128)]
            dst = self.core_got.at[chunk, to]
            copies.append(send(src, dst, self.core_sems, (chunk, to), place.sibling()))
        return copies

    def over(self, to, src, dst, sems, at):
        place = self.place
        return send(src, dst, sems, at, place.device(place.exp, self.chips[to], place.core))

    def first_hops(self, chunk, core):
        half = self.each // 2
        for copy in core:
            copy.wait_recv()
        copies = []
        for near, low in ((1, 0), (2, half)):
            for slot, to in enumerate((near, 3)):
                at = 2 * (near - 1) + slot
                out = self.chip_out.at[chunk, at]
                out[...] = self.mine(chunk, to, low, half).astype(BF)
                got = self.chip_got.at[chunk, at]
                copies.append(self.over(near, out, got, self.chip_sems, (chunk, at)))
        return copies

    def second_hops(self, chunk, first):
        half = self.each // 2
        copies = []
        for near, far, low in ((1, 2, 0), (2, 1, half)):
            at = 2 * (near - 1)
            first[at].wait_recv()
            first[at + 1].wait_recv()
            out = self.turn_out.at[chunk, near - 1]
            got = self.chip_got[chunk, at + 1].astype(F32)
            out[...] = (self.mine(chunk, far, low, half) + got).astype(BF)
            got = self.turn_got.at[chunk, near - 1]
            copies.append(self.over(far, out, got, self.turn_sems, (chunk, near - 1)))
        return copies

    def go_home(self, chunk, second):
        place = self.place
        half = self.each // 2
        for near, low in ((1, 0), (2, half)):
            second[near - 1].wait_recv()
            total = self.mine(chunk, 0, low, half)
            total = total + self.chip_got[chunk, 2 * (near - 1)].astype(F32)
            total = total + self.turn_got[chunk, near - 1].astype(F32)
            self.exp_out[chunk, low : low + half] = total.astype(BF)
        home = self.homes[chunk // place.experts]
        k = 1 + chunk % place.experts
        if k == place.experts:
            home[place.exp] = self.exp_out[chunk]
            return []
        device = place.device(place.other_exp(k), place.chip, place.core)
        return [
            send(self.exp_out.at[chunk], home.at[place.exp], self.exp_sems, (chunk,), device)
        ]

    def run(self):
        chunks = len(self.parts) * self.place.experts
        core = [self.between_cores(chunk) for chunk in range(chunks)]
        first, second, home = [], [], []
        for stage in range(chunks + 2):
            if stage < chunks:
                first.append(self.first_hops(stage, core[stage]))
            if 0 <= stage - 1 < chunks:
                second.append(self.second_hops(stage - 1, first[stage - 1]))
            if 0 <= stage - 2 < chunks:
                home.append(self.go_home(stage - 2, second[stage - 2]))
        for copies in home:
            for copy in copies:
                copy.wait_recv()
        for copies in (*core, *first, *second, *home):
            for copy in copies:
                copy.wait_send()


def start_kernel(sizes, count, moves, *refs):
    place = Place(sizes)
    blocks, refs = take(refs, count)
    (pair_src,), refs = take(refs, 1)
    sources, refs = take(refs, len(moves))
    outs, refs = take(refs, count)
    (pair_out,), refs = take(refs, 1)
    landings, refs = take(refs, len(moves))
    (own_sems, exp_sems, chip_sems, core_sems), refs = take(refs, 4)
    pair_sems, refs = take(refs, 3)
    movers = make_movers(moves, sources, landings, refs)
    pair = Pair(place, pair_src, pair_out, *pair_sems)
    spreads = []
    for i, (rows, out) in enumerate(zip(blocks, outs)):
        quarter = rows.shape[1] // place.tp
        mine = rows.at[:, block(place.tp_at * quarter, quarter, 128)]
        sems = (s.at[i] for s in (exp_sems, chip_sems, core_sems))
        spreads.append(Spread(place, mine, out, True, *sems))
    place.meet(True)
    pair.start()
    for i, spread in enumerate(spreads[:-1]):
        spread.start(own_sems.at[i])
    pair.share()
    for mover in movers:
        mover.start(place, False)
    spreads[-1].start(own_sems.at[count - 1])
    for mover in movers:
        mover.start(place, True)
    for stage in range(place.experts + 2):
        for runner in (*spreads[:-1], pair):
            if stage <= place.experts:
                runner.step(stage)
        if stage:
            spreads[-1].step(stage - 1)
    for runner in (*spreads, pair):
        runner.finish()
    for mover in movers:
        mover.wait()


def take(refs, count):
    return refs[:count], refs[count:]


def turned(left, right):
    return lax.dot_general(left, right, (((0,), (0,)), ((), ())), preferred_element_type=F32)


def row_sums(weights, rows):
    return lax.dot_general(
        weights,
        rows,
        (((1,), (1,)), ((), ())),
        preferred_element_type=F32,
        precision=lax.Precision.HIGHEST,
    )


def make_movers(moves, sources, landings, sems):
    return [
        Mover(i, kind, cuts, source, landing, *sems)
        for i, ((kind, cuts), source, landing) in enumerate(zip(moves, sources, landings))
    ]


def exchange_kernel(sizes, tail, count, extras, moves, *refs):
    place = Place(sizes)
    parts, refs = take(refs, count)
    adds, refs = take(refs, count)
    (put, scale), refs = take(refs, 2)
    if tail == "slots":
        (next_put, linear, square), refs = take(refs, 3)
    elif tail == "tokens":
        (facts, unit, *more), refs = take(refs, extras)
    else:
        (facts,), refs = take(refs, extras)
    sources, refs = take(refs, len(moves))
    raws, refs = take(refs, count)
    (all_facts,), refs = take(refs, 1)
    if tail == "tokens":
        (all_sums,), refs = take(refs, 1)
    outs, refs = take(refs, {"slots": 1, "tokens": extras - 1, None: 0}[tail])
    landings, refs = take(refs, len(moves))
    homes, refs = take(refs, count)
    (own_sems,), refs = take(refs, 1)
    fact_sems, refs = take(refs, 3)
    fold_scratch, refs = take(refs, 10)
    if tail == "slots":
        (picked, facts), refs = take(refs, 2)
        tail_sems, refs = take(refs, 3)
    elif tail == "tokens":
        (mine, sums), refs = take(refs, 2)
        sum_sems, refs = take(refs, 3)
        tail_sems, refs = take(refs, 2 * extras - 2)
    movers = make_movers(moves, sources, landings, refs)
    place.meet(bool(moves))
    told = Spread(place, facts, all_facts, False, *fact_sems)
    if tail != "slots":
        told.start(own_sems.at[0])
    to_tokens = []
    if tail == "tokens":
        for i, rows in enumerate(more):
            to_tokens.append(
                ToTokens(place, rows, outs[1 + i], *tail_sems[2 + 2 * i : 4 + 2 * i])
            )
            to_tokens[-1].start(own_sems.at[2 + i])
    for mover in movers:
        mover.start(place, False)
    Fold(place, parts, homes, fold_scratch).run()
    for i in reversed(range(count)):
        if put.shape[1] == 128:
            summed = jnp.sum(homes[i][...].astype(F32), axis=0)
        else:
            rows = homes[i][...].reshape(-1, homes[i].shape[2])
            summed = jnp.dot(put[...], rows, preferred_element_type=F32)
        value = adds[i][...] + summed
        raws[i][...] = value
    if tail == "slots":
        picked[...] = turned(next_put[...], value.astype(BF)).astype(BF)
        slots = Spread(place, picked, outs[0], False, *tail_sems, pieces=place.experts)
        slots.start(own_sems.at[1])
        facts[...] = row_sums(linear[...], value) + row_sums(square[...], value * value)
        told.start(own_sems.at[0])
    elif tail == "tokens":
        mine[...] = (value * scale[...]).astype(BF)
        to_tokens.append(ToTokens(place, mine, outs[0], *tail_sems[:2]))
        to_tokens[-1].start(own_sems.at[1])
        columns = jnp.sum(value * unit[...], axis=0, keepdims=True)
        sums[...] = jnp.broadcast_to(columns, sums.shape)
        summed = Spread(place, sums, all_sums, False, *sum_sems)
        summed.start(own_sems.at[extras])
    for mover in movers:
        mover.start(place, True)
    if tail == "slots":
        slots.run()
    for rows in to_tokens:
        rows.run()
    told.run()
    if tail == "tokens":
        summed.run()
    for mover in movers:
        mover.wait()


def finish_kernel(sizes, moves, *refs):
    place = Place(sizes)
    (plus, product, unit, next_put), refs = take(refs, 4)
    sources, refs = take(refs, len(moves))
    (raw, out), refs = take(refs, 2)
    landings, refs = take(refs, len(moves))
    (sums, got, picked, own_sem, sum_sems), refs = take(refs, 5)
    tail_sems, refs = take(refs, 3)
    movers = make_movers(moves, sources, landings, refs)
    sums[...] = row_sums(jnp.ones((8, product.shape[1]), F32), product[...])
    place.meet(bool(moves))
    layer = place.chips * 2
    here = place.chip * 2 + place.core
    copies = []
    for k in range(1, layer):
        there = (here + k) % layer
        device = place.device(place.exp, there // 2, there % 2)
        copies.append(send(sums, got.at[k - 1], sum_sems, (k - 1,), device))
    for mover in movers:
        mover.start(place, False)
    total = sums[...]
    for k in range(1, layer):
        copies[k - 1].wait_recv()
        total = total + got[k - 1]
    mean = total.T[:, :1] * (1.0 / (layer * product.shape[1]))
    value = plus[...] - unit[...] * mean
    raw[...] = value
    picked[...] = turned(next_put[...], value.astype(BF)).astype(BF)
    slots = Spread(place, picked, out, False, *tail_sems, pieces=place.experts)
    slots.start(own_sem)
    for mover in movers:
        mover.start(place, True)
    slots.run()
    for copy in copies:
        copy.wait_send()
    for mover in movers:
        mover.wait()


def dma_sems(*shape):
    return pltpu.SemaphoreType.DMA(shape)


def move_scratch(sizes, moves):
    most = max(len(cuts) for _, cuts, _, _ in moves)
    members = sizes[0] * sizes[1]
    return [dma_sems(2, len(moves), most, members - 1), dma_sems(len(moves), most)]


def start(sizes, arrays, pair, moves, number):
    experts, sub, _, tp = sizes
    count = len(arrays)
    exp_sems, chip_sems, core_sems = (
        dma_sems(count, *shape) for shape in spread_shapes(sizes)
    )
    anywhere = pl.BlockSpec(memory_space=pl.ANY)
    total = count + 1 + len(moves)
    results = pl.pallas_call(
        partial(start_kernel, sizes, count, [(kind, cuts) for kind, cuts, _, _ in moves]),
        out_shape=[
            *[
                jax.ShapeDtypeStruct((rows.shape[0] * experts * sub, rows.shape[1]), rows.dtype)
                for rows in arrays
            ],
            jax.ShapeDtypeStruct((pair.shape[1] * experts * sub, 2 * pair.shape[2] // sub), BF),
            *landing_shapes(sizes, moves),
        ],
        in_specs=[anywhere] * total,
        out_specs=[anywhere] * total,
        scratch_shapes=[
            dma_sems(count),
            exp_sems,
            chip_sems,
            core_sems,
            dma_sems(2, 2, experts - 1),
            dma_sems(2, 2, sub - 1),
            dma_sems(2),
            *move_scratch(sizes, moves),
        ],
        compiler_params=pltpu.CompilerParams(
            collective_id=number, has_side_effects=True, vmem_limit_bytes=VMEM_BYTES
        ),
        name=f"start_{number}",
    )(*arrays, pair, *[array for _, _, array, _ in moves])
    return results[:count], results[count], results[count + 1 :]


def landing_shapes(sizes, moves):
    return [
        jax.ShapeDtypeStruct(moved_shape(sizes, kind, array, wide), BF)
        for kind, _, array, wide in moves
    ]


def spread_shapes(sizes):
    experts, sub, _, tp = sizes
    chips = sub * tp // 2
    return (2, 2, experts - 1), (2, experts, chips), (2, experts, chips)


def spread_sems(sizes):
    return [dma_sems(*shape) for shape in spread_shapes(sizes)]


def fact_shapes(sizes, shape):
    experts, sub, _, tp = sizes
    return jax.ShapeDtypeStruct((shape[0] * experts, shape[1] * sub * tp), F32)


def by_device(sizes, all_facts, shape):
    experts, sub, _, tp = sizes
    return all_facts.reshape(experts, shape[0], sub * tp, shape[1]).transpose(0, 2, 1, 3)


def exchange(sizes, parts, adds, put, scale, extra, tail, moves, number):
    experts, sub, ctx, tp = sizes
    chips = sub * tp // 2
    count = len(parts)
    rows, width = parts[0].shape
    tokens, feats = adds[0].shape
    each, chunks = rows // experts, count * experts
    vmem, anywhere = (pl.BlockSpec(memory_space=m) for m in (pltpu.VMEM, pl.ANY))
    if put is None:
        put = jnp.zeros((8, 128), BF)
    fact_shape = (8, tokens) if tail == "slots" else extra[0].shape
    outs, scratch, extra_specs = [], [], [vmem] * len(extra)
    if tail == "slots":
        picks = extra[0].shape[1]
        outs = [jax.ShapeDtypeStruct((picks, width), BF)]
        scratch = [pltpu.VMEM((picks, feats), BF), pltpu.VMEM(fact_shape, F32)]
        scratch += spread_sems(sizes)
    elif tail == "tokens":
        outs = [fact_shapes(sizes, (8, feats))]
        outs += [jax.ShapeDtypeStruct((tokens // sub, width), BF)] * (len(extra) - 1)
        scratch = [pltpu.VMEM((tokens, feats), BF), pltpu.VMEM((8, feats), F32)]
        scratch += spread_sems(sizes)
        scratch += [dma_sems(2, chips - 1), dma_sems(2, chips)] * (len(extra) - 1)
    if tail != "slots":
        extra_specs[0] = anywhere
    results = pl.pallas_call(
        partial(
            exchange_kernel,
            sizes,
            tail,
            count,
            len(extra),
            [(kind, cuts) for kind, cuts, _, _ in moves],
        ),
        out_shape=[
            *[jax.ShapeDtypeStruct((tokens, feats), F32)] * count,
            fact_shapes(sizes, fact_shape),
            *outs,
            *landing_shapes(sizes, moves),
        ],
        in_specs=[vmem] * (2 * count + 2) + extra_specs + [anywhere] * len(moves),
        out_specs=[vmem] * count + [anywhere] * (1 + len(outs) + len(moves)),
        scratch_shapes=[
            *[pltpu.VMEM((experts, each, feats), BF)] * count,
            dma_sems(1 + max(len(extra), 2)),
            *spread_sems(sizes),
            pltpu.VMEM((chunks, 4, each, feats), BF),
            pltpu.VMEM((chunks, 4, each // 2, feats), BF),
            pltpu.VMEM((chunks, 4, each // 2, feats), BF),
            pltpu.VMEM((chunks, 2, each // 2, feats), BF),
            pltpu.VMEM((chunks, 2, each // 2, feats), BF),
            pltpu.VMEM((chunks, each, feats), BF),
            dma_sems(2, chunks, 4),
            dma_sems(2, chunks, 4),
            dma_sems(2, chunks, 2),
            dma_sems(2, chunks),
            *scratch,
            *move_scratch(sizes, moves),
        ],
        compiler_params=pltpu.CompilerParams(
            collective_id=number, has_side_effects=True, vmem_limit_bytes=VMEM_BYTES
        ),
        name=f"exchange_{number}",
    )(*parts, *adds, put, scale, *extra, *[array for _, _, array, _ in moves])
    raws, (all_facts, *results) = results[:count], results[count:]
    outs, moved = results[: len(outs)], results[len(outs) :]
    return raws, outs, by_device(sizes, all_facts, fact_shape), moved


def finish(sizes, plus, product, unit, next_put, moves, number):
    experts, sub, ctx, tp = sizes
    layer = sub * tp
    tokens, feats = plus.shape
    picks = next_put.shape[1]
    vmem, anywhere = (pl.BlockSpec(memory_space=m) for m in (pltpu.VMEM, pl.ANY))
    raw, out, *moved = pl.pallas_call(
        partial(finish_kernel, sizes, [(kind, cuts) for kind, cuts, _, _ in moves]),
        out_shape=[
            jax.ShapeDtypeStruct((tokens, feats), F32),
            jax.ShapeDtypeStruct((picks, feats * layer), BF),
            *landing_shapes(sizes, moves),
        ],
        in_specs=[vmem] * 4 + [anywhere] * len(moves),
        out_specs=[vmem] + [anywhere] * (1 + len(moves)),
        scratch_shapes=[
            pltpu.VMEM((8, tokens), F32),
            pltpu.VMEM((layer - 1, 8, tokens), F32),
            pltpu.VMEM((picks, feats), BF),
            pltpu.SemaphoreType.DMA,
            dma_sems(2, layer - 1),
            *spread_sems(sizes),
            *move_scratch(sizes, moves),
        ],
        compiler_params=pltpu.CompilerParams(
            collective_id=number, has_side_effects=True, vmem_limit_bytes=VMEM_BYTES
        ),
        name=f"finish_{number}",
    )(plus, product, unit, next_put, *[array for _, _, array, _ in moves])
    return raw, out, moved


def parted(pick, table):
    total = None
    for _ in range(3):
        part = table.astype(BF)
        product = jnp.dot(pick, part, preferred_element_type=F32)
        total = product if total is None else total + product
        table = table - part.astype(F32)
    return total


def times(left, right):
    return jnp.dot(left, right, preferred_element_type=F32)


def times_turned(left, right):
    return lax.dot_general(left, right, (((1,), (1,)), ((), ())), preferred_element_type=F32)


def one_hot(places, shape, axis):
    return (lax.broadcasted_iota(jnp.int32, shape, axis).astype(F32) == places).astype(BF)


def allowed_keys(position, span, spans):
    shape = (position.shape[0], spans.shape[1])
    keys = lax.broadcasted_iota(jnp.int32, shape, 1).astype(F32)
    return (keys <= position) | ((span == spans) & (span > 0))


def softmax_rows(scores, allowed):
    scores = jnp.where(allowed, scores, -1e30)
    expo = jnp.exp(scores - jnp.max(scores, axis=-1, keepdims=True))
    return expo / jnp.sum(expo, axis=-1, keepdims=True)


def head_columns(head):
    return pl.ds(head * HD, HD)


def turn_heads(rows, cosine, sine):
    parts = []
    for head in range(rows.shape[1] // HD):
        u = rows[:, head * HD : (head + 1) * HD]
        parts.append(u * cosine + pltpu.roll(u, HD // 2, 1) * sine)
    return jnp.concatenate(parts, axis=1)


def turn_heads_back(rows, cosine, sine):
    parts = []
    for head in range(rows.shape[1] // HD):
        u = rows[:, head * HD : (head + 1) * HD]
        parts.append(u * cosine + pltpu.roll(u * sine, HD // 2, 1))
    return jnp.concatenate(parts, axis=1)


def attend_kernel(
    experts,
    x_ref,
    gain_ref,
    query_ref,
    key_value_ref,
    route_ref,
    rows_ref,
    hits_ref,
    cosine_ref,
    sine_ref,
    mine_ref,
    h1_ref,
    slots_ref,
    queries_ref,
    keys_ref,
    values_ref,
    mixed_ref,
    gates_ref,
    tables_ref,
):
    seq_len = x_ref.shape[0]
    cap = slots_ref.shape[0]
    wide = query_ref.shape[1]
    x = x_ref[...].astype(F32)
    scale_in = lax.rsqrt(jnp.mean(x * x, axis=1, keepdims=True) + EPS)
    h1 = (x * scale_in * gain_ref[...]).astype(BF)
    h1_ref[...] = h1
    cosine, sine = cosine_ref[...], sine_ref[...]
    kv = times(h1, key_value_ref[...])
    keys_ref[...] = turn_heads(kv[:, :wide], cosine, sine).astype(BF)
    values_ref[...] = kv[:, wide:].astype(BF)
    logits = times(h1, route_ref[...])
    hits = hits_ref[...]
    lane = lax.broadcasted_iota(jnp.int32, hits.shape, 1)
    chosen = (hits > 0) & (lane < experts)
    top = jnp.max(jnp.where(chosen, logits, -1e30), axis=1, keepdims=True)
    raised = jnp.where(chosen, jnp.exp(jnp.minimum(logits - top, 0.0)), 0.0)
    gates = raised / jnp.sum(raised, axis=1, keepdims=True)
    gates_ref[...] = gates
    pick = one_hot(rows_ref[0, 0:1], (cap, seq_len), 0)
    slots = times(pick, h1).astype(BF)
    slots_ref[...] = slots
    row = lax.broadcasted_iota(jnp.int32, hits.shape, 0).astype(F32)
    gate_mine = jnp.sum(gates * mine_ref[...], axis=1, keepdims=True)
    facts = jnp.where(lane == 0, gate_mine, jnp.where(lane == 1, row, hits))
    tables = parted(pick, jnp.concatenate([cosine, sine, facts], axis=1))
    tables_ref[...] = tables
    queries = turn_heads(times(slots, query_ref[...]), tables[:, :HD], tables[:, HD : 2 * HD])
    queries_ref[...] = queries.astype(BF)
    at = 2 * HD
    allowed = allowed_keys(
        tables[:, at + 1 : at + 2], tables[:, at + experts : at + experts + 1], rows_ref[0, 1:2]
    )
    for head in range(wide // HD):
        part = head_columns(head)
        scores = times_turned(queries_ref[:, part], keys_ref[:, part]) * HD**-0.5
        probs = softmax_rows(scores, allowed).astype(BF)
        mixed_ref[:, part] = times(probs, values_ref[:, part]).astype(BF)


def attend(experts, seqs, x, gain, query, key_value, route, rows, hits, cosine, sine, mine):
    total, width = x.shape
    seq_len = total // seqs
    cap = 2 * seq_len // experts
    wide = query.shape[1]

    def each(*shape):
        zeros = (0,) * (len(shape) - 1)
        return pl.BlockSpec(shape, lambda s: (s, *zeros))

    def whole(array):
        zeros = (0,) * array.ndim
        return pl.BlockSpec(array.shape, lambda s: zeros)

    def out(rows, columns, dtype):
        return jax.ShapeDtypeStruct((seqs * rows, columns), dtype)

    return pl.pallas_call(
        partial(attend_kernel, experts),
        grid=(seqs,),
        in_specs=[
            each(seq_len, width),
            whole(gain),
            whole(query),
            whole(key_value),
            whole(route),
            each(1, 8, seq_len),
            each(seq_len, HD),
            whole(cosine),
            whole(sine),
            whole(mine),
        ],
        out_specs=[
            each(seq_len, width),
            each(cap, width),
            each(cap, wide),
            each(seq_len, wide),
            each(seq_len, wide),
            each(cap, wide),
            each(seq_len, HD),
            each(cap, 3 * HD),
        ],
        out_shape=[
            out(seq_len, width, BF),
            out(cap, width, BF),
            out(cap, wide, BF),
            out(seq_len, wide, BF),
            out(seq_len, wide, BF),
            out(cap, wide, BF),
            out(seq_len, HD, F32),
            out(cap, 3 * HD, F32),
        ],
        compiler_params=pltpu.CompilerParams(vmem_limit_bytes=LOCAL_VMEM_BYTES),
        cost_estimate=pl.CostEstimate(
            flops=2 * total * width * (3 * wide + seq_len // 2),
            bytes_accessed=6 * total * width,
            transcendentals=total * seq_len,
        ),
        name="attend",
    )(x, gain, query, key_value, route, rows, hits, cosine, sine, mine)


def attend_back_kernel(
    experts,
    grad_ref,
    out_ref,
    query_ref,
    key_value_ref,
    rows_ref,
    hits_ref,
    cosine_ref,
    sine_ref,
    queries_ref,
    keys_ref,
    values_ref,
    mixed_ref,
    tables_ref,
    grad_query_ref,
    grad_kv_ref,
    grad_branch_ref,
    gate_ref,
    first_ref,
):
    seq_len, wide = keys_ref.shape
    cap = queries_ref.shape[0]
    tables = tables_ref[...]
    at = 2 * HD
    gate = tables[:, at : at + 1]
    allowed = allowed_keys(
        tables[:, at + 1 : at + 2], tables[:, at + experts : at + experts + 1], rows_ref[0, 1:2]
    )
    grad = grad_ref[...]
    grad_branch_ref[...] = (grad.astype(F32) * gate).astype(BF)
    grad_mixed = times_turned(grad, out_ref[...])
    gates = jnp.sum(mixed_ref[...].astype(F32) * grad_mixed, axis=1, keepdims=True)
    gate_ref[...] = jnp.broadcast_to(gates, gate_ref.shape)
    grad_mixed = (grad_mixed * gate).astype(BF)
    grad_queries, grad_keys, grad_values = [], [], []
    for head in range(wide // HD):
        part = head_columns(head)
        queries, keys = queries_ref[:, part], keys_ref[:, part]
        own = grad_mixed[:, head * HD : (head + 1) * HD]
        probs = softmax_rows(times_turned(queries, keys) * HD**-0.5, allowed)
        grad_probs = times_turned(own, values_ref[:, part])
        grad_values.append(turned(probs.astype(BF), own))
        inner = jnp.sum(probs * grad_probs, axis=1, keepdims=True)
        grad_scores = (probs * (grad_probs - inner)).astype(BF)
        grad_queries.append(times(grad_scores, keys) * HD**-0.5)
        grad_keys.append(turned(grad_scores, queries) * HD**-0.5)
    grad_queries = jnp.concatenate(grad_queries, axis=1)
    grad_qpre = turn_heads_back(grad_queries, tables[:, :HD], tables[:, HD : 2 * HD]).astype(BF)
    grad_query_ref[...] = grad_qpre
    grad_keys = turn_heads_back(
        jnp.concatenate(grad_keys, axis=1), cosine_ref[...], sine_ref[...]
    )
    kv_low = jnp.concatenate([grad_keys, *grad_values], axis=1).astype(BF)
    grad_kv_ref[...] = kv_low
    taken = times_turned(grad_qpre, query_ref[...]).astype(BF)
    give = one_hot(hits_ref[:, experts + 1 : experts + 2], (seq_len, cap), 1)
    first = times_turned(kv_low, key_value_ref[...]) + times(give, taken)
    first_ref[...] = first.astype(BF)


def attend_back(
    experts, seqs, grad, out, query, key_value, rows, hits, cosine, sine, saved
):
    queries, keys, values, mixed, tables = saved
    width = grad.shape[1]
    cap = grad.shape[0] // seqs
    total, wide = keys.shape
    seq_len = total // seqs

    def each(*shape):
        zeros = (0,) * (len(shape) - 1)
        return pl.BlockSpec(shape, lambda s: (s, *zeros))

    def whole(array):
        zeros = (0,) * array.ndim
        return pl.BlockSpec(array.shape, lambda s: zeros)

    def result(rows, columns, dtype):
        return jax.ShapeDtypeStruct((seqs * rows, columns), dtype)

    return pl.pallas_call(
        partial(attend_back_kernel, experts),
        grid=(seqs,),
        in_specs=[
            each(cap, width),
            whole(out),
            whole(query),
            whole(key_value),
            each(1, 8, seq_len),
            each(seq_len, HD),
            whole(cosine),
            whole(sine),
            each(cap, wide),
            each(seq_len, wide),
            each(seq_len, wide),
            each(cap, wide),
            each(cap, 3 * HD),
        ],
        out_specs=[
            each(cap, wide),
            each(seq_len, 2 * wide),
            each(cap, width),
            each(cap, HD),
            each(seq_len, width),
        ],
        out_shape=[
            result(cap, wide, BF),
            result(seq_len, 2 * wide, BF),
            result(cap, width, BF),
            result(cap, HD, F32),
            result(seq_len, width, BF),
        ],
        compiler_params=pltpu.CompilerParams(vmem_limit_bytes=LOCAL_VMEM_BYTES),
        cost_estimate=pl.CostEstimate(
            flops=2 * total * width * (3 * wide + seq_len // 2),
            bytes_accessed=6 * total * width,
            transcendentals=total * seq_len,
        ),
        name="attend_back",
    )(
        grad, out, query, key_value, rows, hits, cosine, sine, queries, keys, values, mixed, tables
    )


class Axes:
    def __init__(self, experts, shard, ctx, tp):
        self.experts = experts
        self.sub = shard * ctx // experts
        self.tp = tp
        if self.sub == ctx:
            self.layer, self.exp = (("ctx", "tp"), None), ("shard", None)
            self.part = ("ctx", None)
        else:
            devices = np.arange(shard * ctx * tp).reshape(experts, self.sub, tp)
            self.layer = (ALL, devices.reshape(experts, -1).tolist())
            self.exp = (ALL, devices.reshape(experts, -1).T.tolist())
            self.part = (ALL, devices.transpose(0, 2, 1).reshape(-1, self.sub).tolist())

    def swap(self, value, over):
        axes, groups = over
        return lax.all_to_all(value, axes, 0, 0, axis_index_groups=groups)


class Routing:
    def __init__(self, choice, seqs, seq_len, experts, cap, mine, own_first, own_seqs):
        columns = jnp.arange(experts, dtype=jnp.int32)
        hits = jnp.sum((choice[:, :, None] == columns[None, None, :]).astype(F32), axis=1)
        self.hits = hits.reshape(seqs, seq_len, experts)
        rows = jnp.arange(seq_len, dtype=jnp.int32)
        earlier = (rows[None, :] < rows[:, None]).astype(BF)
        before = dot("tu,sue->ste", earlier, self.hits.astype(BF))
        self.valid = self.hits * (before < cap).astype(F32)
        self.place = jnp.where(self.valid > 0, before, -1.0)
        self.cap = cap
        is_mine = (columns == mine).astype(F32)
        place_mine = jnp.sum(self.place * is_mine, axis=2)
        self.place_mine = place_mine
        slots = jnp.arange(cap, dtype=jnp.int32).astype(F32)
        self.is_mine = is_mine
        self.pick = (place_mine[:, None, :] == slots[None, :, None]).astype(BF)
        place_own = lax.dynamic_slice_in_dim(self.place, own_first, own_seqs, 0)
        place_own = place_own.transpose(1, 0, 2)[:, :, :, None]
        seq_of = jnp.arange(own_seqs, dtype=jnp.int32)
        here = place_own == slots
        same = (seq_of[:, None] == seq_of[None, :])[:, None, None, :, None]
        put = here.transpose(1, 0, 2, 3)[:, :, :, None, :] & same
        self.put = put.astype(BF).reshape(own_seqs * seq_len, experts * own_seqs * cap)

    def gates(self, logits):
        logits = logits.reshape(self.hits.shape)
        top = jnp.max(jnp.where(self.hits > 0, logits, -jnp.inf), axis=2, keepdims=True)
        raised = jnp.where(self.hits > 0, jnp.exp(logits - top), 0.0)
        return raised / jnp.sum(raised, axis=2, keepdims=True)

    def slot_gates(self, gates):
        gate_mine = jnp.sum(gates * self.is_mine, axis=2)
        return jnp.sum(self.pick.astype(F32) * gate_mine[:, None, :], axis=2)

    def take(self, rows):
        seqs, cap, seq_len = self.pick.shape
        picked = dot("spt,stf->spf", self.pick, rows.reshape(seqs, seq_len, -1))
        return picked.astype(BF).reshape(seqs * cap, -1)

    def give(self, slots):
        seqs, cap, seq_len = self.pick.shape
        rows = dot("spt,spf->stf", self.pick, slots.reshape(seqs, cap, -1))
        return rows.reshape(seqs * seq_len, -1)

    def token_grads(self, slot_grads):
        slots = jnp.arange(self.cap, dtype=jnp.int32).astype(F32)
        here = self.place[:, :, :, None] == slots[None, None, None, :]
        grads = slot_grads.transpose(1, 0, 2)[:, None, :, :]
        return jnp.sum(jnp.where(here, grads, 0.0), axis=3)


def put_home(put, home):
    return dot("tp,pf->tf", put, home.reshape(-1, home.shape[-1]))


def router_rows(grads, router):
    high = grads.astype(BF)
    low = (grads - high.astype(F32)).astype(BF)
    return dot(
        "te,fe->tf",
        jnp.concatenate([high, low], axis=1),
        jnp.concatenate([router, router], axis=1),
    )


def logit_grads(gates, gate_grads):
    mean = jnp.sum(gates * gate_grads, axis=2, keepdims=True)
    grads = gates * (gate_grads - mean)
    return grads.reshape(-1, grads.shape[-1])


def shards(
    sizes,
    hidden_in,
    att_choice,
    ffn_choice,
    span_ids,
    norm_att,
    router_att,
    w_query,
    w_out,
    w_key,
    w_value,
    norm_ffn,
    router_ffn,
    w_gate,
    w_up,
    w_down,
    cotangent,
):
    shard, ctx, tp = sizes
    experts = w_query.shape[0]
    axes = Axes(experts, shard, ctx, tp)
    sub = axes.sub
    group = experts * sub
    layer = sub * tp
    tokens, width = hidden_in.shape
    total = tokens * group
    seq_len = tokens * ctx
    seqs = total // seq_len
    own_seqs = seqs // experts
    own_tokens = own_seqs * seq_len
    cap = 2 * seq_len // experts
    slots = seqs * cap
    rows_own = width // group
    feats = width // layer
    sizes = (experts, sub, ctx, tp)
    kernels = feats % 128 == 0 and rows_own % 128 == 0 and tokens % 16 == 0
    group_at, tp_at = lax.axis_index(GROUP), lax.axis_index("tp")
    exp_at, sub_at = group_at // sub, group_at % sub
    layer_at = sub_at * tp + tp_at

    token_pack = jnp.concatenate(
        [att_choice, ffn_choice, span_ids[:, None]], axis=1
    ).astype(BF)
    feature_pack = jnp.concatenate(
        [norm_att[:, None], router_att, norm_ffn[:, None], router_ffn], axis=1
    )
    def everywhere(rows):
        quarter = width // tp
        part = lax.dynamic_slice_in_dim(rows, tp_at * quarter, quarter, 1)
        parts = lax.all_gather(part, ALL)
        return parts.reshape(group, tp, tokens, quarter).transpose(0, 2, 1, 3).reshape(total, width)

    def everywhere_layer(rows):
        parts = lax.all_gather(rows, ALL)
        return (
            parts.reshape(experts, layer, own_tokens, feats)
            .transpose(0, 2, 1, 3)
            .reshape(total, width)
        )

    def layer_sum(rows):
        m = rows.shape[0]
        parts = rows.astype(BF).reshape(m, layer, feats).transpose(1, 0, 2)
        parts = axes.swap(parts, axes.layer)
        return jnp.sum(parts.astype(F32), axis=0)

    def go_home(rows):
        return axes.swap(rows.astype(BF).reshape(experts, -1, feats), axes.exp)

    def to_tokens(rows):
        parts = axes.swap(rows.reshape(sub, tokens, feats), axes.part)
        parts = lax.all_gather(parts, "tp")
        return parts.transpose(2, 1, 0, 3).reshape(tokens, width)

    head_parts = math.gcd(sub, w_query.shape[2] // HD)
    copies = sub // head_parts
    heads_wide = w_query.shape[2] // head_parts
    hidden_local = w_gate.shape[2]
    hidden_wide = -(-hidden_local // (sub * 128)) * 128
    windows = sub == 2 and (hidden_local - hidden_wide) % 128 == 0
    hidden_pad = 0 if windows else hidden_wide * sub - hidden_local
    overlap = hidden_wide * sub - hidden_local if windows else 0
    hidden_rows = hidden_local // sub if windows else hidden_wide
    hidden_first = sub_at * (overlap // 2)
    hidden_at = jnp.arange(hidden_wide)
    hidden_mine = (hidden_at >= hidden_first) & (hidden_at < hidden_first + hidden_rows)
    kernels = kernels and windows and copies == 1 and sub == 2 and tp == 4 and experts == 4

    def to_windows(weight, axis):
        if windows:
            size = weight.shape[axis]
            parts = [
                lax.slice_in_dim(weight, 0, hidden_wide, axis=axis),
                lax.slice_in_dim(weight, size - hidden_wide, size, axis=axis),
            ]
        else:
            pad = [(0, 0)] * 3
            pad[axis] = (0, hidden_pad)
            parts = jnp.split(jnp.pad(weight, pad), sub, axis=axis)
        parts = jnp.stack(parts, axis=1)
        return parts.reshape(group, *parts.shape[2:])

    def to_heads(weight, axis):
        parts = jnp.stack(jnp.split(weight, head_parts, axis=axis), axis=1)
        return jnp.repeat(parts, copies, axis=1).reshape(group, *parts.shape[2:])

    def to_all(weight):
        return to_heads(jnp.broadcast_to(weight, (experts, *weight.shape)), 2)

    def swap_group(value):
        return lax.all_to_all(value, GROUP, 0, 0)

    def as_columns(parts):
        return parts.reshape(width, parts.shape[2])

    def as_rows(parts):
        return parts.transpose(1, 0, 2).reshape(parts.shape[1], width)

    pack = jnp.concatenate(
        [jnp.pad(facts.T, ((0, 16 - facts.shape[1]), (0, 0))) for facts in (token_pack, feature_pack)],
        axis=1,
    )
    if kernels:
        (packs, all_in, top_all), my_key_value, (my_query, my_out) = start(
            sizes,
            [pack, hidden_in, cotangent],
            jnp.stack([w_key, w_value]),
            [
                ("columns_out", ((0, heads_wide, False),), w_query, heads_wide),
                ("rows_out", ((0, heads_wide, True),), w_out, heads_wide),
            ],
            0,
        )
        packs = packs.reshape(group, 16, -1)
    else:
        packs = lax.all_gather(pack, GROUP)
        all_in, top_all = everywhere(hidden_in), everywhere(cotangent)
        first = [to_heads(w_query, 2), to_all(w_key), to_all(w_value), to_heads(w_out, 1)]
        first = swap_group(jnp.concatenate(first, axis=2))
        my_query = as_columns(first[:, :, :heads_wide])
        my_key_value = as_columns(first[:, :, heads_wide : 3 * heads_wide])
        my_out = as_rows(first[:, :, 3 * heads_wide :])
    packs = packs.transpose(0, 2, 1)
    token_facts = packs[:, :tokens].reshape(total, 16).astype(jnp.int32)
    feature_facts = packs[:, tokens:].reshape(width, 16)
    gain_att = feature_facts[:, 0].astype(F32)
    route_att = feature_facts[:, 1 : 1 + experts]
    gain_ffn = feature_facts[:, 1 + experts].astype(F32)
    route_ffn = feature_facts[:, 2 + experts : 2 + 2 * experts]

    def move(kind, weight):
        if kind == "columns_out":
            return as_columns(swap_group(to_windows(weight, 2)))
        if kind == "rows_out":
            if not windows:
                return as_rows(swap_group(to_windows(weight, 1)))
            parts = as_rows(swap_group(weight.reshape(group, hidden_rows, rows_own)))
            rows = jnp.zeros((hidden_wide, width), BF)
            return lax.dynamic_update_slice_in_dim(rows, parts, hidden_first, 0)
        if kind == "columns_home":
            return swap_group(weight.reshape(group, rows_own, -1))
        if windows:
            weight = lax.dynamic_slice_in_dim(weight, hidden_first, hidden_rows, 0)
        return swap_group(weight.reshape(-1, group, rows_own).transpose(1, 0, 2))

    def to_cuts(moves):
        return [
            (kind, ((0, early, False), (early, wide - early, True)), weight, wide)
            for kind, weight, wide, early in moves
        ]

    def to_slots(rows, next_put):
        picked = dot("tp,tf->pf", next_put, rows).astype(BF)
        picked = axes.swap(picked.reshape(experts, -1, feats), axes.exp)
        picked = lax.all_gather(
            picked.reshape(-1, feats), axes.layer[0], axis_index_groups=axes.layer[1]
        )
        return picked.transpose(1, 0, 2).reshape(-1, width)

    def exchanged(parts, adds, put, scale, extra, tail, moves, number):
        if kernels:
            return exchange(sizes, parts, adds, put, scale, extra, tail, to_cuts(moves), number)
        raws, outs = [], []
        for part, add in zip(parts, adds):
            home = go_home(layer_sum(part))
            summed = jnp.sum(home.astype(F32), axis=0) if put is None else put_home(put, home)
            raws.append(add + summed)
        raw = raws[0]
        if tail == "slots":
            next_put, linear, square = extra
            outs = [to_slots(raw.astype(BF), next_put)]
            facts = dot_exact("ef,tf->et", linear, raw) + dot_exact("ef,tf->et", square, raw * raw)
        else:
            facts = extra[0]
        told = lax.all_gather(facts, ALL).reshape(experts, layer, *facts.shape)
        if tail == "tokens":
            columns = jnp.broadcast_to(jnp.sum(raw * extra[1], axis=0, keepdims=True), (8, feats))
            columns = lax.all_gather(columns, ALL).reshape(experts, layer, 8, feats)
            columns = columns.transpose(0, 2, 1, 3).reshape(experts * 8, layer * feats)
            outs = [to_tokens(rows) for rows in ((raw * scale).astype(BF), *extra[2:])]
            outs.insert(0, columns)
        return raws, outs, told, [move(kind, weight) for kind, weight, _, _ in moves]

    def finished(plus, product, unit, next_put, moves, number):
        if kernels:
            return finish(sizes, plus, product, unit, next_put, to_cuts(moves), number)
        sums = lax.all_gather(jnp.sum(product, axis=1), ALL).reshape(experts, layer, own_tokens)
        mean = lax.dynamic_index_in_dim(jnp.sum(sums, axis=1), exp_at, 0, keepdims=False) / width
        raw = plus - unit * mean[:, None]
        moved = [move(kind, weight) for kind, weight, _, _ in moves]
        return raw, to_slots(raw.astype(BF), next_put), moved

    own_first = exp_at * own_seqs
    where = partial(
        Routing,
        seqs=seqs,
        seq_len=seq_len,
        experts=experts,
        cap=cap,
        mine=exp_at,
        own_first=own_first,
        own_seqs=own_seqs,
    )
    att = where(token_facts[:, 0:2])
    if copies > 1:
        turn = jnp.arange(seqs, dtype=jnp.int32) % copies == sub_at % copies
        att.pick = att.pick * turn.astype(BF)[:, None, None]
    ffn = where(token_facts[:, 2:4])
    spans = token_facts[:, 4].reshape(seqs, seq_len).astype(F32)
    cosine, sine = rope_tables(seq_len)

    my_gate = move("columns_out", after(w_gate, all_in))
    heads = heads_wide // HD
    scale = 1.0 / math.sqrt(HD)
    if kernels:
        att_rows = jnp.pad(jnp.stack([att.place_mine, spans], axis=1), ((0, 0), (0, 6), (0, 0)))
        att_hits = jnp.concatenate(
            [att.hits, spans[:, :, None], att.place_mine[:, :, None]], axis=2
        ).reshape(total, -1)
        att_hits = jnp.pad(att_hits, ((0, 0), (0, HD - att_hits.shape[1])))
        sine = sine * jnp.where(jnp.arange(HD) < HD // 2, -1.0, 1.0)
        h1, h1_slots, *saved, att_gates, att_tables = attend(
            experts,
            seqs,
            all_in,
            gain_att[None, :],
            my_query,
            my_key_value,
            jnp.pad(route_att, ((0, 0), (0, HD - experts))),
            att_rows,
            att_hits,
            cosine,
            sine,
            (jnp.arange(HD) == exp_at).astype(F32)[None, :],
        )
        mixed = saved[3]
        saved.append(att_tables)
        att_gates = att_gates[:, :experts].reshape(seqs, seq_len, experts)
        att_slot_gate = att_tables[:, 2 * HD : 2 * HD + 1]
    else:
        positions = jnp.arange(seq_len, dtype=jnp.int32).astype(F32)
        pick_f32 = att.pick.astype(F32)
        slot_position = jnp.sum(pick_f32 * positions[None, None, :], axis=2)
        slot_span = jnp.sum(pick_f32 * spans[:, None, :], axis=2)
        slot_cosine = dot_exact("spt,tf->spf", pick_f32, cosine)
        slot_sine = dot_exact("spt,tf->spf", pick_f32, sine)
        allowed = (positions[None, None, :] <= slot_position[:, :, None]) | (
            (slot_span[:, :, None] == spans[:, None, :]) & (slot_span[:, :, None] > 0)
        )
        x_all = all_in.astype(F32)
        scale_in = lax.rsqrt(jnp.mean(x_all * x_all, axis=1, keepdims=True) + EPS)
        h1 = (x_all * scale_in * gain_att[None, :]).astype(BF)
        kv = dot("td,dm->tm", h1, my_key_value)
        keys = rotate(
            kv[:, :heads_wide].reshape(seqs, seq_len, heads, HD),
            cosine[None, :, None, :],
            sine[None, :, None, :],
        ).astype(BF)
        values = kv[:, heads_wide:].astype(BF).reshape(seqs, seq_len, heads, HD)
        att_gates = att.gates(dot("td,de->te", h1, route_att))
        att_slot_gate = att.slot_gates(att_gates).reshape(slots, 1)
        h1_slots = att.take(h1)
        queries = rotate(
            dot("td,dm->tm", h1_slots, my_query).reshape(seqs, cap, heads, HD),
            slot_cosine[:, :, None, :],
            slot_sine[:, :, None, :],
        ).astype(BF)
        scores = dot("sqhd,skhd->shqk", queries, keys) * scale
        scores = jnp.where(allowed[:, None], scores, -1e30)
        expo = jnp.exp(scores - jnp.max(scores, axis=-1, keepdims=True))
        probs = expo / jnp.sum(expo, axis=-1, keepdims=True)
        probs_low = probs.astype(BF)
        mixed = dot("shqk,skhd->sqhd", probs_low, values).astype(BF).reshape(slots, heads_wide)
    branch_att = dot("cm,md->cd", mixed, my_out) * att_slot_gate
    own_at = (exp_at * own_tokens, layer_at * feats)
    own_in = lax.dynamic_slice(all_in, own_at, (own_tokens, feats)).astype(F32)
    own_gain_ffn = lax.dynamic_slice_in_dim(gain_ffn, layer_at * feats, feats, 0)
    own_route_ffn = lax.dynamic_slice_in_dim(
        route_ffn.astype(F32), layer_at * feats, feats, 0
    )
    linear = jnp.pad((own_route_ffn * own_gain_ffn[:, None]).T, ((0, 8 - experts), (0, 0)))
    square = (jnp.arange(8) == experts).astype(F32)[:, None] * jnp.ones((1, feats), F32)
    (mid,), (mid_slots,), ffn_facts, (my_up,) = exchanged(
        [after(branch_att.astype(BF), my_gate)],
        [own_in],
        att.put,
        jnp.ones((1, feats), F32),
        (ffn.put, linear, square),
        "slots",
        [("columns_out", w_up, hidden_wide, hidden_wide // 3)],
        1,
    )
    my_down = move("rows_out", after(w_down, mid_slots))

    ffn_facts = jnp.sum(ffn_facts, axis=1)
    scale_mid = lax.rsqrt(ffn_facts[:, experts].reshape(total, 1) / width + EPS)
    ffn_logits = ffn_facts[:, :experts].transpose(0, 2, 1).reshape(total, experts) * scale_mid
    ffn_gates = ffn.gates(ffn_logits)
    ffn_slot_gate = ffn.slot_gates(ffn_gates).reshape(slots, 1)
    mid_slots = mid_slots.astype(F32)
    scale_slots = lax.rsqrt(jnp.mean(mid_slots * mid_slots, axis=1, keepdims=True) + EPS)
    h2_slots = (mid_slots * scale_slots * gain_ffn[None, :]).astype(BF)
    pre_gate = dot("cd,df->cf", h2_slots, my_gate)
    pre_up = dot("cd,df->cf", h2_slots, my_up)
    sigma = jax.nn.sigmoid(pre_gate)
    swish = pre_gate * sigma
    hidden = jnp.where(hidden_mine, swish * pre_up, 0.0).astype(BF)

    top_slots = ffn.take(top_all)
    grad_branch = (top_slots.astype(F32) * ffn_slot_gate).astype(BF)
    grad_down_w = dot("cf,cd->fd", hidden, grad_branch).astype(BF)
    grad_down = move("rows_home", grad_down_w)
    my_down = after(my_down, grad_down_w)
    branch_ffn = dot("cf,fd->cd", hidden, my_down) * ffn_slot_gate
    grad_hidden = dot("cd,fd->cf", top_slots, my_down)
    ffn_gate_part = jnp.sum(hidden.astype(F32) * grad_hidden, axis=1)
    grad_hidden = jnp.where(hidden_mine, grad_hidden * ffn_slot_gate, 0.0)
    grad_pre_gate = (
        grad_hidden * pre_up * sigma * (1.0 + pre_gate * (1.0 - sigma))
    ).astype(BF)
    grad_pre_up = (grad_hidden * swish).astype(BF)
    ffn_taken = dot("cf,df->cd", grad_pre_gate, my_gate) + dot("cf,df->cd", grad_pre_up, my_up)
    grad_gate_w = dot("cd,cf->df", h2_slots, grad_pre_gate).astype(BF)
    grad_up_w = dot("cd,cf->df", h2_slots, grad_pre_up).astype(BF)
    gate_half = hidden_wide // 256 * 128

    def gate_facts(told):
        return jnp.sum(told, axis=1).reshape(experts, seqs, cap)

    (grad_second, own_out), _, ffn_told, (gate_first,) = exchanged(
        [after(ffn_taken.astype(BF), grad_up_w), branch_ffn.astype(BF)],
        [jnp.zeros((own_tokens, feats), F32), mid],
        ffn.put,
        jnp.ones((1, feats), F32),
        (ffn_gate_part.reshape(-1, 128),),
        None,
        [("columns_home", grad_gate_w[:, :gate_half], gate_half, 128)],
        2,
    )
    ffn_logit_grads = logit_grads(ffn_gates, ffn.token_grads(gate_facts(ffn_told)))
    own_ffn_logits = lax.dynamic_slice_in_dim(
        ffn_logit_grads, exp_at * own_tokens, own_tokens, 0
    )
    own_scale_mid = lax.dynamic_slice_in_dim(scale_mid, exp_at * own_tokens, own_tokens, 0)
    own_unit_mid = mid * own_scale_mid
    grad_second = grad_second + router_rows(own_ffn_logits, own_route_ffn)
    norm_ffn_part = jnp.sum(grad_second * own_unit_mid, axis=0)
    own_second = grad_second * own_gain_ffn[None, :] * own_scale_mid
    gate_rest = hidden_wide - gate_half
    up_early = 128
    grad_mid, mid_slots, (gate_second, up_first) = finished(
        lax.dynamic_slice(top_all, own_at, (own_tokens, feats)).astype(F32) + own_second,
        own_second * own_unit_mid,
        own_unit_mid,
        att.put,
        [
            ("columns_home", grad_gate_w[:, gate_half:], gate_rest, 128),
            ("columns_home", grad_up_w[:, :up_early], up_early, 0),
        ],
        5,
    )
    grad_gate = jnp.concatenate([gate_first, gate_second], axis=2)
    up_second = move("columns_home", after(grad_up_w[:, up_early:], mid_slots))

    def windows_home(back, axis):
        back = back.reshape(experts, sub, *back.shape[1:])
        parts = [lax.index_in_dim(back, i, 1, keepdims=False) for i in range(sub)]
        wide = parts[0].shape[axis]
        if wide * sub > hidden_local and windows:
            cut = partial(lax.slice_in_dim, axis=axis)
            parts = [
                cut(parts[0], 0, wide - overlap),
                cut(parts[0], wide - overlap, wide) + cut(parts[1], 0, overlap),
                cut(parts[1], overlap, wide),
            ]
        whole = jnp.concatenate(parts, axis=axis)
        return lax.slice_in_dim(whole, 0, hidden_local, axis=axis).astype(F32)

    grad_gate = windows_home(grad_gate, 2)
    grad_down = windows_home(after(grad_down, mid_slots), 1)
    mid_slots = after(mid_slots, grad_gate, grad_down)

    if copies > 1:
        mid_slots = mid_slots * jnp.repeat(turn, cap).astype(BF)[:, None]
    if kernels:
        grad_qpre, kv_low, grad_att_branch, att_gate_part, first_part = attend_back(
            experts,
            seqs,
            mid_slots,
            my_out,
            my_query,
            my_key_value,
            att_rows,
            att_hits,
            cosine,
            sine,
            saved,
        )
        att_gate_part = att_gate_part[:, 0]
    else:
        grad_mixed = dot("cd,md->cm", mid_slots, my_out)
        att_gate_part = jnp.sum(mixed.astype(F32) * grad_mixed, axis=1)
        grad_mixed = (grad_mixed * att_slot_gate).astype(BF).reshape(seqs, cap, heads, HD)
        grad_att_branch = (mid_slots.astype(F32) * att_slot_gate).astype(BF)
        grad_soft = dot("sqhd,skhd->shqk", grad_mixed, values)
        grad_values = dot("shqk,sqhd->skhd", probs_low, grad_mixed)
        grad_scores = (
            probs * (grad_soft - jnp.sum(probs * grad_soft, axis=-1, keepdims=True))
        ).astype(BF)
        grad_queries = dot("shqk,skhd->sqhd", grad_scores, keys) * scale
        grad_keys = dot("shqk,sqhd->skhd", grad_scores, queries) * scale
        grad_qpre = (
            rotate_back(grad_queries, slot_cosine[:, :, None, :], slot_sine[:, :, None, :])
            .astype(BF)
            .reshape(slots, heads_wide)
        )
        att_taken = dot("cm,dm->cd", grad_qpre, my_query)
        grad_kpre = rotate_back(
            grad_keys, cosine[None, :, None, :], sine[None, :, None, :]
        ).reshape(total, heads_wide)
        kv_low = jnp.concatenate([grad_kpre, grad_values.reshape(total, heads_wide)], axis=1)
        kv_low = kv_low.astype(BF)
        first_part = dot("tm,dm->td", kv_low, my_key_value) + att.give(att_taken.astype(BF))
    own_rows = lax.dynamic_slice_in_dim(all_in, exp_at * own_tokens, own_tokens, 0).astype(F32)
    own_scale_in = lax.rsqrt(jnp.mean(own_rows * own_rows, axis=1, keepdims=True) + EPS)
    own_gain_att = lax.dynamic_slice_in_dim(gain_att, layer_at * feats, feats, 0)
    grad_query_w = dot("cd,cm->dm", h1_slots, grad_qpre).astype(BF)
    grad_out_w = dot("cm,cd->md", mixed, grad_att_branch).astype(BF)
    grad_kv_w = dot("td,tm->dm", h1, kv_low).astype(BF)
    own_h2 = (own_unit_mid * own_gain_ffn[None, :]).astype(BF).astype(F32)
    gate_rows = slots // feats
    own_parts = jnp.concatenate(
        [
            att_gate_part.reshape(gate_rows, feats),
            norm_ffn_part[None],
            dot_exact("te,tf->ef", own_ffn_logits, own_h2),
        ],
        axis=0,
    )
    own_parts = jnp.pad(own_parts, ((0, -own_parts.shape[0] % 8), (0, 0)))
    own_unit_in = own_in * own_scale_in
    (grad_first,), tokens_out, told, (grad_out, grad_query, kv_first, kv_second) = exchanged(
        [after(first_part.astype(BF), up_second)],
        [jnp.zeros((own_tokens, feats), F32)],
        None,
        own_gain_att[None, :] * own_scale_in,
        (own_parts, own_unit_in, grad_mid.astype(BF), own_out.astype(BF)),
        "tokens",
        [
            ("rows_home", grad_out_w, heads_wide, heads_wide),
            ("columns_home", grad_query_w, heads_wide, heads_wide),
            ("columns_home", grad_kv_w[:, :heads_wide], heads_wide, 0),
            ("columns_home", grad_kv_w[:, heads_wide:], heads_wide, 0),
        ],
        3,
    )
    columns, first_tokens, mid_tokens, hidden_out = tokens_out
    att_logit_grads = logit_grads(
        att_gates, att.token_grads(gate_facts(told[:, :, :gate_rows]))
    )
    token_at = group_at * tokens
    rows_in = hidden_in.astype(F32)
    unit_in = lax.rsqrt(jnp.mean(rows_in * rows_in, axis=1, keepdims=True) + EPS)
    first_tokens = first_tokens.astype(F32) + router_rows(
        lax.dynamic_slice_in_dim(att_logit_grads, token_at, tokens, 0), route_att
    ) * (gain_att[None, :] * unit_in)
    unit_in = rows_in * unit_in
    grad_in = (
        mid_tokens.astype(F32)
        + first_tokens
        - unit_in * jnp.mean(first_tokens * unit_in, axis=1, keepdims=True)
    )


    def heads_home(back, axis):
        back = back.reshape(experts, head_parts, copies, *back.shape[1:])
        if copies > 1:
            back = jnp.sum(back.astype(F32), axis=2, keepdims=True)
        parts = [back[:, i, 0] for i in range(head_parts)]
        return jnp.concatenate(parts, axis=axis).astype(F32)

    def my_rows(table, axis):
        return lax.dynamic_slice_in_dim(table, group_at * rows_own, rows_own, axis)

    ffn_parts = jnp.sum(told[:, :, gate_rows : gate_rows + 1 + experts], axis=0)
    ffn_parts = my_rows(ffn_parts.transpose(1, 0, 2).reshape(1 + experts, width), 1)
    high = att_logit_grads.astype(BF)
    low = (att_logit_grads - high.astype(F32)).astype(BF)
    grad_router_att = dot("tf,te->fe", my_rows(h1, 1), jnp.concatenate([high, low], axis=1))
    grad_router_att = grad_router_att[:, :experts] + grad_router_att[:, experts:]
    norm_att = my_rows(jnp.sum(columns.reshape(experts, 8, width)[:, 0], axis=0), 0)
    norm_att = norm_att + jnp.sum(
        grad_router_att * my_rows(route_att, 0).astype(F32), axis=1
    ) / my_rows(gain_att, 0)
    grad_out = heads_home(grad_out, 1)
    grad_query = heads_home(grad_query, 2)
    grad_key, grad_value = (
        jnp.sum(heads_home(part, 2), axis=0) for part in (kv_first, kv_second)
    )
    return (
        hidden_out,
        grad_in,
        norm_att,
        grad_router_att,
        grad_query,
        grad_out,
        grad_key,
        grad_value,
        ffn_parts[0],
        ffn_parts[1:].T,
        grad_gate,
        windows_home(jnp.concatenate([up_first, up_second], axis=2), 2),
        grad_down,
    )


def solution(mesh):
    ctx, tp = mesh.shape["ctx"], mesh.shape["tp"]
    shard = mesh.shape["shard"]
    by_token, by_feature = P(GROUP, None), P(GROUP)
    columns, rows = P(None, GROUP, "tp"), P(None, "tp", GROUP)

    return jax.shard_map(
        partial(shards, (shard, ctx, tp)),
        mesh=mesh,
        in_specs=(
            by_token,
            by_token,
            by_token,
            P(GROUP),
            by_feature,
            by_token,
            columns,
            rows,
            P(GROUP, "tp"),
            P(GROUP, "tp"),
            by_feature,
            by_token,
            columns,
            columns,
            rows,
            by_token,
        ),
        out_specs=(
            by_token,
            by_token,
            by_feature,
            by_token,
            columns,
            rows,
            P(GROUP, "tp"),
            P(GROUP, "tp"),
            by_feature,
            by_token,
            columns,
            columns,
            rows,
        ),
        check_vma=False,
    )
```

```python
from functools import partial
import math

import numpy as np

import jax
import jax.numpy as jnp
from jax import lax
from jax.experimental import pallas as pl
from jax.experimental.pallas import tpu as pltpu
from jax.sharding import PartitionSpec as P

HD = 128
EPS = 1e-06
BF = jnp.bfloat16
F32 = jnp.float32
MESH = pl.DeviceIdType.MESH
VMEM_BYTES = 60 * 2**20
LOCAL_VMEM_BYTES = 56 * 2**20
GROUP = ("shard", "ctx")
ALL = ("shard", "ctx", "tp")


def dot(spec, left, right):
    return jnp.einsum(spec, left, right, preferred_element_type=F32)


def dot_exact(spec, left, right):
    return jnp.einsum(
        spec, left, right, preferred_element_type=F32, precision=lax.Precision.HIGHEST
    )


def after(value, *others):
    return lax.optimization_barrier((value, *others))[0]


def rope_tables(count):
    half_dim = HD // 2
    freq_index = (jnp.arange(HD) % half_dim).astype(F32)
    frequency = 10000.0 ** (-2.0 * freq_index / HD)
    angles = jnp.arange(count, dtype=F32)[:, None] * frequency[None, :]
    return jnp.cos(angles), jnp.sin(angles)


def rotate(rows, cosine, sine):
    half_dim = HD // 2
    turned = jnp.concatenate([-rows[..., half_dim:], rows[..., :half_dim]], axis=-1)
    return rows * cosine + turned * sine


def rotate_back(rows, cosine, sine):
    half_dim = HD // 2
    turned = rows * sine
    return rows * cosine + jnp.concatenate(
        [turned[..., half_dim:], -turned[..., :half_dim]], axis=-1
    )


class Place:
    def __init__(self, sizes):
        self.experts, self.sub, self.ctx, self.tp = sizes
        self.chips = self.sub * self.tp // 2
        self.members = self.experts * self.sub
        self.group = lax.axis_index(GROUP)
        self.tp_at = lax.axis_index("tp")
        self.exp = self.group // self.sub
        here = (self.group % self.sub) * self.tp + self.tp_at
        self.chip, self.core = here // 2, here % 2

    def device(self, exp, chip, core):
        here = chip * 2 + core
        group = exp * self.sub + here // self.tp
        return (group // self.ctx, group % self.ctx, here % self.tp)

    def member(self, group):
        return (group // self.ctx, group % self.ctx, self.tp_at)

    def sibling(self):
        return self.device(self.exp, self.chip, 1 - self.core)

    def other_exp(self, k):
        return (self.exp + k) % self.experts

    def other_chip(self, k):
        return (self.chip + k) % self.chips

    def meet(self, whole_group):
        barrier = pltpu.get_barrier_semaphore()
        layer = 2 * self.chips
        here = self.chip * 2 + self.core
        others = [(here + k) % layer for k in range(1, layer)]
        peers = [self.device(self.exp, there // 2, there % 2) for there in others]
        if whole_group:
            peers += [
                self.member((self.group + k) % self.members) for k in range(1, self.members)
            ]
        else:
            peers += [
                self.device(self.other_exp(k), self.chip, self.core)
                for k in range(1, self.experts)
            ]
        for peer in peers:
            pl.semaphore_signal(barrier, inc=1, device_id=peer, device_id_type=MESH)
        pl.semaphore_wait(barrier, len(peers))


def block(start, size, unit):
    return pl.ds(pl.multiple_of(start, unit), size)


def send(src, dst, sems, at, device):
    copy = pltpu.make_async_remote_copy(
        src_ref=src,
        dst_ref=dst,
        send_sem=sems.at[(0, *at)],
        recv_sem=sems.at[(1, *at)],
        device_id=device,
        device_id_type=MESH,
    )
    copy.start()
    return copy


class Mover:
    def __init__(self, number, kind, cuts, src, dst, sems, own_sems):
        self.number, self.kind, self.cuts = number, kind, cuts
        self.src, self.dst, self.sems, self.own_sems = src, dst, sems, own_sems
        self.copies = []

    def ends(self, place, group, low, size):
        exp, sub = group // place.sub, group % place.sub
        me, src, dst = place.group, self.src, self.dst
        if self.kind == "columns_out":
            rows, step = src.shape[1], (src.shape[2] - dst.shape[1]) // max(place.sub - 1, 1)
            return (
                src.at[exp, :, block(sub * step + low, size, 128)],
                dst.at[block(me * rows, rows, 16), pl.ds(low, size)],
            )
        if self.kind == "rows_out":
            cols, step = src.shape[2], (src.shape[1] - dst.shape[0]) // max(place.sub - 1, 1)
            return (
                src.at[exp, block(sub * step + low, size, 16)],
                dst.at[pl.ds(low, size), block(me * cols, cols, 128)],
            )
        if self.kind == "columns_home":
            rows = dst.shape[1]
            return (
                src.at[block(group * rows, rows, 16), pl.ds(low, size)],
                dst.at[me, :, pl.ds(low, size)],
            )
        cols = dst.shape[2]
        return (
            src.at[pl.ds(low, size), block(group * cols, cols, 128)],
            dst.at[me, pl.ds(low, size)],
        )

    def start(self, place, late):
        for cut, (low, size, is_late) in enumerate(self.cuts):
            if is_late != late or not size:
                continue
            for k in range(1, place.members):
                group = (place.group + k) % place.members
                src, dst = self.ends(place, group, low, size)
                at = (self.number, cut, k - 1)
                self.copies.append(send(src, dst, self.sems, at, place.member(group)))
            src, dst = self.ends(place, place.group, low, size)
            own = pltpu.make_async_copy(src, dst, self.own_sems.at[self.number, cut])
            own.start()
            self.copies.append(own)

    def wait(self):
        for copy in self.copies:
            copy.wait()


def moved_shape(sizes, kind, array, wide):
    experts, sub, _, _ = sizes
    group = experts * sub
    if kind == "columns_out":
        return (array.shape[1] * group, wide)
    if kind == "rows_out":
        return (wide, array.shape[2] * group)
    if kind == "columns_home":
        return (group, array.shape[0] // group, array.shape[1])
    return (group, array.shape[0], array.shape[1] // group)


class Line:
    def __init__(self, place, spot, sems):
        self.place, self.spot, self.sems = place, spot, sems

    def give(self, src, origin, up, step):
        place = self.place
        to = place.exp + 1 if up else place.exp - 1
        return pltpu.make_async_remote_copy(
            src_ref=src,
            dst_ref=self.spot(origin),
            send_sem=self.sems.at[0, 0 if up else 1, step],
            recv_sem=self.sems.at[1, 0 if up else 1, step],
            device_id=place.device(to, place.chip, place.core),
            device_id_type=MESH,
        )

    def start(self, src):
        place = self.place
        self.src = src

        @pl.when(place.exp < place.experts - 1)
        def _():
            self.give(src, place.exp, True, 0).start()

        @pl.when(place.exp > 0)
        def _():
            self.give(src, place.exp, False, 0).start()

    def origin(self, turn):
        place = self.place
        if place.experts != 4:
            return (place.exp + place.experts - turn) % place.experts
        high = place.exp // 2
        at = place.exp * (1 - high) + (3 - place.exp) * high
        origin = 1 - at if turn == 1 else turn
        return origin * (1 - high) + (3 - origin) * high

    def arrived(self, turn):
        place = self.place
        origin = self.origin(turn)

        @pl.when(origin < place.exp)
        def _():
            step = place.exp - origin - 1
            self.give(self.spot(origin), origin, True, step).wait_recv()

            @pl.when(place.exp < place.experts - 1)
            def _():
                self.give(self.spot(origin), origin, True, step + 1).start()

        @pl.when(origin > place.exp)
        def _():
            step = origin - place.exp - 1
            self.give(self.spot(origin), origin, False, step).wait_recv()

            @pl.when(place.exp > 0)
            def _():
                self.give(self.spot(origin), origin, False, step + 1).start()

        return origin

    def finish(self):
        place = self.place
        for step in range(place.experts - 1):

            @pl.when((place.exp < place.experts - 1) & (place.exp >= step))
            def _():
                self.give(self.src, place.exp, True, step).wait_send()

            @pl.when((place.exp > 0) & (place.exp + step < place.experts))
            def _():
                self.give(self.src, place.exp, False, step).wait_send()


class Spread:
    def __init__(self, place, mine, out, by_token, exp_sems, chip_sems, core_sems, pieces=1):
        self.place, self.mine, self.out, self.by_token = place, mine, out, by_token
        self.rows, self.cols = mine.shape[0] // pieces, mine.shape[1]
        self.pieces = pieces
        self.exp_sems, self.chip_sems, self.core_sems = exp_sems, chip_sems, core_sems
        self.square = place.chips == 4 and place.tp == 4 and self.rows % 64 == 0
        self.line = None
        if pieces == 1 and self.rows % 64 == 0:
            self.line = Line(place, lambda origin: self.spot(origin, place.chip), exp_sems)

    def spot(self, exp, chip, low=0, size=None):
        place = self.place
        here = chip * 2 + place.core
        if self.by_token:
            row = (exp * place.sub + here // place.tp) * self.rows
            col = (here % place.tp) * self.cols
        else:
            row, col = exp * self.rows, here * self.cols
        unit = math.gcd(self.rows, 16)
        size = size or self.rows
        return self.out.at[block(row + low, size, unit), block(col, self.cols, 128)]

    def piece(self, exp):
        if self.pieces == 1:
            return self.mine
        return self.mine.at[block(exp * self.rows, self.rows, 16)]

    def near(self):
        place = self.place
        side = place.chip // 2
        along = place.chip % 2
        return [(1 - side) * 2 + along, side * 2 + 1 - along]

    def to_chip(self, src, dst, turn, k, chip):
        device = self.place.device(self.place.exp, chip, self.place.core)
        self.chip_copies[turn].append(send(src, dst, self.chip_sems, (turn, k), device))

    def to_chips(self, exp, src, turn):
        place = self.place
        if self.square:
            chips = self.near()
        else:
            chips = [place.other_chip(k) for k in range(1, place.chips)]
        for k, chip in enumerate(chips):
            self.to_chip(src, self.spot(exp, place.chip), turn, k, chip)

    def to_core(self, exp, chip, src, turn, k):
        self.core_copies.append(
            send(src, self.spot(exp, chip), self.core_sems, (turn, k), self.place.sibling())
        )

    def start(self, own_sem):
        place = self.place
        home = self.spot(place.exp, place.chip)
        mine = self.piece(place.exp)
        self.own = pltpu.make_async_copy(mine, home, own_sem)
        self.own.start()
        self.chip_copies = [[] for _ in range(place.experts)]
        self.core_copies = []
        if self.line:
            self.line.start(mine)
        else:
            self.exp_copies = [
                send(
                    self.piece(place.other_exp(k)),
                    home,
                    self.exp_sems,
                    (0, k - 1),
                    place.device(place.other_exp(k), place.chip, place.core),
                )
                for k in range(1, place.experts)
            ]
        self.to_chips(place.exp, mine, 0)
        self.to_core(place.exp, place.chip, mine, 0, 0)

    def from_layer(self, turn):
        place = self.place
        if self.line:
            source = self.line.arrived(turn)
        else:
            self.exp_copies[turn - 1].wait_recv()
            source = (place.exp + place.experts - turn) % place.experts
        self.sources[turn] = source
        here = self.spot(source, place.chip)
        self.to_chips(source, here, turn)
        self.to_core(source, place.chip, here, turn, 0)

    def from_near(self, turn):
        source, copies = self.sources[turn], self.chip_copies[turn]
        if not self.square:
            return
        half = self.rows // 2
        side, along = self.near()
        copies[0].wait_recv()
        part = self.spot(source, side, 0, half)
        self.to_chip(part, part, turn, 2, along)
        self.to_core(source, side, self.spot(source, side), turn, 1)
        copies[1].wait_recv()
        part = self.spot(source, along, half, half)
        self.to_chip(part, part, turn, 3, side)
        self.to_core(source, along, self.spot(source, along), turn, 2)

    def from_far(self, turn):
        place = self.place
        source, copies = self.sources[turn], self.chip_copies[turn]
        if self.square:
            copies[2].wait_recv()
            copies[3].wait_recv()
            far = 3 - place.chip
            self.to_core(source, far, self.spot(source, far), turn, 3)
            return
        for k in range(1, place.chips):
            copies[k - 1].wait_recv()
            chip = (place.chip + place.chips - k) % place.chips
            self.to_core(source, chip, self.spot(source, chip), turn, k)

    def run(self):
        for stage in range(self.place.experts + 1):
            self.step(stage)
        self.finish()

    def step(self, stage):
        experts = self.place.experts
        if stage == 0:
            self.sources = {0: self.place.exp}
        if 1 <= stage + 1 < experts:
            self.from_layer(stage + 1)
        if 0 <= stage < experts:
            self.from_near(stage)
        if 0 <= stage - 1 < experts:
            self.from_far(stage - 1)

    def finish(self):
        for copy in self.core_copies:
            copy.wait()
        if self.line:
            self.line.finish()
        else:
            for copy in self.exp_copies:
                copy.wait_send()
        for copies in self.chip_copies:
            for copy in copies:
                copy.wait_send()
        self.own.wait()


class Pair:
    def __init__(self, place, src, out, line_sems, sems, own_sems):
        self.place, self.src, self.out, self.sems, self.own_sems = place, src, out, sems, own_sems
        self.rows = src.shape[1]
        self.half = src.shape[2] // place.sub
        size = self.rows * place.sub

        def spot(exp):
            return out.at[block(exp * size, size, 16)]

        self.line = Line(place, spot, line_sems)

    def start(self):
        place = self.place
        land = block(place.group * self.rows, self.rows, 16)
        sub = place.group % place.sub
        self.copies = []
        for i in range(2):
            dst = self.out.at[land, pl.ds(i * self.half, self.half)]
            for k in range(1, place.sub):
                other = (sub + k) % place.sub
                src = self.src.at[i, :, block(other * self.half, self.half, 128)]
                group = place.exp * place.sub + other
                self.copies.append(send(src, dst, self.sems, (i, k - 1), place.member(group)))
            src = self.src.at[i, :, block(sub * self.half, self.half, 128)]
            own = pltpu.make_async_copy(src, dst, self.own_sems.at[i])
            own.start()
            self.copies.append(own)

    def share(self):
        for copy in self.copies:
            copy.wait()
        self.line.start(self.line.spot(self.place.exp))

    def step(self, stage):
        if stage + 1 < self.place.experts:
            self.line.arrived(stage + 1)

    def finish(self):
        self.line.finish()


class ToTokens:
    def __init__(self, place, mine, out, chip_sems, core_sems):
        self.place, self.mine, self.out = place, mine, out
        self.chip_sems, self.core_sems = chip_sems, core_sems
        self.rows, self.cols = out.shape[0], mine.shape[1]

    def spot(self, chip):
        here = chip * 2 + self.place.core
        return self.out.at[:, block(here * self.cols, self.cols, 128)]

    def part(self, chip):
        sub = (chip * 2) // self.place.tp
        return self.mine.at[block(sub * self.rows, self.rows, 16)]

    def start(self, own_sem):
        place = self.place
        mine = self.part(place.chip)
        self.own = pltpu.make_async_copy(mine, self.spot(place.chip), own_sem)
        self.own.start()
        self.copies = []
        for k in range(1, place.chips):
            chip = place.other_chip(k)
            self.copies.append(
                send(
                    self.part(chip),
                    self.spot(place.chip),
                    self.chip_sems,
                    (k - 1,),
                    place.device(place.exp, chip, place.core),
                )
            )
        self.core = [send(mine, self.spot(place.chip), self.core_sems, (0,), place.sibling())]

    def run(self):
        place, core, copies = self.place, self.core, self.copies
        for k in range(1, place.chips):
            copies[k - 1].wait_recv()
            spot = self.spot((place.chip + place.chips - k) % place.chips)
            core.append(send(spot, spot, self.core_sems, (k,), place.sibling()))
        for copy in core:
            copy.wait()
        for copy in copies:
            copy.wait_send()
        self.own.wait()


class Fold:
    def __init__(self, place, parts, homes, scratch):
        self.place, self.parts, self.homes = place, parts, homes
        (
            self.core_got,
            self.chip_out,
            self.chip_got,
            self.turn_out,
            self.turn_got,
            self.exp_out,
            self.core_sems,
            self.chip_sems,
            self.turn_sems,
            self.exp_sems,
        ) = scratch
        self.each, self.feats = homes[0].shape[1:]
        side, along = place.chip // 2, place.chip % 2
        self.chips = [
            place.chip,
            (1 - side) * 2 + along,
            side * 2 + 1 - along,
            (1 - side) * 2 + 1 - along,
        ]

    def rows(self, chunk):
        return (self.place.exp + 1 + chunk % self.place.experts) % self.place.experts * self.each

    def mine(self, chunk, to, low, size):
        place = self.place
        col = (self.chips[to] * 2 + place.core) * self.feats
        rows = block(self.rows(chunk) + low, size, 16)
        part = self.parts[chunk // place.experts][rows, block(col, self.feats, 128)]
        return part.astype(F32) + self.core_got[chunk, to, low : low + size].astype(F32)

    def between_cores(self, chunk):
        place = self.place
        part = self.parts[chunk // place.experts]
        rows = block(self.rows(chunk), self.each, 16)
        copies = []
        for to in (1, 2, 3, 0):
            col = (self.chips[to] * 2 + 1 - place.core) * self.feats
            src = part.at[rows, block(col, self.feats, 128)]
            dst = self.core_got.at[chunk, to]
            copies.append(send(src, dst, self.core_sems, (chunk, to), place.sibling()))
        return copies

    def over(self, to, src, dst, sems, at):
        place = self.place
        return send(src, dst, sems, at, place.device(place.exp, self.chips[to], place.core))

    def first_hops(self, chunk, core):
        half = self.each // 2
        for copy in core:
            copy.wait_recv()
        copies = []
        for near, low in ((1, 0), (2, half)):
            for slot, to in enumerate((near, 3)):
                at = 2 * (near - 1) + slot
                out = self.chip_out.at[chunk, at]
                out[...] = self.mine(chunk, to, low, half).astype(BF)
                got = self.chip_got.at[chunk, at]
                copies.append(self.over(near, out, got, self.chip_sems, (chunk, at)))
        return copies

    def second_hops(self, chunk, first):
        half = self.each // 2
        copies = []
        for near, far, low in ((1, 2, 0), (2, 1, half)):
            at = 2 * (near - 1)
            first[at].wait_recv()
            first[at + 1].wait_recv()
            out = self.turn_out.at[chunk, near - 1]
            got = self.chip_got[chunk, at + 1].astype(F32)
            out[...] = (self.mine(chunk, far, low, half) + got).astype(BF)
            got = self.turn_got.at[chunk, near - 1]
            copies.append(self.over(far, out, got, self.turn_sems, (chunk, near - 1)))
        return copies

    def go_home(self, chunk, second):
        place = self.place
        half = self.each // 2
        for near, low in ((1, 0), (2, half)):
            second[near - 1].wait_recv()
            total = self.mine(chunk, 0, low, half)
            total = total + self.chip_got[chunk, 2 * (near - 1)].astype(F32)
            total = total + self.turn_got[chunk, near - 1].astype(F32)
            self.exp_out[chunk, low : low + half] = total.astype(BF)
        home = self.homes[chunk // place.experts]
        k = 1 + chunk % place.experts
        if k == place.experts:
            home[place.exp] = self.exp_out[chunk]
            return []
        device = place.device(place.other_exp(k), place.chip, place.core)
        return [
            send(self.exp_out.at[chunk], home.at[place.exp], self.exp_sems, (chunk,), device)
        ]

    def run(self):
        chunks = len(self.parts) * self.place.experts
        core = [self.between_cores(chunk) for chunk in range(chunks)]
        first, second, home = [], [], []
        for stage in range(chunks + 2):
            if stage < chunks:
                first.append(self.first_hops(stage, core[stage]))
            if 0 <= stage - 1 < chunks:
                second.append(self.second_hops(stage - 1, first[stage - 1]))
            if 0 <= stage - 2 < chunks:
                home.append(self.go_home(stage - 2, second[stage - 2]))
        for copies in home:
            for copy in copies:
                copy.wait_recv()
        for copies in (*core, *first, *second, *home):
            for copy in copies:
                copy.wait_send()


def start_kernel(sizes, count, moves, *refs):
    place = Place(sizes)
    blocks, refs = take(refs, count)
    (pair_src,), refs = take(refs, 1)
    sources, refs = take(refs, len(moves))
    outs, refs = take(refs, count)
    (pair_out,), refs = take(refs, 1)
    landings, refs = take(refs, len(moves))
    (own_sems, exp_sems, chip_sems, core_sems), refs = take(refs, 4)
    pair_sems, refs = take(refs, 3)
    movers = make_movers(moves, sources, landings, refs)
    pair = Pair(place, pair_src, pair_out, *pair_sems)
    spreads = []
    for i, (rows, out) in enumerate(zip(blocks, outs)):
        quarter = rows.shape[1] // place.tp
        mine = rows.at[:, block(place.tp_at * quarter, quarter, 128)]
        sems = (s.at[i] for s in (exp_sems, chip_sems, core_sems))
        spreads.append(Spread(place, mine, out, True, *sems))
    place.meet(True)
    pair.start()
    for i, spread in enumerate(spreads[:-1]):
        spread.start(own_sems.at[i])
    pair.share()
    for mover in movers:
        mover.start(place, False)
    spreads[-1].start(own_sems.at[count - 1])
    for mover in movers:
        mover.start(place, True)
    for stage in range(place.experts + 2):
        for runner in (*spreads[:-1], pair):
            if stage <= place.experts:
                runner.step(stage)
        if stage:
            spreads[-1].step(stage - 1)
    for runner in (*spreads, pair):
        runner.finish()
    for mover in movers:
        mover.wait()


def take(refs, count):
    return refs[:count], refs[count:]


def turned(left, right):
    return lax.dot_general(left, right, (((0,), (0,)), ((), ())), preferred_element_type=F32)


def row_sums(weights, rows):
    return lax.dot_general(
        weights,
        rows,
        (((1,), (1,)), ((), ())),
        preferred_element_type=F32,
        precision=lax.Precision.HIGHEST,
    )


def make_movers(moves, sources, landings, sems):
    return [
        Mover(i, kind, cuts, source, landing, *sems)
        for i, ((kind, cuts), source, landing) in enumerate(zip(moves, sources, landings))
    ]


def exchange_kernel(sizes, tail, count, extras, moves, *refs):
    place = Place(sizes)
    parts, refs = take(refs, count)
    adds, refs = take(refs, count)
    (put, scale), refs = take(refs, 2)
    if tail == "slots":
        (next_put, linear, square), refs = take(refs, 3)
    elif tail == "tokens":
        (facts, unit, *more), refs = take(refs, extras)
    else:
        (facts,), refs = take(refs, extras)
    sources, refs = take(refs, len(moves))
    raws, refs = take(refs, count)
    (all_facts,), refs = take(refs, 1)
    if tail == "tokens":
        (all_sums,), refs = take(refs, 1)
    outs, refs = take(refs, {"slots": 1, "tokens": extras - 1, None: 0}[tail])
    landings, refs = take(refs, len(moves))
    homes, refs = take(refs, count)
    (own_sems,), refs = take(refs, 1)
    fact_sems, refs = take(refs, 3)
    fold_scratch, refs = take(refs, 10)
    if tail == "slots":
        (picked, facts), refs = take(refs, 2)
        tail_sems, refs = take(refs, 3)
    elif tail == "tokens":
        (mine, sums), refs = take(refs, 2)
        sum_sems, refs = take(refs, 3)
        tail_sems, refs = take(refs, 2 * extras - 2)
    movers = make_movers(moves, sources, landings, refs)
    place.meet(bool(moves))
    told = Spread(place, facts, all_facts, False, *fact_sems)
    if tail != "slots":
        told.start(own_sems.at[0])
    to_tokens = []
    if tail == "tokens":
        for i, rows in enumerate(more):
            to_tokens.append(
                ToTokens(place, rows, outs[1 + i], *tail_sems[2 + 2 * i : 4 + 2 * i])
            )
            to_tokens[-1].start(own_sems.at[2 + i])
    for mover in movers:
        mover.start(place, False)
    Fold(place, parts, homes, fold_scratch).run()
    for i in reversed(range(count)):
        if put.shape[1] == 128:
            summed = jnp.sum(homes[i][...].astype(F32), axis=0)
        else:
            rows = homes[i][...].reshape(-1, homes[i].shape[2])
            summed = jnp.dot(put[...], rows, preferred_element_type=F32)
        value = adds[i][...] + summed
        raws[i][...] = value
    if tail == "slots":
        picked[...] = turned(next_put[...], value.astype(BF)).astype(BF)
        slots = Spread(place, picked, outs[0], False, *tail_sems, pieces=place.experts)
        slots.start(own_sems.at[1])
        facts[...] = row_sums(linear[...], value) + row_sums(square[...], value * value)
        told.start(own_sems.at[0])
    elif tail == "tokens":
        mine[...] = (value * scale[...]).astype(BF)
        to_tokens.append(ToTokens(place, mine, outs[0], *tail_sems[:2]))
        to_tokens[-1].start(own_sems.at[1])
        columns = jnp.sum(value * unit[...], axis=0, keepdims=True)
        sums[...] = jnp.broadcast_to(columns, sums.shape)
        summed = Spread(place, sums, all_sums, False, *sum_sems)
        summed.start(own_sems.at[extras])
    for mover in movers:
        mover.start(place, True)
    if tail == "slots":
        slots.run()
    for rows in to_tokens:
        rows.run()
    told.run()
    if tail == "tokens":
        summed.run()
    for mover in movers:
        mover.wait()


def finish_kernel(sizes, moves, *refs):
    place = Place(sizes)
    (plus, product, unit, next_put), refs = take(refs, 4)
    sources, refs = take(refs, len(moves))
    (raw, out), refs = take(refs, 2)
    landings, refs = take(refs, len(moves))
    (sums, got, picked, own_sem, sum_sems), refs = take(refs, 5)
    tail_sems, refs = take(refs, 3)
    movers = make_movers(moves, sources, landings, refs)
    sums[...] = row_sums(jnp.ones((8, product.shape[1]), F32), product[...])
    place.meet(bool(moves))
    layer = place.chips * 2
    here = place.chip * 2 + place.core
    copies = []
    for k in range(1, layer):
        there = (here + k) % layer
        device = place.device(place.exp, there // 2, there % 2)
        copies.append(send(sums, got.at[k - 1], sum_sems, (k - 1,), device))
    for mover in movers:
        mover.start(place, False)
    total = sums[...]
    for k in range(1, layer):
        copies[k - 1].wait_recv()
        total = total + got[k - 1]
    mean = total.T[:, :1] * (1.0 / (layer * product.shape[1]))
    value = plus[...] - unit[...] * mean
    raw[...] = value
    picked[...] = turned(next_put[...], value.astype(BF)).astype(BF)
    slots = Spread(place, picked, out, False, *tail_sems, pieces=place.experts)
    slots.start(own_sem)
    for mover in movers:
        mover.start(place, True)
    slots.run()
    for copy in copies:
        copy.wait_send()
    for mover in movers:
        mover.wait()


def dma_sems(*shape):
    return pltpu.SemaphoreType.DMA(shape)


def move_scratch(sizes, moves):
    most = max(len(cuts) for _, cuts, _, _ in moves)
    members = sizes[0] * sizes[1]
    return [dma_sems(2, len(moves), most, members - 1), dma_sems(len(moves), most)]


def start(sizes, arrays, pair, moves, number):
    experts, sub, _, tp = sizes
    count = len(arrays)
    exp_sems, chip_sems, core_sems = (
        dma_sems(count, *shape) for shape in spread_shapes(sizes)
    )
    anywhere = pl.BlockSpec(memory_space=pl.ANY)
    total = count + 1 + len(moves)
    results = pl.pallas_call(
        partial(start_kernel, sizes, count, [(kind, cuts) for kind, cuts, _, _ in moves]),
        out_shape=[
            *[
                jax.ShapeDtypeStruct((rows.shape[0] * experts * sub, rows.shape[1]), rows.dtype)
                for rows in arrays
            ],
            jax.ShapeDtypeStruct((pair.shape[1] * experts * sub, 2 * pair.shape[2] // sub), BF),
            *landing_shapes(sizes, moves),
        ],
        in_specs=[anywhere] * total,
        out_specs=[anywhere] * total,
        scratch_shapes=[
            dma_sems(count),
            exp_sems,
            chip_sems,
            core_sems,
            dma_sems(2, 2, experts - 1),
            dma_sems(2, 2, sub - 1),
            dma_sems(2),
            *move_scratch(sizes, moves),
        ],
        compiler_params=pltpu.CompilerParams(
            collective_id=number, has_side_effects=True, vmem_limit_bytes=VMEM_BYTES
        ),
        name=f"start_{number}",
    )(*arrays, pair, *[array for _, _, array, _ in moves])
    return results[:count], results[count], results[count + 1 :]


def landing_shapes(sizes, moves):
    return [
        jax.ShapeDtypeStruct(moved_shape(sizes, kind, array, wide), BF)
        for kind, _, array, wide in moves
    ]


def spread_shapes(sizes):
    experts, sub, _, tp = sizes
    chips = sub * tp // 2
    return (2, 2, experts - 1), (2, experts, chips), (2, experts, chips)


def spread_sems(sizes):
    return [dma_sems(*shape) for shape in spread_shapes(sizes)]


def fact_shapes(sizes, shape):
    experts, sub, _, tp = sizes
    return jax.ShapeDtypeStruct((shape[0] * experts, shape[1] * sub * tp), F32)


def by_device(sizes, all_facts, shape):
    experts, sub, _, tp = sizes
    return all_facts.reshape(experts, shape[0], sub * tp, shape[1]).transpose(0, 2, 1, 3)


def exchange(sizes, parts, adds, put, scale, extra, tail, moves, number):
    experts, sub, ctx, tp = sizes
    chips = sub * tp // 2
    count = len(parts)
    rows, width = parts[0].shape
    tokens, feats = adds[0].shape
    each, chunks = rows // experts, count * experts
    vmem, anywhere = (pl.BlockSpec(memory_space=m) for m in (pltpu.VMEM, pl.ANY))
    if put is None:
        put = jnp.zeros((8, 128), BF)
    fact_shape = (8, tokens) if tail == "slots" else extra[0].shape
    outs, scratch, extra_specs = [], [], [vmem] * len(extra)
    if tail == "slots":
        picks = extra[0].shape[1]
        outs = [jax.ShapeDtypeStruct((picks, width), BF)]
        scratch = [pltpu.VMEM((picks, feats), BF), pltpu.VMEM(fact_shape, F32)]
        scratch += spread_sems(sizes)
    elif tail == "tokens":
        outs = [fact_shapes(sizes, (8, feats))]
        outs += [jax.ShapeDtypeStruct((tokens // sub, width), BF)] * (len(extra) - 1)
        scratch = [pltpu.VMEM((tokens, feats), BF), pltpu.VMEM((8, feats), F32)]
        scratch += spread_sems(sizes)
        scratch += [dma_sems(2, chips - 1), dma_sems(2, chips)] * (len(extra) - 1)
    if tail != "slots":
        extra_specs[0] = anywhere
    results = pl.pallas_call(
        partial(
            exchange_kernel,
            sizes,
            tail,
            count,
            len(extra),
            [(kind, cuts) for kind, cuts, _, _ in moves],
        ),
        out_shape=[
            *[jax.ShapeDtypeStruct((tokens, feats), F32)] * count,
            fact_shapes(sizes, fact_shape),
            *outs,
            *landing_shapes(sizes, moves),
        ],
        in_specs=[vmem] * (2 * count + 2) + extra_specs + [anywhere] * len(moves),
        out_specs=[vmem] * count + [anywhere] * (1 + len(outs) + len(moves)),
        scratch_shapes=[
            *[pltpu.VMEM((experts, each, feats), BF)] * count,
            dma_sems(1 + max(len(extra), 2)),
            *spread_sems(sizes),
            pltpu.VMEM((chunks, 4, each, feats), BF),
            pltpu.VMEM((chunks, 4, each // 2, feats), BF),
            pltpu.VMEM((chunks, 4, each // 2, feats), BF),
            pltpu.VMEM((chunks, 2, each // 2, feats), BF),
            pltpu.VMEM((chunks, 2, each // 2, feats), BF),
            pltpu.VMEM((chunks, each, feats), BF),
            dma_sems(2, chunks, 4),
            dma_sems(2, chunks, 4),
            dma_sems(2, chunks, 2),
            dma_sems(2, chunks),
            *scratch,
            *move_scratch(sizes, moves),
        ],
        compiler_params=pltpu.CompilerParams(
            collective_id=number, has_side_effects=True, vmem_limit_bytes=VMEM_BYTES
        ),
        name=f"exchange_{number}",
    )(*parts, *adds, put, scale, *extra, *[array for _, _, array, _ in moves])
    raws, (all_facts, *results) = results[:count], results[count:]
    outs, moved = results[: len(outs)], results[len(outs) :]
    return raws, outs, by_device(sizes, all_facts, fact_shape), moved


def finish(sizes, plus, product, unit, next_put, moves, number):
    experts, sub, ctx, tp = sizes
    layer = sub * tp
    tokens, feats = plus.shape
    picks = next_put.shape[1]
    vmem, anywhere = (pl.BlockSpec(memory_space=m) for m in (pltpu.VMEM, pl.ANY))
    raw, out, *moved = pl.pallas_call(
        partial(finish_kernel, sizes, [(kind, cuts) for kind, cuts, _, _ in moves]),
        out_shape=[
            jax.ShapeDtypeStruct((tokens, feats), F32),
            jax.ShapeDtypeStruct((picks, feats * layer), BF),
            *landing_shapes(sizes, moves),
        ],
        in_specs=[vmem] * 4 + [anywhere] * len(moves),
        out_specs=[vmem] + [anywhere] * (1 + len(moves)),
        scratch_shapes=[
            pltpu.VMEM((8, tokens), F32),
            pltpu.VMEM((layer - 1, 8, tokens), F32),
            pltpu.VMEM((picks, feats), BF),
            pltpu.SemaphoreType.DMA,
            dma_sems(2, layer - 1),
            *spread_sems(sizes),
            *move_scratch(sizes, moves),
        ],
        compiler_params=pltpu.CompilerParams(
            collective_id=number, has_side_effects=True, vmem_limit_bytes=VMEM_BYTES
        ),
        name=f"finish_{number}",
    )(plus, product, unit, next_put, *[array for _, _, array, _ in moves])
    return raw, out, moved


def parted(pick, table):
    total = None
    for _ in range(3):
        part = table.astype(BF)
        product = jnp.dot(pick, part, preferred_element_type=F32)
        total = product if total is None else total + product
        table = table - part.astype(F32)
    return total


def times(left, right):
    return jnp.dot(left, right, preferred_element_type=F32)


def times_turned(left, right):
    return lax.dot_general(left, right, (((1,), (1,)), ((), ())), preferred_element_type=F32)


def one_hot(places, shape, axis):
    return (lax.broadcasted_iota(jnp.int32, shape, axis).astype(F32) == places).astype(BF)


def allowed_keys(position, span, spans):
    shape = (position.shape[0], spans.shape[1])
    keys = lax.broadcasted_iota(jnp.int32, shape, 1).astype(F32)
    return (keys <= position) | ((span == spans) & (span > 0))


def softmax_rows(scores, allowed):
    scores = jnp.where(allowed, scores, -1e30)
    expo = jnp.exp(scores - jnp.max(scores, axis=-1, keepdims=True))
    return expo / jnp.sum(expo, axis=-1, keepdims=True)


def head_columns(head):
    return pl.ds(head * HD, HD)


def turn_heads(rows, cosine, sine):
    parts = []
    for head in range(rows.shape[1] // HD):
        u = rows[:, head * HD : (head + 1) * HD]
        parts.append(u * cosine + pltpu.roll(u, HD // 2, 1) * sine)
    return jnp.concatenate(parts, axis=1)


def turn_heads_back(rows, cosine, sine):
    parts = []
    for head in range(rows.shape[1] // HD):
        u = rows[:, head * HD : (head + 1) * HD]
        parts.append(u * cosine + pltpu.roll(u * sine, HD // 2, 1))
    return jnp.concatenate(parts, axis=1)


def attend_kernel(
    experts,
    x_ref,
    gain_ref,
    query_ref,
    key_value_ref,
    route_ref,
    rows_ref,
    hits_ref,
    cosine_ref,
    sine_ref,
    mine_ref,
    h1_ref,
    slots_ref,
    queries_ref,
    keys_ref,
    values_ref,
    mixed_ref,
    gates_ref,
    tables_ref,
):
    seq_len = x_ref.shape[0]
    cap = slots_ref.shape[0]
    wide = query_ref.shape[1]
    x = x_ref[...].astype(F32)
    scale_in = lax.rsqrt(jnp.mean(x * x, axis=1, keepdims=True) + EPS)
    h1 = (x * scale_in * gain_ref[...]).astype(BF)
    h1_ref[...] = h1
    cosine, sine = cosine_ref[...], sine_ref[...]
    kv = times(h1, key_value_ref[...])
    keys_ref[...] = turn_heads(kv[:, :wide], cosine, sine).astype(BF)
    values_ref[...] = kv[:, wide:].astype(BF)
    logits = times(h1, route_ref[...])
    hits = hits_ref[...]
    lane = lax.broadcasted_iota(jnp.int32, hits.shape, 1)
    chosen = (hits > 0) & (lane < experts)
    top = jnp.max(jnp.where(chosen, logits, -1e30), axis=1, keepdims=True)
    raised = jnp.where(chosen, jnp.exp(jnp.minimum(logits - top, 0.0)), 0.0)
    gates = raised / jnp.sum(raised, axis=1, keepdims=True)
    gates_ref[...] = gates
    pick = one_hot(rows_ref[0, 0:1], (cap, seq_len), 0)
    slots = times(pick, h1).astype(BF)
    slots_ref[...] = slots
    row = lax.broadcasted_iota(jnp.int32, hits.shape, 0).astype(F32)
    gate_mine = jnp.sum(gates * mine_ref[...], axis=1, keepdims=True)
    facts = jnp.where(lane == 0, gate_mine, jnp.where(lane == 1, row, hits))
    tables = parted(pick, jnp.concatenate([cosine, sine, facts], axis=1))
    tables_ref[...] = tables
    queries = turn_heads(times(slots, query_ref[...]), tables[:, :HD], tables[:, HD : 2 * HD])
    queries_ref[...] = queries.astype(BF)
    at = 2 * HD
    allowed = allowed_keys(
        tables[:, at + 1 : at + 2], tables[:, at + experts : at + experts + 1], rows_ref[0, 1:2]
    )
    for head in range(wide // HD):
        part = head_columns(head)
        scores = times_turned(queries_ref[:, part], keys_ref[:, part]) * HD**-0.5
        probs = softmax_rows(scores, allowed).astype(BF)
        mixed_ref[:, part] = times(probs, values_ref[:, part]).astype(BF)


def attend(experts, seqs, x, gain, query, key_value, route, rows, hits, cosine, sine, mine):
    total, width = x.shape
    seq_len = total // seqs
    cap = 2 * seq_len // experts
    wide = query.shape[1]

    def each(*shape):
        zeros = (0,) * (len(shape) - 1)
        return pl.BlockSpec(shape, lambda s: (s, *zeros))

    def whole(array):
        zeros = (0,) * array.ndim
        return pl.BlockSpec(array.shape, lambda s: zeros)

    def out(rows, columns, dtype):
        return jax.ShapeDtypeStruct((seqs * rows, columns), dtype)

    return pl.pallas_call(
        partial(attend_kernel, experts),
        grid=(seqs,),
        in_specs=[
            each(seq_len, width),
            whole(gain),
            whole(query),
            whole(key_value),
            whole(route),
            each(1, 8, seq_len),
            each(seq_len, HD),
            whole(cosine),
            whole(sine),
            whole(mine),
        ],
        out_specs=[
            each(seq_len, width),
            each(cap, width),
            each(cap, wide),
            each(seq_len, wide),
            each(seq_len, wide),
            each(cap, wide),
            each(seq_len, HD),
            each(cap, 3 * HD),
        ],
        out_shape=[
            out(seq_len, width, BF),
            out(cap, width, BF),
            out(cap, wide, BF),
            out(seq_len, wide, BF),
            out(seq_len, wide, BF),
            out(cap, wide, BF),
            out(seq_len, HD, F32),
            out(cap, 3 * HD, F32),
        ],
        compiler_params=pltpu.CompilerParams(vmem_limit_bytes=LOCAL_VMEM_BYTES),
        cost_estimate=pl.CostEstimate(
            flops=2 * total * width * (3 * wide + seq_len // 2),
            bytes_accessed=6 * total * width,
            transcendentals=total * seq_len,
        ),
        name="attend",
    )(x, gain, query, key_value, route, rows, hits, cosine, sine, mine)


def attend_back_kernel(
    experts,
    grad_ref,
    out_ref,
    query_ref,
    key_value_ref,
    rows_ref,
    hits_ref,
    cosine_ref,
    sine_ref,
    queries_ref,
    keys_ref,
    values_ref,
    mixed_ref,
    tables_ref,
    grad_query_ref,
    grad_kv_ref,
    grad_branch_ref,
    gate_ref,
    first_ref,
):
    seq_len, wide = keys_ref.shape
    cap = queries_ref.shape[0]
    tables = tables_ref[...]
    at = 2 * HD
    gate = tables[:, at : at + 1]
    allowed = allowed_keys(
        tables[:, at + 1 : at + 2], tables[:, at + experts : at + experts + 1], rows_ref[0, 1:2]
    )
    grad = grad_ref[...]
    grad_branch_ref[...] = (grad.astype(F32) * gate).astype(BF)
    grad_mixed = times_turned(grad, out_ref[...])
    gates = jnp.sum(mixed_ref[...].astype(F32) * grad_mixed, axis=1, keepdims=True)
    gate_ref[...] = jnp.broadcast_to(gates, gate_ref.shape)
    grad_mixed = (grad_mixed * gate).astype(BF)
    grad_queries, grad_keys, grad_values = [], [], []
    for head in range(wide // HD):
        part = head_columns(head)
        queries, keys = queries_ref[:, part], keys_ref[:, part]
        own = grad_mixed[:, head * HD : (head + 1) * HD]
        probs = softmax_rows(times_turned(queries, keys) * HD**-0.5, allowed)
        grad_probs = times_turned(own, values_ref[:, part])
        grad_values.append(turned(probs.astype(BF), own))
        inner = jnp.sum(probs * grad_probs, axis=1, keepdims=True)
        grad_scores = (probs * (grad_probs - inner)).astype(BF)
        grad_queries.append(times(grad_scores, keys) * HD**-0.5)
        grad_keys.append(turned(grad_scores, queries) * HD**-0.5)
    grad_queries = jnp.concatenate(grad_queries, axis=1)
    grad_qpre = turn_heads_back(grad_queries, tables[:, :HD], tables[:, HD : 2 * HD]).astype(BF)
    grad_query_ref[...] = grad_qpre
    grad_keys = turn_heads_back(
        jnp.concatenate(grad_keys, axis=1), cosine_ref[...], sine_ref[...]
    )
    kv_low = jnp.concatenate([grad_keys, *grad_values], axis=1).astype(BF)
    grad_kv_ref[...] = kv_low
    taken = times_turned(grad_qpre, query_ref[...]).astype(BF)
    give = one_hot(hits_ref[:, experts + 1 : experts + 2], (seq_len, cap), 1)
    first = times_turned(kv_low, key_value_ref[...]) + times(give, taken)
    first_ref[...] = first.astype(BF)


def attend_back(
    experts, seqs, grad, out, query, key_value, rows, hits, cosine, sine, saved
):
    queries, keys, values, mixed, tables = saved
    width = grad.shape[1]
    cap = grad.shape[0] // seqs
    total, wide = keys.shape
    seq_len = total // seqs

    def each(*shape):
        zeros = (0,) * (len(shape) - 1)
        return pl.BlockSpec(shape, lambda s: (s, *zeros))

    def whole(array):
        zeros = (0,) * array.ndim
        return pl.BlockSpec(array.shape, lambda s: zeros)

    def result(rows, columns, dtype):
        return jax.ShapeDtypeStruct((seqs * rows, columns), dtype)

    return pl.pallas_call(
        partial(attend_back_kernel, experts),
        grid=(seqs,),
        in_specs=[
            each(cap, width),
            whole(out),
            whole(query),
            whole(key_value),
            each(1, 8, seq_len),
            each(seq_len, HD),
            whole(cosine),
            whole(sine),
            each(cap, wide),
            each(seq_len, wide),
            each(seq_len, wide),
            each(cap, wide),
            each(cap, 3 * HD),
        ],
        out_specs=[
            each(cap, wide),
            each(seq_len, 2 * wide),
            each(cap, width),
            each(cap, HD),
            each(seq_len, width),
        ],
        out_shape=[
            result(cap, wide, BF),
            result(seq_len, 2 * wide, BF),
            result(cap, width, BF),
            result(cap, HD, F32),
            result(seq_len, width, BF),
        ],
        compiler_params=pltpu.CompilerParams(vmem_limit_bytes=LOCAL_VMEM_BYTES),
        cost_estimate=pl.CostEstimate(
            flops=2 * total * width * (3 * wide + seq_len // 2),
            bytes_accessed=6 * total * width,
            transcendentals=total * seq_len,
        ),
        name="attend_back",
    )(
        grad, out, query, key_value, rows, hits, cosine, sine, queries, keys, values, mixed, tables
    )


class Axes:
    def __init__(self, experts, shard, ctx, tp):
        self.experts = experts
        self.sub = shard * ctx // experts
        self.tp = tp
        if self.sub == ctx:
            self.layer, self.exp = (("ctx", "tp"), None), ("shard", None)
            self.part = ("ctx", None)
        else:
            devices = np.arange(shard * ctx * tp).reshape(experts, self.sub, tp)
            self.layer = (ALL, devices.reshape(experts, -1).tolist())
            self.exp = (ALL, devices.reshape(experts, -1).T.tolist())
            self.part = (ALL, devices.transpose(0, 2, 1).reshape(-1, self.sub).tolist())

    def swap(self, value, over):
        axes, groups = over
        return lax.all_to_all(value, axes, 0, 0, axis_index_groups=groups)


class Routing:
    def __init__(self, choice, seqs, seq_len, experts, cap, mine, own_first, own_seqs):
        columns = jnp.arange(experts, dtype=jnp.int32)
        hits = jnp.sum((choice[:, :, None] == columns[None, None, :]).astype(F32), axis=1)
        self.hits = hits.reshape(seqs, seq_len, experts)
        rows = jnp.arange(seq_len, dtype=jnp.int32)
        earlier = (rows[None, :] < rows[:, None]).astype(BF)
        before = dot("tu,sue->ste", earlier, self.hits.astype(BF))
        self.valid = self.hits * (before < cap).astype(F32)
        self.place = jnp.where(self.valid > 0, before, -1.0)
        self.cap = cap
        is_mine = (columns == mine).astype(F32)
        place_mine = jnp.sum(self.place * is_mine, axis=2)
        self.place_mine = place_mine
        slots = jnp.arange(cap, dtype=jnp.int32).astype(F32)
        self.is_mine = is_mine
        self.pick = (place_mine[:, None, :] == slots[None, :, None]).astype(BF)
        place_own = lax.dynamic_slice_in_dim(self.place, own_first, own_seqs, 0)
        place_own = place_own.transpose(1, 0, 2)[:, :, :, None]
        seq_of = jnp.arange(own_seqs, dtype=jnp.int32)
        here = place_own == slots
        same = (seq_of[:, None] == seq_of[None, :])[:, None, None, :, None]
        put = here.transpose(1, 0, 2, 3)[:, :, :, None, :] & same
        self.put = put.astype(BF).reshape(own_seqs * seq_len, experts * own_seqs * cap)

    def gates(self, logits):
        logits = logits.reshape(self.hits.shape)
        top = jnp.max(jnp.where(self.hits > 0, logits, -jnp.inf), axis=2, keepdims=True)
        raised = jnp.where(self.hits > 0, jnp.exp(logits - top), 0.0)
        return raised / jnp.sum(raised, axis=2, keepdims=True)

    def slot_gates(self, gates):
        gate_mine = jnp.sum(gates * self.is_mine, axis=2)
        return jnp.sum(self.pick.astype(F32) * gate_mine[:, None, :], axis=2)

    def take(self, rows):
        seqs, cap, seq_len = self.pick.shape
        picked = dot("spt,stf->spf", self.pick, rows.reshape(seqs, seq_len, -1))
        return picked.astype(BF).reshape(seqs * cap, -1)

    def give(self, slots):
        seqs, cap, seq_len = self.pick.shape
        rows = dot("spt,spf->stf", self.pick, slots.reshape(seqs, cap, -1))
        return rows.reshape(seqs * seq_len, -1)

    def token_grads(self, slot_grads):
        slots = jnp.arange(self.cap, dtype=jnp.int32).astype(F32)
        here = self.place[:, :, :, None] == slots[None, None, None, :]
        grads = slot_grads.transpose(1, 0, 2)[:, None, :, :]
        return jnp.sum(jnp.where(here, grads, 0.0), axis=3)


def put_home(put, home):
    return dot("tp,pf->tf", put, home.reshape(-1, home.shape[-1]))


def router_rows(grads, router):
    high = grads.astype(BF)
    low = (grads - high.astype(F32)).astype(BF)
    return dot(
        "te,fe->tf",
        jnp.concatenate([high, low], axis=1),
        jnp.concatenate([router, router], axis=1),
    )


def logit_grads(gates, gate_grads):
    mean = jnp.sum(gates * gate_grads, axis=2, keepdims=True)
    grads = gates * (gate_grads - mean)
    return grads.reshape(-1, grads.shape[-1])


def shards(
    sizes,
    hidden_in,
    att_choice,
    ffn_choice,
    span_ids,
    norm_att,
    router_att,
    w_query,
    w_out,
    w_key,
    w_value,
    norm_ffn,
    router_ffn,
    w_gate,
    w_up,
    w_down,
    cotangent,
):
    shard, ctx, tp = sizes
    experts = w_query.shape[0]
    axes = Axes(experts, shard, ctx, tp)
    sub = axes.sub
    group = experts * sub
    layer = sub * tp
    tokens, width = hidden_in.shape
    total = tokens * group
    seq_len = tokens * ctx
    seqs = total // seq_len
    own_seqs = seqs // experts
    own_tokens = own_seqs * seq_len
    cap = 2 * seq_len // experts
    slots = seqs * cap
    rows_own = width // group
    feats = width // layer
    sizes = (experts, sub, ctx, tp)
    kernels = feats % 128 == 0 and rows_own % 128 == 0 and tokens % 16 == 0
    group_at, tp_at = lax.axis_index(GROUP), lax.axis_index("tp")
    exp_at, sub_at = group_at // sub, group_at % sub
    layer_at = sub_at * tp + tp_at

    token_pack = jnp.concatenate(
        [att_choice, ffn_choice, span_ids[:, None]], axis=1
    ).astype(BF)
    feature_pack = jnp.concatenate(
        [norm_att[:, None], router_att, norm_ffn[:, None], router_ffn], axis=1
    )
    def everywhere(rows):
        quarter = width // tp
        part = lax.dynamic_slice_in_dim(rows, tp_at * quarter, quarter, 1)
        parts = lax.all_gather(part, ALL)
        return parts.reshape(group, tp, tokens, quarter).transpose(0, 2, 1, 3).reshape(total, width)

    def everywhere_layer(rows):
        parts = lax.all_gather(rows, ALL)
        return (
            parts.reshape(experts, layer, own_tokens, feats)
            .transpose(0, 2, 1, 3)
            .reshape(total, width)
        )

    def layer_sum(rows):
        m = rows.shape[0]
        parts = rows.astype(BF).reshape(m, layer, feats).transpose(1, 0, 2)
        parts = axes.swap(parts, axes.layer)
        return jnp.sum(parts.astype(F32), axis=0)

    def go_home(rows):
        return axes.swap(rows.astype(BF).reshape(experts, -1, feats), axes.exp)

    def to_tokens(rows):
        parts = axes.swap(rows.reshape(sub, tokens, feats), axes.part)
        parts = lax.all_gather(parts, "tp")
        return parts.transpose(2, 1, 0, 3).reshape(tokens, width)

    head_parts = math.gcd(sub, w_query.shape[2] // HD)
    copies = sub // head_parts
    heads_wide = w_query.shape[2] // head_parts
    hidden_local = w_gate.shape[2]
    hidden_wide = -(-hidden_local // (sub * 128)) * 128
    windows = sub == 2 and (hidden_local - hidden_wide) % 128 == 0
    hidden_pad = 0 if windows else hidden_wide * sub - hidden_local
    overlap = hidden_wide * sub - hidden_local if windows else 0
    hidden_rows = hidden_local // sub if windows else hidden_wide
    hidden_first = sub_at * (overlap // 2)
    hidden_at = jnp.arange(hidden_wide)
    hidden_mine = (hidden_at >= hidden_first) & (hidden_at < hidden_first + hidden_rows)
    kernels = kernels and windows and copies == 1 and sub == 2 and tp == 4 and experts == 4

    def to_windows(weight, axis):
        if windows:
            size = weight.shape[axis]
            parts = [
                lax.slice_in_dim(weight, 0, hidden_wide, axis=axis),
                lax.slice_in_dim(weight, size - hidden_wide, size, axis=axis),
            ]
        else:
            pad = [(0, 0)] * 3
            pad[axis] = (0, hidden_pad)
            parts = jnp.split(jnp.pad(weight, pad), sub, axis=axis)
        parts = jnp.stack(parts, axis=1)
        return parts.reshape(group, *parts.shape[2:])

    def to_heads(weight, axis):
        parts = jnp.stack(jnp.split(weight, head_parts, axis=axis), axis=1)
        return jnp.repeat(parts, copies, axis=1).reshape(group, *parts.shape[2:])

    def to_all(weight):
        return to_heads(jnp.broadcast_to(weight, (experts, *weight.shape)), 2)

    def swap_group(value):
        return lax.all_to_all(value, GROUP, 0, 0)

    def as_columns(parts):
        return parts.reshape(width, parts.shape[2])

    def as_rows(parts):
        return parts.transpose(1, 0, 2).reshape(parts.shape[1], width)

    pack = jnp.concatenate(
        [jnp.pad(facts.T, ((0, 16 - facts.shape[1]), (0, 0))) for facts in (token_pack, feature_pack)],
        axis=1,
    )
    if kernels:
        (packs, all_in, top_all), my_key_value, (my_query, my_out) = start(
            sizes,
            [pack, hidden_in, cotangent],
            jnp.stack([w_key, w_value]),
            [
                ("columns_out", ((0, heads_wide, False),), w_query, heads_wide),
                ("rows_out", ((0, heads_wide, True),), w_out, heads_wide),
            ],
            0,
        )
        packs = packs.reshape(group, 16, -1)
    else:
        packs = lax.all_gather(pack, GROUP)
        all_in, top_all = everywhere(hidden_in), everywhere(cotangent)
        first = [to_heads(w_query, 2), to_all(w_key), to_all(w_value), to_heads(w_out, 1)]
        first = swap_group(jnp.concatenate(first, axis=2))
        my_query = as_columns(first[:, :, :heads_wide])
        my_key_value = as_columns(first[:, :, heads_wide : 3 * heads_wide])
        my_out = as_rows(first[:, :, 3 * heads_wide :])
    packs = packs.transpose(0, 2, 1)
    token_facts = packs[:, :tokens].reshape(total, 16).astype(jnp.int32)
    feature_facts = packs[:, tokens:].reshape(width, 16)
    gain_att = feature_facts[:, 0].astype(F32)
    route_att = feature_facts[:, 1 : 1 + experts]
    gain_ffn = feature_facts[:, 1 + experts].astype(F32)
    route_ffn = feature_facts[:, 2 + experts : 2 + 2 * experts]

    def move(kind, weight):
        if kind == "columns_out":
            return as_columns(swap_group(to_windows(weight, 2)))
        if kind == "rows_out":
            if not windows:
                return as_rows(swap_group(to_windows(weight, 1)))
            parts = as_rows(swap_group(weight.reshape(group, hidden_rows, rows_own)))
            rows = jnp.zeros((hidden_wide, width), BF)
            return lax.dynamic_update_slice_in_dim(rows, parts, hidden_first, 0)
        if kind == "columns_home":
            return swap_group(weight.reshape(group, rows_own, -1))
        if windows:
            weight = lax.dynamic_slice_in_dim(weight, hidden_first, hidden_rows, 0)
        return swap_group(weight.reshape(-1, group, rows_own).transpose(1, 0, 2))

    def to_cuts(moves):
        return [
            (kind, ((0, early, False), (early, wide - early, True)), weight, wide)
            for kind, weight, wide, early in moves
        ]

    def to_slots(rows, next_put):
        picked = dot("tp,tf->pf", next_put, rows).astype(BF)
        picked = axes.swap(picked.reshape(experts, -1, feats), axes.exp)
        picked = lax.all_gather(
            picked.reshape(-1, feats), axes.layer[0], axis_index_groups=axes.layer[1]
        )
        return picked.transpose(1, 0, 2).reshape(-1, width)

    def exchanged(parts, adds, put, scale, extra, tail, moves, number):
        if kernels:
            return exchange(sizes, parts, adds, put, scale, extra, tail, to_cuts(moves), number)
        raws, outs = [], []
        for part, add in zip(parts, adds):
            home = go_home(layer_sum(part))
            summed = jnp.sum(home.astype(F32), axis=0) if put is None else put_home(put, home)
            raws.append(add + summed)
        raw = raws[0]
        if tail == "slots":
            next_put, linear, square = extra
            outs = [to_slots(raw.astype(BF), next_put)]
            facts = dot_exact("ef,tf->et", linear, raw) + dot_exact("ef,tf->et", square, raw * raw)
        else:
            facts = extra[0]
        told = lax.all_gather(facts, ALL).reshape(experts, layer, *facts.shape)
        if tail == "tokens":
            columns = jnp.broadcast_to(jnp.sum(raw * extra[1], axis=0, keepdims=True), (8, feats))
            columns = lax.all_gather(columns, ALL).reshape(experts, layer, 8, feats)
            columns = columns.transpose(0, 2, 1, 3).reshape(experts * 8, layer * feats)
            outs = [to_tokens(rows) for rows in ((raw * scale).astype(BF), *extra[2:])]
            outs.insert(0, columns)
        return raws, outs, told, [move(kind, weight) for kind, weight, _, _ in moves]

    def finished(plus, product, unit, next_put, moves, number):
        if kernels:
            return finish(sizes, plus, product, unit, next_put, to_cuts(moves), number)
        sums = lax.all_gather(jnp.sum(product, axis=1), ALL).reshape(experts, layer, own_tokens)
        mean = lax.dynamic_index_in_dim(jnp.sum(sums, axis=1), exp_at, 0, keepdims=False) / width
        raw = plus - unit * mean[:, None]
        moved = [move(kind, weight) for kind, weight, _, _ in moves]
        return raw, to_slots(raw.astype(BF), next_put), moved

    own_first = exp_at * own_seqs
    where = partial(
        Routing,
        seqs=seqs,
        seq_len=seq_len,
        experts=experts,
        cap=cap,
        mine=exp_at,
        own_first=own_first,
        own_seqs=own_seqs,
    )
    att = where(token_facts[:, 0:2])
    if copies > 1:
        turn = jnp.arange(seqs, dtype=jnp.int32) % copies == sub_at % copies
        att.pick = att.pick * turn.astype(BF)[:, None, None]
    ffn = where(token_facts[:, 2:4])
    spans = token_facts[:, 4].reshape(seqs, seq_len).astype(F32)
    cosine, sine = rope_tables(seq_len)

    my_gate = move("columns_out", after(w_gate, all_in))
    heads = heads_wide // HD
    scale = 1.0 / math.sqrt(HD)
    if kernels:
        att_rows = jnp.pad(jnp.stack([att.place_mine, spans], axis=1), ((0, 0), (0, 6), (0, 0)))
        att_hits = jnp.concatenate(
            [att.hits, spans[:, :, None], att.place_mine[:, :, None]], axis=2
        ).reshape(total, -1)
        att_hits = jnp.pad(att_hits, ((0, 0), (0, HD - att_hits.shape[1])))
        sine = sine * jnp.where(jnp.arange(HD) < HD // 2, -1.0, 1.0)
        h1, h1_slots, *saved, att_gates, att_tables = attend(
            experts,
            seqs,
            all_in,
            gain_att[None, :],
            my_query,
            my_key_value,
            jnp.pad(route_att, ((0, 0), (0, HD - experts))),
            att_rows,
            att_hits,
            cosine,
            sine,
            (jnp.arange(HD) == exp_at).astype(F32)[None, :],
        )
        mixed = saved[3]
        saved.append(att_tables)
        att_gates = att_gates[:, :experts].reshape(seqs, seq_len, experts)
        att_slot_gate = att_tables[:, 2 * HD : 2 * HD + 1]
    else:
        positions = jnp.arange(seq_len, dtype=jnp.int32).astype(F32)
        pick_f32 = att.pick.astype(F32)
        slot_position = jnp.sum(pick_f32 * positions[None, None, :], axis=2)
        slot_span = jnp.sum(pick_f32 * spans[:, None, :], axis=2)
        slot_cosine = dot_exact("spt,tf->spf", pick_f32, cosine)
        slot_sine = dot_exact("spt,tf->spf", pick_f32, sine)
        allowed = (positions[None, None, :] <= slot_position[:, :, None]) | (
            (slot_span[:, :, None] == spans[:, None, :]) & (slot_span[:, :, None] > 0)
        )
        x_all = all_in.astype(F32)
        scale_in = lax.rsqrt(jnp.mean(x_all * x_all, axis=1, keepdims=True) + EPS)
        h1 = (x_all * scale_in * gain_att[None, :]).astype(BF)
        kv = dot("td,dm->tm", h1, my_key_value)
        keys = rotate(
            kv[:, :heads_wide].reshape(seqs, seq_len, heads, HD),
            cosine[None, :, None, :],
            sine[None, :, None, :],
        ).astype(BF)
        values = kv[:, heads_wide:].astype(BF).reshape(seqs, seq_len, heads, HD)
        att_gates = att.gates(dot("td,de->te", h1, route_att))
        att_slot_gate = att.slot_gates(att_gates).reshape(slots, 1)
        h1_slots = att.take(h1)
        queries = rotate(
            dot("td,dm->tm", h1_slots, my_query).reshape(seqs, cap, heads, HD),
            slot_cosine[:, :, None, :],
            slot_sine[:, :, None, :],
        ).astype(BF)
        scores = dot("sqhd,skhd->shqk", queries, keys) * scale
        scores = jnp.where(allowed[:, None], scores, -1e30)
        expo = jnp.exp(scores - jnp.max(scores, axis=-1, keepdims=True))
        probs = expo / jnp.sum(expo, axis=-1, keepdims=True)
        probs_low = probs.astype(BF)
        mixed = dot("shqk,skhd->sqhd", probs_low, values).astype(BF).reshape(slots, heads_wide)
    branch_att = dot("cm,md->cd", mixed, my_out) * att_slot_gate
    own_at = (exp_at * own_tokens, layer_at * feats)
    own_in = lax.dynamic_slice(all_in, own_at, (own_tokens, feats)).astype(F32)
    own_gain_ffn = lax.dynamic_slice_in_dim(gain_ffn, layer_at * feats, feats, 0)
    own_route_ffn = lax.dynamic_slice_in_dim(
        route_ffn.astype(F32), layer_at * feats, feats, 0
    )
    linear = jnp.pad((own_route_ffn * own_gain_ffn[:, None]).T, ((0, 8 - experts), (0, 0)))
    square = (jnp.arange(8) == experts).astype(F32)[:, None] * jnp.ones((1, feats), F32)
    (mid,), (mid_slots,), ffn_facts, (my_up,) = exchanged(
        [after(branch_att.astype(BF), my_gate)],
        [own_in],
        att.put,
        jnp.ones((1, feats), F32),
        (ffn.put, linear, square),
        "slots",
        [("columns_out", w_up, hidden_wide, hidden_wide // 3)],
        1,
    )
    my_down = move("rows_out", after(w_down, mid_slots))

    ffn_facts = jnp.sum(ffn_facts, axis=1)
    scale_mid = lax.rsqrt(ffn_facts[:, experts].reshape(total, 1) / width + EPS)
    ffn_logits = ffn_facts[:, :experts].transpose(0, 2, 1).reshape(total, experts) * scale_mid
    ffn_gates = ffn.gates(ffn_logits)
    ffn_slot_gate = ffn.slot_gates(ffn_gates).reshape(slots, 1)
    mid_slots = mid_slots.astype(F32)
    scale_slots = lax.rsqrt(jnp.mean(mid_slots * mid_slots, axis=1, keepdims=True) + EPS)
    h2_slots = (mid_slots * scale_slots * gain_ffn[None, :]).astype(BF)
    pre_gate = dot("cd,df->cf", h2_slots, my_gate)
    pre_up = dot("cd,df->cf", h2_slots, my_up)
    sigma = jax.nn.sigmoid(pre_gate)
    swish = pre_gate * sigma
    hidden = jnp.where(hidden_mine, swish * pre_up, 0.0).astype(BF)

    top_slots = ffn.take(top_all)
    grad_branch = (top_slots.astype(F32) * ffn_slot_gate).astype(BF)
    grad_down_w = dot("cf,cd->fd", hidden, grad_branch).astype(BF)
    grad_down = move("rows_home", grad_down_w)
    my_down = after(my_down, grad_down_w)
    branch_ffn = dot("cf,fd->cd", hidden, my_down) * ffn_slot_gate
    grad_hidden = dot("cd,fd->cf", top_slots, my_down)
    ffn_gate_part = jnp.sum(hidden.astype(F32) * grad_hidden, axis=1)
    grad_hidden = jnp.where(hidden_mine, grad_hidden * ffn_slot_gate, 0.0)
    grad_pre_gate = (
        grad_hidden * pre_up * sigma * (1.0 + pre_gate * (1.0 - sigma))
    ).astype(BF)
    grad_pre_up = (grad_hidden * swish).astype(BF)
    ffn_taken = dot("cf,df->cd", grad_pre_gate, my_gate) + dot("cf,df->cd", grad_pre_up, my_up)
    grad_gate_w = dot("cd,cf->df", h2_slots, grad_pre_gate).astype(BF)
    grad_up_w = dot("cd,cf->df", h2_slots, grad_pre_up).astype(BF)
    gate_half = hidden_wide // 256 * 128

    def gate_facts(told):
        return jnp.sum(told, axis=1).reshape(experts, seqs, cap)

    (grad_second, own_out), _, ffn_told, (gate_first,) = exchanged(
        [after(ffn_taken.astype(BF), grad_up_w), branch_ffn.astype(BF)],
        [jnp.zeros((own_tokens, feats), F32), mid],
        ffn.put,
        jnp.ones((1, feats), F32),
        (ffn_gate_part.reshape(-1, 128),),
        None,
        [("columns_home", grad_gate_w[:, :gate_half], gate_half, 128)],
        2,
    )
    ffn_logit_grads = logit_grads(ffn_gates, ffn.token_grads(gate_facts(ffn_told)))
    own_ffn_logits = lax.dynamic_slice_in_dim(
        ffn_logit_grads, exp_at * own_tokens, own_tokens, 0
    )
    own_scale_mid = lax.dynamic_slice_in_dim(scale_mid, exp_at * own_tokens, own_tokens, 0)
    own_unit_mid = mid * own_scale_mid
    grad_second = grad_second + router_rows(own_ffn_logits, own_route_ffn)
    norm_ffn_part = jnp.sum(grad_second * own_unit_mid, axis=0)
    own_second = grad_second * own_gain_ffn[None, :] * own_scale_mid
    gate_rest = hidden_wide - gate_half
    up_early = 128
    grad_mid, mid_slots, (gate_second, up_first) = finished(
        lax.dynamic_slice(top_all, own_at, (own_tokens, feats)).astype(F32) + own_second,
        own_second * own_unit_mid,
        own_unit_mid,
        att.put,
        [
            ("columns_home", grad_gate_w[:, gate_half:], gate_rest, 128),
            ("columns_home", grad_up_w[:, :up_early], up_early, 0),
        ],
        5,
    )
    grad_gate = jnp.concatenate([gate_first, gate_second], axis=2)
    up_second = move("columns_home", after(grad_up_w[:, up_early:], mid_slots))

    def windows_home(back, axis):
        back = back.reshape(experts, sub, *back.shape[1:])
        parts = [lax.index_in_dim(back, i, 1, keepdims=False) for i in range(sub)]
        wide = parts[0].shape[axis]
        if wide * sub > hidden_local and windows:
            cut = partial(lax.slice_in_dim, axis=axis)
            parts = [
                cut(parts[0], 0, wide - overlap),
                cut(parts[0], wide - overlap, wide) + cut(parts[1], 0, overlap),
                cut(parts[1], overlap, wide),
            ]
        whole = jnp.concatenate(parts, axis=axis)
        return lax.slice_in_dim(whole, 0, hidden_local, axis=axis).astype(F32)

    grad_gate = windows_home(grad_gate, 2)
    grad_down = windows_home(after(grad_down, mid_slots), 1)
    mid_slots = after(mid_slots, grad_gate, grad_down)

    if copies > 1:
        mid_slots = mid_slots * jnp.repeat(turn, cap).astype(BF)[:, None]
    if kernels:
        grad_qpre, kv_low, grad_att_branch, att_gate_part, first_part = attend_back(
            experts,
            seqs,
            mid_slots,
            my_out,
            my_query,
            my_key_value,
            att_rows,
            att_hits,
            cosine,
            sine,
            saved,
        )
        att_gate_part = att_gate_part[:, 0]
    else:
        grad_mixed = dot("cd,md->cm", mid_slots, my_out)
        att_gate_part = jnp.sum(mixed.astype(F32) * grad_mixed, axis=1)
        grad_mixed = (grad_mixed * att_slot_gate).astype(BF).reshape(seqs, cap, heads, HD)
        grad_att_branch = (mid_slots.astype(F32) * att_slot_gate).astype(BF)
        grad_soft = dot("sqhd,skhd->shqk", grad_mixed, values)
        grad_values = dot("shqk,sqhd->skhd", probs_low, grad_mixed)
        grad_scores = (
            probs * (grad_soft - jnp.sum(probs * grad_soft, axis=-1, keepdims=True))
        ).astype(BF)
        grad_queries = dot("shqk,skhd->sqhd", grad_scores, keys) * scale
        grad_keys = dot("shqk,sqhd->skhd", grad_scores, queries) * scale
        grad_qpre = (
            rotate_back(grad_queries, slot_cosine[:, :, None, :], slot_sine[:, :, None, :])
            .astype(BF)
            .reshape(slots, heads_wide)
        )
        att_taken = dot("cm,dm->cd", grad_qpre, my_query)
        grad_kpre = rotate_back(
            grad_keys, cosine[None, :, None, :], sine[None, :, None, :]
        ).reshape(total, heads_wide)
        kv_low = jnp.concatenate([grad_kpre, grad_values.reshape(total, heads_wide)], axis=1)
        kv_low = kv_low.astype(BF)
        first_part = dot("tm,dm->td", kv_low, my_key_value) + att.give(att_taken.astype(BF))
    own_rows = lax.dynamic_slice_in_dim(all_in, exp_at * own_tokens, own_tokens, 0).astype(F32)
    own_scale_in = lax.rsqrt(jnp.mean(own_rows * own_rows, axis=1, keepdims=True) + EPS)
    own_gain_att = lax.dynamic_slice_in_dim(gain_att, layer_at * feats, feats, 0)
    grad_query_w = dot("cd,cm->dm", h1_slots, grad_qpre).astype(BF)
    grad_out_w = dot("cm,cd->md", mixed, grad_att_branch).astype(BF)
    grad_kv_w = dot("td,tm->dm", h1, kv_low).astype(BF)
    own_h2 = (own_unit_mid * own_gain_ffn[None, :]).astype(BF).astype(F32)
    gate_rows = slots // feats
    own_parts = jnp.concatenate(
        [
            att_gate_part.reshape(gate_rows, feats),
            norm_ffn_part[None],
            dot_exact("te,tf->ef", own_ffn_logits, own_h2),
        ],
        axis=0,
    )
    own_parts = jnp.pad(own_parts, ((0, -own_parts.shape[0] % 8), (0, 0)))
    own_unit_in = own_in * own_scale_in
    (grad_first,), tokens_out, told, (grad_out, grad_query, kv_first, kv_second) = exchanged(
        [after(first_part.astype(BF), up_second)],
        [jnp.zeros((own_tokens, feats), F32)],
        None,
        own_gain_att[None, :] * own_scale_in,
        (own_parts, own_unit_in, grad_mid.astype(BF), own_out.astype(BF)),
        "tokens",
        [
            ("rows_home", grad_out_w, heads_wide, heads_wide),
            ("columns_home", grad_query_w, heads_wide, heads_wide),
            ("columns_home", grad_kv_w[:, :heads_wide], heads_wide, 0),
            ("columns_home", grad_kv_w[:, heads_wide:], heads_wide, 0),
        ],
        3,
    )
    columns, first_tokens, mid_tokens, hidden_out = tokens_out
    att_logit_grads = logit_grads(
        att_gates, att.token_grads(gate_facts(told[:, :, :gate_rows]))
    )
    token_at = group_at * tokens
    rows_in = hidden_in.astype(F32)
    unit_in = lax.rsqrt(jnp.mean(rows_in * rows_in, axis=1, keepdims=True) + EPS)
    first_tokens = first_tokens.astype(F32) + router_rows(
        lax.dynamic_slice_in_dim(att_logit_grads, token_at, tokens, 0), route_att
    ) * (gain_att[None, :] * unit_in)
    unit_in = rows_in * unit_in
    grad_in = (
        mid_tokens.astype(F32)
        + first_tokens
        - unit_in * jnp.mean(first_tokens * unit_in, axis=1, keepdims=True)
    )


    def heads_home(back, axis):
        back = back.reshape(experts, head_parts, copies, *back.shape[1:])
        if copies > 1:
            back = jnp.sum(back.astype(F32), axis=2, keepdims=True)
        parts = [back[:, i, 0] for i in range(head_parts)]
        return jnp.concatenate(parts, axis=axis).astype(F32)

    def my_rows(table, axis):
        return lax.dynamic_slice_in_dim(table, group_at * rows_own, rows_own, axis)

    ffn_parts = jnp.sum(told[:, :, gate_rows : gate_rows + 1 + experts], axis=0)
    ffn_parts = my_rows(ffn_parts.transpose(1, 0, 2).reshape(1 + experts, width), 1)
    high = att_logit_grads.astype(BF)
    low = (att_logit_grads - high.astype(F32)).astype(BF)
    grad_router_att = dot("tf,te->fe", my_rows(h1, 1), jnp.concatenate([high, low], axis=1))
    grad_router_att = grad_router_att[:, :experts] + grad_router_att[:, experts:]
    norm_att = my_rows(jnp.sum(columns.reshape(experts, 8, width)[:, 0], axis=0), 0)
    norm_att = norm_att + jnp.sum(
        grad_router_att * my_rows(route_att, 0).astype(F32), axis=1
    ) / my_rows(gain_att, 0)
    grad_out = heads_home(grad_out, 1)
    grad_query = heads_home(grad_query, 2)
    grad_key, grad_value = (
        jnp.sum(heads_home(part, 2), axis=0) for part in (kv_first, kv_second)
    )
    return (
        hidden_out,
        grad_in,
        norm_att,
        grad_router_att,
        grad_query,
        grad_out,
        grad_key,
        grad_value,
        ffn_parts[0],
        ffn_parts[1:].T,
        grad_gate,
        windows_home(jnp.concatenate([up_first, up_second], axis=2), 2),
        grad_down,
    )


def solution(mesh):
    ctx, tp = mesh.shape["ctx"], mesh.shape["tp"]
    shard = mesh.shape["shard"]
    by_token, by_feature = P(GROUP, None), P(GROUP)
    columns, rows = P(None, GROUP, "tp"), P(None, "tp", GROUP)

    return jax.shard_map(
        partial(shards, (shard, ctx, tp)),
        mesh=mesh,
        in_specs=(
            by_token,
            by_token,
            by_token,
            P(GROUP),
            by_feature,
            by_token,
            columns,
            rows,
            P(GROUP, "tp"),
            P(GROUP, "tp"),
            by_feature,
            by_token,
            columns,
            columns,
            rows,
            by_token,
        ),
        out_specs=(
            by_token,
            by_token,
            by_feature,
            by_token,
            columns,
            rows,
            P(GROUP, "tp"),
            P(GROUP, "tp"),
            by_feature,
            by_token,
            columns,
            columns,
            rows,
        ),
        check_vma=False,
    )
```

```python
from functools import partial
import math

import numpy as np

import jax
import jax.numpy as jnp
from jax import lax
from jax.experimental import pallas as pl
from jax.experimental.pallas import tpu as pltpu
from jax.sharding import PartitionSpec as P

HD = 128
EPS = 1e-06
BF = jnp.bfloat16
F32 = jnp.float32
MESH = pl.DeviceIdType.MESH
VMEM_BYTES = 60 * 2**20
LOCAL_VMEM_BYTES = 56 * 2**20
GROUP = ("shard", "ctx")
ALL = ("shard", "ctx", "tp")


def dot(spec, left, right):
    return jnp.einsum(spec, left, right, preferred_element_type=F32)


def dot_exact(spec, left, right):
    return jnp.einsum(
        spec, left, right, preferred_element_type=F32, precision=lax.Precision.HIGHEST
    )


def after(value, *others):
    return lax.optimization_barrier((value, *others))[0]


def rope_tables(count):
    half_dim = HD // 2
    freq_index = (jnp.arange(HD) % half_dim).astype(F32)
    frequency = 10000.0 ** (-2.0 * freq_index / HD)
    angles = jnp.arange(count, dtype=F32)[:, None] * frequency[None, :]
    return jnp.cos(angles), jnp.sin(angles)


def rotate(rows, cosine, sine):
    half_dim = HD // 2
    turned = jnp.concatenate([-rows[..., half_dim:], rows[..., :half_dim]], axis=-1)
    return rows * cosine + turned * sine


def rotate_back(rows, cosine, sine):
    half_dim = HD // 2
    turned = rows * sine
    return rows * cosine + jnp.concatenate(
        [turned[..., half_dim:], -turned[..., :half_dim]], axis=-1
    )


class Place:
    def __init__(self, sizes):
        self.experts, self.sub, self.ctx, self.tp = sizes
        self.chips = self.sub * self.tp // 2
        self.members = self.experts * self.sub
        self.group = lax.axis_index(GROUP)
        self.tp_at = lax.axis_index("tp")
        self.exp = self.group // self.sub
        here = (self.group % self.sub) * self.tp + self.tp_at
        self.chip, self.core = here // 2, here % 2

    def device(self, exp, chip, core):
        here = chip * 2 + core
        group = exp * self.sub + here // self.tp
        return (group // self.ctx, group % self.ctx, here % self.tp)

    def member(self, group):
        return (group // self.ctx, group % self.ctx, self.tp_at)

    def sibling(self):
        return self.device(self.exp, self.chip, 1 - self.core)

    def other_exp(self, k):
        return (self.exp + k) % self.experts

    def other_chip(self, k):
        return (self.chip + k) % self.chips

    def meet(self, whole_group):
        barrier = pltpu.get_barrier_semaphore()
        layer = 2 * self.chips
        here = self.chip * 2 + self.core
        others = [(here + k) % layer for k in range(1, layer)]
        peers = [self.device(self.exp, there // 2, there % 2) for there in others]
        if whole_group:
            peers += [
                self.member((self.group + k) % self.members) for k in range(1, self.members)
            ]
        else:
            peers += [
                self.device(self.other_exp(k), self.chip, self.core)
                for k in range(1, self.experts)
            ]
        for peer in peers:
            pl.semaphore_signal(barrier, inc=1, device_id=peer, device_id_type=MESH)
        pl.semaphore_wait(barrier, len(peers))


def block(start, size, unit):
    return pl.ds(pl.multiple_of(start, unit), size)


def send(src, dst, sems, at, device):
    copy = pltpu.make_async_remote_copy(
        src_ref=src,
        dst_ref=dst,
        send_sem=sems.at[(0, *at)],
        recv_sem=sems.at[(1, *at)],
        device_id=device,
        device_id_type=MESH,
    )
    copy.start()
    return copy


class Mover:
    def __init__(self, number, kind, cuts, src, dst, sems, own_sems):
        self.number, self.kind, self.cuts = number, kind, cuts
        self.src, self.dst, self.sems, self.own_sems = src, dst, sems, own_sems
        self.copies = []

    def ends(self, place, group, low, size):
        exp, sub = group // place.sub, group % place.sub
        me, src, dst = place.group, self.src, self.dst
        if self.kind == "columns_out":
            rows, step = src.shape[1], (src.shape[2] - dst.shape[1]) // max(place.sub - 1, 1)
            return (
                src.at[exp, :, block(sub * step + low, size, 128)],
                dst.at[block(me * rows, rows, 16), pl.ds(low, size)],
            )
        if self.kind == "rows_out":
            cols, step = src.shape[2], (src.shape[1] - dst.shape[0]) // max(place.sub - 1, 1)
            return (
                src.at[exp, block(sub * step + low, size, 16)],
                dst.at[pl.ds(low, size), block(me * cols, cols, 128)],
            )
        if self.kind == "columns_home":
            rows = dst.shape[1]
            return (
                src.at[block(group * rows, rows, 16), pl.ds(low, size)],
                dst.at[me, :, pl.ds(low, size)],
            )
        cols = dst.shape[2]
        return (
            src.at[pl.ds(low, size), block(group * cols, cols, 128)],
            dst.at[me, pl.ds(low, size)],
        )

    def start(self, place, late):
        for cut, (low, size, is_late) in enumerate(self.cuts):
            if is_late != late or not size:
                continue
            for k in range(1, place.members):
                group = (place.group + k) % place.members
                src, dst = self.ends(place, group, low, size)
                at = (self.number, cut, k - 1)
                self.copies.append(send(src, dst, self.sems, at, place.member(group)))
            src, dst = self.ends(place, place.group, low, size)
            own = pltpu.make_async_copy(src, dst, self.own_sems.at[self.number, cut])
            own.start()
            self.copies.append(own)

    def wait(self):
        for copy in self.copies:
            copy.wait()


def moved_shape(sizes, kind, array, wide):
    experts, sub, _, _ = sizes
    group = experts * sub
    if kind == "columns_out":
        return (array.shape[1] * group, wide)
    if kind == "rows_out":
        return (wide, array.shape[2] * group)
    if kind == "columns_home":
        return (group, array.shape[0] // group, array.shape[1])
    return (group, array.shape[0], array.shape[1] // group)


class Line:
    def __init__(self, place, spot, sems):
        self.place, self.spot, self.sems = place, spot, sems

    def give(self, src, origin, up, step):
        place = self.place
        to = place.exp + 1 if up else place.exp - 1
        return pltpu.make_async_remote_copy(
            src_ref=src,
            dst_ref=self.spot(origin),
            send_sem=self.sems.at[0, 0 if up else 1, step],
            recv_sem=self.sems.at[1, 0 if up else 1, step],
            device_id=place.device(to, place.chip, place.core),
            device_id_type=MESH,
        )

    def start(self, src):
        place = self.place
        self.src = src

        @pl.when(place.exp < place.experts - 1)
        def _():
            self.give(src, place.exp, True, 0).start()

        @pl.when(place.exp > 0)
        def _():
            self.give(src, place.exp, False, 0).start()

    def origin(self, turn):
        place = self.place
        if place.experts != 4:
            return (place.exp + place.experts - turn) % place.experts
        high = place.exp // 2
        at = place.exp * (1 - high) + (3 - place.exp) * high
        origin = 1 - at if turn == 1 else turn
        return origin * (1 - high) + (3 - origin) * high

    def arrived(self, turn):
        place = self.place
        origin = self.origin(turn)

        @pl.when(origin < place.exp)
        def _():
            step = place.exp - origin - 1
            self.give(self.spot(origin), origin, True, step).wait_recv()

            @pl.when(place.exp < place.experts - 1)
            def _():
                self.give(self.spot(origin), origin, True, step + 1).start()

        @pl.when(origin > place.exp)
        def _():
            step = origin - place.exp - 1
            self.give(self.spot(origin), origin, False, step).wait_recv()

            @pl.when(place.exp > 0)
            def _():
                self.give(self.spot(origin), origin, False, step + 1).start()

        return origin

    def finish(self):
        place = self.place
        for step in range(place.experts - 1):

            @pl.when((place.exp < place.experts - 1) & (place.exp >= step))
            def _():
                self.give(self.src, place.exp, True, step).wait_send()

            @pl.when((place.exp > 0) & (place.exp + step < place.experts))
            def _():
                self.give(self.src, place.exp, False, step).wait_send()


class Spread:
    def __init__(self, place, mine, out, by_token, exp_sems, chip_sems, core_sems, pieces=1):
        self.place, self.mine, self.out, self.by_token = place, mine, out, by_token
        self.rows, self.cols = mine.shape[0] // pieces, mine.shape[1]
        self.pieces = pieces
        self.exp_sems, self.chip_sems, self.core_sems = exp_sems, chip_sems, core_sems
        self.square = place.chips == 4 and place.tp == 4 and self.rows % 64 == 0
        self.line = None
        if pieces == 1 and self.rows % 64 == 0:
            self.line = Line(place, lambda origin: self.spot(origin, place.chip), exp_sems)

    def spot(self, exp, chip, low=0, size=None):
        place = self.place
        here = chip * 2 + place.core
        if self.by_token:
            row = (exp * place.sub + here // place.tp) * self.rows
            col = (here % place.tp) * self.cols
        else:
            row, col = exp * self.rows, here * self.cols
        unit = math.gcd(self.rows, 16)
        size = size or self.rows
        return self.out.at[block(row + low, size, unit), block(col, self.cols, 128)]

    def piece(self, exp):
        if self.pieces == 1:
            return self.mine
        return self.mine.at[block(exp * self.rows, self.rows, 16)]

    def near(self):
        place = self.place
        side = place.chip // 2
        along = place.chip % 2
        return [(1 - side) * 2 + along, side * 2 + 1 - along]

    def to_chip(self, src, dst, turn, k, chip):
        device = self.place.device(self.place.exp, chip, self.place.core)
        self.chip_copies[turn].append(send(src, dst, self.chip_sems, (turn, k), device))

    def to_chips(self, exp, src, turn):
        place = self.place
        if self.square:
            chips = self.near()
        else:
            chips = [place.other_chip(k) for k in range(1, place.chips)]
        for k, chip in enumerate(chips):
            self.to_chip(src, self.spot(exp, place.chip), turn, k, chip)

    def to_core(self, exp, chip, src, turn, k):
        self.core_copies.append(
            send(src, self.spot(exp, chip), self.core_sems, (turn, k), self.place.sibling())
        )

    def start(self, own_sem):
        place = self.place
        home = self.spot(place.exp, place.chip)
        mine = self.piece(place.exp)
        self.own = pltpu.make_async_copy(mine, home, own_sem)
        self.own.start()
        self.chip_copies = [[] for _ in range(place.experts)]
        self.core_copies = []
        if self.line:
            self.line.start(mine)
        else:
            self.exp_copies = [
                send(
                    self.piece(place.other_exp(k)),
                    home,
                    self.exp_sems,
                    (0, k - 1),
                    place.device(place.other_exp(k), place.chip, place.core),
                )
                for k in range(1, place.experts)
            ]
        self.to_chips(place.exp, mine, 0)
        self.to_core(place.exp, place.chip, mine, 0, 0)

    def from_layer(self, turn):
        place = self.place
        if self.line:
            source = self.line.arrived(turn)
        else:
            self.exp_copies[turn - 1].wait_recv()
            source = (place.exp + place.experts - turn) % place.experts
        self.sources[turn] = source
        here = self.spot(source, place.chip)
        self.to_chips(source, here, turn)
        self.to_core(source, place.chip, here, turn, 0)

    def from_near(self, turn):
        source, copies = self.sources[turn], self.chip_copies[turn]
        if not self.square:
            return
        half = self.rows // 2
        side, along = self.near()
        copies[0].wait_recv()
        part = self.spot(source, side, 0, half)
        self.to_chip(part, part, turn, 2, along)
        self.to_core(source, side, self.spot(source, side), turn, 1)
        copies[1].wait_recv()
        part = self.spot(source, along, half, half)
        self.to_chip(part, part, turn, 3, side)
        self.to_core(source, along, self.spot(source, along), turn, 2)

    def from_far(self, turn):
        place = self.place
        source, copies = self.sources[turn], self.chip_copies[turn]
        if self.square:
            copies[2].wait_recv()
            copies[3].wait_recv()
            far = 3 - place.chip
            self.to_core(source, far, self.spot(source, far), turn, 3)
            return
        for k in range(1, place.chips):
            copies[k - 1].wait_recv()
            chip = (place.chip + place.chips - k) % place.chips
            self.to_core(source, chip, self.spot(source, chip), turn, k)

    def run(self):
        for stage in range(self.place.experts + 1):
            self.step(stage)
        self.finish()

    def step(self, stage):
        experts = self.place.experts
        if stage == 0:
            self.sources = {0: self.place.exp}
        if 1 <= stage + 1 < experts:
            self.from_layer(stage + 1)
        if 0 <= stage < experts:
            self.from_near(stage)
        if 0 <= stage - 1 < experts:
            self.from_far(stage - 1)

    def finish(self):
        for copy in self.core_copies:
            copy.wait()
        if self.line:
            self.line.finish()
        else:
            for copy in self.exp_copies:
                copy.wait_send()
        for copies in self.chip_copies:
            for copy in copies:
                copy.wait_send()
        self.own.wait()


class Pair:
    def __init__(self, place, src, out, line_sems, sems, own_sems):
        self.place, self.src, self.out, self.sems, self.own_sems = place, src, out, sems, own_sems
        self.rows = src.shape[1]
        self.half = src.shape[2] // place.sub
        size = self.rows * place.sub

        def spot(exp):
            return out.at[block(exp * size, size, 16)]

        self.line = Line(place, spot, line_sems)

    def start(self):
        place = self.place
        land = block(place.group * self.rows, self.rows, 16)
        sub = place.group % place.sub
        self.copies = []
        for i in range(2):
            dst = self.out.at[land, pl.ds(i * self.half, self.half)]
            for k in range(1, place.sub):
                other = (sub + k) % place.sub
                src = self.src.at[i, :, block(other * self.half, self.half, 128)]
                group = place.exp * place.sub + other
                self.copies.append(send(src, dst, self.sems, (i, k - 1), place.member(group)))
            src = self.src.at[i, :, block(sub * self.half, self.half, 128)]
            own = pltpu.make_async_copy(src, dst, self.own_sems.at[i])
            own.start()
            self.copies.append(own)

    def share(self):
        for copy in self.copies:
            copy.wait()
        self.line.start(self.line.spot(self.place.exp))

    def step(self, stage):
        if stage + 1 < self.place.experts:
            self.line.arrived(stage + 1)

    def finish(self):
        self.line.finish()


class ToTokens:
    def __init__(self, place, mine, out, chip_sems, core_sems):
        self.place, self.mine, self.out = place, mine, out
        self.chip_sems, self.core_sems = chip_sems, core_sems
        self.rows, self.cols = out.shape[0], mine.shape[1]

    def spot(self, chip):
        here = chip * 2 + self.place.core
        return self.out.at[:, block(here * self.cols, self.cols, 128)]

    def part(self, chip):
        sub = (chip * 2) // self.place.tp
        return self.mine.at[block(sub * self.rows, self.rows, 16)]

    def start(self, own_sem):
        place = self.place
        mine = self.part(place.chip)
        self.own = pltpu.make_async_copy(mine, self.spot(place.chip), own_sem)
        self.own.start()
        self.copies = []
        for k in range(1, place.chips):
            chip = place.other_chip(k)
            self.copies.append(
                send(
                    self.part(chip),
                    self.spot(place.chip),
                    self.chip_sems,
                    (k - 1,),
                    place.device(place.exp, chip, place.core),
                )
            )
        self.core = [send(mine, self.spot(place.chip), self.core_sems, (0,), place.sibling())]

    def run(self):
        place, core, copies = self.place, self.core, self.copies
        for k in range(1, place.chips):
            copies[k - 1].wait_recv()
            spot = self.spot((place.chip + place.chips - k) % place.chips)
            core.append(send(spot, spot, self.core_sems, (k,), place.sibling()))
        for copy in core:
            copy.wait()
        for copy in copies:
            copy.wait_send()
        self.own.wait()


class Fold:
    def __init__(self, place, parts, homes, scratch):
        self.place, self.parts, self.homes = place, parts, homes
        (
            self.core_got,
            self.chip_out,
            self.chip_got,
            self.turn_out,
            self.turn_got,
            self.exp_out,
            self.core_sems,
            self.chip_sems,
            self.turn_sems,
            self.exp_sems,
        ) = scratch
        self.each, self.feats = homes[0].shape[1:]
        side, along = place.chip // 2, place.chip % 2
        self.chips = [
            place.chip,
            (1 - side) * 2 + along,
            side * 2 + 1 - along,
            (1 - side) * 2 + 1 - along,
        ]

    def rows(self, chunk):
        return (self.place.exp + 1 + chunk % self.place.experts) % self.place.experts * self.each

    def mine(self, chunk, to, low, size):
        place = self.place
        col = (self.chips[to] * 2 + place.core) * self.feats
        rows = block(self.rows(chunk) + low, size, 16)
        part = self.parts[chunk // place.experts][rows, block(col, self.feats, 128)]
        return part.astype(F32) + self.core_got[chunk, to, low : low + size].astype(F32)

    def between_cores(self, chunk):
        place = self.place
        part = self.parts[chunk // place.experts]
        rows = block(self.rows(chunk), self.each, 16)
        copies = []
        for to in (1, 2, 3, 0):
            col = (self.chips[to] * 2 + 1 - place.core) * self.feats
            src = part.at[rows, block(col, self.feats, 128)]
            dst = self.core_got.at[chunk, to]
            copies.append(send(src, dst, self.core_sems, (chunk, to), place.sibling()))
        return copies

    def over(self, to, src, dst, sems, at):
        place = self.place
        return send(src, dst, sems, at, place.device(place.exp, self.chips[to], place.core))

    def first_hops(self, chunk, core):
        half = self.each // 2
        for copy in core:
            copy.wait_recv()
        copies = []
        for near, low in ((1, 0), (2, half)):
            for slot, to in enumerate((near, 3)):
                at = 2 * (near - 1) + slot
                out = self.chip_out.at[chunk, at]
                out[...] = self.mine(chunk, to, low, half).astype(BF)
                got = self.chip_got.at[chunk, at]
                copies.append(self.over(near, out, got, self.chip_sems, (chunk, at)))
        return copies

    def second_hops(self, chunk, first):
        half = self.each // 2
        copies = []
        for near, far, low in ((1, 2, 0), (2, 1, half)):
            at = 2 * (near - 1)
            first[at].wait_recv()
            first[at + 1].wait_recv()
            out = self.turn_out.at[chunk, near - 1]
            got = self.chip_got[chunk, at + 1].astype(F32)
            out[...] = (self.mine(chunk, far, low, half) + got).astype(BF)
            got = self.turn_got.at[chunk, near - 1]
            copies.append(self.over(far, out, got, self.turn_sems, (chunk, near - 1)))
        return copies

    def go_home(self, chunk, second):
        place = self.place
        half = self.each // 2
        for near, low in ((1, 0), (2, half)):
            second[near - 1].wait_recv()
            total = self.mine(chunk, 0, low, half)
            total = total + self.chip_got[chunk, 2 * (near - 1)].astype(F32)
            total = total + self.turn_got[chunk, near - 1].astype(F32)
            self.exp_out[chunk, low : low + half] = total.astype(BF)
        home = self.homes[chunk // place.experts]
        k = 1 + chunk % place.experts
        if k == place.experts:
            home[place.exp] = self.exp_out[chunk]
            return []
        device = place.device(place.other_exp(k), place.chip, place.core)
        return [
            send(self.exp_out.at[chunk], home.at[place.exp], self.exp_sems, (chunk,), device)
        ]

    def run(self):
        chunks = len(self.parts) * self.place.experts
        core = [self.between_cores(chunk) for chunk in range(chunks)]
        first, second, home = [], [], []
        for stage in range(chunks + 2):
            if stage < chunks:
                first.append(self.first_hops(stage, core[stage]))
            if 0 <= stage - 1 < chunks:
                second.append(self.second_hops(stage - 1, first[stage - 1]))
            if 0 <= stage - 2 < chunks:
                home.append(self.go_home(stage - 2, second[stage - 2]))
        for copies in home:
            for copy in copies:
                copy.wait_recv()
        for copies in (*core, *first, *second, *home):
            for copy in copies:
                copy.wait_send()


def start_kernel(sizes, count, moves, *refs):
    place = Place(sizes)
    blocks, refs = take(refs, count)
    (pair_src,), refs = take(refs, 1)
    sources, refs = take(refs, len(moves))
    outs, refs = take(refs, count)
    (pair_out,), refs = take(refs, 1)
    landings, refs = take(refs, len(moves))
    (own_sems, exp_sems, chip_sems, core_sems), refs = take(refs, 4)
    pair_sems, refs = take(refs, 3)
    movers = make_movers(moves, sources, landings, refs)
    pair = Pair(place, pair_src, pair_out, *pair_sems)
    spreads = []
    for i, (rows, out) in enumerate(zip(blocks, outs)):
        quarter = rows.shape[1] // place.tp
        mine = rows.at[:, block(place.tp_at * quarter, quarter, 128)]
        sems = (s.at[i] for s in (exp_sems, chip_sems, core_sems))
        spreads.append(Spread(place, mine, out, True, *sems))
    place.meet(True)
    pair.start()
    for i, spread in enumerate(spreads[:-1]):
        spread.start(own_sems.at[i])
    pair.share()
    for mover in movers:
        mover.start(place, False)
    spreads[-1].start(own_sems.at[count - 1])
    for mover in movers:
        mover.start(place, True)
    for stage in range(place.experts + 2):
        for runner in (*spreads[:-1], pair):
            if stage <= place.experts:
                runner.step(stage)
        if stage:
            spreads[-1].step(stage - 1)
    for runner in (*spreads, pair):
        runner.finish()
    for mover in movers:
        mover.wait()


def take(refs, count):
    return refs[:count], refs[count:]


def turned(left, right):
    return lax.dot_general(left, right, (((0,), (0,)), ((), ())), preferred_element_type=F32)


def row_sums(weights, rows):
    return lax.dot_general(
        weights,
        rows,
        (((1,), (1,)), ((), ())),
        preferred_element_type=F32,
        precision=lax.Precision.HIGHEST,
    )


def make_movers(moves, sources, landings, sems):
    return [
        Mover(i, kind, cuts, source, landing, *sems)
        for i, ((kind, cuts), source, landing) in enumerate(zip(moves, sources, landings))
    ]


def exchange_kernel(sizes, tail, count, extras, moves, *refs):
    place = Place(sizes)
    parts, refs = take(refs, count)
    adds, refs = take(refs, count)
    (put, scale), refs = take(refs, 2)
    if tail == "slots":
        (next_put, linear, square), refs = take(refs, 3)
    elif tail == "tokens":
        (facts, unit, *more), refs = take(refs, extras)
    else:
        (facts,), refs = take(refs, extras)
    sources, refs = take(refs, len(moves))
    raws, refs = take(refs, count)
    (all_facts,), refs = take(refs, 1)
    if tail == "tokens":
        (all_sums,), refs = take(refs, 1)
    outs, refs = take(refs, {"slots": 1, "tokens": extras - 1, None: 0}[tail])
    landings, refs = take(refs, len(moves))
    homes, refs = take(refs, count)
    (own_sems,), refs = take(refs, 1)
    fact_sems, refs = take(refs, 3)
    fold_scratch, refs = take(refs, 10)
    if tail == "slots":
        (picked, facts), refs = take(refs, 2)
        tail_sems, refs = take(refs, 3)
    elif tail == "tokens":
        (mine, sums), refs = take(refs, 2)
        sum_sems, refs = take(refs, 3)
        tail_sems, refs = take(refs, 2 * extras - 2)
    movers = make_movers(moves, sources, landings, refs)
    place.meet(bool(moves))
    told = Spread(place, facts, all_facts, False, *fact_sems)
    if tail != "slots":
        told.start(own_sems.at[0])
    to_tokens = []
    if tail == "tokens":
        for i, rows in enumerate(more):
            to_tokens.append(
                ToTokens(place, rows, outs[1 + i], *tail_sems[2 + 2 * i : 4 + 2 * i])
            )
            to_tokens[-1].start(own_sems.at[2 + i])
    for mover in movers:
        mover.start(place, False)
    Fold(place, parts, homes, fold_scratch).run()
    for i in reversed(range(count)):
        if put.shape[1] == 128:
            summed = jnp.sum(homes[i][...].astype(F32), axis=0)
        else:
            rows = homes[i][...].reshape(-1, homes[i].shape[2])
            summed = jnp.dot(put[...], rows, preferred_element_type=F32)
        value = adds[i][...] + summed
        raws[i][...] = value
    if tail == "slots":
        picked[...] = turned(next_put[...], value.astype(BF)).astype(BF)
        slots = Spread(place, picked, outs[0], False, *tail_sems, pieces=place.experts)
        slots.start(own_sems.at[1])
        facts[...] = row_sums(linear[...], value) + row_sums(square[...], value * value)
        told.start(own_sems.at[0])
    elif tail == "tokens":
        mine[...] = (value * scale[...]).astype(BF)
        to_tokens.append(ToTokens(place, mine, outs[0], *tail_sems[:2]))
        to_tokens[-1].start(own_sems.at[1])
        columns = jnp.sum(value * unit[...], axis=0, keepdims=True)
        sums[...] = jnp.broadcast_to(columns, sums.shape)
        summed = Spread(place, sums, all_sums, False, *sum_sems)
        summed.start(own_sems.at[extras])
    for mover in movers:
        mover.start(place, True)
    if tail == "slots":
        slots.run()
    for rows in to_tokens:
        rows.run()
    told.run()
    if tail == "tokens":
        summed.run()
    for mover in movers:
        mover.wait()


def finish_kernel(sizes, moves, *refs):
    place = Place(sizes)
    (plus, product, unit, next_put), refs = take(refs, 4)
    sources, refs = take(refs, len(moves))
    (raw, out), refs = take(refs, 2)
    landings, refs = take(refs, len(moves))
    (sums, got, picked, own_sem, sum_sems), refs = take(refs, 5)
    tail_sems, refs = take(refs, 3)
    movers = make_movers(moves, sources, landings, refs)
    sums[...] = row_sums(jnp.ones((8, product.shape[1]), F32), product[...])
    place.meet(bool(moves))
    layer = place.chips * 2
    here = place.chip * 2 + place.core
    copies = []
    for k in range(1, layer):
        there = (here + k) % layer
        device = place.device(place.exp, there // 2, there % 2)
        copies.append(send(sums, got.at[k - 1], sum_sems, (k - 1,), device))
    for mover in movers:
        mover.start(place, False)
    total = sums[...]
    for k in range(1, layer):
        copies[k - 1].wait_recv()
        total = total + got[k - 1]
    mean = total.T[:, :1] * (1.0 / (layer * product.shape[1]))
    value = plus[...] - unit[...] * mean
    raw[...] = value
    picked[...] = turned(next_put[...], value.astype(BF)).astype(BF)
    slots = Spread(place, picked, out, False, *tail_sems, pieces=place.experts)
    slots.start(own_sem)
    for mover in movers:
        mover.start(place, True)
    slots.run()
    for copy in copies:
        copy.wait_send()
    for mover in movers:
        mover.wait()


def dma_sems(*shape):
    return pltpu.SemaphoreType.DMA(shape)


def move_scratch(sizes, moves):
    most = max(len(cuts) for _, cuts, _, _ in moves)
    members = sizes[0] * sizes[1]
    return [dma_sems(2, len(moves), most, members - 1), dma_sems(len(moves), most)]


def start(sizes, arrays, pair, moves, number):
    experts, sub, _, tp = sizes
    count = len(arrays)
    exp_sems, chip_sems, core_sems = (
        dma_sems(count, *shape) for shape in spread_shapes(sizes)
    )
    anywhere = pl.BlockSpec(memory_space=pl.ANY)
    total = count + 1 + len(moves)
    results = pl.pallas_call(
        partial(start_kernel, sizes, count, [(kind, cuts) for kind, cuts, _, _ in moves]),
        out_shape=[
            *[
                jax.ShapeDtypeStruct((rows.shape[0] * experts * sub, rows.shape[1]), rows.dtype)
                for rows in arrays
            ],
            jax.ShapeDtypeStruct((pair.shape[1] * experts * sub, 2 * pair.shape[2] // sub), BF),
            *landing_shapes(sizes, moves),
        ],
        in_specs=[anywhere] * total,
        out_specs=[anywhere] * total,
        scratch_shapes=[
            dma_sems(count),
            exp_sems,
            chip_sems,
            core_sems,
            dma_sems(2, 2, experts - 1),
            dma_sems(2, 2, sub - 1),
            dma_sems(2),
            *move_scratch(sizes, moves),
        ],
        compiler_params=pltpu.CompilerParams(
            collective_id=number, has_side_effects=True, vmem_limit_bytes=VMEM_BYTES
        ),
        name=f"start_{number}",
    )(*arrays, pair, *[array for _, _, array, _ in moves])
    return results[:count], results[count], results[count + 1 :]


def landing_shapes(sizes, moves):
    return [
        jax.ShapeDtypeStruct(moved_shape(sizes, kind, array, wide), BF)
        for kind, _, array, wide in moves
    ]


def spread_shapes(sizes):
    experts, sub, _, tp = sizes
    chips = sub * tp // 2
    return (2, 2, experts - 1), (2, experts, chips), (2, experts, chips)


def spread_sems(sizes):
    return [dma_sems(*shape) for shape in spread_shapes(sizes)]


def fact_shapes(sizes, shape):
    experts, sub, _, tp = sizes
    return jax.ShapeDtypeStruct((shape[0] * experts, shape[1] * sub * tp), F32)


def by_device(sizes, all_facts, shape):
    experts, sub, _, tp = sizes
    return all_facts.reshape(experts, shape[0], sub * tp, shape[1]).transpose(0, 2, 1, 3)


def exchange(sizes, parts, adds, put, scale, extra, tail, moves, number):
    experts, sub, ctx, tp = sizes
    chips = sub * tp // 2
    count = len(parts)
    rows, width = parts[0].shape
    tokens, feats = adds[0].shape
    each, chunks = rows // experts, count * experts
    vmem, anywhere = (pl.BlockSpec(memory_space=m) for m in (pltpu.VMEM, pl.ANY))
    if put is None:
        put = jnp.zeros((8, 128), BF)
    fact_shape = (8, tokens) if tail == "slots" else extra[0].shape
    outs, scratch, extra_specs = [], [], [vmem] * len(extra)
    if tail == "slots":
        picks = extra[0].shape[1]
        outs = [jax.ShapeDtypeStruct((picks, width), BF)]
        scratch = [pltpu.VMEM((picks, feats), BF), pltpu.VMEM(fact_shape, F32)]
        scratch += spread_sems(sizes)
    elif tail == "tokens":
        outs = [fact_shapes(sizes, (8, feats))]
        outs += [jax.ShapeDtypeStruct((tokens // sub, width), BF)] * (len(extra) - 1)
        scratch = [pltpu.VMEM((tokens, feats), BF), pltpu.VMEM((8, feats), F32)]
        scratch += spread_sems(sizes)
        scratch += [dma_sems(2, chips - 1), dma_sems(2, chips)] * (len(extra) - 1)
    if tail != "slots":
        extra_specs[0] = anywhere
    results = pl.pallas_call(
        partial(
            exchange_kernel,
            sizes,
            tail,
            count,
            len(extra),
            [(kind, cuts) for kind, cuts, _, _ in moves],
        ),
        out_shape=[
            *[jax.ShapeDtypeStruct((tokens, feats), F32)] * count,
            fact_shapes(sizes, fact_shape),
            *outs,
            *landing_shapes(sizes, moves),
        ],
        in_specs=[vmem] * (2 * count + 2) + extra_specs + [anywhere] * len(moves),
        out_specs=[vmem] * count + [anywhere] * (1 + len(outs) + len(moves)),
        scratch_shapes=[
            *[pltpu.VMEM((experts, each, feats), BF)] * count,
            dma_sems(1 + max(len(extra), 2)),
            *spread_sems(sizes),
            pltpu.VMEM((chunks, 4, each, feats), BF),
            pltpu.VMEM((chunks, 4, each // 2, feats), BF),
            pltpu.VMEM((chunks, 4, each // 2, feats), BF),
            pltpu.VMEM((chunks, 2, each // 2, feats), BF),
            pltpu.VMEM((chunks, 2, each // 2, feats), BF),
            pltpu.VMEM((chunks, each, feats), BF),
            dma_sems(2, chunks, 4),
            dma_sems(2, chunks, 4),
            dma_sems(2, chunks, 2),
            dma_sems(2, chunks),
            *scratch,
            *move_scratch(sizes, moves),
        ],
        compiler_params=pltpu.CompilerParams(
            collective_id=number, has_side_effects=True, vmem_limit_bytes=VMEM_BYTES
        ),
        name=f"exchange_{number}",
    )(*parts, *adds, put, scale, *extra, *[array for _, _, array, _ in moves])
    raws, (all_facts, *results) = results[:count], results[count:]
    outs, moved = results[: len(outs)], results[len(outs) :]
    return raws, outs, by_device(sizes, all_facts, fact_shape), moved


def finish(sizes, plus, product, unit, next_put, moves, number):
    experts, sub, ctx, tp = sizes
    layer = sub * tp
    tokens, feats = plus.shape
    picks = next_put.shape[1]
    vmem, anywhere = (pl.BlockSpec(memory_space=m) for m in (pltpu.VMEM, pl.ANY))
    raw, out, *moved = pl.pallas_call(
        partial(finish_kernel, sizes, [(kind, cuts) for kind, cuts, _, _ in moves]),
        out_shape=[
            jax.ShapeDtypeStruct((tokens, feats), F32),
            jax.ShapeDtypeStruct((picks, feats * layer), BF),
            *landing_shapes(sizes, moves),
        ],
        in_specs=[vmem] * 4 + [anywhere] * len(moves),
        out_specs=[vmem] + [anywhere] * (1 + len(moves)),
        scratch_shapes=[
            pltpu.VMEM((8, tokens), F32),
            pltpu.VMEM((layer - 1, 8, tokens), F32),
            pltpu.VMEM((picks, feats), BF),
            pltpu.SemaphoreType.DMA,
            dma_sems(2, layer - 1),
            *spread_sems(sizes),
            *move_scratch(sizes, moves),
        ],
        compiler_params=pltpu.CompilerParams(
            collective_id=number, has_side_effects=True, vmem_limit_bytes=VMEM_BYTES
        ),
        name=f"finish_{number}",
    )(plus, product, unit, next_put, *[array for _, _, array, _ in moves])
    return raw, out, moved


def parted(pick, table):
    total = None
    for _ in range(3):
        part = table.astype(BF)
        product = jnp.dot(pick, part, preferred_element_type=F32)
        total = product if total is None else total + product
        table = table - part.astype(F32)
    return total


def times(left, right):
    return jnp.dot(left, right, preferred_element_type=F32)


def times_turned(left, right):
    return lax.dot_general(left, right, (((1,), (1,)), ((), ())), preferred_element_type=F32)


def one_hot(places, shape, axis):
    return (lax.broadcasted_iota(jnp.int32, shape, axis).astype(F32) == places).astype(BF)


def allowed_keys(position, span, spans):
    shape = (position.shape[0], spans.shape[1])
    keys = lax.broadcasted_iota(jnp.int32, shape, 1).astype(F32)
    return (keys <= position) | ((span == spans) & (span > 0))


def softmax_rows(scores, allowed):
    scores = jnp.where(allowed, scores, -1e30)
    expo = jnp.exp(scores - jnp.max(scores, axis=-1, keepdims=True))
    return expo / jnp.sum(expo, axis=-1, keepdims=True)


def head_columns(head):
    return pl.ds(head * HD, HD)


def turn_heads(rows, cosine, sine):
    parts = []
    for head in range(rows.shape[1] // HD):
        u = rows[:, head * HD : (head + 1) * HD]
        parts.append(u * cosine + pltpu.roll(u, HD // 2, 1) * sine)
    return jnp.concatenate(parts, axis=1)


def turn_heads_back(rows, cosine, sine):
    parts = []
    for head in range(rows.shape[1] // HD):
        u = rows[:, head * HD : (head + 1) * HD]
        parts.append(u * cosine + pltpu.roll(u * sine, HD // 2, 1))
    return jnp.concatenate(parts, axis=1)


def attend_kernel(
    experts,
    x_ref,
    gain_ref,
    query_ref,
    key_value_ref,
    route_ref,
    rows_ref,
    hits_ref,
    cosine_ref,
    sine_ref,
    mine_ref,
    h1_ref,
    slots_ref,
    queries_ref,
    keys_ref,
    values_ref,
    mixed_ref,
    gates_ref,
    tables_ref,
):
    seq_len = x_ref.shape[0]
    cap = slots_ref.shape[0]
    wide = query_ref.shape[1]
    x = x_ref[...].astype(F32)
    scale_in = lax.rsqrt(jnp.mean(x * x, axis=1, keepdims=True) + EPS)
    h1 = (x * scale_in * gain_ref[...]).astype(BF)
    h1_ref[...] = h1
    cosine, sine = cosine_ref[...], sine_ref[...]
    kv = times(h1, key_value_ref[...])
    keys_ref[...] = turn_heads(kv[:, :wide], cosine, sine).astype(BF)
    values_ref[...] = kv[:, wide:].astype(BF)
    logits = times(h1, route_ref[...])
    hits = hits_ref[...]
    lane = lax.broadcasted_iota(jnp.int32, hits.shape, 1)
    chosen = (hits > 0) & (lane < experts)
    top = jnp.max(jnp.where(chosen, logits, -1e30), axis=1, keepdims=True)
    raised = jnp.where(chosen, jnp.exp(jnp.minimum(logits - top, 0.0)), 0.0)
    gates = raised / jnp.sum(raised, axis=1, keepdims=True)
    gates_ref[...] = gates
    pick = one_hot(rows_ref[0, 0:1], (cap, seq_len), 0)
    slots = times(pick, h1).astype(BF)
    slots_ref[...] = slots
    row = lax.broadcasted_iota(jnp.int32, hits.shape, 0).astype(F32)
    gate_mine = jnp.sum(gates * mine_ref[...], axis=1, keepdims=True)
    facts = jnp.where(lane == 0, gate_mine, jnp.where(lane == 1, row, hits))
    tables = parted(pick, jnp.concatenate([cosine, sine, facts], axis=1))
    tables_ref[...] = tables
    queries = turn_heads(times(slots, query_ref[...]), tables[:, :HD], tables[:, HD : 2 * HD])
    queries_ref[...] = queries.astype(BF)
    at = 2 * HD
    allowed = allowed_keys(
        tables[:, at + 1 : at + 2], tables[:, at + experts : at + experts + 1], rows_ref[0, 1:2]
    )
    for head in range(wide // HD):
        part = head_columns(head)
        scores = times_turned(queries_ref[:, part], keys_ref[:, part]) * HD**-0.5
        probs = softmax_rows(scores, allowed).astype(BF)
        mixed_ref[:, part] = times(probs, values_ref[:, part]).astype(BF)


def attend(experts, seqs, x, gain, query, key_value, route, rows, hits, cosine, sine, mine):
    total, width = x.shape
    seq_len = total // seqs
    cap = 2 * seq_len // experts
    wide = query.shape[1]

    def each(*shape):
        zeros = (0,) * (len(shape) - 1)
        return pl.BlockSpec(shape, lambda s: (s, *zeros))

    def whole(array):
        zeros = (0,) * array.ndim
        return pl.BlockSpec(array.shape, lambda s: zeros)

    def out(rows, columns, dtype):
        return jax.ShapeDtypeStruct((seqs * rows, columns), dtype)

    return pl.pallas_call(
        partial(attend_kernel, experts),
        grid=(seqs,),
        in_specs=[
            each(seq_len, width),
            whole(gain),
            whole(query),
            whole(key_value),
            whole(route),
            each(1, 8, seq_len),
            each(seq_len, HD),
            whole(cosine),
            whole(sine),
            whole(mine),
        ],
        out_specs=[
            each(seq_len, width),
            each(cap, width),
            each(cap, wide),
            each(seq_len, wide),
            each(seq_len, wide),
            each(cap, wide),
            each(seq_len, HD),
            each(cap, 3 * HD),
        ],
        out_shape=[
            out(seq_len, width, BF),
            out(cap, width, BF),
            out(cap, wide, BF),
            out(seq_len, wide, BF),
            out(seq_len, wide, BF),
            out(cap, wide, BF),
            out(seq_len, HD, F32),
            out(cap, 3 * HD, F32),
        ],
        compiler_params=pltpu.CompilerParams(vmem_limit_bytes=LOCAL_VMEM_BYTES),
        cost_estimate=pl.CostEstimate(
            flops=2 * total * width * (3 * wide + seq_len // 2),
            bytes_accessed=6 * total * width,
            transcendentals=total * seq_len,
        ),
        name="attend",
    )(x, gain, query, key_value, route, rows, hits, cosine, sine, mine)


def attend_back_kernel(
    experts,
    grad_ref,
    out_ref,
    query_ref,
    key_value_ref,
    rows_ref,
    hits_ref,
    cosine_ref,
    sine_ref,
    queries_ref,
    keys_ref,
    values_ref,
    mixed_ref,
    tables_ref,
    grad_query_ref,
    grad_kv_ref,
    grad_branch_ref,
    gate_ref,
    first_ref,
):
    seq_len, wide = keys_ref.shape
    cap = queries_ref.shape[0]
    tables = tables_ref[...]
    at = 2 * HD
    gate = tables[:, at : at + 1]
    allowed = allowed_keys(
        tables[:, at + 1 : at + 2], tables[:, at + experts : at + experts + 1], rows_ref[0, 1:2]
    )
    grad = grad_ref[...]
    grad_branch_ref[...] = (grad.astype(F32) * gate).astype(BF)
    grad_mixed = times_turned(grad, out_ref[...])
    gates = jnp.sum(mixed_ref[...].astype(F32) * grad_mixed, axis=1, keepdims=True)
    gate_ref[...] = jnp.broadcast_to(gates, gate_ref.shape)
    grad_mixed = (grad_mixed * gate).astype(BF)
    grad_queries, grad_keys, grad_values = [], [], []
    for head in range(wide // HD):
        part = head_columns(head)
        queries, keys = queries_ref[:, part], keys_ref[:, part]
        own = grad_mixed[:, head * HD : (head + 1) * HD]
        probs = softmax_rows(times_turned(queries, keys) * HD**-0.5, allowed)
        grad_probs = times_turned(own, values_ref[:, part])
        grad_values.append(turned(probs.astype(BF), own))
        inner = jnp.sum(probs * grad_probs, axis=1, keepdims=True)
        grad_scores = (probs * (grad_probs - inner)).astype(BF)
        grad_queries.append(times(grad_scores, keys) * HD**-0.5)
        grad_keys.append(turned(grad_scores, queries) * HD**-0.5)
    grad_queries = jnp.concatenate(grad_queries, axis=1)
    grad_qpre = turn_heads_back(grad_queries, tables[:, :HD], tables[:, HD : 2 * HD]).astype(BF)
    grad_query_ref[...] = grad_qpre
    grad_keys = turn_heads_back(
        jnp.concatenate(grad_keys, axis=1), cosine_ref[...], sine_ref[...]
    )
    kv_low = jnp.concatenate([grad_keys, *grad_values], axis=1).astype(BF)
    grad_kv_ref[...] = kv_low
    taken = times_turned(grad_qpre, query_ref[...]).astype(BF)
    give = one_hot(hits_ref[:, experts + 1 : experts + 2], (seq_len, cap), 1)
    first = times_turned(kv_low, key_value_ref[...]) + times(give, taken)
    first_ref[...] = first.astype(BF)


def attend_back(
    experts, seqs, grad, out, query, key_value, rows, hits, cosine, sine, saved
):
    queries, keys, values, mixed, tables = saved
    width = grad.shape[1]
    cap = grad.shape[0] // seqs
    total, wide = keys.shape
    seq_len = total // seqs

    def each(*shape):
        zeros = (0,) * (len(shape) - 1)
        return pl.BlockSpec(shape, lambda s: (s, *zeros))

    def whole(array):
        zeros = (0,) * array.ndim
        return pl.BlockSpec(array.shape, lambda s: zeros)

    def result(rows, columns, dtype):
        return jax.ShapeDtypeStruct((seqs * rows, columns), dtype)

    return pl.pallas_call(
        partial(attend_back_kernel, experts),
        grid=(seqs,),
        in_specs=[
            each(cap, width),
            whole(out),
            whole(query),
            whole(key_value),
            each(1, 8, seq_len),
            each(seq_len, HD),
            whole(cosine),
            whole(sine),
            each(cap, wide),
            each(seq_len, wide),
            each(seq_len, wide),
            each(cap, wide),
            each(cap, 3 * HD),
        ],
        out_specs=[
            each(cap, wide),
            each(seq_len, 2 * wide),
            each(cap, width),
            each(cap, HD),
            each(seq_len, width),
        ],
        out_shape=[
            result(cap, wide, BF),
            result(seq_len, 2 * wide, BF),
            result(cap, width, BF),
            result(cap, HD, F32),
            result(seq_len, width, BF),
        ],
        compiler_params=pltpu.CompilerParams(vmem_limit_bytes=LOCAL_VMEM_BYTES),
        cost_estimate=pl.CostEstimate(
            flops=2 * total * width * (3 * wide + seq_len // 2),
            bytes_accessed=6 * total * width,
            transcendentals=total * seq_len,
        ),
        name="attend_back",
    )(
        grad, out, query, key_value, rows, hits, cosine, sine, queries, keys, values, mixed, tables
    )


class Axes:
    def __init__(self, experts, shard, ctx, tp):
        self.experts = experts
        self.sub = shard * ctx // experts
        self.tp = tp
        if self.sub == ctx:
            self.layer, self.exp = (("ctx", "tp"), None), ("shard", None)
            self.part = ("ctx", None)
        else:
            devices = np.arange(shard * ctx * tp).reshape(experts, self.sub, tp)
            self.layer = (ALL, devices.reshape(experts, -1).tolist())
            self.exp = (ALL, devices.reshape(experts, -1).T.tolist())
            self.part = (ALL, devices.transpose(0, 2, 1).reshape(-1, self.sub).tolist())

    def swap(self, value, over):
        axes, groups = over
        return lax.all_to_all(value, axes, 0, 0, axis_index_groups=groups)


class Routing:
    def __init__(self, choice, seqs, seq_len, experts, cap, mine, own_first, own_seqs):
        columns = jnp.arange(experts, dtype=jnp.int32)
        hits = jnp.sum((choice[:, :, None] == columns[None, None, :]).astype(F32), axis=1)
        self.hits = hits.reshape(seqs, seq_len, experts)
        rows = jnp.arange(seq_len, dtype=jnp.int32)
        earlier = (rows[None, :] < rows[:, None]).astype(BF)
        before = dot("tu,sue->ste", earlier, self.hits.astype(BF))
        self.valid = self.hits * (before < cap).astype(F32)
        self.place = jnp.where(self.valid > 0, before, -1.0)
        self.cap = cap
        is_mine = (columns == mine).astype(F32)
        place_mine = jnp.sum(self.place * is_mine, axis=2)
        self.place_mine = place_mine
        slots = jnp.arange(cap, dtype=jnp.int32).astype(F32)
        self.is_mine = is_mine
        self.pick = (place_mine[:, None, :] == slots[None, :, None]).astype(BF)
        place_own = lax.dynamic_slice_in_dim(self.place, own_first, own_seqs, 0)
        place_own = place_own.transpose(1, 0, 2)[:, :, :, None]
        seq_of = jnp.arange(own_seqs, dtype=jnp.int32)
        here = place_own == slots
        same = (seq_of[:, None] == seq_of[None, :])[:, None, None, :, None]
        put = here.transpose(1, 0, 2, 3)[:, :, :, None, :] & same
        self.put = put.astype(BF).reshape(own_seqs * seq_len, experts * own_seqs * cap)

    def gates(self, logits):
        logits = logits.reshape(self.hits.shape)
        top = jnp.max(jnp.where(self.hits > 0, logits, -jnp.inf), axis=2, keepdims=True)
        raised = jnp.where(self.hits > 0, jnp.exp(logits - top), 0.0)
        return raised / jnp.sum(raised, axis=2, keepdims=True)

    def slot_gates(self, gates):
        gate_mine = jnp.sum(gates * self.is_mine, axis=2)
        return jnp.sum(self.pick.astype(F32) * gate_mine[:, None, :], axis=2)

    def take(self, rows):
        seqs, cap, seq_len = self.pick.shape
        picked = dot("spt,stf->spf", self.pick, rows.reshape(seqs, seq_len, -1))
        return picked.astype(BF).reshape(seqs * cap, -1)

    def give(self, slots):
        seqs, cap, seq_len = self.pick.shape
        rows = dot("spt,spf->stf", self.pick, slots.reshape(seqs, cap, -1))
        return rows.reshape(seqs * seq_len, -1)

    def token_grads(self, slot_grads):
        slots = jnp.arange(self.cap, dtype=jnp.int32).astype(F32)
        here = self.place[:, :, :, None] == slots[None, None, None, :]
        grads = slot_grads.transpose(1, 0, 2)[:, None, :, :]
        return jnp.sum(jnp.where(here, grads, 0.0), axis=3)


def put_home(put, home):
    return dot("tp,pf->tf", put, home.reshape(-1, home.shape[-1]))


def router_rows(grads, router):
    high = grads.astype(BF)
    low = (grads - high.astype(F32)).astype(BF)
    return dot(
        "te,fe->tf",
        jnp.concatenate([high, low], axis=1),
        jnp.concatenate([router, router], axis=1),
    )


def logit_grads(gates, gate_grads):
    mean = jnp.sum(gates * gate_grads, axis=2, keepdims=True)
    grads = gates * (gate_grads - mean)
    return grads.reshape(-1, grads.shape[-1])


def shards(
    sizes,
    hidden_in,
    att_choice,
    ffn_choice,
    span_ids,
    norm_att,
    router_att,
    w_query,
    w_out,
    w_key,
    w_value,
    norm_ffn,
    router_ffn,
    w_gate,
    w_up,
    w_down,
    cotangent,
):
    shard, ctx, tp = sizes
    experts = w_query.shape[0]
    axes = Axes(experts, shard, ctx, tp)
    sub = axes.sub
    group = experts * sub
    layer = sub * tp
    tokens, width = hidden_in.shape
    total = tokens * group
    seq_len = tokens * ctx
    seqs = total // seq_len
    own_seqs = seqs // experts
    own_tokens = own_seqs * seq_len
    cap = 2 * seq_len // experts
    slots = seqs * cap
    rows_own = width // group
    feats = width // layer
    sizes = (experts, sub, ctx, tp)
    kernels = feats % 128 == 0 and rows_own % 128 == 0 and tokens % 16 == 0
    group_at, tp_at = lax.axis_index(GROUP), lax.axis_index("tp")
    exp_at, sub_at = group_at // sub, group_at % sub
    layer_at = sub_at * tp + tp_at

    span_own = lax.dynamic_slice_in_dim(span_ids, group_at % ctx * tokens, tokens, 0)
    token_pack = jnp.concatenate(
        [att_choice, ffn_choice, span_own[:, None]], axis=1
    ).astype(BF)
    feature_pack = jnp.concatenate(
        [norm_att[:, None], router_att, norm_ffn[:, None], router_ffn], axis=1
    )
    def everywhere(rows):
        quarter = width // tp
        part = lax.dynamic_slice_in_dim(rows, tp_at * quarter, quarter, 1)
        parts = lax.all_gather(part, ALL)
        return parts.reshape(group, tp, tokens, quarter).transpose(0, 2, 1, 3).reshape(total, width)

    def everywhere_layer(rows):
        parts = lax.all_gather(rows, ALL)
        return (
            parts.reshape(experts, layer, own_tokens, feats)
            .transpose(0, 2, 1, 3)
            .reshape(total, width)
        )

    def layer_sum(rows):
        m = rows.shape[0]
        parts = rows.astype(BF).reshape(m, layer, feats).transpose(1, 0, 2)
        parts = axes.swap(parts, axes.layer)
        return jnp.sum(parts.astype(F32), axis=0)

    def go_home(rows):
        return axes.swap(rows.astype(BF).reshape(experts, -1, feats), axes.exp)

    def to_tokens(rows):
        parts = axes.swap(rows.reshape(sub, tokens, feats), axes.part)
        parts = lax.all_gather(parts, "tp")
        return parts.transpose(2, 1, 0, 3).reshape(tokens, width)

    head_parts = math.gcd(sub, w_query.shape[2] // HD)
    copies = sub // head_parts
    heads_wide = w_query.shape[2] // head_parts
    hidden_local = w_gate.shape[2]
    hidden_wide = -(-hidden_local // (sub * 128)) * 128
    windows = sub == 2 and (hidden_local - hidden_wide) % 128 == 0
    hidden_pad = 0 if windows else hidden_wide * sub - hidden_local
    overlap = hidden_wide * sub - hidden_local if windows else 0
    hidden_rows = hidden_local // sub if windows else hidden_wide
    hidden_first = sub_at * (overlap // 2)
    hidden_at = jnp.arange(hidden_wide)
    hidden_mine = (hidden_at >= hidden_first) & (hidden_at < hidden_first + hidden_rows)
    kernels = kernels and windows and copies == 1 and sub == 2 and tp == 4 and experts == 4

    def to_windows(weight, axis):
        if windows:
            size = weight.shape[axis]
            parts = [
                lax.slice_in_dim(weight, 0, hidden_wide, axis=axis),
                lax.slice_in_dim(weight, size - hidden_wide, size, axis=axis),
            ]
        else:
            pad = [(0, 0)] * 3
            pad[axis] = (0, hidden_pad)
            parts = jnp.split(jnp.pad(weight, pad), sub, axis=axis)
        parts = jnp.stack(parts, axis=1)
        return parts.reshape(group, *parts.shape[2:])

    def to_heads(weight, axis):
        parts = jnp.stack(jnp.split(weight, head_parts, axis=axis), axis=1)
        return jnp.repeat(parts, copies, axis=1).reshape(group, *parts.shape[2:])

    def to_all(weight):
        return to_heads(jnp.broadcast_to(weight, (experts, *weight.shape)), 2)

    def swap_group(value):
        return lax.all_to_all(value, GROUP, 0, 0)

    def as_columns(parts):
        return parts.reshape(width, parts.shape[2])

    def as_rows(parts):
        return parts.transpose(1, 0, 2).reshape(parts.shape[1], width)

    pack = jnp.concatenate(
        [jnp.pad(facts.T, ((0, 16 - facts.shape[1]), (0, 0))) for facts in (token_pack, feature_pack)],
        axis=1,
    )
    if kernels:
        (packs, all_in, top_all), my_key_value, (my_query, my_out) = start(
            sizes,
            [pack, hidden_in, cotangent],
            jnp.stack([w_key, w_value]),
            [
                ("columns_out", ((0, heads_wide, False),), w_query, heads_wide),
                ("rows_out", ((0, heads_wide, True),), w_out, heads_wide),
            ],
            0,
        )
        packs = packs.reshape(group, 16, -1)
    else:
        packs = lax.all_gather(pack, GROUP)
        all_in, top_all = everywhere(hidden_in), everywhere(cotangent)
        first = [to_heads(w_query, 2), to_all(w_key), to_all(w_value), to_heads(w_out, 1)]
        first = swap_group(jnp.concatenate(first, axis=2))
        my_query = as_columns(first[:, :, :heads_wide])
        my_key_value = as_columns(first[:, :, heads_wide : 3 * heads_wide])
        my_out = as_rows(first[:, :, 3 * heads_wide :])
    packs = packs.transpose(0, 2, 1)
    token_facts = packs[:, :tokens].reshape(total, 16).astype(jnp.int32)
    feature_facts = packs[:, tokens:].reshape(width, 16)
    gain_att = feature_facts[:, 0].astype(F32)
    route_att = feature_facts[:, 1 : 1 + experts]
    gain_ffn = feature_facts[:, 1 + experts].astype(F32)
    route_ffn = feature_facts[:, 2 + experts : 2 + 2 * experts]

    def move(kind, weight):
        if kind == "columns_out":
            return as_columns(swap_group(to_windows(weight, 2)))
        if kind == "rows_out":
            if not windows:
                return as_rows(swap_group(to_windows(weight, 1)))
            parts = as_rows(swap_group(weight.reshape(group, hidden_rows, rows_own)))
            rows = jnp.zeros((hidden_wide, width), BF)
            return lax.dynamic_update_slice_in_dim(rows, parts, hidden_first, 0)
        if kind == "columns_home":
            return swap_group(weight.reshape(group, rows_own, -1))
        if windows:
            weight = lax.dynamic_slice_in_dim(weight, hidden_first, hidden_rows, 0)
        return swap_group(weight.reshape(-1, group, rows_own).transpose(1, 0, 2))

    def to_cuts(moves):
        return [
            (kind, ((0, early, False), (early, wide - early, True)), weight, wide)
            for kind, weight, wide, early in moves
        ]

    def to_slots(rows, next_put):
        picked = dot("tp,tf->pf", next_put, rows).astype(BF)
        picked = axes.swap(picked.reshape(experts, -1, feats), axes.exp)
        picked = lax.all_gather(
            picked.reshape(-1, feats), axes.layer[0], axis_index_groups=axes.layer[1]
        )
        return picked.transpose(1, 0, 2).reshape(-1, width)

    def exchanged(parts, adds, put, scale, extra, tail, moves, number):
        if kernels:
            return exchange(sizes, parts, adds, put, scale, extra, tail, to_cuts(moves), number)
        raws, outs = [], []
        for part, add in zip(parts, adds):
            home = go_home(layer_sum(part))
            summed = jnp.sum(home.astype(F32), axis=0) if put is None else put_home(put, home)
            raws.append(add + summed)
        raw = raws[0]
        if tail == "slots":
            next_put, linear, square = extra
            outs = [to_slots(raw.astype(BF), next_put)]
            facts = dot_exact("ef,tf->et", linear, raw) + dot_exact("ef,tf->et", square, raw * raw)
        else:
            facts = extra[0]
        told = lax.all_gather(facts, ALL).reshape(experts, layer, *facts.shape)
        if tail == "tokens":
            columns = jnp.broadcast_to(jnp.sum(raw * extra[1], axis=0, keepdims=True), (8, feats))
            columns = lax.all_gather(columns, ALL).reshape(experts, layer, 8, feats)
            columns = columns.transpose(0, 2, 1, 3).reshape(experts * 8, layer * feats)
            outs = [to_tokens(rows) for rows in ((raw * scale).astype(BF), *extra[2:])]
            outs.insert(0, columns)
        return raws, outs, told, [move(kind, weight) for kind, weight, _, _ in moves]

    def finished(plus, product, unit, next_put, moves, number):
        if kernels:
            return finish(sizes, plus, product, unit, next_put, to_cuts(moves), number)
        sums = lax.all_gather(jnp.sum(product, axis=1), ALL).reshape(experts, layer, own_tokens)
        mean = lax.dynamic_index_in_dim(jnp.sum(sums, axis=1), exp_at, 0, keepdims=False) / width
        raw = plus - unit * mean[:, None]
        moved = [move(kind, weight) for kind, weight, _, _ in moves]
        return raw, to_slots(raw.astype(BF), next_put), moved

    own_first = exp_at * own_seqs
    where = partial(
        Routing,
        seqs=seqs,
        seq_len=seq_len,
        experts=experts,
        cap=cap,
        mine=exp_at,
        own_first=own_first,
        own_seqs=own_seqs,
    )
    att = where(token_facts[:, 0:2])
    if copies > 1:
        turn = jnp.arange(seqs, dtype=jnp.int32) % copies == sub_at % copies
        att.pick = att.pick * turn.astype(BF)[:, None, None]
    ffn = where(token_facts[:, 2:4])
    spans = token_facts[:, 4].reshape(seqs, seq_len).astype(F32)
    cosine, sine = rope_tables(seq_len)

    my_gate = move("columns_out", after(w_gate, all_in))
    heads = heads_wide // HD
    scale = 1.0 / math.sqrt(HD)
    if kernels:
        att_rows = jnp.pad(jnp.stack([att.place_mine, spans], axis=1), ((0, 0), (0, 6), (0, 0)))
        att_hits = jnp.concatenate(
            [att.hits, spans[:, :, None], att.place_mine[:, :, None]], axis=2
        ).reshape(total, -1)
        att_hits = jnp.pad(att_hits, ((0, 0), (0, HD - att_hits.shape[1])))
        sine = sine * jnp.where(jnp.arange(HD) < HD // 2, -1.0, 1.0)
        h1, h1_slots, *saved, att_gates, att_tables = attend(
            experts,
            seqs,
            all_in,
            gain_att[None, :],
            my_query,
            my_key_value,
            jnp.pad(route_att, ((0, 0), (0, HD - experts))),
            att_rows,
            att_hits,
            cosine,
            sine,
            (jnp.arange(HD) == exp_at).astype(F32)[None, :],
        )
        mixed = saved[3]
        saved.append(att_tables)
        att_gates = att_gates[:, :experts].reshape(seqs, seq_len, experts)
        att_slot_gate = att_tables[:, 2 * HD : 2 * HD + 1]
    else:
        positions = jnp.arange(seq_len, dtype=jnp.int32).astype(F32)
        pick_f32 = att.pick.astype(F32)
        slot_position = jnp.sum(pick_f32 * positions[None, None, :], axis=2)
        slot_span = jnp.sum(pick_f32 * spans[:, None, :], axis=2)
        slot_cosine = dot_exact("spt,tf->spf", pick_f32, cosine)
        slot_sine = dot_exact("spt,tf->spf", pick_f32, sine)
        allowed = (positions[None, None, :] <= slot_position[:, :, None]) | (
            (slot_span[:, :, None] == spans[:, None, :]) & (slot_span[:, :, None] > 0)
        )
        x_all = all_in.astype(F32)
        scale_in = lax.rsqrt(jnp.mean(x_all * x_all, axis=1, keepdims=True) + EPS)
        h1 = (x_all * scale_in * gain_att[None, :]).astype(BF)
        kv = dot("td,dm->tm", h1, my_key_value)
        keys = rotate(
            kv[:, :heads_wide].reshape(seqs, seq_len, heads, HD),
            cosine[None, :, None, :],
            sine[None, :, None, :],
        ).astype(BF)
        values = kv[:, heads_wide:].astype(BF).reshape(seqs, seq_len, heads, HD)
        att_gates = att.gates(dot("td,de->te", h1, route_att))
        att_slot_gate = att.slot_gates(att_gates).reshape(slots, 1)
        h1_slots = att.take(h1)
        queries = rotate(
            dot("td,dm->tm", h1_slots, my_query).reshape(seqs, cap, heads, HD),
            slot_cosine[:, :, None, :],
            slot_sine[:, :, None, :],
        ).astype(BF)
        scores = dot("sqhd,skhd->shqk", queries, keys) * scale
        scores = jnp.where(allowed[:, None], scores, -1e30)
        expo = jnp.exp(scores - jnp.max(scores, axis=-1, keepdims=True))
        probs = expo / jnp.sum(expo, axis=-1, keepdims=True)
        probs_low = probs.astype(BF)
        mixed = dot("shqk,skhd->sqhd", probs_low, values).astype(BF).reshape(slots, heads_wide)
    branch_att = dot("cm,md->cd", mixed, my_out) * att_slot_gate
    own_at = (exp_at * own_tokens, layer_at * feats)
    own_in = lax.dynamic_slice(all_in, own_at, (own_tokens, feats)).astype(F32)
    own_gain_ffn = lax.dynamic_slice_in_dim(gain_ffn, layer_at * feats, feats, 0)
    own_route_ffn = lax.dynamic_slice_in_dim(
        route_ffn.astype(F32), layer_at * feats, feats, 0
    )
    linear = jnp.pad((own_route_ffn * own_gain_ffn[:, None]).T, ((0, 8 - experts), (0, 0)))
    square = (jnp.arange(8) == experts).astype(F32)[:, None] * jnp.ones((1, feats), F32)
    (mid,), (mid_slots,), ffn_facts, (my_up,) = exchanged(
        [after(branch_att.astype(BF), my_gate)],
        [own_in],
        att.put,
        jnp.ones((1, feats), F32),
        (ffn.put, linear, square),
        "slots",
        [("columns_out", w_up, hidden_wide, hidden_wide // 3)],
        1,
    )
    my_down = move("rows_out", after(w_down, mid_slots))

    ffn_facts = jnp.sum(ffn_facts, axis=1)
    scale_mid = lax.rsqrt(ffn_facts[:, experts].reshape(total, 1) / width + EPS)
    ffn_logits = ffn_facts[:, :experts].transpose(0, 2, 1).reshape(total, experts) * scale_mid
    ffn_gates = ffn.gates(ffn_logits)
    ffn_slot_gate = ffn.slot_gates(ffn_gates).reshape(slots, 1)
    mid_slots = mid_slots.astype(F32)
    scale_slots = lax.rsqrt(jnp.mean(mid_slots * mid_slots, axis=1, keepdims=True) + EPS)
    h2_slots = (mid_slots * scale_slots * gain_ffn[None, :]).astype(BF)
    pre_gate = dot("cd,df->cf", h2_slots, my_gate)
    pre_up = dot("cd,df->cf", h2_slots, my_up)
    sigma = jax.nn.sigmoid(pre_gate)
    swish = pre_gate * sigma
    hidden = jnp.where(hidden_mine, swish * pre_up, 0.0).astype(BF)

    top_slots = ffn.take(top_all)
    grad_branch = (top_slots.astype(F32) * ffn_slot_gate).astype(BF)
    grad_down_w = dot("cf,cd->fd", hidden, grad_branch).astype(BF)
    grad_down = move("rows_home", grad_down_w)
    my_down = after(my_down, grad_down_w)
    branch_ffn = dot("cf,fd->cd", hidden, my_down) * ffn_slot_gate
    grad_hidden = dot("cd,fd->cf", top_slots, my_down)
    ffn_gate_part = jnp.sum(hidden.astype(F32) * grad_hidden, axis=1)
    grad_hidden = jnp.where(hidden_mine, grad_hidden * ffn_slot_gate, 0.0)
    grad_pre_gate = (
        grad_hidden * pre_up * sigma * (1.0 + pre_gate * (1.0 - sigma))
    ).astype(BF)
    grad_pre_up = (grad_hidden * swish).astype(BF)
    ffn_taken = dot("cf,df->cd", grad_pre_gate, my_gate) + dot("cf,df->cd", grad_pre_up, my_up)
    grad_gate_w = dot("cd,cf->df", h2_slots, grad_pre_gate).astype(BF)
    grad_up_w = dot("cd,cf->df", h2_slots, grad_pre_up).astype(BF)
    gate_half = hidden_wide // 256 * 128

    def gate_facts(told):
        return jnp.sum(told, axis=1).reshape(experts, seqs, cap)

    (grad_second, own_out), _, ffn_told, (gate_first,) = exchanged(
        [after(ffn_taken.astype(BF), grad_up_w), branch_ffn.astype(BF)],
        [jnp.zeros((own_tokens, feats), F32), mid],
        ffn.put,
        jnp.ones((1, feats), F32),
        (ffn_gate_part.reshape(-1, 128),),
        None,
        [("columns_home", grad_gate_w[:, :gate_half], gate_half, 128)],
        2,
    )
    ffn_logit_grads = logit_grads(ffn_gates, ffn.token_grads(gate_facts(ffn_told)))
    own_ffn_logits = lax.dynamic_slice_in_dim(
        ffn_logit_grads, exp_at * own_tokens, own_tokens, 0
    )
    own_scale_mid = lax.dynamic_slice_in_dim(scale_mid, exp_at * own_tokens, own_tokens, 0)
    own_unit_mid = mid * own_scale_mid
    grad_second = grad_second + router_rows(own_ffn_logits, own_route_ffn)
    norm_ffn_part = jnp.sum(grad_second * own_unit_mid, axis=0)
    own_second = grad_second * own_gain_ffn[None, :] * own_scale_mid
    gate_rest = hidden_wide - gate_half
    up_early = 128
    grad_mid, mid_slots, (gate_second, up_first) = finished(
        lax.dynamic_slice(top_all, own_at, (own_tokens, feats)).astype(F32) + own_second,
        own_second * own_unit_mid,
        own_unit_mid,
        att.put,
        [
            ("columns_home", grad_gate_w[:, gate_half:], gate_rest, 128),
            ("columns_home", grad_up_w[:, :up_early], up_early, 0),
        ],
        5,
    )
    grad_gate = jnp.concatenate([gate_first, gate_second], axis=2)
    up_second = move("columns_home", after(grad_up_w[:, up_early:], mid_slots))

    def windows_home(back, axis):
        back = back.reshape(experts, sub, *back.shape[1:])
        parts = [lax.index_in_dim(back, i, 1, keepdims=False) for i in range(sub)]
        wide = parts[0].shape[axis]
        if wide * sub > hidden_local and windows:
            cut = partial(lax.slice_in_dim, axis=axis)
            parts = [
                cut(parts[0], 0, wide - overlap),
                cut(parts[0], wide - overlap, wide) + cut(parts[1], 0, overlap),
                cut(parts[1], overlap, wide),
            ]
        whole = jnp.concatenate(parts, axis=axis)
        return lax.slice_in_dim(whole, 0, hidden_local, axis=axis).astype(F32)

    grad_gate = windows_home(grad_gate, 2)
    grad_down = windows_home(after(grad_down, mid_slots), 1)
    mid_slots = after(mid_slots, grad_gate, grad_down)

    if copies > 1:
        mid_slots = mid_slots * jnp.repeat(turn, cap).astype(BF)[:, None]
    if kernels:
        grad_qpre, kv_low, grad_att_branch, att_gate_part, first_part = attend_back(
            experts,
            seqs,
            mid_slots,
            my_out,
            my_query,
            my_key_value,
            att_rows,
            att_hits,
            cosine,
            sine,
            saved,
        )
        att_gate_part = att_gate_part[:, 0]
    else:
        grad_mixed = dot("cd,md->cm", mid_slots, my_out)
        att_gate_part = jnp.sum(mixed.astype(F32) * grad_mixed, axis=1)
        grad_mixed = (grad_mixed * att_slot_gate).astype(BF).reshape(seqs, cap, heads, HD)
        grad_att_branch = (mid_slots.astype(F32) * att_slot_gate).astype(BF)
        grad_soft = dot("sqhd,skhd->shqk", grad_mixed, values)
        grad_values = dot("shqk,sqhd->skhd", probs_low, grad_mixed)
        grad_scores = (
            probs * (grad_soft - jnp.sum(probs * grad_soft, axis=-1, keepdims=True))
        ).astype(BF)
        grad_queries = dot("shqk,skhd->sqhd", grad_scores, keys) * scale
        grad_keys = dot("shqk,sqhd->skhd", grad_scores, queries) * scale
        grad_qpre = (
            rotate_back(grad_queries, slot_cosine[:, :, None, :], slot_sine[:, :, None, :])
            .astype(BF)
            .reshape(slots, heads_wide)
        )
        att_taken = dot("cm,dm->cd", grad_qpre, my_query)
        grad_kpre = rotate_back(
            grad_keys, cosine[None, :, None, :], sine[None, :, None, :]
        ).reshape(total, heads_wide)
        kv_low = jnp.concatenate([grad_kpre, grad_values.reshape(total, heads_wide)], axis=1)
        kv_low = kv_low.astype(BF)
        first_part = dot("tm,dm->td", kv_low, my_key_value) + att.give(att_taken.astype(BF))
    own_rows = lax.dynamic_slice_in_dim(all_in, exp_at * own_tokens, own_tokens, 0).astype(F32)
    own_scale_in = lax.rsqrt(jnp.mean(own_rows * own_rows, axis=1, keepdims=True) + EPS)
    own_gain_att = lax.dynamic_slice_in_dim(gain_att, layer_at * feats, feats, 0)
    grad_query_w = dot("cd,cm->dm", h1_slots, grad_qpre).astype(BF)
    grad_out_w = dot("cm,cd->md", mixed, grad_att_branch).astype(BF)
    grad_kv_w = dot("td,tm->dm", h1, kv_low).astype(BF)
    own_h2 = (own_unit_mid * own_gain_ffn[None, :]).astype(BF).astype(F32)
    gate_rows = slots // feats
    own_parts = jnp.concatenate(
        [
            att_gate_part.reshape(gate_rows, feats),
            norm_ffn_part[None],
            dot_exact("te,tf->ef", own_ffn_logits, own_h2),
        ],
        axis=0,
    )
    own_parts = jnp.pad(own_parts, ((0, -own_parts.shape[0] % 8), (0, 0)))
    own_unit_in = own_in * own_scale_in
    (grad_first,), tokens_out, told, (grad_out, grad_query, kv_first, kv_second) = exchanged(
        [after(first_part.astype(BF), up_second)],
        [jnp.zeros((own_tokens, feats), F32)],
        None,
        own_gain_att[None, :] * own_scale_in,
        (own_parts, own_unit_in, grad_mid.astype(BF), own_out.astype(BF)),
        "tokens",
        [
            ("rows_home", grad_out_w, heads_wide, heads_wide),
            ("columns_home", grad_query_w, heads_wide, heads_wide),
            ("columns_home", grad_kv_w[:, :heads_wide], heads_wide, 0),
            ("columns_home", grad_kv_w[:, heads_wide:], heads_wide, 0),
        ],
        3,
    )
    columns, first_tokens, mid_tokens, hidden_out = tokens_out
    att_logit_grads = logit_grads(
        att_gates, att.token_grads(gate_facts(told[:, :, :gate_rows]))
    )
    token_at = group_at * tokens
    rows_in = hidden_in.astype(F32)
    unit_in = lax.rsqrt(jnp.mean(rows_in * rows_in, axis=1, keepdims=True) + EPS)
    first_tokens = first_tokens.astype(F32) + router_rows(
        lax.dynamic_slice_in_dim(att_logit_grads, token_at, tokens, 0), route_att
    ) * (gain_att[None, :] * unit_in)
    unit_in = rows_in * unit_in
    grad_in = (
        mid_tokens.astype(F32)
        + first_tokens
        - unit_in * jnp.mean(first_tokens * unit_in, axis=1, keepdims=True)
    )


    def heads_home(back, axis):
        back = back.reshape(experts, head_parts, copies, *back.shape[1:])
        if copies > 1:
            back = jnp.sum(back.astype(F32), axis=2, keepdims=True)
        parts = [back[:, i, 0] for i in range(head_parts)]
        return jnp.concatenate(parts, axis=axis).astype(F32)

    def my_rows(table, axis):
        return lax.dynamic_slice_in_dim(table, group_at * rows_own, rows_own, axis)

    ffn_parts = jnp.sum(told[:, :, gate_rows : gate_rows + 1 + experts], axis=0)
    ffn_parts = my_rows(ffn_parts.transpose(1, 0, 2).reshape(1 + experts, width), 1)
    high = att_logit_grads.astype(BF)
    low = (att_logit_grads - high.astype(F32)).astype(BF)
    grad_router_att = dot("tf,te->fe", my_rows(h1, 1), jnp.concatenate([high, low], axis=1))
    grad_router_att = grad_router_att[:, :experts] + grad_router_att[:, experts:]
    norm_att = my_rows(jnp.sum(columns.reshape(experts, 8, width)[:, 0], axis=0), 0)
    norm_att = norm_att + jnp.sum(
        grad_router_att * my_rows(route_att, 0).astype(F32), axis=1
    ) / my_rows(gain_att, 0)
    grad_out = heads_home(grad_out, 1)
    grad_query = heads_home(grad_query, 2)
    grad_key, grad_value = (
        jnp.sum(heads_home(part, 2), axis=0) for part in (kv_first, kv_second)
    )
    return (
        hidden_out,
        grad_in,
        norm_att,
        grad_router_att,
        grad_query,
        grad_out,
        grad_key,
        grad_value,
        ffn_parts[0],
        ffn_parts[1:].T,
        grad_gate,
        windows_home(jnp.concatenate([up_first, up_second], axis=2), 2),
        grad_down,
    )


def solution(mesh):
    ctx, tp = mesh.shape["ctx"], mesh.shape["tp"]
    shard = mesh.shape["shard"]
    by_token, by_feature = P(GROUP, None), P(GROUP)
    columns, rows = P(None, GROUP, "tp"), P(None, "tp", GROUP)

    return jax.shard_map(
        partial(shards, (shard, ctx, tp)),
        mesh=mesh,
        in_specs=(
            by_token,
            by_token,
            by_token,
            P("shard"),
            by_feature,
            by_token,
            columns,
            rows,
            P(GROUP, "tp"),
            P(GROUP, "tp"),
            by_feature,
            by_token,
            columns,
            columns,
            rows,
            by_token,
        ),
        out_specs=(
            by_token,
            by_token,
            by_feature,
            by_token,
            columns,
            rows,
            P(GROUP, "tp"),
            P(GROUP, "tp"),
            by_feature,
            by_token,
            columns,
            columns,
            rows,
        ),
        check_vma=False,
    )
```
